32 devices in a mesh: dp: 16 (over z, x, core), tensor: 2 (over y).
Axes of the slice: x: 2, y: 2, z: 4, core: 2. Of those that a mesh axis runs over, the one named last changes fastest.
Arguments:
- tokens: bfloat16 [16384, 512], P('dp'), may hold values from -6 to 6
- cotangent: bfloat16 [16384, 512], P('dp'), may hold values from -6 to 6
- source_index: int32 [16384], P('dp'), may hold values from 0 to 16383, as said below
- tract_starts: int32 [256], P('dp'), may hold values from 0 to 1, as said below
- memory_rates: float32 [3, 256, 8], P(None, 'dp', 'tensor'), may hold values from 0 to 1
- mixer_gain: float32 [512], replicated, may hold values from 0.5 to 1.5
- query_proj: bfloat16 [512, 512], P(None, 'tensor'), may hold values from -0.375 to 0.375
- key_proj: bfloat16 [512, 512], P(None, 'tensor'), may hold values from -0.375 to 0.375
- value_proj: bfloat16 [512, 512], P(None, 'tensor'), may hold values from -0.5 to 0.5
- gate_proj: bfloat16 [512, 512], P(None, 'tensor'), may hold values from -0.25 to 0.25
- out_proj: bfloat16 [512, 512], P('tensor'), may hold values from -0.5 to 0.5
- persist_keys: bfloat16 [16, 512], P(None, 'tensor'), may hold values from -6 to 6
- persist_values: bfloat16 [16, 512], P(None, 'tensor'), may hold values from -6 to 6
- memory_first: float32 [8, 64, 128], P('tensor'), may hold values from -0.75 to 0.75
- memory_second: float32 [8, 128, 64], P('tensor'), may hold values from -0.5 to 0.5
- dense_gain: float32 [512], replicated, may hold values from 0.5 to 1.5
- dense_gate: bfloat16 [512, 1376], P(None, 'tensor'), may hold values from -0.25 to 0.25
- dense_lift: bfloat16 [512, 1376], P(None, 'tensor'), may hold values from -0.25 to 0.25
- dense_down: bfloat16 [1376, 512], P('tensor'), may hold values from -0.21875 to 0.21875
Outputs:
- layer_output: bfloat16 [16384, 512], P('dp')
- input_grad: bfloat16 [16384, 512], P('dp')
- grad_mixergain: float32 [512], replicated
- grad_queryproj: float32 [512, 512], P(None, 'tensor')
- grad_keyproj: float32 [512, 512], P(None, 'tensor')
- grad_valueproj: float32 [512, 512], P(None, 'tensor')
- grad_gateproj: float32 [512, 512], P(None, 'tensor')
- grad_outproj: float32 [512, 512], P('tensor')
- grad_persistkeys: float32 [16, 512], P(None, 'tensor')
- grad_persistvalues: float32 [16, 512], P(None, 'tensor')
- grad_memoryfirst: float32 [8, 64, 128], P('tensor')
- grad_memorysecond: float32 [8, 128, 64], P('tensor')
- grad_densegain: float32 [512], replicated
- grad_densegate: float32 [512, 1376], P(None, 'tensor')
- grad_denselift: float32 [512, 1376], P(None, 'tensor')
- grad_densedown: float32 [1376, 512], P('tensor')
The draws below stay inside these ranges and needn't reach their ends.
Inputs may be any that keep to these rules, and one draw needn't show every extreme that they name: `source_index`: A permutation; of the 1024 positions of each dp index, exactly 1024 / (number of dp indices) come from the rows of each dp index. `tract_starts`: the first update of each dp index starts a sequence, so sequences lie whole on one dp index; they are 256 to 1024 tokens long in whole multiples of 256, and every multiple of 1024 among a dp index's positions starts one. Some dp index holds sequences of 1024 tokens, and some dp index holds only sequences of 256 tokens.
All inputs are finite; a program needn't handle non-finite values.
Results may differ from the reference program's by a relative error of at most 0.013.
The reference program's roundings to bfloat16 on the way count: a program that leaves them out, or rounds other values in their place, can miss the bound.
Values may be sent and summed in bfloat16 or wider, within the bound.
A program may use at most 192 MiB of HBM per device.

```python
import math
import jax
import jax.numpy as jnp
from jax import lax

D = 512
HEADS = 8
HEAD_DIM = 64
FF = 1376
MEM_HIDDEN = 128
PERSIST = 16
STRETCH = 64
LMIN = 256
LONG = 1024
TOK_DEV = 1024
TOKENS = 16384
NCH = 256
N_DP = 16


def draw_source_index(key, part):
    key = jax.random.fold_in(key, 11)
    share = TOK_DEV // N_DP
    lookup_entries = jax.random.split(key, 2 * N_DP)
    within = jax.vmap(lambda sub_key: jax.random.permutation(sub_key, TOK_DEV))(lookup_entries[:N_DP]).astype(jnp.int32)
    offsets = jnp.arange(N_DP, dtype=jnp.int32) * TOK_DEV
    targets = (within + offsets[:, None]).reshape(N_DP, N_DP, share)
    listing = jnp.transpose(targets, (1, 0, 2)).reshape(N_DP, TOK_DEV)
    shuffle = jax.vmap(lambda sub_key: jax.random.permutation(sub_key, TOK_DEV))(lookup_entries[N_DP:])
    placed = jnp.take_along_axis(listing, shuffle, axis=1)
    return jnp.zeros((TOKENS,), jnp.int32).at[placed.reshape(-1)].set(jnp.arange(TOKENS, dtype=jnp.int32))


def draw_tract_starts(key, part):
    key = jax.random.fold_in(key, 23)
    units = TOK_DEV // LMIN
    span = LONG // LMIN
    per_unit = LMIN // STRETCH
    pick_key, coin_key = jax.random.split(key)
    chosen = jax.random.randint(pick_key, (), 0, N_DP)
    device = jnp.arange(N_DP)[:, None]
    index = jnp.arange(units)[None, :]
    coin = jax.random.randint(coin_key, (N_DP, units), 0, 2)
    forced = (index % span == 0) | (device == (chosen + 1) % N_DP)
    unit_start = jnp.where(forced, 1, jnp.where(device == chosen, 0, coin))
    starts = jnp.zeros((N_DP, units, per_unit), jnp.int32).at[:, :, 0].set(unit_start.astype(jnp.int32))
    return starts.reshape(-1)


def draw_memory_rates(key, part):
    key = jax.random.fold_in(key, 37)
    lookup_entries = jax.random.split(key, 5)
    tensor_extent_tuple = (NCH, HEADS)
    step_size = jax.random.uniform(lookup_entries[0], tensor_extent_tuple, jnp.float32, 0.003, 0.012)
    momentum = jax.random.uniform(lookup_entries[1], tensor_extent_tuple, jnp.float32, 0.3, 0.85)
    low_end, high_end = (0.005, 0.3)
    starting_level = jnp.exp(jax.random.uniform(lookup_entries[2], (N_DP, 1, HEADS), jnp.float32, math.log(low_end), math.log(high_end)))
    starting_level = jnp.broadcast_to(starting_level, (N_DP, NCH // N_DP, HEADS)).reshape(tensor_extent_tuple)
    recall_stretch_update = jax.random.randint(lookup_entries[3], tensor_extent_tuple, 0, 8) == 0
    decay_factor_vector = jnp.where(recall_stretch_update, jax.random.uniform(lookup_entries[4], tensor_extent_tuple, jnp.float32, 0.2, 0.5), starting_level)
    return jnp.stack([step_size, momentum, decay_factor_vector])


def level_of(stream_key, shape, pieces, smallest, largest):
    def one(dim, shards_of):
        draws = jax.random.uniform(jax.random.fold_in(jax.random.fold_in(stream_key, 6), dim), (shards_of,), jnp.float32, smallest / len(pieces), largest / len(pieces))
        return jnp.repeat(jnp.exp(draws), shape[dim] // shards_of).reshape((-1,) + (1,) * (len(shape) - dim - 1))

    loudness = one(*pieces[0])
    for cut in pieces[1:]:
        loudness = loudness * one(*cut)
    return loudness


def gaussian(rng, extent, scale, reach, pieces=(), held_as=jnp.bfloat16):
    level = level_of(rng, extent, pieces, -0.22, 0.18) if pieces else 1.0
    values = jax.random.normal(rng, extent, jnp.float32) * scale * level
    return jnp.minimum(jnp.maximum(values, -reach), reach).astype(held_as)


def setup_inputs(seed: int = 0) -> dict:
    arg_keys = jax.random.split(jax.random.key(seed), 20)
    return {
        "tokens": gaussian(arg_keys[0], (TOKENS, D), 1.0, 6.0, ((0, 16),)),
        "cotangent": gaussian(arg_keys[1], (TOKENS, D), 1.0, 6.0, ((0, 16),)),
        "source_index": draw_source_index(jax.random.fold_in(arg_keys[19], 71), 0),
        "tract_starts": draw_tract_starts(jax.random.fold_in(arg_keys[19], 71), 0),
        "memory_rates": draw_memory_rates(jax.random.fold_in(arg_keys[19], 71), 0),
        "mixer_gain": jnp.clip(1.0 + 0.1 * jax.random.normal(arg_keys[5], (D,), jnp.float32), 0.5, 1.5),
        "query_proj": gaussian(arg_keys[6], (D, HEADS * HEAD_DIM), (D // 2) ** -0.5, 0.375, ((1, 2),)),
        "key_proj": gaussian(arg_keys[7], (D, HEADS * HEAD_DIM), (D // 2) ** -0.5, 0.375, ((1, 2),)),
        "value_proj": gaussian(arg_keys[8], (D, HEADS * HEAD_DIM), (D // 4) ** -0.5, 0.5, ((1, 2),)),
        "gate_proj": gaussian(arg_keys[9], (D, HEADS * HEAD_DIM), D ** -0.5, 0.25, ((1, 2),)),
        "out_proj": gaussian(arg_keys[10], (HEADS * HEAD_DIM, D), (HEADS * HEAD_DIM // 4) ** -0.5, 0.5, ((0, 2),)),
        "persist_keys": gaussian(arg_keys[11], (PERSIST, HEADS * HEAD_DIM), 1.4, 6.0, ((1, 2),)),
        "persist_values": gaussian(arg_keys[12], (PERSIST, HEADS * HEAD_DIM), 2.0, 6.0, ((1, 2),)),
        "memory_first": gaussian(arg_keys[13], (HEADS, HEAD_DIM, MEM_HIDDEN), HEAD_DIM ** -0.5, 0.75, ((0, 2),), jnp.float32),
        "memory_second": gaussian(arg_keys[14], (HEADS, MEM_HIDDEN, HEAD_DIM), MEM_HIDDEN ** -0.5, 0.5, ((0, 2),), jnp.float32),
        "dense_gain": jnp.clip(1.0 + 0.1 * jax.random.normal(arg_keys[15], (D,), jnp.float32), 0.5, 1.5),
        "dense_gate": gaussian(arg_keys[16], (D, FF), D ** -0.5, 0.25, ((1, 2),)),
        "dense_lift": gaussian(arg_keys[17], (D, FF), D ** -0.5, 0.25, ((1, 2),)),
        "dense_down": gaussian(arg_keys[18], (FF, D), (FF // 2) ** -0.5, 0.21875, ((0, 2),)),
    }


EPSILON = 1e-06
MASKED = -1e+30

@jax.custom_vjp
def low(v):
    return lax.optimization_barrier(v.astype(jnp.bfloat16)).astype(jnp.float32)

@jax.custom_vjp
def low_back(v):
    return v

def low_keep(v):
    return (low(v), None)

def low_pass(kept, grad):
    return (grad,)

def back_keep(v):
    return (v, None)

def back_low(kept, grad):
    return (low(grad),)
low.defvjp(low_keep, low_pass)
low_back.defvjp(back_keep, back_low)

def round_both(value):
    return low_back(low(value))

def high_dot(left, right):
    return jnp.dot(left, right, precision=lax.Precision.HIGHEST)

def norm_scaled(value, gain):
    return value * lax.rsqrt(lax.optimization_barrier(jnp.mean(value * value, axis=-1, keepdims=True)) + EPSILON) * gain

def silu_slope(pre):
    sigma = jax.nn.sigmoid(pre)
    return sigma + pre * sigma * (1.0 - sigma)

def memory_head(query, lookup_entries, values, starts, rates, first_w, latter_weight_matrix):
    nsteps = starts.shape[0]
    length = query.shape[0] // nsteps
    width = query.shape[1]
    query_c = query.reshape(nsteps, length, width)
    keys_c = lookup_entries.reshape(nsteps, length, width)
    values_c = values.reshape(nsteps, length, width)
    zero_one = jnp.zeros_like(first_w)
    zero_two = jnp.zeros_like(latter_weight_matrix)

    def advance(carry, item):
        w_one, w_two, s_one, s_two = carry
        q_rows, k_rows, v_rows, begin, rate = item
        fresh = begin > 0
        w_one = jnp.where(fresh, first_w, w_one)
        w_two = jnp.where(fresh, latter_weight_matrix, w_two)
        s_one = jnp.where(fresh, zero_one, s_one)
        s_two = jnp.where(fresh, zero_two, s_two)
        recall = high_dot(jax.nn.silu(high_dot(q_rows, w_one)), w_two)
        pre = high_dot(k_rows, w_one)
        active = jax.nn.silu(pre)
        error = high_dot(active, w_two) - v_rows
        grad_two = high_dot(active.T, error) / length
        grad_one = high_dot(k_rows.T, high_dot(error, w_two.T) * silu_slope(pre)) / length
        s_one = rate[1] * s_one - rate[0] * grad_one
        s_two = rate[1] * s_two - rate[0] * grad_two
        w_one = (1.0 - rate[2]) * w_one + s_one
        w_two = (1.0 - rate[2]) * w_two + s_two
        return ((w_one, w_two, s_one, s_two), recall)
    _, recalls = lax.scan(advance, (first_w, latter_weight_matrix, zero_one, zero_two), (query_c, keys_c, values_c, starts, rates))
    return recalls.reshape(query.shape)

def attention_block(qblock, query_pos, seq_key, seq_value, persist_key, persist_value, seq_id):
    factor = HEAD_DIM ** (-0.5)
    key_pos = jnp.arange(seq_key.shape[0])
    visible = (seq_id[None, :] == seq_id[query_pos][:, None]) & (key_pos[None, :] <= query_pos[:, None])
    s_seq = low_back(jnp.einsum('qhd,khd->hqk', qblock, seq_key, precision=lax.Precision.HIGHEST) * factor)
    s_per = low_back(jnp.einsum('qhd,khd->hqk', qblock, persist_key, precision=lax.Precision.HIGHEST) * factor)
    s_seq = jnp.where(visible[None], s_seq, MASKED)
    peak = jnp.maximum(lax.optimization_barrier(jnp.max(s_seq, axis=-1, keepdims=True)), lax.optimization_barrier(jnp.max(s_per, axis=-1, keepdims=True)))
    e_seq = jnp.exp(s_seq - peak)
    e_per = jnp.exp(s_per - peak)
    totals = lax.optimization_barrier(jnp.sum(e_seq, axis=-1, keepdims=True)) + lax.optimization_barrier(jnp.sum(e_per, axis=-1, keepdims=True))
    result = jnp.einsum('hqk,khd->qhd', low(e_seq / totals), seq_value, precision=lax.Precision.HIGHEST)
    return result + jnp.einsum('hqk,khd->qhd', low(e_per / totals), persist_value, precision=lax.Precision.HIGHEST)

def group_forward(xgroup, starts, rates, params):
    mixer_gain, query_proj, key_proj, value_proj, gate_proj, out_proj, persist_keys, persist_values, memory_first, memory_second, dense_gain, dense_gate, dense_lift, dense_down = params
    count = xgroup.shape[0]
    heads = query_proj.shape[1] // HEAD_DIM
    h_one = low(norm_scaled(xgroup, mixer_gain))
    query = round_both(high_dot(h_one, query_proj))
    lookup_entries = round_both(high_dot(h_one, key_proj))
    values = round_both(high_dot(h_one, value_proj))
    gate = jax.nn.sigmoid(low_back(high_dot(h_one, gate_proj)))
    seq_id = jnp.cumsum(jnp.repeat(starts, count // starts.shape[0]))
    query3 = query.reshape(count, heads, HEAD_DIM)
    keys3 = lookup_entries.reshape(count, heads, HEAD_DIM)
    values3 = values.reshape(count, heads, HEAD_DIM)
    pkeys3 = persist_keys.reshape(-1, heads, HEAD_DIM)
    lasting_payloads3 = persist_values.reshape(-1, heads, HEAD_DIM)
    block = min(512, count)
    qblocks = query3.reshape(count // block, block, heads, HEAD_DIM)
    positions = jnp.arange(count).reshape(count // block, block)
    saved = jax.checkpoint(attention_block)
    attended = lax.map(lambda item: saved(item[0], item[1], keys3, values3, pkeys3, lasting_payloads3, seq_id), (qblocks, positions))
    attended = attended.reshape(count, heads * HEAD_DIM)

    def heads_first(value):
        return value.reshape(count, heads, HEAD_DIM).transpose(1, 0, 2)
    recall = jax.vmap(memory_head, in_axes=(0, 0, 0, None, 0, 0, 0))(heads_first(query), heads_first(lookup_entries), heads_first(values), starts, jnp.transpose(rates, (2, 1, 0)), memory_first, memory_second)
    recall = recall.transpose(1, 0, 2).reshape(count, heads * HEAD_DIM)
    mixed = round_both(attended + gate * recall)
    resid = xgroup + low_back(high_dot(mixed, out_proj))
    h_two = low(norm_scaled(resid, dense_gain))
    gated = low_back(high_dot(h_two, dense_gate))
    lifted = low_back(high_dot(h_two, dense_lift))
    hidden = low(jax.nn.silu(gated) * lifted)
    return resid + low_back(high_dot(hidden, dense_down))

def reference(tokens, cotangent, source_index, tract_starts, memory_rates, mixer_gain, query_proj, key_proj, value_proj, gate_proj, out_proj, persist_keys, persist_values, memory_first, memory_second, dense_gain, dense_gate, dense_lift, dense_down):
    placing = jnp.argsort(source_index)
    groups_starts = tract_starts.reshape(N_DP, -1)
    groups_rates = memory_rates.reshape(3, N_DP, -1, HEADS).transpose(1, 0, 2, 3)

    def forward(xgiven, params):
        xseq = xgiven[source_index].reshape(N_DP, TOK_DEV, D)

        def advance(carry, item):
            return (carry, group_forward(item[0], item[1], item[2], carry))
        _, outs = lax.scan(jax.checkpoint(advance), params, (xseq, groups_starts, groups_rates))
        return outs.reshape(TOKENS, D)[placing]
    params = tuple((weight.astype(jnp.float32) for weight in (mixer_gain, query_proj, key_proj, value_proj, gate_proj, out_proj, persist_keys, persist_values, memory_first, memory_second, dense_gain, dense_gate, dense_lift, dense_down)))
    result, backward = jax.vjp(forward, tokens.astype(jnp.float32), params)
    x_grad, grads = backward(cotangent.astype(jnp.float32))
    return (result.astype(jnp.bfloat16), x_grad.astype(jnp.bfloat16), grads[0], grads[1], grads[2], grads[3], grads[4], grads[5], grads[6], grads[7], grads[8], grads[9], grads[10], grads[11], grads[12], grads[13])
```

```python
import jax
import jax.numpy as jnp
from jax import lax
from jax.experimental import pallas as pl
from jax.experimental.pallas import tpu as pltpu
from jax.sharding import PartitionSpec as P

HEAD_DIM = 64


EPSILON = 1e-06
MASKED = -1e30


def product(left, right):
    return jnp.dot(left, right, preferred_element_type=jnp.float32)


def norm_forward(value):
    factor = lax.rsqrt(jnp.mean(value * value, axis=-1, keepdims=True) + EPSILON)
    return (value * factor, factor)


def norm_backward(grad, normed, factor, gain):
    inner = grad * gain
    back = factor * (inner - normed * jnp.mean(inner * normed, axis=-1, keepdims=True))
    return (back, jnp.sum(grad * normed, axis=0))


F32, BF16 = jnp.float32, jnp.bfloat16
PAIR = 2 * HEAD_DIM
ROWS = 256
STRETCH = 64


def nn(a, b):
    return lax.dot_general(a, b, (((1,), (0,)), ((), ())), preferred_element_type=F32)


def nt(a, b):
    return lax.dot_general(a, b, (((1,), (1,)), ((), ())), preferred_element_type=F32)


def tn(a, b):
    return lax.dot_general(a, b, (((0,), (0,)), ((), ())), preferred_element_type=F32)


def sigmoid(v):
    return 1.0 / (1.0 + jnp.exp(-v))


def lanes_of(half, rows=1):
    return (lax.broadcasted_iota(jnp.int32, (rows, PAIR), 1) // HEAD_DIM) == half


def keep(value, half):
    return jnp.where(lanes_of(half), value, jnp.zeros_like(value))


def both(value):
    return jnp.concatenate([keep(value, 0), keep(value, 1)], axis=0)


def joined(stacked):
    rows = stacked.shape[0] // 2
    return jnp.where(lanes_of(0), stacked[:rows], stacked[rows:])


def scaled(pair, scalars):
    return jnp.concatenate([pair[:HEAD_DIM] * scalars[0], pair[HEAD_DIM:] * scalars[1]], axis=0)


def same_sequence(starts, early, late, per):
    count = jnp.int32(0)
    for c in range(early * per + 1, late * per + 1):
        count = count + starts[c]
    return count == 0


def earlier(s, starts, kb, qb, per):
    open_all = jnp.where(same_sequence(starts, kb, qb, per), 0.0, MASKED).astype(F32)
    open_head = jnp.where(starts[kb * per] > 0, MASKED, open_all).astype(F32)
    row = lax.broadcasted_iota(jnp.int32, (STRETCH, s.shape[1]), 0)
    top = s[:STRETCH] + jnp.where(row < STRETCH - 1, open_head, open_all)
    return jnp.concatenate([top, s[STRETCH:] + open_all], axis=0)


def fill_diagonal(ref, start):
    key = lax.broadcasted_iota(jnp.int32, ref.shape, 0)
    query = lax.broadcasted_iota(jnp.int32, ref.shape, 1)
    plain = jnp.where(key <= query, 0.0, MASKED)
    opening = jnp.where((key == query) | ((key < query) & (key >= STRETCH - 1)), 0.0, MASKED)
    ref[...] = jnp.where(start > 0, opening, plain).astype(F32)


def forward_kernel(
    starts, rates, tok, gain, w, pk, pvt, first, second,
    h1, q, k, v, gate, recall, mixed, kt, lse, a_all, c_all, pre_all, e_all, u_all, atth,
    vt, att, diagonal, a_s, c_s, sa_s, sc_s,
):
    count = tok.shape[0]
    pairs = first.shape[0]
    wide = pairs * PAIR
    per = ROWS // STRETCH

    def project(b, _):
        rows = pl.ds(pl.multiple_of(b * ROWS, ROWS), ROWS)
        x = tok[rows, :].astype(F32)
        factor = lax.rsqrt(jnp.mean(x * x, axis=-1, keepdims=True) + EPSILON)
        h = (x * factor * gain[...]).astype(BF16)
        h1[rows, :] = h
        for part, ref in ((0, q), (1, k), (2, v)):
            made = nn(h, w[:, part * wide:(part + 1) * wide])
            low = made.astype(BF16)
            for p in range(pairs):
                ref[p, rows, :] = low[:, p * PAIR:(p + 1) * PAIR]
            if part > 0:
                made_t = jnp.transpose(made).astype(BF16)
                target = kt if part == 1 else vt
                for h_i in range(2 * pairs):
                    target[h_i, :, rows] = made_t[h_i * HEAD_DIM:(h_i + 1) * HEAD_DIM]
        g = sigmoid(nn(h, w[:, 3 * wide:]))
        for p in range(pairs):
            gate[p, rows, :] = g[:, p * PAIR:(p + 1) * PAIR]
        return 0

    lax.fori_loop(0, count // ROWS, project, 0)
    a_s[...] = first[...]
    c_s[...] = second[...]
    sa_s[...] = jnp.zeros_like(sa_s)
    sc_s[...] = jnp.zeros_like(sc_s)

    def memory_step(t):
        rows = pl.ds(pl.multiple_of(t * STRETCH, STRETCH), STRETCH)
        fresh = starts[t] > 0
        for p in range(pairs):
            a = jnp.where(fresh, first[p], a_s[p])
            c = jnp.where(fresh, second[p], c_s[p])
            sa = jnp.where(fresh, 0.0, sa_s[p])
            sc = jnp.where(fresh, 0.0, sc_s[p])
            ab, cb = a.astype(BF16), c.astype(BF16)
            a_all[t, p] = ab
            c_all[t, p] = cb
            km = both(k[p, rows, :])
            lhs = jnp.concatenate([both(q[p, rows, :]), km], axis=0)
            pre = nn(lhs, ab)
            pre_all[t, p] = pre
            sig = sigmoid(pre)
            act = pre * sig
            actb = act.astype(BF16)
            out = nt(actb, cb)
            recall[p, rows, :] = joined(out[:PAIR])
            e = joined(out[PAIR:]) - v[p, rows, :].astype(F32)
            eb = e.astype(BF16)
            e_all[p, rows, :] = eb
            em = both(eb)
            u = nn(em, cb)
            u_all[t, p] = u
            sigk, actk = sig[PAIR:], act[PAIR:]
            wgt = (u * (sigk + actk * (1.0 - sigk))).astype(BF16)
            ga = tn(km, wgt)
            gc = tn(em, actb[PAIR:])
            th = [rates[0, t, 2 * p + i] * (1.0 / STRETCH) for i in range(2)]
            eta = [rates[1, t, 2 * p + i] for i in range(2)]
            al = [1.0 - rates[2, t, 2 * p + i] for i in range(2)]
            sa = scaled(sa, eta) - scaled(ga, th)
            sc = scaled(sc, eta) - scaled(gc, th)
            sa_s[p] = sa
            sc_s[p] = sc
            a_s[p] = scaled(a, al) + sa
            c_s[p] = scaled(c, al) + sc

    def attention_unit(qb, head):
        p, half = head // 2, head % 2
        rows = pl.ds(qb * ROWS, ROWS)
        qh = keep(q[p, rows, :], half) * jnp.asarray(HEAD_DIM ** -0.5, BF16)
        scores = []
        for kb in range(qb + 1):
            s = nt(k[p, kb * ROWS:(kb + 1) * ROWS, :], qh)
            if kb == qb:
                s = s + diagonal[...]
            else:
                s = earlier(s, starts, kb, qb, per)
            scores.append(s)
        sp = nt(pk[p], qh)
        peak = jnp.max(sp, axis=0, keepdims=True)
        for s in scores:
            peak = jnp.maximum(peak, jnp.max(s, axis=0, keepdims=True))
        ep = jnp.exp(sp - peak)
        total = jnp.sum(ep, axis=0, keepdims=True)
        out = nn(pvt[head], ep.astype(BF16))
        for kb, s in enumerate(scores):
            e = jnp.exp(s - peak)
            total = total + jnp.sum(e, axis=0, keepdims=True)
            out = out + nn(vt[head, :, kb * ROWS:(kb + 1) * ROWS], e.astype(BF16))
        att[head, :, rows] = out * (1.0 / total)
        lse[head, :, rows] = peak + jnp.log(total)

    heads = 2 * pairs
    for qb in range(count // ROWS):
        fill_diagonal(diagonal, starts[qb * per])

        def run(i, _, qb=qb):
            memory_step(qb * per + i)
            attention_unit(qb, i)
            return 0
        lax.fori_loop(0, per, run, 0)
    for b in range(count // ROWS):
        rows = pl.ds(b * ROWS, ROWS)
        for p in range(pairs):
            got = jnp.concatenate([att[2 * p, :, rows], att[2 * p + 1, :, rows]], axis=0)
            wide_att = jnp.transpose(got)
            atth[p, rows, :] = wide_att
            mixed[rows, p * PAIR:(p + 1) * PAIR] = (wide_att + gate[p, rows, :] * recall[p, rows, :]).astype(BF16)


def backward_kernel(
    starts, rates, bm, q, k, v, gate, recall, kt, pk, pkt, pv, lse, a_all, c_all, pre_all, e_all, u_all, atth,
    dq, dk, dv, dg, dpk, dpv, dfirst, dsecond,
    dqt, dd, dks, dvs, mq, bmp, diagonal, da_s, dc_s, dsa_s, dsc_s,
):
    count = bm.shape[0]
    pairs = q.shape[0]
    heads = 2 * pairs
    per = ROWS // STRETCH
    nblocks = count // ROWS
    ones = [jnp.where(lanes_of(i, 8), 1.0, 0.0).astype(F32) for i in range(2)]
    for b in range(nblocks):
        rows = pl.ds(b * ROWS, ROWS)
        for p in range(pairs):
            gb = bm[rows, p * PAIR:(p + 1) * PAIR]
            bmp[p, rows, :] = gb
            g = gb.astype(F32)
            inner = g * atth[p, rows, :]
            for i in range(2):
                row = lax.dot_general(ones[i], inner, (((1,), (1,)), ((), ())), precision=lax.Precision.HIGHEST, preferred_element_type=F32)
                dd[2 * p + i, :, rows] = row[:1]
            gt = gate[p, rows, :]
            dg[rows, p * PAIR:(p + 1) * PAIR] = (g * recall[p, rows, :] * gt * (1.0 - gt)).astype(BF16)
    for ref in (dpk, dpv, dfirst, dsecond, dks, dvs, da_s, dc_s, dsa_s, dsc_s):
        ref[...] = jnp.zeros_like(ref)

    def memory_step(t):
        rows = pl.ds(pl.multiple_of(t * STRETCH, STRETCH), STRETCH)
        fresh = starts[t] > 0
        for p in range(pairs):
            th = [rates[0, t, 2 * p + i] * (-1.0 / STRETCH) for i in range(2)]
            eta = [rates[1, t, 2 * p + i] for i in range(2)]
            al = [1.0 - rates[2, t, 2 * p + i] for i in range(2)]
            da, dc = da_s[p], dc_s[p]
            dsa = dsa_s[p] + da
            dsc = dsc_s[p] + dc
            dga = scaled(dsa, th).astype(BF16)
            dgc = scaled(dsc, th).astype(BF16)
            ab, cb = a_all[t, p], c_all[t, p]
            km, qm = both(k[p, rows, :]), both(q[p, rows, :])
            em = both(e_all[p, rows, :])
            pre = pre_all[t, p]
            sig = sigmoid(pre)
            act = pre * sig
            actb = act.astype(BF16)
            slope = sig + act * (1.0 - sig)
            sigk, prek, slopek = sig[PAIR:], pre[PAIR:], slope[PAIR:]
            u = u_all[t, p]
            curve = sigk * (1.0 - sigk) * (2.0 + prek * (1.0 - 2.0 * sigk))
            wgt = (u * slopek).astype(BF16)
            back = bmp[p, rows, :].astype(F32) * gate[p, rows, :]
            rm = both(back.astype(BF16))
            dpre_q = (nn(rm, cb) * slope[:PAIR]).astype(BF16)
            mq[0, p, rows, :] = joined(nt(dpre_q, ab))
            dw = nn(km, dga)
            du = (dw * slopek).astype(BF16)
            cc = jnp.concatenate([dgc, cb], axis=1)
            de = joined(nt(jnp.concatenate([actb[PAIR:], du], axis=1), cc))
            mq[2, p, rows, :] = -de
            dem = both(de.astype(BF16))
            dsk = nn(jnp.concatenate([em, dem], axis=1), jnp.concatenate([dgc, cb], axis=0))
            dpre = (dsk * slopek + dw * u * curve).astype(BF16)
            mq[1, p, rows, :] = joined(nt(jnp.concatenate([wgt, dpre], axis=1), jnp.concatenate([dga, ab], axis=1)))
            ga = tn(jnp.concatenate([km, qm], axis=0), jnp.concatenate([dpre, dpre_q], axis=0))
            gc = tn(jnp.concatenate([em, dem], axis=0), jnp.concatenate([du, actb[PAIR:]], axis=0))
            gc = gc + tn(rm, actb[:PAIR])
            da = scaled(da, al) + ga
            dc = scaled(dc, al) + gc
            dfirst[p] = dfirst[p] + jnp.where(fresh, da, 0.0)
            dsecond[p] = dsecond[p] + jnp.where(fresh, dc, 0.0)
            da_s[p] = jnp.where(fresh, 0.0, da)
            dc_s[p] = jnp.where(fresh, 0.0, dc)
            dsa_s[p] = jnp.where(fresh, 0.0, scaled(dsa, eta))
            dsc_s[p] = jnp.where(fresh, 0.0, scaled(dsc, eta))

    def attention_unit(qb, head):
        p, half = head // 2, head % 2
        rows = pl.ds(qb * ROWS, ROWS)
        qh = keep(q[p, rows, :], half) * jnp.asarray(HEAD_DIM ** -0.5, BF16)
        gh = keep(bmp[p, rows, :], half)
        lrow, drow = lse[head, :, rows], dd[head, :, rows]
        acc = jnp.zeros((HEAD_DIM, ROWS), F32)
        for kb in range(qb + 1):
            krows = slice(kb * ROWS, (kb + 1) * ROWS)
            s = nt(k[p, krows, :], qh) - lrow
            if kb == qb:
                s = s + diagonal[...]
            else:
                s = earlier(s, starts, kb, qb, per)
            prob = jnp.exp(s)
            ds = (prob * (nt(v[p, krows, :], gh) - drow)).astype(BF16)
            dvs[p, krows, :] = dvs[p, krows, :] + nn(prob.astype(BF16), gh)
            dks[p, krows, :] = dks[p, krows, :] + nn(ds, qh)
            acc = acc + nn(kt[head, :, krows], ds)
        prob = jnp.exp(nt(pk[p], qh) - lrow)
        ds = (prob * (nt(pv[p], gh) - drow)).astype(BF16)
        dpv[p] = dpv[p] + nn(prob.astype(BF16), gh)
        dpk[p] = dpk[p] + nn(ds, qh)
        acc = acc + nn(pkt[head], ds)
        dqt[head, :, rows] = acc * (HEAD_DIM ** -0.5)

    for qb in reversed(range(nblocks)):
        fill_diagonal(diagonal, starts[qb * per])

        def run(i, _, qb=qb):
            memory_step(qb * per + per - 1 - i)
            attention_unit(qb, i)
            return 0
        lax.fori_loop(0, per, run, 0)
    for b in range(nblocks):
        rows = pl.ds(b * ROWS, ROWS)
        for p in range(pairs):
            cols = slice(p * PAIR, (p + 1) * PAIR)
            got = jnp.concatenate([dqt[2 * p, :, rows], dqt[2 * p + 1, :, rows]], axis=0)
            dq[rows, cols] = (jnp.transpose(got) + mq[0, p, rows, :]).astype(BF16)
            dk[rows, cols] = (dks[p, rows, :] + mq[1, p, rows, :]).astype(BF16)
            dv[rows, cols] = (dvs[p, rows, :] + mq[2, p, rows, :]).astype(BF16)


def shape(*dims, dtype=F32):
    return jax.ShapeDtypeStruct(dims, dtype)


VMEM = pl.BlockSpec(memory_space=pltpu.VMEM)
SMEM = pl.BlockSpec(memory_space=pltpu.SMEM)
LIMIT = 56 * 1024 * 1024


def mixer_forward(starts, rates, tok, gain, w, pk, pvt, first, second):
    count, width = tok.shape
    pairs = first.shape[0]
    heads, steps = 2 * pairs, starts.shape[0]
    flat = lambda dtype: shape(pairs, count, PAIR, dtype=dtype)
    outs = (
        shape(count, width, dtype=BF16), flat(BF16), flat(BF16), flat(BF16), flat(F32), flat(F32),
        shape(count, pairs * PAIR, dtype=BF16), shape(heads, HEAD_DIM, count, dtype=BF16), shape(heads, 1, count),
        shape(steps, pairs, PAIR, PAIR, dtype=BF16), shape(steps, pairs, PAIR, PAIR, dtype=BF16),
        shape(steps, pairs, 2 * PAIR, PAIR), flat(BF16), shape(steps, pairs, PAIR, PAIR), flat(F32),
    )
    state = pltpu.VMEM((pairs, PAIR, PAIR), F32)
    return pl.pallas_call(
        forward_kernel,
        out_shape=outs,
        in_specs=[SMEM, SMEM] + [VMEM] * 7,
        out_specs=[VMEM] * len(outs),
        scratch_shapes=[
            pltpu.VMEM((heads, HEAD_DIM, count), BF16), pltpu.VMEM((heads, HEAD_DIM, count), F32),
            pltpu.VMEM((ROWS, ROWS), F32), state, state, state, state,
        ],
        compiler_params=pltpu.CompilerParams(vmem_limit_bytes=LIMIT),
        name="mixer_forward",
    )(starts, rates, tok, gain, w, pk, pvt, first, second)


def mixer_backward(starts, rates, bm, q, k, v, gate, recall, kt, pk, pkt, pv, lse, a_all, c_all, pre_all, e_all, u_all, atth):
    count, wide = bm.shape
    pairs = q.shape[0]
    heads = 2 * pairs
    outs = (
        shape(count, wide, dtype=BF16), shape(count, wide, dtype=BF16), shape(count, wide, dtype=BF16), shape(count, wide, dtype=BF16),
        shape(*pk.shape), shape(*pv.shape), shape(pairs, PAIR, PAIR), shape(pairs, PAIR, PAIR),
    )
    state = pltpu.VMEM((pairs, PAIR, PAIR), F32)
    flat = pltpu.VMEM((pairs, count, PAIR), F32)
    return pl.pallas_call(
        backward_kernel,
        out_shape=outs,
        in_specs=[SMEM, SMEM] + [VMEM] * 17,
        out_specs=[VMEM] * len(outs),
        scratch_shapes=[
            pltpu.VMEM((heads, HEAD_DIM, count), F32), pltpu.VMEM((heads, 1, count), F32), flat, flat,
            pltpu.VMEM((3, pairs, count, PAIR), F32), pltpu.VMEM((pairs, count, PAIR), BF16),
            pltpu.VMEM((ROWS, ROWS), F32), state, state, state, state,
        ],
        compiler_params=pltpu.CompilerParams(vmem_limit_bytes=LIMIT),
        name="mixer_backward",
    )(starts, rates, bm, q, k, v, gate, recall, kt, pk, pkt, pv, lse, a_all, c_all, pre_all, e_all, u_all, atth)


def body(
    tokens,
    cotangent,
    source_index,
    tract_starts,
    memory_rates,
    mixer_gain,
    query_proj,
    key_proj,
    value_proj,
    gate_proj,
    out_proj,
    persist_keys,
    persist_values,
    memory_first,
    memory_second,
    dense_gain,
    dense_gate,
    dense_lift,
    dense_down,
):
    count = tokens.shape[0]
    width = tokens.shape[1]
    peers = lax.axis_size("dp")
    share = count // peers
    arrival = jnp.argsort(source_index)
    wanted = (source_index[arrival] % count).reshape(peers, share)
    asked = lax.all_to_all(wanted, "dp", split_axis=0, concat_axis=0, tiled=True).reshape(count)
    got_tokens, got_cot = (
        lax.all_to_all(
            tokens[asked].reshape(peers, share, width),
            "dp",
            split_axis=0,
            concat_axis=0,
            tiled=True,
        ),
        lax.all_to_all(
            cotangent[asked].reshape(peers, share, width),
            "dp",
            split_axis=0,
            concat_axis=0,
            tiled=True,
        ),
    )
    placing = jnp.argsort(arrival)
    seq_tokens = got_tokens.reshape(count, width)[placing]
    seq_cot = got_cot.reshape(count, width)[placing]
    seq_x = seq_tokens.astype(jnp.float32)
    first_norm, factor_one = norm_forward(seq_x)
    pairs = query_proj.shape[1] // PAIR
    by_pair = lambda value: value.reshape(-1, pairs, PAIR).transpose(1, 0, 2)
    by_head = lambda value: value.T.reshape(2 * pairs, HEAD_DIM, -1)
    weights = jnp.concatenate([query_proj, key_proj, value_proj, gate_proj], axis=1)
    pk, pv = by_pair(persist_keys), by_pair(persist_values)
    first = memory_first.reshape(pairs, PAIR, PAIR)
    second = memory_second.transpose(0, 2, 1).reshape(pairs, PAIR, PAIR)
    h_one, query, keys, values, gate, recall, mixed, keys_t, lse, a_all, c_all, pre_all, e_all, u_all, attended = mixer_forward(
        tract_starts, memory_rates, seq_tokens, mixer_gain[None], weights, pk, by_head(persist_values), first, second
    )
    first_out = lax.psum(product(mixed, out_proj), "tensor")
    resid = seq_x + first_out
    norm_two, factor_two = norm_forward(resid)
    h_two = (norm_two * dense_gain).astype(jnp.bfloat16)
    gated = product(h_two, dense_gate)
    lifted = product(h_two, dense_lift)
    sigma = jax.nn.sigmoid(gated)
    active = gated * sigma
    hidden = (active * lifted).astype(jnp.bfloat16)
    second_out = lax.psum(product(hidden, dense_down).astype(jnp.bfloat16), "tensor").astype(
        jnp.float32
    )
    seq_out = (resid + second_out).astype(jnp.bfloat16)
    grad_down = product(hidden.T, seq_cot)
    back_hidden = product(seq_cot, dense_down.T)
    back_gated = (back_hidden * lifted * (sigma + gated * sigma * (1.0 - sigma))).astype(
        jnp.bfloat16
    )
    back_lifted = (back_hidden * active).astype(jnp.bfloat16)
    grad_gate = product(h_two.T, back_gated)
    grad_lift = product(h_two.T, back_lifted)
    back_two = lax.psum(
        product(back_gated, dense_gate.T) + product(back_lifted, dense_lift.T), "tensor"
    )
    back_norm_two, grad_dgain = norm_backward(back_two, norm_two, factor_two, dense_gain)
    residual_gradient = seq_cot.astype(jnp.float32) + back_norm_two
    back_first = residual_gradient.astype(jnp.bfloat16)
    grad_out = product(mixed.T, back_first)
    back_mixed = product(back_first, out_proj.T).astype(jnp.bfloat16)
    back_query, back_keys, cotangent_payloads, back_gate, grad_pk, grad_pv, grad_first, grad_second = mixer_backward(
        tract_starts, memory_rates, back_mixed, query, keys, values, gate, recall, keys_t, pk, by_head(persist_keys), pv,
        lse, a_all, c_all, pre_all, e_all, u_all, attended,
    )
    grad_first = grad_first.reshape(memory_first.shape)
    grad_second = grad_second.reshape(memory_first.shape).transpose(0, 2, 1)
    grad_query = product(h_one.T, back_query)
    grad_key = product(h_one.T, back_keys)
    grad_value = product(h_one.T, cotangent_payloads)
    grad_gproj = product(h_one.T, back_gate)
    back_one = lax.psum(
        product(back_query, query_proj.T)
        + product(back_keys, key_proj.T)
        + product(cotangent_payloads, value_proj.T)
        + product(back_gate, gate_proj.T),
        "tensor",
    )
    back_norm_one, grad_mgain = norm_backward(back_one, first_norm, factor_one, mixer_gain)
    back_x = (residual_gradient + back_norm_one).astype(jnp.bfloat16)
    grad_pkeys = grad_pk.transpose(1, 0, 2).reshape(persist_keys.shape)
    grad_pvalues = grad_pv.transpose(1, 0, 2).reshape(persist_values.shape)
    (
        grad_mgain,
        grad_query,
        grad_key,
        grad_value,
        grad_gproj,
        grad_out,
        grad_pkeys,
        grad_pvalues,
        grad_first,
        grad_second,
        grad_dgain,
        grad_gate,
        grad_lift,
        grad_down,
    ) = lax.psum(
        (
            grad_mgain,
            grad_query,
            grad_key,
            grad_value,
            grad_gproj,
            grad_out,
            grad_pkeys,
            grad_pvalues,
            grad_first,
            grad_second,
            grad_dgain,
            grad_gate,
            grad_lift,
            grad_down,
        ),
        "dp",
    )
    ret_out, ret_grad = (
        lax.all_to_all(
            seq_out[arrival].reshape(peers, share, width),
            "dp",
            split_axis=0,
            concat_axis=0,
            tiled=True,
        ),
        lax.all_to_all(
            back_x[arrival].reshape(peers, share, width),
            "dp",
            split_axis=0,
            concat_axis=0,
            tiled=True,
        ),
    )
    undo = jnp.argsort(asked)
    layer_output = ret_out.reshape(count, width)[undo]
    input_grad = ret_grad.reshape(count, width)[undo]
    return (
        layer_output,
        input_grad,
        grad_mgain,
        grad_query,
        grad_key,
        grad_value,
        grad_gproj,
        grad_out,
        grad_pkeys,
        grad_pvalues,
        grad_first,
        grad_second,
        grad_dgain,
        grad_gate,
        grad_lift,
        grad_down,
    )


def solution(mesh):
    in_specs = (
        P("dp", None),
        P("dp", None),
        P("dp"),
        P("dp"),
        P(None, "dp", "tensor"),
        P(),
        P(None, "tensor"),
        P(None, "tensor"),
        P(None, "tensor"),
        P(None, "tensor"),
        P("tensor", None),
        P(None, "tensor"),
        P(None, "tensor"),
        P("tensor", None, None),
        P("tensor", None, None),
        P(),
        P(None, "tensor"),
        P(None, "tensor"),
        P("tensor", None),
    )
    out_specs = (
        P("dp", None),
        P("dp", None),
        P(),
        P(None, "tensor"),
        P(None, "tensor"),
        P(None, "tensor"),
        P(None, "tensor"),
        P("tensor", None),
        P(None, "tensor"),
        P(None, "tensor"),
        P("tensor", None, None),
        P("tensor", None, None),
        P(),
        P(None, "tensor"),
        P(None, "tensor"),
        P("tensor", None),
    )
    return jax.shard_map(body, mesh=mesh, in_specs=in_specs, out_specs=out_specs, check_vma=False)
```

```python
import jax
import jax.numpy as jnp
from jax import lax
from jax.experimental import pallas as pl
from jax.experimental.pallas import tpu as pltpu
from jax.sharding import PartitionSpec as P

HEAD_DIM = 64


EPSILON = 1e-06
MASKED = -1e30


def product(left, right):
    return jnp.dot(left, right, preferred_element_type=jnp.float32)


def norm_forward(value):
    factor = lax.rsqrt(jnp.mean(value * value, axis=-1, keepdims=True) + EPSILON)
    return (value * factor, factor)


def norm_backward(grad, normed, factor, gain):
    inner = grad * gain
    back = factor * (inner - normed * jnp.mean(inner * normed, axis=-1, keepdims=True))
    return (back, jnp.sum(grad * normed, axis=0))


F32, BF16 = jnp.float32, jnp.bfloat16
PAIR = 2 * HEAD_DIM
ROWS = 256
STRETCH = 64


def nn(a, b):
    return lax.dot_general(a, b, (((1,), (0,)), ((), ())), preferred_element_type=F32)


def nt(a, b):
    return lax.dot_general(a, b, (((1,), (1,)), ((), ())), preferred_element_type=F32)


def tn(a, b):
    return lax.dot_general(a, b, (((0,), (0,)), ((), ())), preferred_element_type=F32)


def sigmoid(v):
    return 1.0 / (1.0 + jnp.exp(-v))


def lanes_of(half, rows=1):
    return (lax.broadcasted_iota(jnp.int32, (rows, PAIR), 1) // HEAD_DIM) == half


def keep(value, half):
    return jnp.where(lanes_of(half), value, jnp.zeros_like(value))


def both(value):
    return jnp.concatenate([keep(value, 0), keep(value, 1)], axis=0)


def joined(stacked):
    rows = stacked.shape[0] // 2
    return jnp.where(lanes_of(0), stacked[:rows], stacked[rows:])


def scaled(pair, scalars):
    return jnp.concatenate([pair[:HEAD_DIM] * scalars[0], pair[HEAD_DIM:] * scalars[1]], axis=0)


def same_sequence(starts, early, late, per):
    count = jnp.int32(0)
    for c in range(early * per + 1, late * per + 1):
        count = count + starts[c]
    return count == 0


def earlier(s, starts, kb, qb, per):
    open_all = jnp.where(same_sequence(starts, kb, qb, per), 0.0, MASKED).astype(F32)
    open_head = jnp.where(starts[kb * per] > 0, MASKED, open_all).astype(F32)
    row = lax.broadcasted_iota(jnp.int32, (STRETCH, s.shape[1]), 0)
    top = s[:STRETCH] + jnp.where(row < STRETCH - 1, open_head, open_all)
    return jnp.concatenate([top, s[STRETCH:] + open_all], axis=0)


def fill_diagonal(ref, start):
    key = lax.broadcasted_iota(jnp.int32, ref.shape, 0)
    query = lax.broadcasted_iota(jnp.int32, ref.shape, 1)
    plain = jnp.where(key <= query, 0.0, MASKED)
    opening = jnp.where((key == query) | ((key < query) & (key >= STRETCH - 1)), 0.0, MASKED)
    ref[...] = jnp.where(start > 0, opening, plain).astype(F32)


def forward_kernel(
    starts, rates, tok, gain, w, pk, pvt, first, second,
    h1, q, k, v, gate, recall, mixed, kt, lse, a_all, c_all, pre_all, e_all, u_all, atth,
    vt, att, diagonal, a_s, c_s, sa_s, sc_s,
):
    count = tok.shape[0]
    pairs = first.shape[0]
    wide = pairs * PAIR
    per = ROWS // STRETCH

    def project(b, _):
        rows = pl.ds(pl.multiple_of(b * ROWS, ROWS), ROWS)
        x = tok[rows, :].astype(F32)
        factor = lax.rsqrt(jnp.mean(x * x, axis=-1, keepdims=True) + EPSILON)
        h = (x * factor * gain[...]).astype(BF16)
        h1[rows, :] = h
        for part, ref in ((0, q), (1, k), (2, v)):
            made = nn(h, w[:, part * wide:(part + 1) * wide])
            low = made.astype(BF16)
            for p in range(pairs):
                ref[p, rows, :] = low[:, p * PAIR:(p + 1) * PAIR]
            if part > 0:
                made_t = jnp.transpose(made).astype(BF16)
                target = kt if part == 1 else vt
                for h_i in range(2 * pairs):
                    target[h_i, :, rows] = made_t[h_i * HEAD_DIM:(h_i + 1) * HEAD_DIM]
        g = sigmoid(nn(h, w[:, 3 * wide:]))
        for p in range(pairs):
            gate[p, rows, :] = g[:, p * PAIR:(p + 1) * PAIR]
        return 0

    lax.fori_loop(0, count // ROWS, project, 0)
    a_s[...] = first[...]
    c_s[...] = second[...]
    sa_s[...] = jnp.zeros_like(sa_s)
    sc_s[...] = jnp.zeros_like(sc_s)

    def memory_step(t):
        rows = pl.ds(pl.multiple_of(t * STRETCH, STRETCH), STRETCH)
        fresh = starts[t] > 0
        for p in range(pairs):
            a = jnp.where(fresh, first[p], a_s[p])
            c = jnp.where(fresh, second[p], c_s[p])
            sa = jnp.where(fresh, 0.0, sa_s[p])
            sc = jnp.where(fresh, 0.0, sc_s[p])
            ab, cb = a.astype(BF16), c.astype(BF16)
            a_all[t, p] = ab
            c_all[t, p] = cb
            km = both(k[p, rows, :])
            lhs = jnp.concatenate([both(q[p, rows, :]), km], axis=0)
            pre = nn(lhs, ab)
            pre_all[t, p] = pre
            sig = sigmoid(pre)
            act = pre * sig
            actb = act.astype(BF16)
            out = nt(actb, cb)
            recall[p, rows, :] = joined(out[:PAIR])
            e = joined(out[PAIR:]) - v[p, rows, :].astype(F32)
            eb = e.astype(BF16)
            e_all[p, rows, :] = eb
            em = both(eb)
            u = nn(em, cb)
            u_all[t, p] = u
            sigk, actk = sig[PAIR:], act[PAIR:]
            wgt = (u * (sigk + actk * (1.0 - sigk))).astype(BF16)
            ga = tn(km, wgt)
            gc = tn(em, actb[PAIR:])
            th = [rates[0, t, 2 * p + i] * (1.0 / STRETCH) for i in range(2)]
            eta = [rates[1, t, 2 * p + i] for i in range(2)]
            al = [1.0 - rates[2, t, 2 * p + i] for i in range(2)]
            sa = scaled(sa, eta) - scaled(ga, th)
            sc = scaled(sc, eta) - scaled(gc, th)
            sa_s[p] = sa
            sc_s[p] = sc
            a_s[p] = scaled(a, al) + sa
            c_s[p] = scaled(c, al) + sc

    def attention_unit(qb, head):
        p, half = head // 2, head % 2
        rows = pl.ds(qb * ROWS, ROWS)
        qh = keep(q[p, rows, :], half) * jnp.asarray(HEAD_DIM ** -0.5, BF16)
        scores = []
        for kb in range(qb + 1):
            s = nt(k[p, kb * ROWS:(kb + 1) * ROWS, :], qh)
            if kb == qb:
                s = s + diagonal[...]
            else:
                s = earlier(s, starts, kb, qb, per)
            scores.append(s)
        sp = nt(pk[p], qh)
        peak = jnp.max(sp, axis=0, keepdims=True)
        for s in scores:
            peak = jnp.maximum(peak, jnp.max(s, axis=0, keepdims=True))
        ep = jnp.exp(sp - peak)
        total = jnp.sum(ep, axis=0, keepdims=True)
        out = nn(pvt[head], ep.astype(BF16))
        for kb, s in enumerate(scores):
            e = jnp.exp(s - peak)
            total = total + jnp.sum(e, axis=0, keepdims=True)
            out = out + nn(vt[head, :, kb * ROWS:(kb + 1) * ROWS], e.astype(BF16))
        att[head, :, rows] = out * (1.0 / total)
        lse[head, :, rows] = peak + jnp.log(total)

    heads = 2 * pairs
    for qb in range(count // ROWS):
        fill_diagonal(diagonal, starts[qb * per])

        def run(i, _, qb=qb):
            memory_step(qb * per + i)
            attention_unit(qb, i)
            return 0
        lax.fori_loop(0, per, run, 0)
    for b in range(count // ROWS):
        rows = pl.ds(b * ROWS, ROWS)
        for p in range(pairs):
            got = jnp.concatenate([att[2 * p, :, rows], att[2 * p + 1, :, rows]], axis=0)
            wide_att = jnp.transpose(got)
            atth[p, rows, :] = wide_att
            mixed[rows, p * PAIR:(p + 1) * PAIR] = (wide_att + gate[p, rows, :] * recall[p, rows, :]).astype(BF16)


def backward_kernel(
    starts, rates, bm, q, k, v, gate, recall, kt, pk, pkt, pv, lse, a_all, c_all, pre_all, e_all, u_all, atth,
    dq, dk, dv, dg, dpk, dpv, dfirst, dsecond,
    dqt, dd, dks, dvs, mq, bmp, diagonal, da_s, dc_s, dsa_s, dsc_s,
):
    count = bm.shape[0]
    pairs = q.shape[0]
    heads = 2 * pairs
    per = ROWS // STRETCH
    nblocks = count // ROWS
    ones = [jnp.where(lanes_of(i, 8), 1.0, 0.0).astype(F32) for i in range(2)]
    for b in range(nblocks):
        rows = pl.ds(b * ROWS, ROWS)
        for p in range(pairs):
            gb = bm[rows, p * PAIR:(p + 1) * PAIR]
            bmp[p, rows, :] = gb
            g = gb.astype(F32)
            inner = g * atth[p, rows, :]
            for i in range(2):
                row = lax.dot_general(ones[i], inner, (((1,), (1,)), ((), ())), precision=lax.Precision.HIGHEST, preferred_element_type=F32)
                dd[2 * p + i, :, rows] = row[:1]
            gt = gate[p, rows, :]
            dg[rows, p * PAIR:(p + 1) * PAIR] = (g * recall[p, rows, :] * gt * (1.0 - gt)).astype(BF16)
    for ref in (dpk, dpv, dfirst, dsecond, dks, dvs, da_s, dc_s, dsa_s, dsc_s):
        ref[...] = jnp.zeros_like(ref)

    def memory_step(t):
        rows = pl.ds(pl.multiple_of(t * STRETCH, STRETCH), STRETCH)
        fresh = starts[t] > 0
        for p in range(pairs):
            th = [rates[0, t, 2 * p + i] * (-1.0 / STRETCH) for i in range(2)]
            eta = [rates[1, t, 2 * p + i] for i in range(2)]
            al = [1.0 - rates[2, t, 2 * p + i] for i in range(2)]
            da, dc = da_s[p], dc_s[p]
            dsa = dsa_s[p] + da
            dsc = dsc_s[p] + dc
            dga = scaled(dsa, th).astype(BF16)
            dgc = scaled(dsc, th).astype(BF16)
            ab, cb = a_all[t, p], c_all[t, p]
            km, qm = both(k[p, rows, :]), both(q[p, rows, :])
            em = both(e_all[p, rows, :])
            pre = pre_all[t, p]
            sig = sigmoid(pre)
            act = pre * sig
            actb = act.astype(BF16)
            slope = sig + act * (1.0 - sig)
            sigk, prek, slopek = sig[PAIR:], pre[PAIR:], slope[PAIR:]
            u = u_all[t, p]
            curve = sigk * (1.0 - sigk) * (2.0 + prek * (1.0 - 2.0 * sigk))
            wgt = (u * slopek).astype(BF16)
            back = bmp[p, rows, :].astype(F32) * gate[p, rows, :]
            rm = both(back.astype(BF16))
            dpre_q = (nn(rm, cb) * slope[:PAIR]).astype(BF16)
            mq[0, p, rows, :] = joined(nt(dpre_q, ab))
            dw = nn(km, dga)
            du = (dw * slopek).astype(BF16)
            cc = jnp.concatenate([dgc, cb], axis=1)
            de = joined(nt(jnp.concatenate([actb[PAIR:], du], axis=1), cc))
            mq[2, p, rows, :] = -de
            dem = both(de.astype(BF16))
            dsk = nn(jnp.concatenate([em, dem], axis=1), jnp.concatenate([dgc, cb], axis=0))
            dpre = (dsk * slopek + dw * u * curve).astype(BF16)
            mq[1, p, rows, :] = joined(nt(jnp.concatenate([wgt, dpre], axis=1), jnp.concatenate([dga, ab], axis=1)))
            ga = tn(jnp.concatenate([km, qm], axis=0), jnp.concatenate([dpre, dpre_q], axis=0))
            gc = tn(jnp.concatenate([em, dem], axis=0), jnp.concatenate([du, actb[PAIR:]], axis=0))
            gc = gc + tn(rm, actb[:PAIR])
            da = scaled(da, al) + ga
            dc = scaled(dc, al) + gc
            dfirst[p] = dfirst[p] + jnp.where(fresh, da, 0.0)
            dsecond[p] = dsecond[p] + jnp.where(fresh, dc, 0.0)
            da_s[p] = jnp.where(fresh, 0.0, da)
            dc_s[p] = jnp.where(fresh, 0.0, dc)
            dsa_s[p] = jnp.where(fresh, 0.0, scaled(dsa, eta))
            dsc_s[p] = jnp.where(fresh, 0.0, scaled(dsc, eta))

    def attention_unit(qb, head):
        p, half = head // 2, head % 2
        rows = pl.ds(qb * ROWS, ROWS)
        qh = keep(q[p, rows, :], half) * jnp.asarray(HEAD_DIM ** -0.5, BF16)
        gh = keep(bmp[p, rows, :], half)
        lrow, drow = lse[head, :, rows], dd[head, :, rows]
        acc = jnp.zeros((HEAD_DIM, ROWS), F32)
        for kb in range(qb + 1):
            krows = slice(kb * ROWS, (kb + 1) * ROWS)
            s = nt(k[p, krows, :], qh) - lrow
            if kb == qb:
                s = s + diagonal[...]
            else:
                s = earlier(s, starts, kb, qb, per)
            prob = jnp.exp(s)
            ds = (prob * (nt(v[p, krows, :], gh) - drow)).astype(BF16)
            dvs[p, krows, :] = dvs[p, krows, :] + nn(prob.astype(BF16), gh)
            dks[p, krows, :] = dks[p, krows, :] + nn(ds, qh)
            acc = acc + nn(kt[head, :, krows], ds)
        prob = jnp.exp(nt(pk[p], qh) - lrow)
        ds = (prob * (nt(pv[p], gh) - drow)).astype(BF16)
        dpv[p] = dpv[p] + nn(prob.astype(BF16), gh)
        dpk[p] = dpk[p] + nn(ds, qh)
        acc = acc + nn(pkt[head], ds)
        dqt[head, :, rows] = acc * (HEAD_DIM ** -0.5)

    for qb in reversed(range(nblocks)):
        fill_diagonal(diagonal, starts[qb * per])

        def run(i, _, qb=qb):
            memory_step(qb * per + per - 1 - i)
            attention_unit(qb, i)
            return 0
        lax.fori_loop(0, per, run, 0)
    for b in range(nblocks):
        rows = pl.ds(b * ROWS, ROWS)
        for p in range(pairs):
            cols = slice(p * PAIR, (p + 1) * PAIR)
            got = jnp.concatenate([dqt[2 * p, :, rows], dqt[2 * p + 1, :, rows]], axis=0)
            dq[rows, cols] = (jnp.transpose(got) + mq[0, p, rows, :]).astype(BF16)
            dk[rows, cols] = (dks[p, rows, :] + mq[1, p, rows, :]).astype(BF16)
            dv[rows, cols] = (dvs[p, rows, :] + mq[2, p, rows, :]).astype(BF16)


def shape(*dims, dtype=F32):
    return jax.ShapeDtypeStruct(dims, dtype)


VMEM = pl.BlockSpec(memory_space=pltpu.VMEM)
SMEM = pl.BlockSpec(memory_space=pltpu.SMEM)
LIMIT = 56 * 1024 * 1024


def mixer_forward(starts, rates, tok, gain, w, pk, pvt, first, second):
    count, width = tok.shape
    pairs = first.shape[0]
    heads, steps = 2 * pairs, starts.shape[0]
    flat = lambda dtype: shape(pairs, count, PAIR, dtype=dtype)
    outs = (
        shape(count, width, dtype=BF16), flat(BF16), flat(BF16), flat(BF16), flat(F32), flat(F32),
        shape(count, pairs * PAIR, dtype=BF16), shape(heads, HEAD_DIM, count, dtype=BF16), shape(heads, 1, count),
        shape(steps, pairs, PAIR, PAIR, dtype=BF16), shape(steps, pairs, PAIR, PAIR, dtype=BF16),
        shape(steps, pairs, 2 * PAIR, PAIR), flat(BF16), shape(steps, pairs, PAIR, PAIR), flat(F32),
    )
    state = pltpu.VMEM((pairs, PAIR, PAIR), F32)
    return pl.pallas_call(
        forward_kernel,
        out_shape=outs,
        in_specs=[SMEM, SMEM] + [VMEM] * 7,
        out_specs=[VMEM] * len(outs),
        scratch_shapes=[
            pltpu.VMEM((heads, HEAD_DIM, count), BF16), pltpu.VMEM((heads, HEAD_DIM, count), F32),
            pltpu.VMEM((ROWS, ROWS), F32), state, state, state, state,
        ],
        compiler_params=pltpu.CompilerParams(vmem_limit_bytes=LIMIT),
        name="mixer_forward",
    )(starts, rates, tok, gain, w, pk, pvt, first, second)


def mixer_backward(starts, rates, bm, q, k, v, gate, recall, kt, pk, pkt, pv, lse, a_all, c_all, pre_all, e_all, u_all, atth):
    count, wide = bm.shape
    pairs = q.shape[0]
    heads = 2 * pairs
    outs = (
        shape(count, wide, dtype=BF16), shape(count, wide, dtype=BF16), shape(count, wide, dtype=BF16), shape(count, wide, dtype=BF16),
        shape(*pk.shape), shape(*pv.shape), shape(pairs, PAIR, PAIR), shape(pairs, PAIR, PAIR),
    )
    state = pltpu.VMEM((pairs, PAIR, PAIR), F32)
    flat = pltpu.VMEM((pairs, count, PAIR), F32)
    return pl.pallas_call(
        backward_kernel,
        out_shape=outs,
        in_specs=[SMEM, SMEM] + [VMEM] * 17,
        out_specs=[VMEM] * len(outs),
        scratch_shapes=[
            pltpu.VMEM((heads, HEAD_DIM, count), F32), pltpu.VMEM((heads, 1, count), F32), flat, flat,
            pltpu.VMEM((3, pairs, count, PAIR), F32), pltpu.VMEM((pairs, count, PAIR), BF16),
            pltpu.VMEM((ROWS, ROWS), F32), state, state, state, state,
        ],
        compiler_params=pltpu.CompilerParams(vmem_limit_bytes=LIMIT),
        name="mixer_backward",
    )(starts, rates, bm, q, k, v, gate, recall, kt, pk, pkt, pv, lse, a_all, c_all, pre_all, e_all, u_all, atth)


MESH = pl.DeviceIdType.MESH
HALF_SHARE = 32
PEERS = 16


def place():
    return lax.axis_index("dp"), lax.axis_index("tensor")


def flipped(index, mask):
    result = index
    bit = 1
    while bit <= mask:
        if mask & bit:
            result = result + bit * (1 - 2 * (lax.div(index, bit) % 2))
        bit *= 2
    return result


def greet(devices):
    barrier = pltpu.get_barrier_semaphore()
    for device in devices:
        pl.semaphore_signal(barrier, inc=1, device_id=device, device_id_type=MESH)
    pl.semaphore_wait(barrier, len(devices))


def remote(src, dst, send_sem, recv_sem, device):
    return pltpu.make_async_remote_copy(
        src_ref=src, dst_ref=dst, send_sem=send_sem, recv_sem=recv_sem, device_id=device, device_id_type=MESH
    )


def iota(rows, columns, dimension):
    return lax.broadcasted_iota(jnp.int32, (rows, columns), dimension)


def at_rows(start, size):
    return pl.ds(pl.multiple_of(start, size), size)


def spread(ref, dp, t, sent, peer_sems, y_sems):
    base = t * (PEERS * HALF_SHARE)
    copies = []
    for m in range(1, PEERS):
        peer = flipped(dp, m)
        copy = remote(
            sent.at[at_rows(peer * HALF_SHARE, HALF_SHARE)], ref.at[at_rows(base + dp * HALF_SHARE, HALF_SHARE)],
            peer_sems.at[0, m], peer_sems.at[1, m], (peer, t),
        )
        copy.start()
        copies.append(copy)
    ref[at_rows(base + dp * HALF_SHARE, HALF_SHARE), :] = sent[at_rows(dp * HALF_SHARE, HALF_SHARE), :]
    return copies


def pass_on(ref, dp, t, copies, y_sems):
    base = t * (PEERS * HALF_SHARE)
    passed = []
    for m in range(PEERS):
        peer = flipped(dp, m)
        rows = at_rows(base + peer * HALF_SHARE, HALF_SHARE)
        if m:
            copies[m - 1].wait_recv()
        copy = remote(ref.at[rows], ref.at[rows], y_sems.at[0, m], y_sems.at[1, m], (dp, 1 - t))
        copy.start()
        passed.append(copy)
    for copy in copies:
        copy.wait_send()
    return passed


def rows_in_kernel(
    idx, tok, cot, xs_out, cs_out, seq, g, gt, asked_out,
    xs, cs, asked, want, sent_t, sent_c, ask_sems, t_sems, ty_sems, c_sems, cy_sems,
):
    dp, t = place()
    count, width = tok.shape
    half = count // 2
    share = 2 * HALF_SHARE
    index = idx[...]
    dev = lax.div(index, count)
    row = index - dev * count
    held = jnp.where(iota(PEERS, count, 0) == dev, 1.0, 0.0).astype(BF16)
    upper = jnp.where(iota(PAIR, PAIR, 0) < iota(PAIR, PAIR, 1), 1.0, 0.0).astype(BF16)
    run = jnp.zeros((PEERS, 1), F32)
    ranks = []
    for c in range(count // PAIR):
        part = held[:, c * PAIR:(c + 1) * PAIR]
        wide = part.astype(F32)
        ranks.append(jnp.sum(wide * (nn(part, upper) + run), axis=0, keepdims=True))
        run = run + jnp.sum(wide, axis=1, keepdims=True)
    rank = jnp.concatenate(ranks, axis=1)
    column = jnp.transpose(jnp.broadcast_to(rank, (PAIR, count)))
    pick = jnp.where(column == iota(count, PAIR, 1).astype(F32), 1.0, 0.0).astype(BF16)
    high = lax.div(row, 32)
    low = row - high * 32
    held_wide = held.astype(F32)
    wanted = 32.0 * nn((held_wide * high.astype(F32)).astype(BF16), pick) + nn((held_wide * low.astype(F32)).astype(BF16), pick)
    for j in range(PEERS):
        want[j] = jnp.broadcast_to(wanted[j:j + 1], (8, PAIR))
    greet([(flipped(dp, m), t) for m in range(1, PEERS)] + [(dp, 1 - t)])
    asks = []
    for m in range(1, PEERS):
        peer = flipped(dp, m)
        copy = remote(want.at[peer], asked.at[dp], ask_sems.at[0, m], ask_sems.at[1, m], (peer, t))
        copy.start()
        asks.append(copy)
    asked[dp] = want[dp]
    rank_i = rank.astype(jnp.int32)
    half_of = lax.div(rank_i, HALF_SHARE)
    slot = half_of * (half - HALF_SHARE) + dev * HALF_SHARE + rank_i
    for c in range(count // ROWS):
        gt[c * ROWS:(c + 1) * ROWS, :] = jnp.where(iota(ROWS, count, 0) + c * ROWS == slot, 1.0, 0.0).astype(BF16)
    slots = jnp.transpose(jnp.broadcast_to(slot.astype(F32), (PAIR, count)))
    for c in range(count // PAIR):
        g[:, c * PAIR:(c + 1) * PAIR] = jnp.where(slots == (iota(count, PAIR, 1) + c * PAIR).astype(F32), 1.0, 0.0).astype(BF16)
    for copy in asks:
        copy.wait()
    asks_in = asked[:, 0, :]
    asked_out[...] = asks_in
    asks_high = jnp.floor(asks_in * (1.0 / 32.0))
    asks_low = asks_in - 32.0 * asks_high
    owner = jnp.where(lax.div(iota(half, PEERS, 0), HALF_SHARE) == iota(half, PEERS, 1), 1.0, 0.0).astype(BF16)
    lane = iota(half, PAIR, 1) == iota(half, PAIR, 0) % HALF_SHARE + t * HALF_SHARE
    ones = jnp.ones((PAIR, PAIR), BF16)
    value = jnp.zeros((half, PAIR), F32)
    for digit, scale in ((asks_high, 32.0), (asks_low, 1.0)):
        picked = jnp.where(lane, nn(owner, digit.astype(BF16)), 0.0).astype(BF16)
        value = value + scale * nn(picked, ones)
    chosen = jnp.concatenate(
        [jnp.where(value == (iota(half, PAIR, 1) + c * PAIR).astype(F32), 1.0, 0.0).astype(BF16) for c in range(count // PAIR)], axis=1
    )
    sent_t[...] = nn(chosen, tok[...]).astype(BF16)
    copies = spread(xs, dp, t, sent_t, t_sems, ty_sems)
    sent_c[...] = nn(chosen, cot[...]).astype(BF16)
    passed = pass_on(xs, dp, t, copies, ty_sems)
    copies = spread(cs, dp, t, sent_c, c_sems, cy_sems)
    for copy in passed:
        copy.wait()
    xs_out[...] = xs[...]
    for c in range(count // ROWS):
        seq[c * ROWS:(c + 1) * ROWS, :] = nn(g[c * ROWS:(c + 1) * ROWS, :], xs[...]).astype(BF16)
    for copy in pass_on(cs, dp, t, copies, cy_sems):
        copy.wait()
    cs_out[...] = cs[...]


def rows_in(source_index, tokens, cotangent):
    count, width = tokens.shape
    rows = shape(count, width, dtype=BF16)
    square = shape(count, count, dtype=BF16)
    buffer = pltpu.VMEM((count, width), BF16)
    half = pltpu.VMEM((count // 2, width), BF16)
    small = pltpu.VMEM((PEERS, 8, PAIR), F32)
    sems = pltpu.SemaphoreType.DMA((2, PEERS))
    return pl.pallas_call(
        rows_in_kernel,
        out_shape=(rows, rows, rows, square, square, shape(PEERS, PAIR)),
        in_specs=[VMEM] * 3,
        out_specs=[VMEM] * 6,
        scratch_shapes=[buffer, buffer, small, small, half, half, sems, sems, sems, sems, sems],
        compiler_params=pltpu.CompilerParams(collective_id=0, has_side_effects=True, vmem_limit_bytes=LIMIT),
        name="rows_in",
    )(source_index.reshape(1, count), tokens, cotangent)


def dense_kernel(
    mixed, gt, g, xs, cs, op, dg, dl, dd, gain,
    bm, lo, br, facc, dgain,
    mx, ops, ms, h2s, hid, bgs, bls, ps_s, pb_s, ps_r, pb_r, own_s, own_b, resid, bf, sems,
):
    dp, t = place()
    other = (dp, 1 - t)
    count, width = xs.shape
    half = count // 2
    hidden = dg.shape[1]
    wide = mixed.shape[1]
    padded = bgs.shape[1]
    mx[t] = mixed[...]
    ops[t] = op[...]
    greet([other])
    first = remote(mx.at[t], mx.at[t], sems.at[0, 0], sems.at[1, 0], other)
    second = remote(ops.at[t], ops.at[t], sems.at[0, 1], sems.at[1, 1], other)
    first.start()
    second.start()
    pad = jnp.zeros((count, PAIR), BF16)
    for ref in (hid, bgs, bls):
        ref[:, padded - PAIR:] = pad
    ms[t] = nn(gt[...], mixed[...]).astype(BF16)
    first.wait()
    ms[1 - t] = nn(gt[...], mx[1 - t]).astype(BF16)
    second.wait()

    def chunk(rows, store):
        x = xs[rows, :].astype(F32) + nn(ms[0, rows, :], ops[0]) + nn(ms[1, rows, :], ops[1])
        factor = lax.rsqrt(jnp.mean(x * x, axis=-1, keepdims=True) + EPSILON)
        h2 = (x * factor * gain[...]).astype(BF16)
        h2s[rows, :] = h2
        gated, lifted = nn(h2, dg[...]), nn(h2, dl[...])
        sig = sigmoid(gated)
        act = gated * sig
        low = (act * lifted).astype(BF16)
        hid[rows, :hidden] = low
        back = nt(cs[rows, :], dd[...])
        back_g = (back * lifted * (sig + act * (1.0 - sig))).astype(BF16)
        back_l = (back * act).astype(BF16)
        bgs[rows, :hidden] = back_g
        bls[rows, :hidden] = back_l
        store(x, nn(low, dd[...]), nt(back_g, dg[...]) + nt(back_l, dl[...]))

    copies = []
    for c in range(half // ROWS):
        here = pl.ds(c * ROWS, ROWS)

        def send(x, down, back, here=here):
            ps_s[here, :] = down.astype(BF16)
            pb_s[here, :] = back.astype(BF16)

        chunk(at_rows((1 - t) * half + c * ROWS, ROWS), send)
        for src, dst, n in ((pb_s, pb_r, 2 + 2 * c), (ps_s, ps_r, 3 + 2 * c)):
            copy = remote(src.at[here], dst.at[here], sems.at[0, n], sems.at[1, n], other)
            copy.start()
            copies.append(copy)
    for c in range(half // ROWS):
        here = pl.ds(c * ROWS, ROWS)

        def hold(x, down, back, here=here):
            resid[here, :] = x
            own_s[here, :] = down
            own_b[here, :] = back

        chunk(at_rows(t * half + c * ROWS, ROWS), hold)
    total = jnp.zeros((8, width), F32)
    back_copies = []
    for c in range(half // ROWS):
        here = pl.ds(c * ROWS, ROWS)
        rows = at_rows(t * half + c * ROWS, ROWS)
        copies[2 * c].wait()
        x = resid[here, :]
        factor = lax.rsqrt(jnp.mean(x * x, axis=-1, keepdims=True) + EPSILON)
        norm = x * factor
        back = own_b[here, :] + pb_r[here, :].astype(F32)
        inner = back * gain[...]
        result = cs[rows, :].astype(F32) + factor * (inner - norm * jnp.mean(inner * norm, axis=-1, keepdims=True))
        br[here, :] = result
        bf[rows, :] = result.astype(BF16)
        copy = remote(bf.at[rows], bf.at[rows], sems.at[0, 6 + c], sems.at[1, 6 + c], other)
        copy.start()
        back_copies.append(copy)
        total = total + jnp.sum((back * norm).reshape(ROWS // 8, 8, width), axis=0)
    dgain[...] = total
    facc[:, :padded] = tn(h2s[...], bgs[...])
    facc[:, padded:2 * padded] = tn(h2s[...], bls[...])
    facc[:, 2 * padded:3 * padded] = tn(cs[...], hid[...])
    for c in range(half // ROWS):
        here = pl.ds(c * ROWS, ROWS)
        copies[2 * c + 1].wait()
        lo[here, :] = (resid[here, :] + (own_s[here, :] + ps_r[here, :].astype(F32))).astype(BF16)
    for copy in back_copies:
        copy.wait()
    bm_slot = nt(bf[...], op[...]).astype(BF16)
    bm[...] = nn(g[...], bm_slot).astype(BF16)
    facc[:, 3 * padded:] = tn(bf[...], ms[t])


def dense(mixed, gt, g, xs, cs, op, dg, dl, dd, gain):
    count, width = xs.shape
    wide = mixed.shape[1]
    half = count // 2
    padded = -(-dg.shape[1] // PAIR) * PAIR
    half32, half16 = pltpu.VMEM((half, width), F32), pltpu.VMEM((half, width), BF16)
    hiddens = pltpu.VMEM((count, padded), BF16)
    return pl.pallas_call(
        dense_kernel,
        out_shape=(
            shape(count, wide, dtype=BF16), shape(half, width, dtype=BF16), shape(half, width),
            shape(width, 3 * padded + wide), shape(8, width),
        ),
        in_specs=[VMEM] * 10,
        out_specs=[VMEM] * 5,
        scratch_shapes=[
            pltpu.VMEM((2, count, wide), BF16), pltpu.VMEM((2, wide, width), BF16), pltpu.VMEM((2, count, wide), BF16),
            pltpu.VMEM((count, width), BF16), hiddens, hiddens, hiddens, half16, half16, half16, half16, half32, half32, half32,
            pltpu.VMEM((count, width), BF16), pltpu.SemaphoreType.DMA((2, 8)),
        ],
        compiler_params=pltpu.CompilerParams(collective_id=1, has_side_effects=True, vmem_limit_bytes=LIMIT),
        name="dense",
    )(mixed, gt, g, xs, cs, op, dg, dl, dd, gain)


class Sum:
    def __init__(self, dp, t, acc, out, scratch):
        self.dp, self.t, self.acc, self.out = dp, t, acc, out
        self.s1, self.r1, self.s2, self.r2, self.s3, self.r3, self.sems = scratch
        self.c0, self.c1, self.c2 = dp % 2, lax.div(dp, 2) % 2, lax.div(dp, 4)
        rows = acc.shape[0]
        self.n1, self.n2, self.n3 = rows // 2, rows // 4, rows // 16
        self.b1 = self.c0 * self.n1
        self.b2 = self.b1 + self.c1 * self.n2
        self.b3 = self.b2 + self.c2 * self.n3
        self.live = []

    @staticmethod
    def scratch(rows, lanes):
        full = lambda *dims: pltpu.VMEM(dims + (lanes,), BF16)
        return [
            full(rows // 2), full(rows // 2), full(rows // 4), full(rows // 4), full(3, rows // 16), full(3, rows // 16),
            pltpu.SemaphoreType.DMA((2, 10)),
        ]

    @staticmethod
    def peers(dp, t):
        c2 = lax.div(dp, 4)
        return [(flipped(dp, 1), t), (flipped(dp, 2), t)] + [(dp + 4 * ((c2 + k) % 4 - c2), t) for k in (1, 2, 3)]

    def go(self, n, src, dst, peer):
        copy = remote(src, dst, self.sems.at[0, n], self.sems.at[1, n], (peer, self.t))
        copy.start()
        self.live.append(copy)

    def done(self):
        for copy in self.live:
            copy.wait()
        self.live = []

    def z_peer(self, k):
        d = (self.c2 + k) % 4
        return d, self.dp + 4 * (d - self.c2)

    def step(self, n):
        acc, out = self.acc, self.out
        if n == 0:
            self.s1[...] = acc[at_rows((1 - self.c0) * self.n1, self.n1), :].astype(BF16)
            self.go(0, self.s1, self.r1, flipped(self.dp, 1))
        elif n == 1:
            self.done()
            for i in range(2):
                side = (1 - self.c1) if i == 0 else self.c1
                rows = at_rows(self.b1 + side * self.n2, self.n2)
                total = acc[rows, :] + self.r1[at_rows(side * self.n2, self.n2), :].astype(F32)
                if i == 0:
                    self.s2[...] = total.astype(BF16)
                    self.go(1, self.s2, self.r2, flipped(self.dp, 2))
                else:
                    acc[rows, :] = total
        elif n == 2:
            self.done()
            for k in (1, 2, 3, 0):
                d, peer = self.z_peer(k)
                rows = at_rows(self.b2 + d * self.n3, self.n3)
                total = acc[rows, :] + self.r2[at_rows(d * self.n3, self.n3), :].astype(F32)
                if k:
                    self.s3[k - 1] = total.astype(BF16)
                    self.go(1 + k, self.s3.at[k - 1], self.r3.at[k - 1], peer)
                else:
                    acc[rows, :] = total
        elif n == 3:
            self.done()
            rows = at_rows(self.b3, self.n3)
            total = acc[rows, :]
            for k in range(3):
                total = total + self.r3[k].astype(F32)
            out[rows, :] = total.astype(BF16)
            for k in (1, 2, 3):
                self.go(4 + k, out.at[rows], out.at[rows], self.z_peer(k)[1])
        elif n == 4:
            self.done()
            rows = at_rows(self.b2, self.n2)
            self.go(8, out.at[rows], out.at[rows], flipped(self.dp, 2))
        elif n == 5:
            self.done()
            rows = at_rows(self.b1, self.n1)
            self.go(9, out.at[rows], out.at[rows], flipped(self.dp, 1))
        elif n == 6:
            self.done()


def tail_kernel(
    bq, bk, bv, bg, h1, gt, wq, wk, wv, wg, xs, br, gain, lo, asked, facc, dgain, dfirst, dsecond, dpk, dpv,
    red_out, gains_out, ret,
    acc, red, part_s, part_r, bx, rec_l, rec_x, gains_s, gains_r, ht,
    y_sems, l_sems, ly_sems, x_sems, xy_sems, g_sems, *sum_scratch,
):
    dp, t = place()
    other = (dp, 1 - t)
    count, width = xs.shape
    half = count // 2
    wide = bq.shape[1]
    fwide = facc.shape[1]
    acc[:, :fwide] = facc[...]
    for n, b in enumerate((bq, bk, bv, bg)):
        acc[:, fwide + n * wide:fwide + (n + 1) * wide] = tn(h1[...], b[...])
    at = fwide + 4 * wide
    pairs = dfirst.shape[0]
    few = dpk.shape[1]
    acc[:, at + PAIR:] = jnp.zeros((width, PAIR), F32)
    for p in range(pairs):
        acc[p * PAIR:(p + 1) * PAIR, at:at + PAIR] = dfirst[p]
        acc[(pairs + p) * PAIR:(pairs + p + 1) * PAIR, at:at + PAIR] = dsecond[p]
        acc[p * few:(p + 1) * few, at + PAIR:] = dpk[p]
        acc[(pairs + p) * few:(pairs + p + 1) * few, at + PAIR:] = dpv[p]
    peers = [(flipped(dp, m), t) for m in range(1, PEERS)]
    greet(peers + [other])
    total = Sum(dp, t, acc, red, sum_scratch)
    total.step(0)

    def partial(rows):
        result = jnp.zeros((ROWS, width), F32)
        for b, w in ((bq, wq), (bk, wk), (bv, wv), (bg, wg)):
            result = result + nt(nn(gt[rows, :], b[...]).astype(BF16), w[...])
        return result

    copies = []
    for c in range(half // ROWS):
        here = pl.ds(c * ROWS, ROWS)
        part_s[here, :] = partial(at_rows((1 - t) * half + c * ROWS, ROWS)).astype(BF16)
        copy = remote(part_s.at[here], part_r.at[here], y_sems.at[0, c], y_sems.at[1, c], other)
        copy.start()
        copies.append(copy)
    back_l = spread(rec_l, dp, t, lo, l_sems, ly_sems)
    total.step(1)
    mgain = jnp.zeros((8, width), F32)
    for c in range(half // ROWS):
        here = pl.ds(c * ROWS, ROWS)
        rows = at_rows(t * half + c * ROWS, ROWS)
        own = partial(rows)
        copies[c].wait()
        back = own + part_r[here, :].astype(F32)
        x = xs[rows, :].astype(F32)
        factor = lax.rsqrt(jnp.mean(x * x, axis=-1, keepdims=True) + EPSILON)
        norm = x * factor
        inner = back * gain[...]
        bx[here, :] = (br[here, :] + factor * (inner - norm * jnp.mean(inner * norm, axis=-1, keepdims=True))).astype(BF16)
        mgain = mgain + jnp.sum((back * norm).reshape(ROWS // 8, 8, width), axis=0)
    back_x = spread(rec_x, dp, t, bx, x_sems, xy_sems)
    gains_s[0, 0] = mgain
    gains_s[0, 1] = dgain[...]
    groups = [[other], [(flipped(dp, 1), t)], [(flipped(dp, 2), t)], Sum.peers(dp, t)[2:]]
    gain_copies = []

    def gain_step(n):
        if n:
            for copy in gain_copies:
                copy.wait()
            gain_copies.clear()
            value = gains_s[n - 1]
            for i in range(len(groups[n - 1])):
                value = value + gains_r[n - 1, i]
            gains_s[n] = value
        if n < 4:
            for i, peer in enumerate(groups[n]):
                copy = remote(gains_s.at[n], gains_r.at[n, i], g_sems.at[0, n, i], g_sems.at[1, n, i], peer)
                copy.start()
                gain_copies.append(copy)

    gain_step(0)
    passed_l = pass_on(rec_l, dp, t, back_l, ly_sems)
    gain_step(1)
    total.step(2)
    asks = asked[...]
    asks_high = jnp.floor(asks * (1.0 / 32.0))
    asks_low = asks - 32.0 * asks_high
    slot = iota(PAIR, count, 1)
    rank = lax.div(slot, half) * HALF_SHARE + slot % HALF_SHARE
    pick = jnp.where(iota(PAIR, count, 0) == rank, 1.0, 0.0).astype(BF16)
    slot = iota(PEERS, count, 1)
    mine = iota(PEERS, count, 0) == lax.div(slot % half, HALF_SHARE)
    spread_out = 32.0 * nn(asks_high.astype(BF16), pick) + nn(asks_low.astype(BF16), pick)
    row = jnp.sum(jnp.where(mine, spread_out, 0.0), axis=0, keepdims=True)
    for c in range(count // ROWS):
        ht[c * ROWS:(c + 1) * ROWS, :] = jnp.where((iota(ROWS, count, 0) + c * ROWS).astype(F32) == row, 1.0, 0.0).astype(BF16)
    gain_step(2)
    passed_x = pass_on(rec_x, dp, t, back_x, xy_sems)
    total.step(3)
    gain_step(3)
    for copy in passed_l:
        copy.wait()
    ret[0] = nn(ht[...], rec_l[...]).astype(BF16)
    total.step(4)
    for copy in passed_x:
        copy.wait()
    ret[1] = nn(ht[...], rec_x[...]).astype(BF16)
    gain_step(4)
    gains_out[...] = gains_s[4]
    total.step(5)
    total.step(6)
    red_out[...] = red[...]


def tail(bq, bk, bv, bg, h1, gt, wq, wk, wv, wg, xs, br, gain, lo, asked, facc, dgain, dfirst, dsecond, dpk, dpv):
    count, width = xs.shape
    half = count // 2
    lanes = facc.shape[1] + 4 * bq.shape[1] + 2 * PAIR
    half16 = pltpu.VMEM((half, width), BF16)
    full16 = pltpu.VMEM((count, width), BF16)
    sems = pltpu.SemaphoreType.DMA((2, PEERS))
    return pl.pallas_call(
        tail_kernel,
        out_shape=(shape(width, lanes, dtype=BF16), shape(2, 8, width), shape(2, count, width, dtype=BF16)),
        in_specs=[VMEM] * 21,
        out_specs=[VMEM] * 3,
        scratch_shapes=[
            pltpu.VMEM((width, lanes), F32), pltpu.VMEM((width, lanes), BF16), half16, half16, half16, full16, full16,
            pltpu.VMEM((5, 2, 8, width), F32), pltpu.VMEM((4, 3, 2, 8, width), F32), pltpu.VMEM((count, count), BF16),
            pltpu.SemaphoreType.DMA((2, 2)), sems, sems, sems, sems, pltpu.SemaphoreType.DMA((2, 4, 3)),
            *Sum.scratch(width, lanes),
        ],
        compiler_params=pltpu.CompilerParams(collective_id=2, has_side_effects=True, vmem_limit_bytes=LIMIT),
        name="tail",
    )(bq, bk, bv, bg, h1, gt, wq, wk, wv, wg, xs, br, gain, lo, asked, facc, dgain, dfirst, dsecond, dpk, dpv)


def finish_kernel(
    red, gains, ret, lo, bx, mgain, gq, gk, gv, gg, gout, gpk, gpv, first, second, dgain, ggate, glift, gdown,
):
    hidden = ggate.shape[1]
    padded = -(-hidden // PAIR) * PAIR
    wide = gq.shape[1]
    pairs = wide // PAIR
    few = gpk.shape[0]
    lo[...] = ret[0]
    bx[...] = ret[1]
    mgain[...] = jnp.sum(gains[0], axis=0, keepdims=True)
    dgain[...] = jnp.sum(gains[1], axis=0, keepdims=True)
    ggate[...] = red[:, :hidden].astype(F32)
    glift[...] = red[:, padded:padded + hidden].astype(F32)
    gdown[...] = jnp.transpose(red[:, 2 * padded:3 * padded].astype(F32))[:hidden]
    at = 3 * padded
    gout[...] = jnp.transpose(red[:, at:at + wide].astype(F32))
    at += wide
    for ref in (gq, gk, gv, gg):
        ref[...] = red[:, at:at + wide].astype(F32)
        at += wide
    for p in range(pairs):
        first[p] = red[p * PAIR:(p + 1) * PAIR, at:at + PAIR].astype(F32)
        both_heads = jnp.transpose(red[(pairs + p) * PAIR:(pairs + p + 1) * PAIR, at:at + PAIR].astype(F32))
        second[2 * p] = both_heads[:, :HEAD_DIM]
        second[2 * p + 1] = both_heads[:, HEAD_DIM:]
        gpk[:, p * PAIR:(p + 1) * PAIR] = red[p * few:(p + 1) * few, at + PAIR:].astype(F32)
        gpv[:, p * PAIR:(p + 1) * PAIR] = red[(pairs + p) * few:(pairs + p + 1) * few, at + PAIR:].astype(F32)


def finish(red, gains, ret, hidden, wide, few):
    width = red.shape[0]
    count = ret.shape[1]
    pairs = wide // PAIR
    rows = shape(count, width, dtype=BF16)
    square = shape(width, wide)
    outs = (
        rows, rows, shape(1, width), square, square, square, square, shape(wide, width), shape(few, wide), shape(few, wide),
        shape(pairs, PAIR, PAIR), shape(2 * pairs, PAIR, HEAD_DIM), shape(1, width),
        shape(width, hidden), shape(width, hidden), shape(hidden, width),
    )
    return pl.pallas_call(
        finish_kernel,
        out_shape=outs,
        in_specs=[VMEM] * 3,
        out_specs=[VMEM] * len(outs),
        compiler_params=pltpu.CompilerParams(vmem_limit_bytes=LIMIT),
        name="finish",
    )(red, gains, ret)


def block_body(
    tokens, cotangent, source_index, tract_starts, memory_rates, mixer_gain, query_proj, key_proj, value_proj, gate_proj,
    out_proj, persist_keys, persist_values, memory_first, memory_second, dense_gain, dense_gate, dense_lift, dense_down,
):
    pairs = query_proj.shape[1] // PAIR
    by_pair = lambda value: value.reshape(-1, pairs, PAIR).transpose(1, 0, 2)
    by_head = lambda value: value.T.reshape(2 * pairs, HEAD_DIM, -1)
    weights = jnp.concatenate([query_proj, key_proj, value_proj, gate_proj], axis=1)
    pk, pv = by_pair(persist_keys), by_pair(persist_values)
    first = memory_first.reshape(pairs, PAIR, PAIR)
    second = memory_second.transpose(0, 2, 1).reshape(pairs, PAIR, PAIR)
    xs, cs, seq, g, gt, asked = rows_in(source_index, tokens, cotangent)
    h1, query, keys, values, gate, recall, mixed, keys_t, lse, a_all, c_all, pre_all, e_all, u_all, attended = mixer_forward(
        tract_starts, memory_rates, seq, mixer_gain[None], weights, pk, by_head(persist_values), first, second
    )
    back_mixed, lo, back_resid, dense_grads, gain_two = dense(
        mixed, gt, g, xs, cs, out_proj, dense_gate, dense_lift, dense_down, dense_gain[None]
    )
    bq, bk, bv, bg, grad_pk, grad_pv, grad_first, grad_second = mixer_backward(
        tract_starts, memory_rates, back_mixed, query, keys, values, gate, recall, keys_t, pk, by_head(persist_keys), pv,
        lse, a_all, c_all, pre_all, e_all, u_all, attended,
    )
    red, gains, ret = tail(
        bq, bk, bv, bg, h1, gt, query_proj, key_proj, value_proj, gate_proj, xs, back_resid, mixer_gain[None], lo, asked,
        dense_grads, gain_two, grad_first, grad_second, grad_pk, grad_pv,
    )
    outs = list(finish(red, gains, ret, dense_gate.shape[1], query_proj.shape[1], persist_keys.shape[0]))
    outs[2] = outs[2][0]
    outs[10] = outs[10].reshape(memory_first.shape)
    outs[12] = outs[12][0]
    return tuple(outs)


def body(
    tokens,
    cotangent,
    source_index,
    tract_starts,
    memory_rates,
    mixer_gain,
    query_proj,
    key_proj,
    value_proj,
    gate_proj,
    out_proj,
    persist_keys,
    persist_values,
    memory_first,
    memory_second,
    dense_gain,
    dense_gate,
    dense_lift,
    dense_down,
):
    count = tokens.shape[0]
    width = tokens.shape[1]
    peers = lax.axis_size("dp")
    share = count // peers
    arrival = jnp.argsort(source_index)
    wanted = (source_index[arrival] % count).reshape(peers, share)
    asked = lax.all_to_all(wanted, "dp", split_axis=0, concat_axis=0, tiled=True).reshape(count)
    got_tokens, got_cot = (
        lax.all_to_all(
            tokens[asked].reshape(peers, share, width),
            "dp",
            split_axis=0,
            concat_axis=0,
            tiled=True,
        ),
        lax.all_to_all(
            cotangent[asked].reshape(peers, share, width),
            "dp",
            split_axis=0,
            concat_axis=0,
            tiled=True,
        ),
    )
    placing = jnp.argsort(arrival)
    seq_tokens = got_tokens.reshape(count, width)[placing]
    seq_cot = got_cot.reshape(count, width)[placing]
    seq_x = seq_tokens.astype(jnp.float32)
    first_norm, factor_one = norm_forward(seq_x)
    pairs = query_proj.shape[1] // PAIR
    by_pair = lambda value: value.reshape(-1, pairs, PAIR).transpose(1, 0, 2)
    by_head = lambda value: value.T.reshape(2 * pairs, HEAD_DIM, -1)
    weights = jnp.concatenate([query_proj, key_proj, value_proj, gate_proj], axis=1)
    pk, pv = by_pair(persist_keys), by_pair(persist_values)
    first = memory_first.reshape(pairs, PAIR, PAIR)
    second = memory_second.transpose(0, 2, 1).reshape(pairs, PAIR, PAIR)
    h_one, query, keys, values, gate, recall, mixed, keys_t, lse, a_all, c_all, pre_all, e_all, u_all, attended = mixer_forward(
        tract_starts, memory_rates, seq_tokens, mixer_gain[None], weights, pk, by_head(persist_values), first, second
    )
    first_out = lax.psum(product(mixed, out_proj), "tensor")
    resid = seq_x + first_out
    norm_two, factor_two = norm_forward(resid)
    h_two = (norm_two * dense_gain).astype(jnp.bfloat16)
    gated = product(h_two, dense_gate)
    lifted = product(h_two, dense_lift)
    sigma = jax.nn.sigmoid(gated)
    active = gated * sigma
    hidden = (active * lifted).astype(jnp.bfloat16)
    second_out = lax.psum(product(hidden, dense_down).astype(jnp.bfloat16), "tensor").astype(
        jnp.float32
    )
    seq_out = (resid + second_out).astype(jnp.bfloat16)
    grad_down = product(hidden.T, seq_cot)
    back_hidden = product(seq_cot, dense_down.T)
    back_gated = (back_hidden * lifted * (sigma + gated * sigma * (1.0 - sigma))).astype(
        jnp.bfloat16
    )
    back_lifted = (back_hidden * active).astype(jnp.bfloat16)
    grad_gate = product(h_two.T, back_gated)
    grad_lift = product(h_two.T, back_lifted)
    back_two = lax.psum(
        product(back_gated, dense_gate.T) + product(back_lifted, dense_lift.T), "tensor"
    )
    back_norm_two, grad_dgain = norm_backward(back_two, norm_two, factor_two, dense_gain)
    residual_gradient = seq_cot.astype(jnp.float32) + back_norm_two
    back_first = residual_gradient.astype(jnp.bfloat16)
    grad_out = product(mixed.T, back_first)
    back_mixed = product(back_first, out_proj.T).astype(jnp.bfloat16)
    back_query, back_keys, cotangent_payloads, back_gate, grad_pk, grad_pv, grad_first, grad_second = mixer_backward(
        tract_starts, memory_rates, back_mixed, query, keys, values, gate, recall, keys_t, pk, by_head(persist_keys), pv,
        lse, a_all, c_all, pre_all, e_all, u_all, attended,
    )
    grad_first = grad_first.reshape(memory_first.shape)
    grad_second = grad_second.reshape(memory_first.shape).transpose(0, 2, 1)
    grad_query = product(h_one.T, back_query)
    grad_key = product(h_one.T, back_keys)
    grad_value = product(h_one.T, cotangent_payloads)
    grad_gproj = product(h_one.T, back_gate)
    back_one = lax.psum(
        product(back_query, query_proj.T)
        + product(back_keys, key_proj.T)
        + product(cotangent_payloads, value_proj.T)
        + product(back_gate, gate_proj.T),
        "tensor",
    )
    back_norm_one, grad_mgain = norm_backward(back_one, first_norm, factor_one, mixer_gain)
    back_x = (residual_gradient + back_norm_one).astype(jnp.bfloat16)
    grad_pkeys = grad_pk.transpose(1, 0, 2).reshape(persist_keys.shape)
    grad_pvalues = grad_pv.transpose(1, 0, 2).reshape(persist_values.shape)
    (
        grad_mgain,
        grad_query,
        grad_key,
        grad_value,
        grad_gproj,
        grad_out,
        grad_pkeys,
        grad_pvalues,
        grad_first,
        grad_second,
        grad_dgain,
        grad_gate,
        grad_lift,
        grad_down,
    ) = lax.psum(
        (
            grad_mgain,
            grad_query,
            grad_key,
            grad_value,
            grad_gproj,
            grad_out,
            grad_pkeys,
            grad_pvalues,
            grad_first,
            grad_second,
            grad_dgain,
            grad_gate,
            grad_lift,
            grad_down,
        ),
        "dp",
    )
    ret_out, ret_grad = (
        lax.all_to_all(
            seq_out[arrival].reshape(peers, share, width),
            "dp",
            split_axis=0,
            concat_axis=0,
            tiled=True,
        ),
        lax.all_to_all(
            back_x[arrival].reshape(peers, share, width),
            "dp",
            split_axis=0,
            concat_axis=0,
            tiled=True,
        ),
    )
    undo = jnp.argsort(asked)
    layer_output = ret_out.reshape(count, width)[undo]
    input_grad = ret_grad.reshape(count, width)[undo]
    return (
        layer_output,
        input_grad,
        grad_mgain,
        grad_query,
        grad_key,
        grad_value,
        grad_gproj,
        grad_out,
        grad_pkeys,
        grad_pvalues,
        grad_first,
        grad_second,
        grad_dgain,
        grad_gate,
        grad_lift,
        grad_down,
    )


def solution(mesh):
    chosen = block_body if mesh.shape["dp"] == PEERS else body
    in_specs = (
        P("dp", None),
        P("dp", None),
        P("dp"),
        P("dp"),
        P(None, "dp", "tensor"),
        P(),
        P(None, "tensor"),
        P(None, "tensor"),
        P(None, "tensor"),
        P(None, "tensor"),
        P("tensor", None),
        P(None, "tensor"),
        P(None, "tensor"),
        P("tensor", None, None),
        P("tensor", None, None),
        P(),
        P(None, "tensor"),
        P(None, "tensor"),
        P("tensor", None),
    )
    out_specs = (
        P("dp", None),
        P("dp", None),
        P(),
        P(None, "tensor"),
        P(None, "tensor"),
        P(None, "tensor"),
        P(None, "tensor"),
        P("tensor", None),
        P(None, "tensor"),
        P(None, "tensor"),
        P("tensor", None, None),
        P("tensor", None, None),
        P(),
        P(None, "tensor"),
        P(None, "tensor"),
        P("tensor", None),
    )
    return jax.shard_map(chosen, mesh=mesh, in_specs=in_specs, out_specs=out_specs, check_vma=False)
```

```python
import jax
import jax.numpy as jnp
from jax import lax
from jax.experimental import pallas as pl
from jax.experimental.pallas import tpu as pltpu
from jax.sharding import PartitionSpec as P

HEAD_DIM = 64


EPSILON = 1e-06
MASKED = -1e30


def product(left, right):
    return jnp.dot(left, right, preferred_element_type=jnp.float32)


def norm_forward(value):
    factor = lax.rsqrt(jnp.mean(value * value, axis=-1, keepdims=True) + EPSILON)
    return (value * factor, factor)


def norm_backward(grad, normed, factor, gain):
    inner = grad * gain
    back = factor * (inner - normed * jnp.mean(inner * normed, axis=-1, keepdims=True))
    return (back, jnp.sum(grad * normed, axis=0))


F32, BF16 = jnp.float32, jnp.bfloat16
PAIR = 2 * HEAD_DIM
ROWS = 256
STRETCH = 64


def nn(a, b):
    return lax.dot_general(a, b, (((1,), (0,)), ((), ())), preferred_element_type=F32)


def nt(a, b):
    return lax.dot_general(a, b, (((1,), (1,)), ((), ())), preferred_element_type=F32)


def tn(a, b):
    return lax.dot_general(a, b, (((0,), (0,)), ((), ())), preferred_element_type=F32)


def sigmoid(v):
    return 1.0 / (1.0 + jnp.exp(-v))


def lanes_of(half, rows=1):
    return (lax.broadcasted_iota(jnp.int32, (rows, PAIR), 1) // HEAD_DIM) == half


def keep(value, half):
    return jnp.where(lanes_of(half), value, jnp.zeros_like(value))


def both(value):
    return jnp.concatenate([keep(value, 0), keep(value, 1)], axis=0)


def joined(stacked):
    rows = stacked.shape[0] // 2
    return jnp.where(lanes_of(0), stacked[:rows], stacked[rows:])


def scaled(pair, scalars):
    return jnp.concatenate([pair[:HEAD_DIM] * scalars[0], pair[HEAD_DIM:] * scalars[1]], axis=0)


def same_sequence(starts, early, late, per):
    count = jnp.int32(0)
    for c in range(early * per + 1, late * per + 1):
        count = count + starts[c]
    return count == 0


def earlier(s, starts, kb, qb, per):
    open_all = jnp.where(same_sequence(starts, kb, qb, per), 0.0, MASKED).astype(F32)
    open_head = jnp.where(starts[kb * per] > 0, MASKED, open_all).astype(F32)
    row = lax.broadcasted_iota(jnp.int32, (STRETCH, s.shape[1]), 0)
    top = s[:STRETCH] + jnp.where(row < STRETCH - 1, open_head, open_all)
    return jnp.concatenate([top, s[STRETCH:] + open_all], axis=0)


def fill_diagonal(ref, start):
    key = lax.broadcasted_iota(jnp.int32, ref.shape, 0)
    query = lax.broadcasted_iota(jnp.int32, ref.shape, 1)
    plain = jnp.where(key <= query, 0.0, MASKED)
    opening = jnp.where((key == query) | ((key < query) & (key >= STRETCH - 1)), 0.0, MASKED)
    ref[...] = jnp.where(start > 0, opening, plain).astype(F32)


def forward_kernel(
    starts, rates, tok, gain, w, pk, pvt, first, second,
    h1, q, k, v, gate, recall, mixed, kt, lse, a_all, c_all, pre_all, e_all, u_all, atth,
    vt, att, diagonal, a_s, c_s, sa_s, sc_s,
):
    count = tok.shape[0]
    pairs = first.shape[0]
    wide = pairs * PAIR
    per = ROWS // STRETCH

    def project(b, _):
        rows = pl.ds(pl.multiple_of(b * ROWS, ROWS), ROWS)
        x = tok[rows, :].astype(F32)
        factor = lax.rsqrt(jnp.mean(x * x, axis=-1, keepdims=True) + EPSILON)
        h = (x * factor * gain[...]).astype(BF16)
        h1[rows, :] = h
        for part, ref in ((0, q), (1, k), (2, v)):
            made = nn(h, w[:, part * wide:(part + 1) * wide])
            low = made.astype(BF16)
            for p in range(pairs):
                ref[p, rows, :] = low[:, p * PAIR:(p + 1) * PAIR]
            if part > 0:
                made_t = jnp.transpose(made).astype(BF16)
                target = kt if part == 1 else vt
                for h_i in range(2 * pairs):
                    target[h_i, :, rows] = made_t[h_i * HEAD_DIM:(h_i + 1) * HEAD_DIM]
        g = sigmoid(nn(h, w[:, 3 * wide:]))
        for p in range(pairs):
            gate[p, rows, :] = g[:, p * PAIR:(p + 1) * PAIR]
        return 0

    lax.fori_loop(0, count // ROWS, project, 0)
    a_s[...] = first[...]
    c_s[...] = second[...]
    sa_s[...] = jnp.zeros_like(sa_s)
    sc_s[...] = jnp.zeros_like(sc_s)

    def memory_step(t):
        rows = pl.ds(pl.multiple_of(t * STRETCH, STRETCH), STRETCH)
        fresh = starts[t] > 0
        for p in range(pairs):
            a = jnp.where(fresh, first[p], a_s[p])
            c = jnp.where(fresh, second[p], c_s[p])
            sa = jnp.where(fresh, 0.0, sa_s[p])
            sc = jnp.where(fresh, 0.0, sc_s[p])
            ab, cb = a.astype(BF16), c.astype(BF16)
            a_all[t, p] = ab
            c_all[t, p] = cb
            km = both(k[p, rows, :])
            lhs = jnp.concatenate([both(q[p, rows, :]), km], axis=0)
            pre = nn(lhs, ab)
            pre_all[t, p] = pre
            sig = sigmoid(pre)
            act = pre * sig
            actb = act.astype(BF16)
            out = nt(actb, cb)
            recall[p, rows, :] = joined(out[:PAIR])
            e = joined(out[PAIR:]) - v[p, rows, :].astype(F32)
            eb = e.astype(BF16)
            e_all[p, rows, :] = eb
            em = both(eb)
            u = nn(em, cb)
            u_all[t, p] = u
            sigk, actk = sig[PAIR:], act[PAIR:]
            wgt = (u * (sigk + actk * (1.0 - sigk))).astype(BF16)
            ga = tn(km, wgt)
            gc = tn(em, actb[PAIR:])
            th = [rates[0, t, 2 * p + i] * (1.0 / STRETCH) for i in range(2)]
            eta = [rates[1, t, 2 * p + i] for i in range(2)]
            al = [1.0 - rates[2, t, 2 * p + i] for i in range(2)]
            sa = scaled(sa, eta) - scaled(ga, th)
            sc = scaled(sc, eta) - scaled(gc, th)
            sa_s[p] = sa
            sc_s[p] = sc
            a_s[p] = scaled(a, al) + sa
            c_s[p] = scaled(c, al) + sc

    def attention_unit(qb, head):
        p, half = head // 2, head % 2
        rows = pl.ds(qb * ROWS, ROWS)
        qh = keep(q[p, rows, :], half) * jnp.asarray(HEAD_DIM ** -0.5, BF16)
        scores = []
        for kb in range(qb + 1):
            s = nt(k[p, kb * ROWS:(kb + 1) * ROWS, :], qh)
            if kb == qb:
                s = s + diagonal[...]
            else:
                s = earlier(s, starts, kb, qb, per)
            scores.append(s)
        sp = nt(pk[p], qh)
        peak = jnp.max(sp, axis=0, keepdims=True)
        for s in scores:
            peak = jnp.maximum(peak, jnp.max(s, axis=0, keepdims=True))
        ep = jnp.exp(sp - peak)
        total = jnp.sum(ep, axis=0, keepdims=True)
        out = nn(pvt[head], ep.astype(BF16))
        for kb, s in enumerate(scores):
            e = jnp.exp(s - peak)
            total = total + jnp.sum(e, axis=0, keepdims=True)
            out = out + nn(vt[head, :, kb * ROWS:(kb + 1) * ROWS], e.astype(BF16))
        att[head, :, rows] = out * (1.0 / total)
        lse[head, :, rows] = peak + jnp.log(total)

    heads = 2 * pairs
    for qb in range(count // ROWS):
        fill_diagonal(diagonal, starts[qb * per])

        def run(i, _, qb=qb):
            memory_step(qb * per + i)
            attention_unit(qb, i)
            return 0
        lax.fori_loop(0, per, run, 0)
    for b in range(count // ROWS):
        rows = pl.ds(b * ROWS, ROWS)
        for p in range(pairs):
            got = jnp.concatenate([att[2 * p, :, rows], att[2 * p + 1, :, rows]], axis=0)
            wide_att = jnp.transpose(got)
            atth[p, rows, :] = wide_att
            mixed[rows, p * PAIR:(p + 1) * PAIR] = (wide_att + gate[p, rows, :] * recall[p, rows, :]).astype(BF16)


def backward_kernel(
    starts, rates, bm, q, k, v, gate, recall, kt, pk, pkt, pv, lse, a_all, c_all, pre_all, e_all, u_all, atth,
    dq, dk, dv, dg, dpk, dpv, dfirst, dsecond,
    dqt, dd, dks, dvs, mq, bmp, diagonal, da_s, dc_s, dsa_s, dsc_s,
):
    count = bm.shape[0]
    pairs = q.shape[0]
    heads = 2 * pairs
    per = ROWS // STRETCH
    nblocks = count // ROWS
    ones = [jnp.where(lanes_of(i, 8), 1.0, 0.0).astype(F32) for i in range(2)]
    for b in range(nblocks):
        rows = pl.ds(b * ROWS, ROWS)
        for p in range(pairs):
            gb = bm[rows, p * PAIR:(p + 1) * PAIR]
            bmp[p, rows, :] = gb
            g = gb.astype(F32)
            inner = g * atth[p, rows, :]
            for i in range(2):
                row = lax.dot_general(ones[i], inner, (((1,), (1,)), ((), ())), precision=lax.Precision.HIGHEST, preferred_element_type=F32)
                dd[2 * p + i, :, rows] = row[:1]
            gt = gate[p, rows, :]
            dg[rows, p * PAIR:(p + 1) * PAIR] = (g * recall[p, rows, :] * gt * (1.0 - gt)).astype(BF16)
    for ref in (dpk, dpv, dfirst, dsecond, dks, dvs, da_s, dc_s, dsa_s, dsc_s):
        ref[...] = jnp.zeros_like(ref)

    def memory_step(t):
        rows = pl.ds(pl.multiple_of(t * STRETCH, STRETCH), STRETCH)
        fresh = starts[t] > 0
        for p in range(pairs):
            th = [rates[0, t, 2 * p + i] * (-1.0 / STRETCH) for i in range(2)]
            eta = [rates[1, t, 2 * p + i] for i in range(2)]
            al = [1.0 - rates[2, t, 2 * p + i] for i in range(2)]
            da, dc = da_s[p], dc_s[p]
            dsa = dsa_s[p] + da
            dsc = dsc_s[p] + dc
            dga = scaled(dsa, th).astype(BF16)
            dgc = scaled(dsc, th).astype(BF16)
            ab, cb = a_all[t, p], c_all[t, p]
            km, qm = both(k[p, rows, :]), both(q[p, rows, :])
            em = both(e_all[p, rows, :])
            pre = pre_all[t, p]
            sig = sigmoid(pre)
            act = pre * sig
            actb = act.astype(BF16)
            slope = sig + act * (1.0 - sig)
            sigk, prek, slopek = sig[PAIR:], pre[PAIR:], slope[PAIR:]
            u = u_all[t, p]
            curve = sigk * (1.0 - sigk) * (2.0 + prek * (1.0 - 2.0 * sigk))
            wgt = (u * slopek).astype(BF16)
            back = bmp[p, rows, :].astype(F32) * gate[p, rows, :]
            rm = both(back.astype(BF16))
            dpre_q = (nn(rm, cb) * slope[:PAIR]).astype(BF16)
            mq[0, p, rows, :] = joined(nt(dpre_q, ab))
            dw = nn(km, dga)
            du = (dw * slopek).astype(BF16)
            cc = jnp.concatenate([dgc, cb], axis=1)
            de = joined(nt(jnp.concatenate([actb[PAIR:], du], axis=1), cc))
            mq[2, p, rows, :] = -de
            dem = both(de.astype(BF16))
            dsk = nn(jnp.concatenate([em, dem], axis=1), jnp.concatenate([dgc, cb], axis=0))
            dpre = (dsk * slopek + dw * u * curve).astype(BF16)
            mq[1, p, rows, :] = joined(nt(jnp.concatenate([wgt, dpre], axis=1), jnp.concatenate([dga, ab], axis=1)))
            ga = tn(jnp.concatenate([km, qm], axis=0), jnp.concatenate([dpre, dpre_q], axis=0))
            gc = tn(jnp.concatenate([em, dem], axis=0), jnp.concatenate([du, actb[PAIR:]], axis=0))
            gc = gc + tn(rm, actb[:PAIR])
            da = scaled(da, al) + ga
            dc = scaled(dc, al) + gc
            dfirst[p] = dfirst[p] + jnp.where(fresh, da, 0.0)
            dsecond[p] = dsecond[p] + jnp.where(fresh, dc, 0.0)
            da_s[p] = jnp.where(fresh, 0.0, da)
            dc_s[p] = jnp.where(fresh, 0.0, dc)
            dsa_s[p] = jnp.where(fresh, 0.0, scaled(dsa, eta))
            dsc_s[p] = jnp.where(fresh, 0.0, scaled(dsc, eta))

    def attention_unit(qb, head):
        p, half = head // 2, head % 2
        rows = pl.ds(qb * ROWS, ROWS)
        qh = keep(q[p, rows, :], half) * jnp.asarray(HEAD_DIM ** -0.5, BF16)
        gh = keep(bmp[p, rows, :], half)
        lrow, drow = lse[head, :, rows], dd[head, :, rows]
        acc = jnp.zeros((HEAD_DIM, ROWS), F32)
        for kb in range(qb + 1):
            krows = slice(kb * ROWS, (kb + 1) * ROWS)
            s = nt(k[p, krows, :], qh) - lrow
            if kb == qb:
                s = s + diagonal[...]
            else:
                s = earlier(s, starts, kb, qb, per)
            prob = jnp.exp(s)
            ds = (prob * (nt(v[p, krows, :], gh) - drow)).astype(BF16)
            dvs[p, krows, :] = dvs[p, krows, :] + nn(prob.astype(BF16), gh)
            dks[p, krows, :] = dks[p, krows, :] + nn(ds, qh)
            acc = acc + nn(kt[head, :, krows], ds)
        prob = jnp.exp(nt(pk[p], qh) - lrow)
        ds = (prob * (nt(pv[p], gh) - drow)).astype(BF16)
        dpv[p] = dpv[p] + nn(prob.astype(BF16), gh)
        dpk[p] = dpk[p] + nn(ds, qh)
        acc = acc + nn(pkt[head], ds)
        dqt[head, :, rows] = acc * (HEAD_DIM ** -0.5)

    for qb in reversed(range(nblocks)):
        fill_diagonal(diagonal, starts[qb * per])

        def run(i, _, qb=qb):
            memory_step(qb * per + per - 1 - i)
            attention_unit(qb, i)
            return 0
        lax.fori_loop(0, per, run, 0)
    for b in range(nblocks):
        rows = pl.ds(b * ROWS, ROWS)
        for p in range(pairs):
            cols = slice(p * PAIR, (p + 1) * PAIR)
            got = jnp.concatenate([dqt[2 * p, :, rows], dqt[2 * p + 1, :, rows]], axis=0)
            dq[rows, cols] = (jnp.transpose(got) + mq[0, p, rows, :]).astype(BF16)
            dk[rows, cols] = (dks[p, rows, :] + mq[1, p, rows, :]).astype(BF16)
            dv[rows, cols] = (dvs[p, rows, :] + mq[2, p, rows, :]).astype(BF16)


def shape(*dims, dtype=F32):
    return jax.ShapeDtypeStruct(dims, dtype)


VMEM = pl.BlockSpec(memory_space=pltpu.VMEM)
SMEM = pl.BlockSpec(memory_space=pltpu.SMEM)
LIMIT = 56 * 1024 * 1024


def mixer_forward(starts, rates, tok, gain, w, pk, pvt, first, second):
    count, width = tok.shape
    pairs = first.shape[0]
    heads, steps = 2 * pairs, starts.shape[0]
    flat = lambda dtype: shape(pairs, count, PAIR, dtype=dtype)
    outs = (
        shape(count, width, dtype=BF16), flat(BF16), flat(BF16), flat(BF16), flat(F32), flat(F32),
        shape(count, pairs * PAIR, dtype=BF16), shape(heads, HEAD_DIM, count, dtype=BF16), shape(heads, 1, count),
        shape(steps, pairs, PAIR, PAIR, dtype=BF16), shape(steps, pairs, PAIR, PAIR, dtype=BF16),
        shape(steps, pairs, 2 * PAIR, PAIR), flat(BF16), shape(steps, pairs, PAIR, PAIR), flat(F32),
    )
    state = pltpu.VMEM((pairs, PAIR, PAIR), F32)
    return pl.pallas_call(
        forward_kernel,
        out_shape=outs,
        in_specs=[SMEM, SMEM] + [VMEM] * 7,
        out_specs=[VMEM] * len(outs),
        scratch_shapes=[
            pltpu.VMEM((heads, HEAD_DIM, count), BF16), pltpu.VMEM((heads, HEAD_DIM, count), F32),
            pltpu.VMEM((ROWS, ROWS), F32), state, state, state, state,
        ],
        compiler_params=pltpu.CompilerParams(vmem_limit_bytes=LIMIT),
        name="mixer_forward",
    )(starts, rates, tok, gain, w, pk, pvt, first, second)


def mixer_backward(starts, rates, bm, q, k, v, gate, recall, kt, pk, pkt, pv, lse, a_all, c_all, pre_all, e_all, u_all, atth):
    count, wide = bm.shape
    pairs = q.shape[0]
    heads = 2 * pairs
    outs = (
        shape(count, wide, dtype=BF16), shape(count, wide, dtype=BF16), shape(count, wide, dtype=BF16), shape(count, wide, dtype=BF16),
        shape(*pk.shape), shape(*pv.shape), shape(pairs, PAIR, PAIR), shape(pairs, PAIR, PAIR),
    )
    state = pltpu.VMEM((pairs, PAIR, PAIR), F32)
    flat = pltpu.VMEM((pairs, count, PAIR), F32)
    return pl.pallas_call(
        backward_kernel,
        out_shape=outs,
        in_specs=[SMEM, SMEM] + [VMEM] * 17,
        out_specs=[VMEM] * len(outs),
        scratch_shapes=[
            pltpu.VMEM((heads, HEAD_DIM, count), F32), pltpu.VMEM((heads, 1, count), F32), flat, flat,
            pltpu.VMEM((3, pairs, count, PAIR), F32), pltpu.VMEM((pairs, count, PAIR), BF16),
            pltpu.VMEM((ROWS, ROWS), F32), state, state, state, state,
        ],
        compiler_params=pltpu.CompilerParams(vmem_limit_bytes=LIMIT),
        name="mixer_backward",
    )(starts, rates, bm, q, k, v, gate, recall, kt, pk, pkt, pv, lse, a_all, c_all, pre_all, e_all, u_all, atth)


MESH = pl.DeviceIdType.MESH
HALF_SHARE = 32
PEERS = 16


def place():
    return lax.axis_index("dp"), lax.axis_index("tensor")


def flipped(index, mask):
    result = index
    bit = 1
    while bit <= mask:
        if mask & bit:
            result = result + bit * (1 - 2 * (lax.div(index, bit) % 2))
        bit *= 2
    return result


def greet(devices):
    barrier = pltpu.get_barrier_semaphore()
    for device in devices:
        pl.semaphore_signal(barrier, inc=1, device_id=device, device_id_type=MESH)
    pl.semaphore_wait(barrier, len(devices))


def remote(src, dst, send_sem, recv_sem, device):
    return pltpu.make_async_remote_copy(
        src_ref=src, dst_ref=dst, send_sem=send_sem, recv_sem=recv_sem, device_id=device, device_id_type=MESH
    )


def iota(rows, columns, dimension):
    return lax.broadcasted_iota(jnp.int32, (rows, columns), dimension)


def at_rows(start, size):
    return pl.ds(pl.multiple_of(start, size), size)


def spread(ref, dp, t, sent, peer_sems, y_sems):
    base = t * (PEERS * HALF_SHARE)
    copies = []
    for m in range(1, PEERS):
        peer = flipped(dp, m)
        copy = remote(
            sent.at[at_rows(peer * HALF_SHARE, HALF_SHARE)], ref.at[at_rows(base + dp * HALF_SHARE, HALF_SHARE)],
            peer_sems.at[0, m], peer_sems.at[1, m], (peer, t),
        )
        copy.start()
        copies.append(copy)
    ref[at_rows(base + dp * HALF_SHARE, HALF_SHARE), :] = sent[at_rows(dp * HALF_SHARE, HALF_SHARE), :]
    return copies


def pass_on(ref, dp, t, copies, y_sems):
    base = t * (PEERS * HALF_SHARE)
    passed = []
    for m in range(PEERS):
        peer = flipped(dp, m)
        rows = at_rows(base + peer * HALF_SHARE, HALF_SHARE)
        if m:
            copies[m - 1].wait_recv()
        copy = remote(ref.at[rows], ref.at[rows], y_sems.at[0, m], y_sems.at[1, m], (dp, 1 - t))
        copy.start()
        passed.append(copy)
    for copy in copies:
        copy.wait_send()
    return passed


def rows_in_kernel(
    idx, tok, cot, xs_out, sent_c, seq, g, gt, asked_out,
    xs, asked, want, sent_t, ask_sems, t_sems, ty_sems,
):
    dp, t = place()
    count, width = tok.shape
    half = count // 2
    share = 2 * HALF_SHARE
    index = idx[...]
    dev = lax.div(index, count)
    row = index - dev * count
    held = jnp.where(iota(PEERS, count, 0) == dev, 1.0, 0.0).astype(BF16)
    upper = jnp.where(iota(PAIR, PAIR, 0) < iota(PAIR, PAIR, 1), 1.0, 0.0).astype(BF16)
    run = jnp.zeros((PEERS, 1), F32)
    ranks = []
    for c in range(count // PAIR):
        part = held[:, c * PAIR:(c + 1) * PAIR]
        wide = part.astype(F32)
        ranks.append(jnp.sum(wide * (nn(part, upper) + run), axis=0, keepdims=True))
        run = run + jnp.sum(wide, axis=1, keepdims=True)
    rank = jnp.concatenate(ranks, axis=1)
    column = jnp.transpose(jnp.broadcast_to(rank, (PAIR, count)))
    pick = jnp.where(column == iota(count, PAIR, 1).astype(F32), 1.0, 0.0).astype(BF16)
    high = lax.div(row, 32)
    low = row - high * 32
    held_wide = held.astype(F32)
    wanted = 32.0 * nn((held_wide * high.astype(F32)).astype(BF16), pick) + nn((held_wide * low.astype(F32)).astype(BF16), pick)
    for j in range(PEERS):
        want[j] = jnp.broadcast_to(wanted[j:j + 1], (8, PAIR))
    greet([(flipped(dp, m), t) for m in range(1, PEERS)] + [(dp, 1 - t)])
    asks = []
    for m in range(1, PEERS):
        peer = flipped(dp, m)
        copy = remote(want.at[peer], asked.at[dp], ask_sems.at[0, m], ask_sems.at[1, m], (peer, t))
        copy.start()
        asks.append(copy)
    asked[dp] = want[dp]
    rank_i = rank.astype(jnp.int32)
    half_of = lax.div(rank_i, HALF_SHARE)
    slot = half_of * (half - HALF_SHARE) + dev * HALF_SHARE + rank_i
    for c in range(count // ROWS):
        gt[c * ROWS:(c + 1) * ROWS, :] = jnp.where(iota(ROWS, count, 0) + c * ROWS == slot, 1.0, 0.0).astype(BF16)
    slots = jnp.transpose(jnp.broadcast_to(slot.astype(F32), (PAIR, count)))
    for c in range(count // PAIR):
        g[:, c * PAIR:(c + 1) * PAIR] = jnp.where(slots == (iota(count, PAIR, 1) + c * PAIR).astype(F32), 1.0, 0.0).astype(BF16)
    for copy in asks:
        copy.wait()
    asks_in = asked[:, 0, :]
    asked_out[...] = asks_in
    asks_high = jnp.floor(asks_in * (1.0 / 32.0))
    asks_low = asks_in - 32.0 * asks_high
    owner = jnp.where(lax.div(iota(half, PEERS, 0), HALF_SHARE) == iota(half, PEERS, 1), 1.0, 0.0).astype(BF16)
    lane = iota(half, PAIR, 1) == iota(half, PAIR, 0) % HALF_SHARE + t * HALF_SHARE
    ones = jnp.ones((PAIR, PAIR), BF16)
    value = jnp.zeros((half, PAIR), F32)
    for digit, scale in ((asks_high, 32.0), (asks_low, 1.0)):
        picked = jnp.where(lane, nn(owner, digit.astype(BF16)), 0.0).astype(BF16)
        value = value + scale * nn(picked, ones)
    chosen = jnp.concatenate(
        [jnp.where(value == (iota(half, PAIR, 1) + c * PAIR).astype(F32), 1.0, 0.0).astype(BF16) for c in range(count // PAIR)], axis=1
    )
    sent_t[...] = nn(chosen, tok[...]).astype(BF16)
    copies = spread(xs, dp, t, sent_t, t_sems, ty_sems)
    sent_c[...] = nn(chosen, cot[...]).astype(BF16)
    passed = pass_on(xs, dp, t, copies, ty_sems)
    for copy in passed:
        copy.wait()
    xs_out[...] = xs[...]
    for c in range(count // ROWS):
        seq[c * ROWS:(c + 1) * ROWS, :] = nn(g[c * ROWS:(c + 1) * ROWS, :], xs[...]).astype(BF16)


def rows_in(source_index, tokens, cotangent):
    count, width = tokens.shape
    rows = shape(count, width, dtype=BF16)
    square = shape(count, count, dtype=BF16)
    buffer = pltpu.VMEM((count, width), BF16)
    half = pltpu.VMEM((count // 2, width), BF16)
    small = pltpu.VMEM((PEERS, 8, PAIR), F32)
    sems = pltpu.SemaphoreType.DMA((2, PEERS))
    return pl.pallas_call(
        rows_in_kernel,
        out_shape=(rows, shape(count // 2, width, dtype=BF16), rows, square, square, shape(PEERS, PAIR)),
        in_specs=[VMEM] * 3,
        out_specs=[VMEM] * 6,
        scratch_shapes=[buffer, small, small, half, sems, sems, sems],
        compiler_params=pltpu.CompilerParams(collective_id=0, has_side_effects=True, vmem_limit_bytes=LIMIT),
        name="rows_in",
    )(source_index.reshape(1, count), tokens, cotangent)


def dense_kernel(
    mixed, gt, g, xs, cs, ops, dg, dl, dd, gain,
    bm, ps_s, own_s, br, facc, gout, gother, dgain,
    ms, h2s, hid, bgs, bls, pb_s, pb_r, own_b, resid, bf, bms_s, bms, sems,
):
    dp, t = place()
    other = (dp, 1 - t)
    count, width = xs.shape
    half = count // 2
    hidden = dg.shape[0]
    padded = bgs.shape[1]
    greet([other])
    pad = jnp.zeros((count, PAIR), BF16)
    for ref in (hid, bgs, bls):
        ref[:, padded - PAIR:] = pad
    for n in range(2):
        ms[n] = nn(gt[...], mixed[n]).astype(BF16)

    def chunk(rows, store):
        x = xs[rows, :].astype(F32) + nn(ms[0, rows, :], ops[0]) + nn(ms[1, rows, :], ops[1])
        factor = lax.rsqrt(jnp.mean(x * x, axis=-1, keepdims=True) + EPSILON)
        h2 = (x * factor * gain[...]).astype(BF16)
        h2s[rows, :] = h2
        gated, lifted = nt(h2, dg[...]), nt(h2, dl[...])
        sig = sigmoid(gated)
        act = gated * sig
        low = (act * lifted).astype(BF16)
        hid[rows, :hidden] = low
        back = nt(cs[rows, :], dd[...])
        back_g = (back * lifted * (sig + act * (1.0 - sig))).astype(BF16)
        back_l = (back * act).astype(BF16)
        bgs[rows, :hidden] = back_g
        bls[rows, :hidden] = back_l
        store(x, low, nn(back_g, dg[...]) + nn(back_l, dl[...]))

    copies = []
    for c in range(half // ROWS):
        here = pl.ds(c * ROWS, ROWS)

        def send(x, low, back, here=here):
            pb_s[here, :] = back.astype(BF16)
            ps_s[here, :] = nn(low, dd[...]).astype(BF16)

        chunk(at_rows((1 - t) * half + c * ROWS, ROWS), send)
        copy = remote(pb_s.at[here], pb_r.at[here], sems.at[0, c], sems.at[1, c], other)
        copy.start()
        copies.append(copy)
    for c in range(half // ROWS):
        here = pl.ds(c * ROWS, ROWS)

        def hold(x, low, back, here=here):
            resid[here, :] = x
            own_s[here, :] = x + nn(low, dd[...])
            own_b[here, :] = back

        chunk(at_rows(t * half + c * ROWS, ROWS), hold)
    total = jnp.zeros((8, width), F32)
    back_copies = []
    for c in range(half // ROWS):
        here = pl.ds(c * ROWS, ROWS)
        rows = at_rows(t * half + c * ROWS, ROWS)
        copies[c].wait()
        x = resid[here, :]
        factor = lax.rsqrt(jnp.mean(x * x, axis=-1, keepdims=True) + EPSILON)
        norm = x * factor
        back = own_b[here, :] + pb_r[here, :].astype(F32)
        inner = back * gain[...]
        result = cs[rows, :].astype(F32) + factor * (inner - norm * jnp.mean(inner * norm, axis=-1, keepdims=True))
        br[here, :] = result
        low = result.astype(BF16)
        bf[here, :] = low
        bms_s[here, :] = nt(low, ops[1 - t]).astype(BF16)
        copy = remote(bms_s.at[here], bms.at[rows], sems.at[0, 2 + c], sems.at[1, 2 + c], other)
        copy.start()
        back_copies.append(copy)
        bms[rows, :] = nt(low, ops[t]).astype(BF16)
        total = total + jnp.sum((back * norm).reshape(ROWS // 8, 8, width), axis=0)
    dgain[...] = total
    facc[:padded, :] = tn(bgs[...], h2s[...]).astype(BF16)
    facc[padded:2 * padded, :] = tn(bls[...], h2s[...]).astype(BF16)
    facc[2 * padded:, :] = tn(hid[...], cs[...]).astype(BF16)
    mine = at_rows(t * half, half)
    gout[...] = tn(ms[t, mine, :], bf[...])
    gother[...] = tn(ms[1 - t, mine, :], bf[...]).astype(BF16)
    for copy in back_copies:
        copy.wait()
    bm[...] = nn(g[...], bms[...]).astype(BF16)


def dense(mixed, gt, g, xs, cs, ops, dg, dl, dd, gain):
    count, width = xs.shape
    wide = mixed.shape[2]
    half = count // 2
    padded = -(-dg.shape[0] // 256) * 256
    half32, half16 = pltpu.VMEM((half, width), F32), pltpu.VMEM((half, width), BF16)
    hiddens = pltpu.VMEM((count, padded), BF16)
    return pl.pallas_call(
        dense_kernel,
        out_shape=(
            shape(count, wide, dtype=BF16), shape(half, width, dtype=BF16), shape(half, width), shape(half, width),
            shape(3 * padded, width, dtype=BF16), shape(wide, width), shape(wide, width, dtype=BF16), shape(8, width),
        ),
        in_specs=[VMEM] * 10,
        out_specs=[VMEM] * 8,
        scratch_shapes=[
            pltpu.VMEM((2, count, wide), BF16), pltpu.VMEM((count, width), BF16), hiddens, hiddens, hiddens,
            half16, half16, half32, half32, half16, pltpu.VMEM((half, wide), BF16), pltpu.VMEM((count, wide), BF16),
            pltpu.SemaphoreType.DMA((2, 4)),
        ],
        compiler_params=pltpu.CompilerParams(collective_id=1, has_side_effects=True, vmem_limit_bytes=LIMIT),
        name="dense",
    )(mixed, gt, g, xs, cs, ops, dg, dl, dd, gain)


def sixteens(start, size):
    return pl.ds(pl.multiple_of(start, 16), size)


class Sum:
    def __init__(self, dp, t, src, base, out, order, scratch):
        self.dp, self.t, self.src, self.base, self.out, self.order = dp, t, src, base, out, order
        self.acc, self.sems = scratch[0], scratch[1]
        self.rcv = scratch[2:5]
        self.snd = (None,) + tuple(scratch[5:7])
        self.at = [lax.div(dp, stride) % size for stride, size in order]
        self.rows = [out.shape[0]]
        self.start = [0]
        for (stride, size), c in zip(order, self.at):
            self.rows.append(self.rows[-1] // size)
            self.start.append(self.start[-1] + c * self.rows[-1])
        self.live = []

    @staticmethod
    def scratch(rows, lanes, order):
        counts, sizes = [], [rows]
        for stride, size in order:
            sizes.append(sizes[-1] // size)
            counts.append(size - 1)
        block = lambda n: pltpu.VMEM((counts[n], sizes[n + 1], lanes), BF16)
        return [
            pltpu.VMEM((sizes[1], lanes), F32), pltpu.SemaphoreType.DMA((2, 2 * sum(counts))),
            block(0), block(1), block(2), block(1), block(2),
        ]

    def peer(self, s, k):
        stride, size = self.order[s]
        d = (self.at[s] + k) % size
        return d, self.dp + stride * (d - self.at[s])

    def go(self, back, s, k, src, dst, peer):
        n = sum(size - 1 for _, size in self.order[:s]) + k - 1
        if back:
            n += sum(size - 1 for _, size in self.order)
        copy = remote(src, dst, self.sems.at[0, n], self.sems.at[1, n], (peer, self.t))
        copy.start()
        self.live.append(copy)

    def done(self):
        for copy in self.live:
            copy.wait()
        self.live = []

    def step(self, n):
        if n == 0:
            for k in range(1, self.order[0][1]):
                d, peer = self.peer(0, k)
                self.go(False, 0, k, self.src.at[sixteens(self.base + d * self.rows[1], self.rows[1])], self.rcv[0].at[k - 1], peer)
            return
        self.done()
        if n in (1, 2):
            size = self.rows[n + 1]
            inside = self.start[n] - self.start[1]
            for k in list(range(1, self.order[n][1])) + [0]:
                d, peer = self.peer(n, k)
                here = sixteens(inside + d * size, size)
                if n == 1:
                    total = self.src[sixteens(self.base + self.start[1] + d * size, size), :].astype(F32)
                else:
                    total = self.acc[here, :]
                for j in range(self.order[n - 1][1] - 1):
                    total = total + self.rcv[n - 1][j, sixteens(d * size, size), :].astype(F32)
                if k:
                    self.snd[n][k - 1] = total.astype(BF16)
                    self.go(False, n, k, self.snd[n].at[k - 1], self.rcv[n].at[k - 1], peer)
                else:
                    self.acc[here, :] = total
            return
        if n == 3:
            size = self.rows[3]
            total = self.acc[sixteens(self.start[3] - self.start[1], size), :]
            for j in range(self.order[2][1] - 1):
                total = total + self.rcv[2][j].astype(F32)
            self.out[sixteens(self.start[3], size), :] = total.astype(BF16)
        if n in (3, 4, 5):
            s = 5 - n
            rows = sixteens(self.start[s + 1], self.rows[s + 1])
            for k in range(1, self.order[s][1]):
                self.go(True, s, k, self.out.at[rows], self.out.at[rows], self.peer(s, k)[1])


ORDERS = (((1, 2), (2, 2), (4, 4)), ((1, 2), (4, 4), (2, 2)))


def tail_kernel(
    bq, bk, bv, bg, h1, gt, wq, wk, wv, wg, xs, br, gain, rec_l, asked, gout, dgain, dfirst, dsecond, dpk, dpv,
    red_a, red_b, gains_out, ret,
    src, out_a, out_b, part_s, part_r, bx, rec_x, gains_s, gains_r, ht, y_sems, x_sems, xy_sems, g_sems, *sums,
):
    dp, t = place()
    other = (dp, 1 - t)
    count, width = xs.shape
    half = count // 2
    wide = bq.shape[1]
    for n, b in enumerate((bq, bk, bv, bg)):
        rows = slice((n // 2) * width, (n // 2 + 1) * width)
        src[rows, (n % 2) * wide:(n % 2 + 1) * wide] = tn(h1[...], b[...]).astype(BF16)
    src[2 * width:2 * width + wide, :] = gout[...].astype(BF16)
    at = 2 * width + wide
    few = dpk.shape[1]
    src[at + PAIR:, :] = jnp.zeros((src.shape[0] - at - PAIR, width), BF16)
    for n in range(4):
        lanes = slice(n * PAIR, (n + 1) * PAIR)
        src[at:at + PAIR, lanes] = (dfirst, dsecond)[n // 2][n % 2].astype(BF16)
        src[at + PAIR:at + PAIR + few, lanes] = (dpk, dpv)[n // 2][n % 2].astype(BF16)
    greet([(flipped(dp, m), t) for m in range(1, PEERS)] + [other])
    totals = [
        Sum(dp, t, src, 0, out_a, ORDERS[0], sums[:7]),
        Sum(dp, t, src, out_a.shape[0], out_b, ORDERS[1], sums[7:]),
    ]

    def step(n):
        for total in totals:
            total.step(n)

    step(0)

    def partial(rows):
        result = jnp.zeros((ROWS, width), F32)
        for b, w in ((bq, wq), (bk, wk), (bv, wv), (bg, wg)):
            result = result + nt(nn(gt[rows, :], b[...]).astype(BF16), w[...])
        return result

    copies = []
    for c in range(half // ROWS):
        here = pl.ds(c * ROWS, ROWS)
        part_s[here, :] = partial(at_rows((1 - t) * half + c * ROWS, ROWS)).astype(BF16)
        copy = remote(part_s.at[here], part_r.at[here], y_sems.at[0, c], y_sems.at[1, c], other)
        copy.start()
        copies.append(copy)
        if c == 0:
            step(1)
    mgain = jnp.zeros((8, width), F32)
    for c in range(half // ROWS):
        here = pl.ds(c * ROWS, ROWS)
        rows = at_rows(t * half + c * ROWS, ROWS)
        own = partial(rows)
        copies[c].wait()
        back = own + part_r[here, :].astype(F32)
        x = xs[rows, :].astype(F32)
        factor = lax.rsqrt(jnp.mean(x * x, axis=-1, keepdims=True) + EPSILON)
        norm = x * factor
        inner = back * gain[...]
        bx[here, :] = (br[here, :] + factor * (inner - norm * jnp.mean(inner * norm, axis=-1, keepdims=True))).astype(BF16)
        mgain = mgain + jnp.sum((back * norm).reshape(ROWS // 8, 8, width), axis=0)
    back_x = spread(rec_x, dp, t, bx, x_sems, xy_sems)
    gains_s[0, 0] = mgain
    gains_s[0, 1] = dgain[...]
    c2 = lax.div(dp, 4)
    groups = [[other], [(flipped(dp, 1), t)], [(flipped(dp, 2), t)], [(dp + 4 * ((c2 + k) % 4 - c2), t) for k in (1, 2, 3)]]
    gain_copies = []

    def gain_step(n):
        if n:
            for copy in gain_copies:
                copy.wait()
            gain_copies.clear()
            value = gains_s[n - 1]
            for i in range(len(groups[n - 1])):
                value = value + gains_r[n - 1, i]
            gains_s[n] = value
        if n < 4:
            for i, peer in enumerate(groups[n]):
                copy = remote(gains_s.at[n], gains_r.at[n, i], g_sems.at[0, n, i], g_sems.at[1, n, i], peer)
                copy.start()
                gain_copies.append(copy)

    gain_step(0)
    step(2)
    asks = asked[...]
    asks_high = jnp.floor(asks * (1.0 / 32.0))
    asks_low = asks - 32.0 * asks_high
    slot = iota(PAIR, count, 1)
    rank = lax.div(slot, half) * HALF_SHARE + slot % HALF_SHARE
    pick = jnp.where(iota(PAIR, count, 0) == rank, 1.0, 0.0).astype(BF16)
    slot = iota(PEERS, count, 1)
    mine = iota(PEERS, count, 0) == lax.div(slot % half, HALF_SHARE)
    spread_out = 32.0 * nn(asks_high.astype(BF16), pick) + nn(asks_low.astype(BF16), pick)
    row = jnp.sum(jnp.where(mine, spread_out, 0.0), axis=0, keepdims=True)
    for c in range(count // ROWS):
        ht[c * ROWS:(c + 1) * ROWS, :] = jnp.where((iota(ROWS, count, 0) + c * ROWS).astype(F32) == row, 1.0, 0.0).astype(BF16)
    gain_step(1)
    ret[0] = nn(ht[...], rec_l[...]).astype(BF16)
    passed_x = pass_on(rec_x, dp, t, back_x, xy_sems)
    gain_step(2)
    step(3)
    gain_step(3)
    step(4)
    for copy in passed_x:
        copy.wait()
    ret[1] = nn(ht[...], rec_x[...]).astype(BF16)
    gain_step(4)
    gains_out[...] = gains_s[4]
    step(5)
    step(6)
    red_a[...] = out_a[...]
    red_b[...] = out_b[...]


def tail(bq, bk, bv, bg, h1, gt, wq, wk, wv, wg, xs, br, gain, rec_l, asked, gout, dgain, dfirst, dsecond, dpk, dpv):
    count, width = xs.shape
    half = count // 2
    wide = bq.shape[1]
    rows = -(-(2 * width + wide + PAIR + dpk.shape[1]) // 512) * 512
    part = rows // 2
    half16 = pltpu.VMEM((half, width), BF16)
    full16 = pltpu.VMEM((count, width), BF16)
    sems = pltpu.SemaphoreType.DMA((2, PEERS))
    reduced = pltpu.VMEM((part, width), BF16)
    return pl.pallas_call(
        tail_kernel,
        out_shape=(shape(part, width, dtype=BF16), shape(part, width, dtype=BF16), shape(2, 8, width), shape(2, count, width, dtype=BF16)),
        in_specs=[VMEM] * 21,
        out_specs=[VMEM] * 4,
        scratch_shapes=[
            pltpu.VMEM((rows, width), BF16), reduced, reduced, half16, half16, half16, full16,
            pltpu.VMEM((5, 2, 8, width), F32), pltpu.VMEM((4, 3, 2, 8, width), F32), pltpu.VMEM((count, count), BF16),
            pltpu.SemaphoreType.DMA((2, 2)), sems, sems, pltpu.SemaphoreType.DMA((2, 4, 3)),
            *Sum.scratch(part, width, ORDERS[0]), *Sum.scratch(part, width, ORDERS[1]),
        ],
        compiler_params=pltpu.CompilerParams(collective_id=2, has_side_effects=True, vmem_limit_bytes=LIMIT),
        name="tail",
    )(bq, bk, bv, bg, h1, gt, wq, wk, wv, wg, xs, br, gain, rec_l, asked, gout, dgain, dfirst, dsecond, dpk, dpv)


def finish_kernel(
    fa, fb, qa, qb, gains, ret, lo, bx, mgain, gq, gk, gv, gg, gout, gpk, gpv, first, second, dgain, ggate, glift, gdown,
):
    hidden, width = ggate.shape
    padded = -(-hidden // 256) * 256
    wide = gq.shape[1]
    few = gpk.shape[0]

    def fetch(pair, begin, rows, lanes=slice(None)):
        a, b = pair
        cut = a.shape[0]
        pieces = []
        if begin < cut:
            pieces.append(a[begin:min(begin + rows, cut), lanes])
        if begin + rows > cut:
            pieces.append(b[max(begin - cut, 0):begin + rows - cut, lanes])
        return jnp.concatenate(pieces, axis=0).astype(F32) if len(pieces) > 1 else pieces[0].astype(F32)

    lo[...] = ret[0]
    bx[...] = ret[1]
    mgain[...] = jnp.sum(gains[0], axis=0, keepdims=True)
    dgain[...] = jnp.sum(gains[1], axis=0, keepdims=True)
    for n, ref in enumerate((ggate, glift, gdown)):
        ref[...] = fetch((fa, fb), n * padded, hidden)
    for n, ref in enumerate((gq, gk, gv, gg)):
        ref[...] = fetch((qa, qb), (n // 2) * width, width, slice((n % 2) * wide, (n % 2 + 1) * wide))
    gout[...] = fetch((qa, qb), 2 * width, wide)
    at = 2 * width + wide
    for n in range(4):
        lanes = slice(n * PAIR, (n + 1) * PAIR)
        (first, second)[n // 2][n % 2] = fetch((qa, qb), at, PAIR, lanes)
        (gpk, gpv)[n // 2][:, (n % 2) * PAIR:(n % 2 + 1) * PAIR] = fetch((qa, qb), at + PAIR, few, lanes)


def finish(fa, fb, qa, qb, gains, ret, hidden, wide, few):
    count, width = ret.shape[1:]
    pairs = wide // PAIR
    rows = shape(count, width, dtype=BF16)
    square = shape(width, wide)
    state = shape(pairs, PAIR, PAIR)
    outs = (
        rows, rows, shape(1, width), square, square, square, square, shape(wide, width), shape(few, wide), shape(few, wide),
        state, state, shape(1, width), shape(hidden, width), shape(hidden, width), shape(hidden, width),
    )
    return pl.pallas_call(
        finish_kernel,
        out_shape=outs,
        in_specs=[VMEM] * 6,
        out_specs=[VMEM] * len(outs),
        compiler_params=pltpu.CompilerParams(vmem_limit_bytes=LIMIT),
        name="finish",
    )(fa, fb, qa, qb, gains, ret)


def forward_remote(
    starts, rates, tok, gain, wq, wk, wv, wg, pk, pvt, first, second, sent_c, op,
    h1, q, k, v, gate, recall, mixed, cs_out, ops_out, kt, lse, a_all, c_all, pre_all, e_all, u_all, atth,
    vt, att, diagonal, a_s, c_s, sa_s, sc_s, mx, cs, ops, c_sems, cy_sems, y_sems,
):
    dp, t = place()
    other = (dp, 1 - t)
    count = tok.shape[0]
    pairs = first.shape[0]
    per = ROWS // STRETCH

    def project(b, _):
        rows = pl.ds(pl.multiple_of(b * ROWS, ROWS), ROWS)
        x = tok[rows, :].astype(F32)
        factor = lax.rsqrt(jnp.mean(x * x, axis=-1, keepdims=True) + EPSILON)
        h = (x * factor * gain[...]).astype(BF16)
        h1[rows, :] = h
        for part, (ref, w) in enumerate(((q, wq), (k, wk), (v, wv))):
            made = nn(h, w[...])
            low = made.astype(BF16)
            for p in range(pairs):
                ref[p, rows, :] = low[:, p * PAIR:(p + 1) * PAIR]
            if part > 0:
                made_t = jnp.transpose(made).astype(BF16)
                target = kt if part == 1 else vt
                for h_i in range(2 * pairs):
                    target[h_i, :, rows] = made_t[h_i * HEAD_DIM:(h_i + 1) * HEAD_DIM]
        g = sigmoid(nn(h, wg[...]))
        for p in range(pairs):
            gate[p, rows, :] = g[:, p * PAIR:(p + 1) * PAIR]
        return 0

    lax.fori_loop(0, count // ROWS, project, 0)
    greet([(flipped(dp, m), t) for m in range(1, PEERS)] + [other])
    ops[t] = op[...]
    waits = [remote(ops.at[t], ops.at[t], y_sems.at[0, 0], y_sems.at[1, 0], other)]
    waits[0].start()
    cot_copies = spread(cs, dp, t, sent_c, c_sems, cy_sems)
    a_s[...] = first[...]
    c_s[...] = second[...]
    sa_s[...] = jnp.zeros_like(sa_s)
    sc_s[...] = jnp.zeros_like(sc_s)

    def memory_step(u):
        rows = pl.ds(pl.multiple_of(u * STRETCH, STRETCH), STRETCH)
        fresh = starts[u] > 0
        for p in range(pairs):
            a = jnp.where(fresh, first[p], a_s[p])
            c = jnp.where(fresh, second[p], c_s[p])
            sa = jnp.where(fresh, 0.0, sa_s[p])
            sc = jnp.where(fresh, 0.0, sc_s[p])
            ab, cb = a.astype(BF16), c.astype(BF16)
            a_all[u, p] = ab
            c_all[u, p] = cb
            km = both(k[p, rows, :])
            lhs = jnp.concatenate([both(q[p, rows, :]), km], axis=0)
            pre = nn(lhs, ab)
            pre_all[u, p] = pre
            sig = sigmoid(pre)
            act = pre * sig
            actb = act.astype(BF16)
            out = nt(actb, cb)
            recall[p, rows, :] = joined(out[:PAIR])
            e = joined(out[PAIR:]) - v[p, rows, :].astype(F32)
            eb = e.astype(BF16)
            e_all[p, rows, :] = eb
            em = both(eb)
            dev = nn(em, cb)
            u_all[u, p] = dev
            sigk, actk = sig[PAIR:], act[PAIR:]
            wgt = (dev * (sigk + actk * (1.0 - sigk))).astype(BF16)
            ga = tn(km, wgt)
            gc = tn(em, actb[PAIR:])
            th = [rates[0, 2 * p + i, u] * (1.0 / STRETCH) for i in range(2)]
            eta = [rates[1, 2 * p + i, u] for i in range(2)]
            al = [1.0 - rates[2, 2 * p + i, u] for i in range(2)]
            sa = scaled(sa, eta) - scaled(ga, th)
            sc = scaled(sc, eta) - scaled(gc, th)
            sa_s[p] = sa
            sc_s[p] = sc
            a_s[p] = scaled(a, al) + sa
            c_s[p] = scaled(c, al) + sc

    def attention_unit(qb, head):
        p, half = head // 2, head % 2
        rows = pl.ds(qb * ROWS, ROWS)
        qh = keep(q[p, rows, :], half) * jnp.asarray(HEAD_DIM ** -0.5, BF16)
        scores = []
        for kb in range(qb + 1):
            s = nt(k[p, kb * ROWS:(kb + 1) * ROWS, :], qh)
            if kb == qb:
                s = s + diagonal[...]
            else:
                s = earlier(s, starts, kb, qb, per)
            scores.append(s)
        sp = nt(pk[p], qh)
        peak = jnp.max(sp, axis=0, keepdims=True)
        for s in scores:
            peak = jnp.maximum(peak, jnp.max(s, axis=0, keepdims=True))
        ep = jnp.exp(sp - peak)
        total = jnp.sum(ep, axis=0, keepdims=True)
        out = nn(pvt[head], ep.astype(BF16))
        for kb, s in enumerate(scores):
            e = jnp.exp(s - peak)
            total = total + jnp.sum(e, axis=0, keepdims=True)
            out = out + nn(vt[head, :, kb * ROWS:(kb + 1) * ROWS], e.astype(BF16))
        att[head, :, rows] = out * (1.0 / total)
        lse[head, :, rows] = peak + jnp.log(total)

    heads = 2 * pairs
    for qb in range(count // ROWS):
        fill_diagonal(diagonal, starts[qb * per])

        def run(i, _, qb=qb):
            memory_step(qb * per + i)
            attention_unit(qb, i)
            return 0
        lax.fori_loop(0, per, run, 0)
        rows = pl.ds(qb * ROWS, ROWS)
        for p in range(pairs):
            got = jnp.concatenate([att[2 * p, :, rows], att[2 * p + 1, :, rows]], axis=0)
            wide_att = jnp.transpose(got)
            atth[p, rows, :] = wide_att
            mx[t, rows, p * PAIR:(p + 1) * PAIR] = (wide_att + gate[p, rows, :] * recall[p, rows, :]).astype(BF16)
        copy = remote(mx.at[t, rows], mx.at[t, rows], y_sems.at[0, 1 + qb], y_sems.at[1, 1 + qb], other)
        copy.start()
        waits.append(copy)
        if qb == 1:
            waits.extend(pass_on(cs, dp, t, cot_copies, cy_sems))
    for copy in waits:
        copy.wait()
    mixed[...] = mx[...]
    cs_out[...] = cs[...]
    ops_out[...] = ops[...]


def backward_remote(
    starts, rates, bm, q, k, v, gate, recall, kt, pk, pkt, pv, lse, a_all, c_all, pre_all, e_all, u_all, atth, facc, second_s, second_own, gout, gother,
    dq, dk, dv, dg, dpk, dpv, dfirst, dsecond, fa, fb, recl_out, gout_out,
    dqt, dd, dks, dvs, mq, bmp, diagonal, da_s, dc_s, dsa_s, dsc_s,
    out_a, out_b, second_r, gother_r, lo, rec_l, y_sems, l_sems, ly_sems, *sums,
):
    dp, t = place()
    other = (dp, 1 - t)
    count = bm.shape[0]
    pairs = q.shape[0]
    heads = 2 * pairs
    per = ROWS // STRETCH
    nblocks = count // ROWS
    ones = [jnp.where(lanes_of(i, 8), 1.0, 0.0).astype(F32) for i in range(2)]
    for b in range(nblocks):
        rows = pl.ds(b * ROWS, ROWS)
        for p in range(pairs):
            gb = bm[rows, p * PAIR:(p + 1) * PAIR]
            bmp[p, rows, :] = gb
            g = gb.astype(F32)
            inner = g * atth[p, rows, :]
            for i in range(2):
                row = lax.dot_general(ones[i], inner, (((1,), (1,)), ((), ())), precision=lax.Precision.HIGHEST, preferred_element_type=F32)
                dd[2 * p + i, :, rows] = row[:1]
            gt = gate[p, rows, :]
            dg[rows, p * PAIR:(p + 1) * PAIR] = (g * recall[p, rows, :] * gt * (1.0 - gt)).astype(BF16)
    for ref in (dpk, dpv, dfirst, dsecond, dks, dvs, da_s, dc_s, dsa_s, dsc_s):
        ref[...] = jnp.zeros_like(ref)

    def memory_step(u):
        rows = pl.ds(pl.multiple_of(u * STRETCH, STRETCH), STRETCH)
        fresh = starts[u] > 0
        for p in range(pairs):
            th = [rates[0, 2 * p + i, u] * (-1.0 / STRETCH) for i in range(2)]
            eta = [rates[1, 2 * p + i, u] for i in range(2)]
            al = [1.0 - rates[2, 2 * p + i, u] for i in range(2)]
            da, dc = da_s[p], dc_s[p]
            dsa = dsa_s[p] + da
            dsc = dsc_s[p] + dc
            dga = scaled(dsa, th).astype(BF16)
            dgc = scaled(dsc, th).astype(BF16)
            ab, cb = a_all[u, p], c_all[u, p]
            km, qm = both(k[p, rows, :]), both(q[p, rows, :])
            em = both(e_all[p, rows, :])
            pre = pre_all[u, p]
            sig = sigmoid(pre)
            act = pre * sig
            actb = act.astype(BF16)
            slope = sig + act * (1.0 - sig)
            sigk, prek, slopek = sig[PAIR:], pre[PAIR:], slope[PAIR:]
            dev = u_all[u, p]
            curve = sigk * (1.0 - sigk) * (2.0 + prek * (1.0 - 2.0 * sigk))
            wgt = (dev * slopek).astype(BF16)
            back = bmp[p, rows, :].astype(F32) * gate[p, rows, :]
            rm = both(back.astype(BF16))
            dpre_q = (nn(rm, cb) * slope[:PAIR]).astype(BF16)
            mq[0, p, rows, :] = joined(nt(dpre_q, ab))
            dw = nn(km, dga)
            du = (dw * slopek).astype(BF16)
            cc = jnp.concatenate([dgc, cb], axis=1)
            de = joined(nt(jnp.concatenate([actb[PAIR:], du], axis=1), cc))
            mq[2, p, rows, :] = -de
            dem = both(de.astype(BF16))
            dsk = nn(jnp.concatenate([em, dem], axis=1), jnp.concatenate([dgc, cb], axis=0))
            dpre = (dsk * slopek + dw * dev * curve).astype(BF16)
            mq[1, p, rows, :] = joined(nt(jnp.concatenate([wgt, dpre], axis=1), jnp.concatenate([dga, ab], axis=1)))
            ga = tn(jnp.concatenate([km, qm], axis=0), jnp.concatenate([dpre, dpre_q], axis=0))
            gc = tn(jnp.concatenate([em, dem], axis=0), jnp.concatenate([du, actb[PAIR:]], axis=0))
            gc = gc + tn(rm, actb[:PAIR])
            da = scaled(da, al) + ga
            dc = scaled(dc, al) + gc
            dfirst[p] = dfirst[p] + jnp.where(fresh, da, 0.0)
            dsecond[p] = dsecond[p] + jnp.where(fresh, dc, 0.0)
            da_s[p] = jnp.where(fresh, 0.0, da)
            dc_s[p] = jnp.where(fresh, 0.0, dc)
            dsa_s[p] = jnp.where(fresh, 0.0, scaled(dsa, eta))
            dsc_s[p] = jnp.where(fresh, 0.0, scaled(dsc, eta))

    def attention_unit(qb, head):
        p, half = head // 2, head % 2
        rows = pl.ds(qb * ROWS, ROWS)
        qh = keep(q[p, rows, :], half) * jnp.asarray(HEAD_DIM ** -0.5, BF16)
        gh = keep(bmp[p, rows, :], half)
        lrow, drow = lse[head, :, rows], dd[head, :, rows]
        acc = jnp.zeros((HEAD_DIM, ROWS), F32)
        for kb in range(qb + 1):
            krows = slice(kb * ROWS, (kb + 1) * ROWS)
            s = nt(k[p, krows, :], qh) - lrow
            if kb == qb:
                s = s + diagonal[...]
            else:
                s = earlier(s, starts, kb, qb, per)
            prob = jnp.exp(s)
            ds = (prob * (nt(v[p, krows, :], gh) - drow)).astype(BF16)
            dvs[p, krows, :] = dvs[p, krows, :] + nn(prob.astype(BF16), gh)
            dks[p, krows, :] = dks[p, krows, :] + nn(ds, qh)
            acc = acc + nn(kt[head, :, krows], ds)
        prob = jnp.exp(nt(pk[p], qh) - lrow)
        ds = (prob * (nt(pv[p], gh) - drow)).astype(BF16)
        dpv[p] = dpv[p] + nn(prob.astype(BF16), gh)
        dpk[p] = dpk[p] + nn(ds, qh)
        acc = acc + nn(pkt[head], ds)
        dqt[head, :, rows] = acc * (HEAD_DIM ** -0.5)

    greet([(flipped(dp, m), t) for m in range(1, PEERS)] + [other])
    totals = [
        Sum(dp, t, facc, 0, out_a, ORDERS[0], sums[:7]),
        Sum(dp, t, facc, out_a.shape[0], out_b, ORDERS[1], sums[7:]),
    ]
    waits = []
    lo_copies = []

    def step(n):
        for total in totals:
            total.step(n)

    def background(point):
        if point == 0:
            for n, (src, dst) in enumerate(((second_s, second_r), (gother, gother_r))):
                copy = remote(src, dst, y_sems.at[0, n], y_sems.at[1, n], other)
                copy.start()
                waits.append(copy)
        if point == 3:
            for copy in waits:
                copy.wait()
            waits.clear()
            lo[...] = (second_own[...] + second_r[...].astype(F32)).astype(BF16)
            gout_out[...] = gout[...] + gother_r[...].astype(F32)
            lo_copies.extend(spread(rec_l, dp, t, lo, l_sems, ly_sems))
        if point == 7:
            waits.extend(pass_on(rec_l, dp, t, lo_copies, ly_sems))
        plan = {0: 0, 1: 1, 3: 2, 5: 3, 6: 4, 7: 5}
        if point in plan:
            step(plan[point])

    for qb in reversed(range(nblocks)):
        fill_diagonal(diagonal, starts[qb * per])

        def run(i, _, qb=qb):
            memory_step(qb * per + per - 1 - i)
            attention_unit(qb, i)
            return 0
        for part in range(2):
            background((nblocks - 1 - qb) * 2 + part)
            lax.fori_loop(part * per // 2, (part + 1) * per // 2, run, 0)
    step(6)
    for copy in waits:
        copy.wait()
    fa[...] = out_a[...]
    fb[...] = out_b[...]
    recl_out[...] = rec_l[...]
    for b in range(nblocks):
        rows = pl.ds(b * ROWS, ROWS)
        for p in range(pairs):
            cols = slice(p * PAIR, (p + 1) * PAIR)
            got = jnp.concatenate([dqt[2 * p, :, rows], dqt[2 * p + 1, :, rows]], axis=0)
            dq[rows, cols] = (jnp.transpose(got) + mq[0, p, rows, :]).astype(BF16)
            dk[rows, cols] = (dks[p, rows, :] + mq[1, p, rows, :]).astype(BF16)
            dv[rows, cols] = (dvs[p, rows, :] + mq[2, p, rows, :]).astype(BF16)


def remote_forward(starts, rates, tok, gain, wq, wk, wv, wg, pk, pvt, first, second, sent_c, op):
    count, width = tok.shape
    pairs = first.shape[0]
    heads, steps = 2 * pairs, starts.shape[0]
    flat = lambda dtype: shape(pairs, count, PAIR, dtype=dtype)
    outs = (
        shape(count, width, dtype=BF16), flat(BF16), flat(BF16), flat(BF16), flat(F32), flat(F32),
        shape(2, count, pairs * PAIR, dtype=BF16),
        shape(count, width, dtype=BF16), shape(2, *op.shape, dtype=BF16), shape(heads, HEAD_DIM, count, dtype=BF16), shape(heads, 1, count),
        shape(steps, pairs, PAIR, PAIR, dtype=BF16), shape(steps, pairs, PAIR, PAIR, dtype=BF16),
        shape(steps, pairs, 2 * PAIR, PAIR), flat(BF16), shape(steps, pairs, PAIR, PAIR), flat(F32),
    )
    sems = pltpu.SemaphoreType.DMA((2, PEERS))
    state = pltpu.VMEM((pairs, PAIR, PAIR), F32)
    return pl.pallas_call(
        forward_remote,
        out_shape=outs,
        in_specs=[SMEM, SMEM] + [VMEM] * 12,
        out_specs=[VMEM] * len(outs),
        scratch_shapes=[
            pltpu.VMEM((heads, HEAD_DIM, count), BF16), pltpu.VMEM((heads, HEAD_DIM, count), F32),
            pltpu.VMEM((ROWS, ROWS), F32), state, state, state, state,
            pltpu.VMEM((2, count, pairs * PAIR), BF16), pltpu.VMEM((count, width), BF16), pltpu.VMEM((2,) + op.shape, BF16),
            sems, sems, pltpu.SemaphoreType.DMA((2, 8)),
        ],
        compiler_params=pltpu.CompilerParams(collective_id=3, has_side_effects=True, vmem_limit_bytes=LIMIT),
        name="mixer_forward",
    )(starts, rates, tok, gain, wq, wk, wv, wg, pk, pvt, first, second, sent_c, op)


def remote_backward(starts, rates, bm, q, k, v, gate, recall, kt, pk, pkt, pv, lse, a_all, c_all, pre_all, e_all, u_all, atth, facc, second_s, second_own, gout, gother):
    count, wide = bm.shape
    pairs = q.shape[0]
    heads = 2 * pairs
    total, width = facc.shape
    rows_b = total // 512 * 256
    rows_a = total - rows_b
    half = second_s.shape[0]
    sems = pltpu.SemaphoreType.DMA((2, PEERS))
    outs = (
        shape(count, wide, dtype=BF16), shape(count, wide, dtype=BF16), shape(count, wide, dtype=BF16), shape(count, wide, dtype=BF16),
        shape(*pk.shape), shape(*pv.shape), shape(pairs, PAIR, PAIR), shape(pairs, PAIR, PAIR),
        shape(rows_a, width, dtype=BF16), shape(rows_b, width, dtype=BF16), shape(count, width, dtype=BF16), shape(*gout.shape),
    )
    state = pltpu.VMEM((pairs, PAIR, PAIR), F32)
    flat = pltpu.VMEM((pairs, count, PAIR), F32)
    return pl.pallas_call(
        backward_remote,
        out_shape=outs,
        in_specs=[SMEM, SMEM] + [VMEM] * 22,
        out_specs=[VMEM] * len(outs),
        scratch_shapes=[
            pltpu.VMEM((heads, HEAD_DIM, count), F32), pltpu.VMEM((heads, 1, count), F32), flat, flat,
            pltpu.VMEM((3, pairs, count, PAIR), F32), pltpu.VMEM((pairs, count, PAIR), BF16),
            pltpu.VMEM((ROWS, ROWS), F32), state, state, state, state,
            pltpu.VMEM((rows_a, width), BF16), pltpu.VMEM((rows_b, width), BF16), pltpu.VMEM((half, width), BF16),
            pltpu.VMEM(gother.shape, BF16), pltpu.VMEM((half, width), BF16), pltpu.VMEM((count, width), BF16),
            pltpu.SemaphoreType.DMA((2, 2)), sems, sems,
            *Sum.scratch(rows_a, width, ORDERS[0]), *Sum.scratch(rows_b, width, ORDERS[1]),
        ],
        compiler_params=pltpu.CompilerParams(collective_id=4, has_side_effects=True, vmem_limit_bytes=LIMIT),
        name="mixer_backward",
    )(starts, rates, bm, q, k, v, gate, recall, kt, pk, pkt, pv, lse, a_all, c_all, pre_all, e_all, u_all, atth, facc, second_s, second_own, gout, gother)


def block_body(
    tokens, cotangent, source_index, tract_starts, memory_rates, mixer_gain, query_proj, key_proj, value_proj, gate_proj,
    out_proj, persist_keys, persist_values, memory_first, memory_second, dense_gain, dense_gate, dense_lift, dense_down,
):
    pairs = query_proj.shape[1] // PAIR
    by_pair = lambda value: value.reshape(-1, pairs, PAIR).transpose(1, 0, 2)
    by_head = lambda value: value.T.reshape(2 * pairs, HEAD_DIM, -1)
    rates = memory_rates.transpose(0, 2, 1)
    pk, pv = by_pair(persist_keys), by_pair(persist_values)
    pkt, pvt = by_head(persist_keys), by_head(persist_values)
    first = memory_first.reshape(pairs, PAIR, PAIR)
    second = memory_second.transpose(0, 2, 1).reshape(pairs, PAIR, PAIR)
    xs, sent_c, seq, g, gt, asked = rows_in(source_index, tokens, cotangent)
    h1, query, keys, values, gate, recall, mixed, cs, ops, keys_t, lse, a_all, c_all, pre_all, e_all, u_all, attended = remote_forward(
        tract_starts, rates, seq, mixer_gain[None], query_proj, key_proj, value_proj, gate_proj, pk, pvt, first, second, sent_c, out_proj
    )
    back_mixed, second_s, second_own, back_resid, dense_grads, gout, gother, gain_two = dense(
        mixed, gt, g, xs, cs, ops, dense_gate.T, dense_lift.T, dense_down, dense_gain[None]
    )
    bq, bk, bv, bg, grad_pk, grad_pv, grad_first, grad_second, fa, fb, rec_l, gout = remote_backward(
        tract_starts, rates, back_mixed, query, keys, values, gate, recall, keys_t, pk, pkt, pv,
        lse, a_all, c_all, pre_all, e_all, u_all, attended, dense_grads, second_s, second_own, gout, gother,
    )
    qa, qb, gains, ret = tail(
        bq, bk, bv, bg, h1, gt, query_proj, key_proj, value_proj, gate_proj, xs, back_resid, mixer_gain[None], rec_l, asked,
        gout, gain_two, grad_first, grad_second, grad_pk, grad_pv,
    )
    outs = list(finish(fa, fb, qa, qb, gains, ret, dense_gate.shape[1], query_proj.shape[1], persist_keys.shape[0]))
    outs[2] = outs[2][0]
    outs[10] = outs[10].reshape(memory_first.shape)
    outs[11] = outs[11].reshape(memory_first.shape).transpose(0, 2, 1)
    outs[12] = outs[12][0]
    outs[13], outs[14] = outs[13].T, outs[14].T
    return tuple(outs)


def body(
    tokens,
    cotangent,
    source_index,
    tract_starts,
    memory_rates,
    mixer_gain,
    query_proj,
    key_proj,
    value_proj,
    gate_proj,
    out_proj,
    persist_keys,
    persist_values,
    memory_first,
    memory_second,
    dense_gain,
    dense_gate,
    dense_lift,
    dense_down,
):
    count = tokens.shape[0]
    width = tokens.shape[1]
    peers = lax.axis_size("dp")
    share = count // peers
    arrival = jnp.argsort(source_index)
    wanted = (source_index[arrival] % count).reshape(peers, share)
    asked = lax.all_to_all(wanted, "dp", split_axis=0, concat_axis=0, tiled=True).reshape(count)
    got_tokens, got_cot = (
        lax.all_to_all(
            tokens[asked].reshape(peers, share, width),
            "dp",
            split_axis=0,
            concat_axis=0,
            tiled=True,
        ),
        lax.all_to_all(
            cotangent[asked].reshape(peers, share, width),
            "dp",
            split_axis=0,
            concat_axis=0,
            tiled=True,
        ),
    )
    placing = jnp.argsort(arrival)
    seq_tokens = got_tokens.reshape(count, width)[placing]
    seq_cot = got_cot.reshape(count, width)[placing]
    seq_x = seq_tokens.astype(jnp.float32)
    first_norm, factor_one = norm_forward(seq_x)
    pairs = query_proj.shape[1] // PAIR
    by_pair = lambda value: value.reshape(-1, pairs, PAIR).transpose(1, 0, 2)
    by_head = lambda value: value.T.reshape(2 * pairs, HEAD_DIM, -1)
    weights = jnp.concatenate([query_proj, key_proj, value_proj, gate_proj], axis=1)
    pk, pv = by_pair(persist_keys), by_pair(persist_values)
    first = memory_first.reshape(pairs, PAIR, PAIR)
    second = memory_second.transpose(0, 2, 1).reshape(pairs, PAIR, PAIR)
    h_one, query, keys, values, gate, recall, mixed, keys_t, lse, a_all, c_all, pre_all, e_all, u_all, attended = mixer_forward(
        tract_starts, memory_rates, seq_tokens, mixer_gain[None], weights, pk, by_head(persist_values), first, second
    )
    first_out = lax.psum(product(mixed, out_proj), "tensor")
    resid = seq_x + first_out
    norm_two, factor_two = norm_forward(resid)
    h_two = (norm_two * dense_gain).astype(jnp.bfloat16)
    gated = product(h_two, dense_gate)
    lifted = product(h_two, dense_lift)
    sigma = jax.nn.sigmoid(gated)
    active = gated * sigma
    hidden = (active * lifted).astype(jnp.bfloat16)
    second_out = lax.psum(product(hidden, dense_down).astype(jnp.bfloat16), "tensor").astype(
        jnp.float32
    )
    seq_out = (resid + second_out).astype(jnp.bfloat16)
    grad_down = product(hidden.T, seq_cot)
    back_hidden = product(seq_cot, dense_down.T)
    back_gated = (back_hidden * lifted * (sigma + gated * sigma * (1.0 - sigma))).astype(
        jnp.bfloat16
    )
    back_lifted = (back_hidden * active).astype(jnp.bfloat16)
    grad_gate = product(h_two.T, back_gated)
    grad_lift = product(h_two.T, back_lifted)
    back_two = lax.psum(
        product(back_gated, dense_gate.T) + product(back_lifted, dense_lift.T), "tensor"
    )
    back_norm_two, grad_dgain = norm_backward(back_two, norm_two, factor_two, dense_gain)
    residual_gradient = seq_cot.astype(jnp.float32) + back_norm_two
    back_first = residual_gradient.astype(jnp.bfloat16)
    grad_out = product(mixed.T, back_first)
    back_mixed = product(back_first, out_proj.T).astype(jnp.bfloat16)
    back_query, back_keys, cotangent_payloads, back_gate, grad_pk, grad_pv, grad_first, grad_second = mixer_backward(
        tract_starts, memory_rates, back_mixed, query, keys, values, gate, recall, keys_t, pk, by_head(persist_keys), pv,
        lse, a_all, c_all, pre_all, e_all, u_all, attended,
    )
    grad_first = grad_first.reshape(memory_first.shape)
    grad_second = grad_second.reshape(memory_first.shape).transpose(0, 2, 1)
    grad_query = product(h_one.T, back_query)
    grad_key = product(h_one.T, back_keys)
    grad_value = product(h_one.T, cotangent_payloads)
    grad_gproj = product(h_one.T, back_gate)
    back_one = lax.psum(
        product(back_query, query_proj.T)
        + product(back_keys, key_proj.T)
        + product(cotangent_payloads, value_proj.T)
        + product(back_gate, gate_proj.T),
        "tensor",
    )
    back_norm_one, grad_mgain = norm_backward(back_one, first_norm, factor_one, mixer_gain)
    back_x = (residual_gradient + back_norm_one).astype(jnp.bfloat16)
    grad_pkeys = grad_pk.transpose(1, 0, 2).reshape(persist_keys.shape)
    grad_pvalues = grad_pv.transpose(1, 0, 2).reshape(persist_values.shape)
    (
        grad_mgain,
        grad_query,
        grad_key,
        grad_value,
        grad_gproj,
        grad_out,
        grad_pkeys,
        grad_pvalues,
        grad_first,
        grad_second,
        grad_dgain,
        grad_gate,
        grad_lift,
        grad_down,
    ) = lax.psum(
        (
            grad_mgain,
            grad_query,
            grad_key,
            grad_value,
            grad_gproj,
            grad_out,
            grad_pkeys,
            grad_pvalues,
            grad_first,
            grad_second,
            grad_dgain,
            grad_gate,
            grad_lift,
            grad_down,
        ),
        "dp",
    )
    ret_out, ret_grad = (
        lax.all_to_all(
            seq_out[arrival].reshape(peers, share, width),
            "dp",
            split_axis=0,
            concat_axis=0,
            tiled=True,
        ),
        lax.all_to_all(
            back_x[arrival].reshape(peers, share, width),
            "dp",
            split_axis=0,
            concat_axis=0,
            tiled=True,
        ),
    )
    undo = jnp.argsort(asked)
    layer_output = ret_out.reshape(count, width)[undo]
    input_grad = ret_grad.reshape(count, width)[undo]
    return (
        layer_output,
        input_grad,
        grad_mgain,
        grad_query,
        grad_key,
        grad_value,
        grad_gproj,
        grad_out,
        grad_pkeys,
        grad_pvalues,
        grad_first,
        grad_second,
        grad_dgain,
        grad_gate,
        grad_lift,
        grad_down,
    )


def solution(mesh):
    chosen = block_body if mesh.shape["dp"] == PEERS else body
    in_specs = (
        P("dp", None),
        P("dp", None),
        P("dp"),
        P("dp"),
        P(None, "dp", "tensor"),
        P(),
        P(None, "tensor"),
        P(None, "tensor"),
        P(None, "tensor"),
        P(None, "tensor"),
        P("tensor", None),
        P(None, "tensor"),
        P(None, "tensor"),
        P("tensor", None, None),
        P("tensor", None, None),
        P(),
        P(None, "tensor"),
        P(None, "tensor"),
        P("tensor", None),
    )
    out_specs = (
        P("dp", None),
        P("dp", None),
        P(),
        P(None, "tensor"),
        P(None, "tensor"),
        P(None, "tensor"),
        P(None, "tensor"),
        P("tensor", None),
        P(None, "tensor"),
        P(None, "tensor"),
        P("tensor", None, None),
        P("tensor", None, None),
        P(),
        P(None, "tensor"),
        P(None, "tensor"),
        P("tensor", None),
    )
    return jax.shard_map(chosen, mesh=mesh, in_specs=in_specs, out_specs=out_specs, check_vma=False)
```

```python
import jax
import jax.numpy as jnp
from jax import lax
from jax.experimental import pallas as pl
from jax.experimental.pallas import tpu as pltpu
from jax.sharding import PartitionSpec as P

HEAD_DIM = 64


EPSILON = 1e-06
MASKED = -1e30


def product(left, right):
    return jnp.dot(left, right, preferred_element_type=jnp.float32)


def norm_forward(value):
    factor = lax.rsqrt(jnp.mean(value * value, axis=-1, keepdims=True) + EPSILON)
    return (value * factor, factor)


def norm_backward(grad, normed, factor, gain):
    inner = grad * gain
    back = factor * (inner - normed * jnp.mean(inner * normed, axis=-1, keepdims=True))
    return (back, jnp.sum(grad * normed, axis=0))


F32, BF16 = jnp.float32, jnp.bfloat16
PAIR = 2 * HEAD_DIM
ROWS = 256
STRETCH = 64


def nn(a, b):
    return lax.dot_general(a, b, (((1,), (0,)), ((), ())), preferred_element_type=F32)


def nt(a, b):
    return lax.dot_general(a, b, (((1,), (1,)), ((), ())), preferred_element_type=F32)


def tn(a, b):
    return lax.dot_general(a, b, (((0,), (0,)), ((), ())), preferred_element_type=F32)


def sigmoid(v):
    return 1.0 / (1.0 + jnp.exp(-v))


def lanes_of(half, rows=1):
    return (lax.broadcasted_iota(jnp.int32, (rows, PAIR), 1) // HEAD_DIM) == half


def keep(value, half):
    return jnp.where(lanes_of(half), value, jnp.zeros_like(value))


def both(value):
    return jnp.concatenate([keep(value, 0), keep(value, 1)], axis=0)


def joined(stacked):
    rows = stacked.shape[0] // 2
    return jnp.where(lanes_of(0), stacked[:rows], stacked[rows:])


def scaled(pair, scalars):
    return jnp.concatenate([pair[:HEAD_DIM] * scalars[0], pair[HEAD_DIM:] * scalars[1]], axis=0)


def same_sequence(starts, early, late, per):
    count = jnp.int32(0)
    for c in range(early * per + 1, late * per + 1):
        count = count + starts[c]
    return count == 0


def earlier(s, starts, kb, qb, per):
    open_all = jnp.where(same_sequence(starts, kb, qb, per), 0.0, MASKED).astype(F32)
    open_head = jnp.where(starts[kb * per] > 0, MASKED, open_all).astype(F32)
    row = lax.broadcasted_iota(jnp.int32, (STRETCH, s.shape[1]), 0)
    top = s[:STRETCH] + jnp.where(row < STRETCH - 1, open_head, open_all)
    return jnp.concatenate([top, s[STRETCH:] + open_all], axis=0)


def fill_diagonal(ref, start):
    key = lax.broadcasted_iota(jnp.int32, ref.shape, 0)
    query = lax.broadcasted_iota(jnp.int32, ref.shape, 1)
    plain = jnp.where(key <= query, 0.0, MASKED)
    opening = jnp.where((key == query) | ((key < query) & (key >= STRETCH - 1)), 0.0, MASKED)
    ref[...] = jnp.where(start > 0, opening, plain).astype(F32)


def forward_kernel(
    starts, rates, tok, gain, w, pk, pvt, first, second,
    h1, q, k, v, gate, recall, mixed, kt, lse, a_all, c_all, pre_all, e_all, u_all, atth,
    vt, att, diagonal, a_s, c_s, sa_s, sc_s,
):
    count = tok.shape[0]
    pairs = first.shape[0]
    wide = pairs * PAIR
    per = ROWS // STRETCH

    def project(b, _):
        rows = pl.ds(pl.multiple_of(b * ROWS, ROWS), ROWS)
        x = tok[rows, :].astype(F32)
        factor = lax.rsqrt(jnp.mean(x * x, axis=-1, keepdims=True) + EPSILON)
        h = (x * factor * gain[...]).astype(BF16)
        h1[rows, :] = h
        for part, ref in ((0, q), (1, k), (2, v)):
            made = nn(h, w[:, part * wide:(part + 1) * wide])
            low = made.astype(BF16)
            for p in range(pairs):
                ref[p, rows, :] = low[:, p * PAIR:(p + 1) * PAIR]
            if part > 0:
                made_t = jnp.transpose(made).astype(BF16)
                target = kt if part == 1 else vt
                for h_i in range(2 * pairs):
                    target[h_i, :, rows] = made_t[h_i * HEAD_DIM:(h_i + 1) * HEAD_DIM]
        g = sigmoid(nn(h, w[:, 3 * wide:]))
        for p in range(pairs):
            gate[p, rows, :] = g[:, p * PAIR:(p + 1) * PAIR]
        return 0

    lax.fori_loop(0, count // ROWS, project, 0)
    a_s[...] = first[...]
    c_s[...] = second[...]
    sa_s[...] = jnp.zeros_like(sa_s)
    sc_s[...] = jnp.zeros_like(sc_s)

    def memory_step(t):
        rows = pl.ds(pl.multiple_of(t * STRETCH, STRETCH), STRETCH)
        fresh = starts[t] > 0
        for p in range(pairs):
            a = jnp.where(fresh, first[p], a_s[p])
            c = jnp.where(fresh, second[p], c_s[p])
            sa = jnp.where(fresh, 0.0, sa_s[p])
            sc = jnp.where(fresh, 0.0, sc_s[p])
            ab, cb = a.astype(BF16), c.astype(BF16)
            a_all[t, p] = ab
            c_all[t, p] = cb
            km = both(k[p, rows, :])
            lhs = jnp.concatenate([both(q[p, rows, :]), km], axis=0)
            pre = nn(lhs, ab)
            pre_all[t, p] = pre
            sig = sigmoid(pre)
            act = pre * sig
            actb = act.astype(BF16)
            out = nt(actb, cb)
            recall[p, rows, :] = joined(out[:PAIR])
            e = joined(out[PAIR:]) - v[p, rows, :].astype(F32)
            eb = e.astype(BF16)
            e_all[p, rows, :] = eb
            em = both(eb)
            u = nn(em, cb)
            u_all[t, p] = u
            sigk, actk = sig[PAIR:], act[PAIR:]
            wgt = (u * (sigk + actk * (1.0 - sigk))).astype(BF16)
            ga = tn(km, wgt)
            gc = tn(em, actb[PAIR:])
            th = [rates[0, t, 2 * p + i] * (1.0 / STRETCH) for i in range(2)]
            eta = [rates[1, t, 2 * p + i] for i in range(2)]
            al = [1.0 - rates[2, t, 2 * p + i] for i in range(2)]
            sa = scaled(sa, eta) - scaled(ga, th)
            sc = scaled(sc, eta) - scaled(gc, th)
            sa_s[p] = sa
            sc_s[p] = sc
            a_s[p] = scaled(a, al) + sa
            c_s[p] = scaled(c, al) + sc

    def attention_unit(qb, head):
        p, half = head // 2, head % 2
        rows = pl.ds(qb * ROWS, ROWS)
        qh = keep(q[p, rows, :], half) * jnp.asarray(HEAD_DIM ** -0.5, BF16)
        scores = []
        for kb in range(qb + 1):
            s = nt(k[p, kb * ROWS:(kb + 1) * ROWS, :], qh)
            if kb == qb:
                s = s + diagonal[...]
            else:
                s = earlier(s, starts, kb, qb, per)
            scores.append(s)
        sp = nt(pk[p], qh)
        peak = jnp.max(sp, axis=0, keepdims=True)
        for s in scores:
            peak = jnp.maximum(peak, jnp.max(s, axis=0, keepdims=True))
        ep = jnp.exp(sp - peak)
        total = jnp.sum(ep, axis=0, keepdims=True)
        out = nn(pvt[head], ep.astype(BF16))
        for kb, s in enumerate(scores):
            e = jnp.exp(s - peak)
            total = total + jnp.sum(e, axis=0, keepdims=True)
            out = out + nn(vt[head, :, kb * ROWS:(kb + 1) * ROWS], e.astype(BF16))
        att[head, :, rows] = out * (1.0 / total)
        lse[head, :, rows] = peak + jnp.log(total)

    heads = 2 * pairs
    for qb in range(count // ROWS):
        fill_diagonal(diagonal, starts[qb * per])

        def run(i, _, qb=qb):
            memory_step(qb * per + i)
            attention_unit(qb, i)
            return 0
        lax.fori_loop(0, per, run, 0)
    for b in range(count // ROWS):
        rows = pl.ds(b * ROWS, ROWS)
        for p in range(pairs):
            got = jnp.concatenate([att[2 * p, :, rows], att[2 * p + 1, :, rows]], axis=0)
            wide_att = jnp.transpose(got)
            atth[p, rows, :] = wide_att
            mixed[rows, p * PAIR:(p + 1) * PAIR] = (wide_att + gate[p, rows, :] * recall[p, rows, :]).astype(BF16)


def backward_kernel(
    starts, rates, bm, q, k, v, gate, recall, kt, pk, pkt, pv, lse, a_all, c_all, pre_all, e_all, u_all, atth,
    dq, dk, dv, dg, dpk, dpv, dfirst, dsecond,
    dqt, dd, dks, dvs, mq, bmp, diagonal, da_s, dc_s, dsa_s, dsc_s,
):
    count = bm.shape[0]
    pairs = q.shape[0]
    heads = 2 * pairs
    per = ROWS // STRETCH
    nblocks = count // ROWS
    ones = [jnp.where(lanes_of(i, 8), 1.0, 0.0).astype(F32) for i in range(2)]
    for b in range(nblocks):
        rows = pl.ds(b * ROWS, ROWS)
        for p in range(pairs):
            gb = bm[rows, p * PAIR:(p + 1) * PAIR]
            bmp[p, rows, :] = gb
            g = gb.astype(F32)
            inner = g * atth[p, rows, :]
            for i in range(2):
                row = lax.dot_general(ones[i], inner, (((1,), (1,)), ((), ())), precision=lax.Precision.HIGHEST, preferred_element_type=F32)
                dd[2 * p + i, :, rows] = row[:1]
            gt = gate[p, rows, :]
            dg[rows, p * PAIR:(p + 1) * PAIR] = (g * recall[p, rows, :] * gt * (1.0 - gt)).astype(BF16)
    for ref in (dpk, dpv, dfirst, dsecond, dks, dvs, da_s, dc_s, dsa_s, dsc_s):
        ref[...] = jnp.zeros_like(ref)

    def memory_step(t):
        rows = pl.ds(pl.multiple_of(t * STRETCH, STRETCH), STRETCH)
        fresh = starts[t] > 0
        for p in range(pairs):
            th = [rates[0, t, 2 * p + i] * (-1.0 / STRETCH) for i in range(2)]
            eta = [rates[1, t, 2 * p + i] for i in range(2)]
            al = [1.0 - rates[2, t, 2 * p + i] for i in range(2)]
            da, dc = da_s[p], dc_s[p]
            dsa = dsa_s[p] + da
            dsc = dsc_s[p] + dc
            dga = scaled(dsa, th).astype(BF16)
            dgc = scaled(dsc, th).astype(BF16)
            ab, cb = a_all[t, p], c_all[t, p]
            km, qm = both(k[p, rows, :]), both(q[p, rows, :])
            em = both(e_all[p, rows, :])
            pre = pre_all[t, p]
            sig = sigmoid(pre)
            act = pre * sig
            actb = act.astype(BF16)
            slope = sig + act * (1.0 - sig)
            sigk, prek, slopek = sig[PAIR:], pre[PAIR:], slope[PAIR:]
            u = u_all[t, p]
            curve = sigk * (1.0 - sigk) * (2.0 + prek * (1.0 - 2.0 * sigk))
            wgt = (u * slopek).astype(BF16)
            back = bmp[p, rows, :].astype(F32) * gate[p, rows, :]
            rm = both(back.astype(BF16))
            dpre_q = (nn(rm, cb) * slope[:PAIR]).astype(BF16)
            mq[0, p, rows, :] = joined(nt(dpre_q, ab))
            dw = nn(km, dga)
            du = (dw * slopek).astype(BF16)
            cc = jnp.concatenate([dgc, cb], axis=1)
            de = joined(nt(jnp.concatenate([actb[PAIR:], du], axis=1), cc))
            mq[2, p, rows, :] = -de
            dem = both(de.astype(BF16))
            dsk = nn(jnp.concatenate([em, dem], axis=1), jnp.concatenate([dgc, cb], axis=0))
            dpre = (dsk * slopek + dw * u * curve).astype(BF16)
            mq[1, p, rows, :] = joined(nt(jnp.concatenate([wgt, dpre], axis=1), jnp.concatenate([dga, ab], axis=1)))
            ga = tn(jnp.concatenate([km, qm], axis=0), jnp.concatenate([dpre, dpre_q], axis=0))
            gc = tn(jnp.concatenate([em, dem], axis=0), jnp.concatenate([du, actb[PAIR:]], axis=0))
            gc = gc + tn(rm, actb[:PAIR])
            da = scaled(da, al) + ga
            dc = scaled(dc, al) + gc
            dfirst[p] = dfirst[p] + jnp.where(fresh, da, 0.0)
            dsecond[p] = dsecond[p] + jnp.where(fresh, dc, 0.0)
            da_s[p] = jnp.where(fresh, 0.0, da)
            dc_s[p] = jnp.where(fresh, 0.0, dc)
            dsa_s[p] = jnp.where(fresh, 0.0, scaled(dsa, eta))
            dsc_s[p] = jnp.where(fresh, 0.0, scaled(dsc, eta))

    def attention_unit(qb, head):
        p, half = head // 2, head % 2
        rows = pl.ds(qb * ROWS, ROWS)
        qh = keep(q[p, rows, :], half) * jnp.asarray(HEAD_DIM ** -0.5, BF16)
        gh = keep(bmp[p, rows, :], half)
        lrow, drow = lse[head, :, rows], dd[head, :, rows]
        acc = jnp.zeros((HEAD_DIM, ROWS), F32)
        for kb in range(qb + 1):
            krows = slice(kb * ROWS, (kb + 1) * ROWS)
            s = nt(k[p, krows, :], qh) - lrow
            if kb == qb:
                s = s + diagonal[...]
            else:
                s = earlier(s, starts, kb, qb, per)
            prob = jnp.exp(s)
            ds = (prob * (nt(v[p, krows, :], gh) - drow)).astype(BF16)
            dvs[p, krows, :] = dvs[p, krows, :] + nn(prob.astype(BF16), gh)
            dks[p, krows, :] = dks[p, krows, :] + nn(ds, qh)
            acc = acc + nn(kt[head, :, krows], ds)
        prob = jnp.exp(nt(pk[p], qh) - lrow)
        ds = (prob * (nt(pv[p], gh) - drow)).astype(BF16)
        dpv[p] = dpv[p] + nn(prob.astype(BF16), gh)
        dpk[p] = dpk[p] + nn(ds, qh)
        acc = acc + nn(pkt[head], ds)
        dqt[head, :, rows] = acc * (HEAD_DIM ** -0.5)

    for qb in reversed(range(nblocks)):
        fill_diagonal(diagonal, starts[qb * per])

        def run(i, _, qb=qb):
            memory_step(qb * per + per - 1 - i)
            attention_unit(qb, i)
            return 0
        lax.fori_loop(0, per, run, 0)
    for b in range(nblocks):
        rows = pl.ds(b * ROWS, ROWS)
        for p in range(pairs):
            cols = slice(p * PAIR, (p + 1) * PAIR)
            got = jnp.concatenate([dqt[2 * p, :, rows], dqt[2 * p + 1, :, rows]], axis=0)
            dq[rows, cols] = (jnp.transpose(got) + mq[0, p, rows, :]).astype(BF16)
            dk[rows, cols] = (dks[p, rows, :] + mq[1, p, rows, :]).astype(BF16)
            dv[rows, cols] = (dvs[p, rows, :] + mq[2, p, rows, :]).astype(BF16)


def shape(*dims, dtype=F32):
    return jax.ShapeDtypeStruct(dims, dtype)


VMEM = pl.BlockSpec(memory_space=pltpu.VMEM)
SMEM = pl.BlockSpec(memory_space=pltpu.SMEM)
LIMIT = 56 * 1024 * 1024


def mixer_forward(starts, rates, tok, gain, w, pk, pvt, first, second):
    count, width = tok.shape
    pairs = first.shape[0]
    heads, steps = 2 * pairs, starts.shape[0]
    flat = lambda dtype: shape(pairs, count, PAIR, dtype=dtype)
    outs = (
        shape(count, width, dtype=BF16), flat(BF16), flat(BF16), flat(BF16), flat(F32), flat(F32),
        shape(count, pairs * PAIR, dtype=BF16), shape(heads, HEAD_DIM, count, dtype=BF16), shape(heads, 1, count),
        shape(steps, pairs, PAIR, PAIR, dtype=BF16), shape(steps, pairs, PAIR, PAIR, dtype=BF16),
        shape(steps, pairs, 2 * PAIR, PAIR), flat(BF16), shape(steps, pairs, PAIR, PAIR), flat(F32),
    )
    state = pltpu.VMEM((pairs, PAIR, PAIR), F32)
    return pl.pallas_call(
        forward_kernel,
        out_shape=outs,
        in_specs=[SMEM, SMEM] + [VMEM] * 7,
        out_specs=[VMEM] * len(outs),
        scratch_shapes=[
            pltpu.VMEM((heads, HEAD_DIM, count), BF16), pltpu.VMEM((heads, HEAD_DIM, count), F32),
            pltpu.VMEM((ROWS, ROWS), F32), state, state, state, state,
        ],
        compiler_params=pltpu.CompilerParams(vmem_limit_bytes=LIMIT),
        name="mixer_forward",
    )(starts, rates, tok, gain, w, pk, pvt, first, second)


def mixer_backward(starts, rates, bm, q, k, v, gate, recall, kt, pk, pkt, pv, lse, a_all, c_all, pre_all, e_all, u_all, atth):
    count, wide = bm.shape
    pairs = q.shape[0]
    heads = 2 * pairs
    outs = (
        shape(count, wide, dtype=BF16), shape(count, wide, dtype=BF16), shape(count, wide, dtype=BF16), shape(count, wide, dtype=BF16),
        shape(*pk.shape), shape(*pv.shape), shape(pairs, PAIR, PAIR), shape(pairs, PAIR, PAIR),
    )
    state = pltpu.VMEM((pairs, PAIR, PAIR), F32)
    flat = pltpu.VMEM((pairs, count, PAIR), F32)
    return pl.pallas_call(
        backward_kernel,
        out_shape=outs,
        in_specs=[SMEM, SMEM] + [VMEM] * 17,
        out_specs=[VMEM] * len(outs),
        scratch_shapes=[
            pltpu.VMEM((heads, HEAD_DIM, count), F32), pltpu.VMEM((heads, 1, count), F32), flat, flat,
            pltpu.VMEM((3, pairs, count, PAIR), F32), pltpu.VMEM((pairs, count, PAIR), BF16),
            pltpu.VMEM((ROWS, ROWS), F32), state, state, state, state,
        ],
        compiler_params=pltpu.CompilerParams(vmem_limit_bytes=LIMIT),
        name="mixer_backward",
    )(starts, rates, bm, q, k, v, gate, recall, kt, pk, pkt, pv, lse, a_all, c_all, pre_all, e_all, u_all, atth)


MESH = pl.DeviceIdType.MESH
HALF_SHARE = 32
PEERS = 16


def place():
    return lax.axis_index("dp"), lax.axis_index("tensor")


def flipped(index, mask):
    result = index
    bit = 1
    while bit <= mask:
        if mask & bit:
            result = result + bit * (1 - 2 * (lax.div(index, bit) % 2))
        bit *= 2
    return result


def greet(devices):
    barrier = pltpu.get_barrier_semaphore()
    for device in devices:
        pl.semaphore_signal(barrier, inc=1, device_id=device, device_id_type=MESH)
    pl.semaphore_wait(barrier, len(devices))


def remote(src, dst, send_sem, recv_sem, device):
    return pltpu.make_async_remote_copy(
        src_ref=src, dst_ref=dst, send_sem=send_sem, recv_sem=recv_sem, device_id=device, device_id_type=MESH
    )


def iota(rows, columns, dimension):
    return lax.broadcasted_iota(jnp.int32, (rows, columns), dimension)


def at_rows(start, size):
    return pl.ds(pl.multiple_of(start, size), size)


def lot(peer):
    return peer % 2 * (PEERS // 2) + lax.div(peer, 2)


SAME_CORE, OTHER_CORE = tuple(range(0, PEERS, 2)), tuple(range(1, PEERS, 2))


def spread(ref, dp, t, sent, sems, masks):
    base = t * (PEERS * HALF_SHARE) + lot(dp) * HALF_SHARE
    copies = {}
    for m in masks:
        if m == 0:
            ref[at_rows(base, HALF_SHARE), :] = sent[at_rows(lot(dp) * HALF_SHARE, HALF_SHARE), :]
            continue
        peer = flipped(dp, m)
        copies[m] = remote(
            sent.at[at_rows(lot(peer) * HALF_SHARE, HALF_SHARE)], ref.at[at_rows(base, HALF_SHARE)],
            sems.at[0, m], sems.at[1, m], (peer, t),
        )
        copies[m].start()
    return copies


def pass_on(ref, dp, t, copies, sems):
    base = t * (PEERS * HALF_SHARE)
    passed = []
    for m in SAME_CORE + OTHER_CORE:
        rows = at_rows(base + lot(flipped(dp, m)) * HALF_SHARE, HALF_SHARE)
        if m:
            copies[m].wait_recv()
        passed.append(remote(ref.at[rows], ref.at[rows], sems.at[0, m], sems.at[1, m], (dp, 1 - t)))
        passed[-1].start()
    for copy in copies.values():
        copy.wait_send()
    return passed


def rows_in_kernel(
    idx, tok, cot, xs_out, sent_c, seq, g, gt, asked_out,
    xs, asked, want, sent_t, ask_sems, t_sems, ty_sems,
):
    dp, t = place()
    count, width = tok.shape
    half = count // 2
    share = 2 * HALF_SHARE
    index = idx[...]
    dev = lax.div(index, count)
    row = index - dev * count
    held = jnp.where(iota(PEERS, count, 0) == dev, 1.0, 0.0).astype(BF16)
    upper = jnp.where(iota(PAIR, PAIR, 0) < iota(PAIR, PAIR, 1), 1.0, 0.0).astype(BF16)
    run = jnp.zeros((PEERS, 1), F32)
    ranks = []
    for c in range(count // PAIR):
        part = held[:, c * PAIR:(c + 1) * PAIR]
        wide = part.astype(F32)
        ranks.append(jnp.sum(wide * (nn(part, upper) + run), axis=0, keepdims=True))
        run = run + jnp.sum(wide, axis=1, keepdims=True)
    rank = jnp.concatenate(ranks, axis=1)
    column = jnp.transpose(jnp.broadcast_to(rank, (PAIR, count)))
    pick = jnp.where(column == iota(count, PAIR, 1).astype(F32), 1.0, 0.0).astype(BF16)
    high = lax.div(row, 32)
    low = row - high * 32
    held_wide = held.astype(F32)
    wanted = 32.0 * nn((held_wide * high.astype(F32)).astype(BF16), pick) + nn((held_wide * low.astype(F32)).astype(BF16), pick)
    for j in range(PEERS):
        want[j] = jnp.broadcast_to(wanted[j:j + 1], (8, PAIR))
    greet([(flipped(dp, m), t) for m in range(1, PEERS)] + [(dp, 1 - t)])
    asks = []
    for m in range(1, PEERS):
        peer = flipped(dp, m)
        copy = remote(want.at[peer], asked.at[dp], ask_sems.at[0, m], ask_sems.at[1, m], (peer, t))
        copy.start()
        asks.append(copy)
    asked[dp] = want[dp]
    rank_i = rank.astype(jnp.int32)
    half_of = lax.div(rank_i, HALF_SHARE)
    slot = half_of * (half - HALF_SHARE) + lot(dev) * HALF_SHARE + rank_i
    for c in range(count // ROWS):
        gt[c * ROWS:(c + 1) * ROWS, :] = jnp.where(iota(ROWS, count, 0) + c * ROWS == slot, 1.0, 0.0).astype(BF16)
    slots = jnp.transpose(jnp.broadcast_to(slot.astype(F32), (PAIR, count)))
    for c in range(count // PAIR):
        g[:, c * PAIR:(c + 1) * PAIR] = jnp.where(slots == (iota(count, PAIR, 1) + c * PAIR).astype(F32), 1.0, 0.0).astype(BF16)
    for copy in asks:
        copy.wait()
    asks_in = asked[:, 0, :]
    asked_out[...] = asks_in
    asks_high = jnp.floor(asks_in * (1.0 / 32.0))
    asks_low = asks_in - 32.0 * asks_high
    owner = jnp.where(lax.div(iota(half, PEERS, 0), HALF_SHARE) == lot(iota(half, PEERS, 1)), 1.0, 0.0).astype(BF16)
    lane = iota(half, PAIR, 1) == iota(half, PAIR, 0) % HALF_SHARE + t * HALF_SHARE
    ones = jnp.ones((PAIR, PAIR), BF16)
    value = jnp.zeros((half, PAIR), F32)
    for digit, scale in ((asks_high, 32.0), (asks_low, 1.0)):
        picked = jnp.where(lane, nn(owner, digit.astype(BF16)), 0.0).astype(BF16)
        value = value + scale * nn(picked, ones)
    chosen = jnp.concatenate(
        [jnp.where(value == (iota(half, PAIR, 1) + c * PAIR).astype(F32), 1.0, 0.0).astype(BF16) for c in range(count // PAIR)], axis=1
    )
    sent_t[...] = nn(chosen, tok[...]).astype(BF16)
    copies = spread(xs, dp, t, sent_t, t_sems, SAME_CORE + OTHER_CORE)
    sent_c[...] = nn(chosen, cot[...]).astype(BF16)
    passed = pass_on(xs, dp, t, copies, ty_sems)
    for copy in passed:
        copy.wait()
    xs_out[...] = xs[...]
    for c in range(count // ROWS):
        seq[c * ROWS:(c + 1) * ROWS, :] = nn(g[c * ROWS:(c + 1) * ROWS, :], xs[...]).astype(BF16)


def rows_in(source_index, tokens, cotangent):
    count, width = tokens.shape
    rows = shape(count, width, dtype=BF16)
    square = shape(count, count, dtype=BF16)
    buffer = pltpu.VMEM((count, width), BF16)
    half = pltpu.VMEM((count // 2, width), BF16)
    small = pltpu.VMEM((PEERS, 8, PAIR), F32)
    sems = pltpu.SemaphoreType.DMA((2, PEERS))
    return pl.pallas_call(
        rows_in_kernel,
        out_shape=(rows, shape(count // 2, width, dtype=BF16), rows, square, square, shape(PEERS, PAIR)),
        in_specs=[VMEM] * 3,
        out_specs=[VMEM] * 6,
        scratch_shapes=[buffer, small, small, half, sems, sems, sems],
        compiler_params=pltpu.CompilerParams(collective_id=0, has_side_effects=True, vmem_limit_bytes=LIMIT),
        name="rows_in",
    )(source_index.reshape(1, count), tokens, cotangent)


def dense_kernel(
    mixed, gt, g, xs, cs, ops, dg, dl, dd, gain,
    bm, ps_s, own_s, br, facc, gout, gother, dgain,
    ms, h2s, hid, bgs, bls, pb_s, pb_r, own_b, resid, bf, bms_s, bms, sems,
):
    dp, t = place()
    other = (dp, 1 - t)
    count, width = xs.shape
    half = count // 2
    hidden = dg.shape[0]
    padded = bgs.shape[1]
    greet([other])
    pad = jnp.zeros((count, PAIR), BF16)
    for ref in (hid, bgs, bls):
        ref[:, padded - PAIR:] = pad
    for n in range(2):
        ms[n] = nn(gt[...], mixed[n]).astype(BF16)

    def chunk(rows, store):
        x = xs[rows, :].astype(F32) + nn(ms[0, rows, :], ops[0]) + nn(ms[1, rows, :], ops[1])
        factor = lax.rsqrt(jnp.mean(x * x, axis=-1, keepdims=True) + EPSILON)
        h2 = (x * factor * gain[...]).astype(BF16)
        h2s[rows, :] = h2
        gated, lifted = nt(h2, dg[...]), nt(h2, dl[...])
        sig = sigmoid(gated)
        act = gated * sig
        low = (act * lifted).astype(BF16)
        hid[rows, :hidden] = low
        back = nt(cs[rows, :], dd[...])
        back_g = (back * lifted * (sig + act * (1.0 - sig))).astype(BF16)
        back_l = (back * act).astype(BF16)
        bgs[rows, :hidden] = back_g
        bls[rows, :hidden] = back_l
        store(x, low, nn(back_g, dg[...]) + nn(back_l, dl[...]))

    copies = []
    for c in range(half // ROWS):
        here = pl.ds(c * ROWS, ROWS)

        def send(x, low, back, here=here):
            pb_s[here, :] = back.astype(BF16)
            ps_s[here, :] = nn(low, dd[...]).astype(BF16)

        chunk(at_rows((1 - t) * half + c * ROWS, ROWS), send)
        copy = remote(pb_s.at[here], pb_r.at[here], sems.at[0, c], sems.at[1, c], other)
        copy.start()
        copies.append(copy)
    for c in range(half // ROWS):
        here = pl.ds(c * ROWS, ROWS)

        def hold(x, low, back, here=here):
            resid[here, :] = x
            own_s[here, :] = x + nn(low, dd[...])
            own_b[here, :] = back

        chunk(at_rows(t * half + c * ROWS, ROWS), hold)
    total = jnp.zeros((8, width), F32)
    back_copies = []
    for c in range(half // ROWS):
        here = pl.ds(c * ROWS, ROWS)
        rows = at_rows(t * half + c * ROWS, ROWS)
        copies[c].wait()
        x = resid[here, :]
        factor = lax.rsqrt(jnp.mean(x * x, axis=-1, keepdims=True) + EPSILON)
        norm = x * factor
        back = own_b[here, :] + pb_r[here, :].astype(F32)
        inner = back * gain[...]
        result = cs[rows, :].astype(F32) + factor * (inner - norm * jnp.mean(inner * norm, axis=-1, keepdims=True))
        br[here, :] = result
        low = result.astype(BF16)
        bf[here, :] = low
        bms_s[here, :] = nt(low, ops[1 - t]).astype(BF16)
        copy = remote(bms_s.at[here], bms.at[rows], sems.at[0, 2 + c], sems.at[1, 2 + c], other)
        copy.start()
        back_copies.append(copy)
        bms[rows, :] = nt(low, ops[t]).astype(BF16)
        total = total + jnp.sum((back * norm).reshape(ROWS // 8, 8, width), axis=0)
    dgain[...] = total
    facc[:padded, :] = tn(bgs[...], h2s[...]).astype(BF16)
    facc[padded:2 * padded, :] = tn(bls[...], h2s[...]).astype(BF16)
    facc[2 * padded:, :] = tn(hid[...], cs[...]).astype(BF16)
    mine = at_rows(t * half, half)
    gout[...] = tn(ms[t, mine, :], bf[...])
    gother[...] = tn(ms[1 - t, mine, :], bf[...]).astype(BF16)
    for copy in back_copies:
        copy.wait()
    bm[...] = nn(g[...], bms[...]).astype(BF16)


def dense(mixed, gt, g, xs, cs, ops, dg, dl, dd, gain):
    count, width = xs.shape
    wide = mixed.shape[2]
    half = count // 2
    padded = -(-dg.shape[0] // 256) * 256
    half32, half16 = pltpu.VMEM((half, width), F32), pltpu.VMEM((half, width), BF16)
    hiddens = pltpu.VMEM((count, padded), BF16)
    return pl.pallas_call(
        dense_kernel,
        out_shape=(
            shape(count, wide, dtype=BF16), shape(half, width, dtype=BF16), shape(half, width), shape(half, width),
            shape(3 * padded, width, dtype=BF16), shape(wide, width), shape(wide, width, dtype=BF16), shape(8, width),
        ),
        in_specs=[VMEM] * 10,
        out_specs=[VMEM] * 8,
        scratch_shapes=[
            pltpu.VMEM((2, count, wide), BF16), pltpu.VMEM((count, width), BF16), hiddens, hiddens, hiddens,
            half16, half16, half32, half32, half16, pltpu.VMEM((half, wide), BF16), pltpu.VMEM((count, wide), BF16),
            pltpu.SemaphoreType.DMA((2, 4)),
        ],
        compiler_params=pltpu.CompilerParams(collective_id=1, has_side_effects=True, vmem_limit_bytes=LIMIT),
        name="dense",
    )(mixed, gt, g, xs, cs, ops, dg, dl, dd, gain)


def sixteens(start, size):
    return pl.ds(pl.multiple_of(start, 16), size)


class Sum:
    def __init__(self, dp, t, src, base, out, order, scratch):
        self.dp, self.t, self.src, self.base, self.out, self.order = dp, t, src, base, out, order
        n = len(order)
        self.acc, self.sems = scratch[0], scratch[1]
        self.rcv = scratch[2:2 + n]
        self.snd = (None,) + tuple(scratch[2 + n:1 + 2 * n])
        self.at = [lax.div(dp, stride) % size for stride, size in order]
        self.rows = [out.shape[0]]
        self.start = [0]
        for (stride, size), c in zip(order, self.at):
            self.rows.append(self.rows[-1] // size)
            self.start.append(self.start[-1] + c * self.rows[-1])
        self.live = []
        self.next = 0

    @staticmethod
    def scratch(rows, lanes, order):
        counts, sizes = [], [rows]
        for stride, size in order:
            sizes.append(sizes[-1] // size)
            counts.append(size - 1)
        blocks = [pltpu.VMEM((count, size, lanes), BF16) for count, size in zip(counts, sizes[1:])]
        return [pltpu.VMEM((sizes[1], lanes), F32), pltpu.SemaphoreType.DMA((2, 2 * sum(counts)))] + blocks + blocks[1:]

    @staticmethod
    def refs(order):
        return 1 + 2 * len(order)

    def peer(self, s, k):
        stride, size = self.order[s]
        d = (self.at[s] + k) % size
        return d, self.dp + stride * (d - self.at[s])

    def go(self, back, s, k, src, dst, peer):
        n = sum(size - 1 for _, size in self.order[:s]) + k - 1
        if back:
            n += sum(size - 1 for _, size in self.order)
        copy = remote(src, dst, self.sems.at[0, n], self.sems.at[1, n], (peer, self.t))
        copy.start()
        self.live.append(copy)

    def step(self):
        n, stages = self.next, len(self.order)
        self.next += 1
        for copy in self.live:
            copy.wait()
        self.live = []
        if n == 0:
            for k in range(1, self.order[0][1]):
                d, peer = self.peer(0, k)
                self.go(False, 0, k, self.src.at[sixteens(self.base + d * self.rows[1], self.rows[1])], self.rcv[0].at[k - 1], peer)
        elif n < stages:
            size = self.rows[n + 1]
            inside = self.start[n] - self.start[1]
            for k in list(range(1, self.order[n][1])) + [0]:
                d, peer = self.peer(n, k)
                here = sixteens(inside + d * size, size)
                if n == 1:
                    total = self.src[sixteens(self.base + self.start[1] + d * size, size), :].astype(F32)
                else:
                    total = self.acc[here, :]
                for j in range(self.order[n - 1][1] - 1):
                    total = total + self.rcv[n - 1][j, sixteens(d * size, size), :].astype(F32)
                if k:
                    self.snd[n][k - 1] = total.astype(BF16)
                    self.go(False, n, k, self.snd[n].at[k - 1], self.rcv[n].at[k - 1], peer)
                else:
                    self.acc[here, :] = total
        elif n < 2 * stages:
            if n == stages:
                size = self.rows[stages]
                total = self.acc[sixteens(self.start[stages] - self.start[1], size), :]
                for j in range(self.order[-1][1] - 1):
                    total = total + self.rcv[stages - 1][j].astype(F32)
                self.out[sixteens(self.start[stages], size), :] = total.astype(BF16)
            s = 2 * stages - 1 - n
            rows = sixteens(self.start[s + 1], self.rows[s + 1])
            for k in range(1, self.order[s][1]):
                self.go(True, s, k, self.out.at[rows], self.out.at[rows], self.peer(s, k)[1])


LONG_ORDER = ((1, 2), (2, 2), (4, 2), (8, 2))
SHORT_ORDER = ((1, 2), (2, 2), (4, 4))


def back_kernel(
    starts, rates, bm, q, k, v, gate, recall, kt, pk, pkt, pv, lse, a_all, c_all, pre_all, e_all, u_all, atth,
    facc, second_s, second_own, gout, gother, h1, gt, wq, wk, wv, wg, xs, br, gain, asked, dgain,
    fa_out, fb_out, qc_out, gains_out, ret,
    dqt, dd, dks, dvs, mq, bmp, diagonal, da_s, dc_s, dsa_s, dsc_s, dpk, dpv, dfirst, dsecond, dq, dk, dv, dg,
    src_b, src_c, out_a, out_b, out_c, second_r, gother_r, lo, rec_l, part_s, part_r, bx, rec_x, gains_s, gains_r, ht, final,
    y_sems, l_sems, ly_sems, x_sems, xy_sems, g_sems, o_sems, *sums,
):
    dp, t = place()
    other = (dp, 1 - t)
    core = dp % 2
    width = h1.shape[1]
    half = h1.shape[0] // 2
    wide = bm.shape[1]
    few = pk.shape[1]
    count = bm.shape[0]
    pairs = q.shape[0]
    heads = 2 * pairs
    per = ROWS // STRETCH
    nblocks = count // ROWS
    ones = [jnp.where(lanes_of(i, 8), 1.0, 0.0).astype(F32) for i in range(2)]
    for b in range(nblocks):
        rows = pl.ds(b * ROWS, ROWS)
        for p in range(pairs):
            gb = bm[rows, p * PAIR:(p + 1) * PAIR]
            bmp[p, rows, :] = gb
            g = gb.astype(F32)
            inner = g * atth[p, rows, :]
            for i in range(2):
                row = lax.dot_general(ones[i], inner, (((1,), (1,)), ((), ())), precision=lax.Precision.HIGHEST, preferred_element_type=F32)
                dd[2 * p + i, :, rows] = row[:1]
            gv = gate[p, rows, :]
            dg[rows, p * PAIR:(p + 1) * PAIR] = (g * recall[p, rows, :] * gv * (1.0 - gv)).astype(BF16)
    for ref in (dpk, dpv, dfirst, dsecond, dks, dvs, da_s, dc_s, dsa_s, dsc_s):
        ref[...] = jnp.zeros_like(ref)

    def memory_step(u):
        rows = pl.ds(pl.multiple_of(u * STRETCH, STRETCH), STRETCH)
        fresh = starts[u] > 0
        for p in range(pairs):
            th = [rates[0, 2 * p + i, u] * (-1.0 / STRETCH) for i in range(2)]
            eta = [rates[1, 2 * p + i, u] for i in range(2)]
            al = [1.0 - rates[2, 2 * p + i, u] for i in range(2)]
            da, dc = da_s[p], dc_s[p]
            dsa = dsa_s[p] + da
            dsc = dsc_s[p] + dc
            dga = scaled(dsa, th).astype(BF16)
            dgc = scaled(dsc, th).astype(BF16)
            ab, cb = a_all[u, p], c_all[u, p]
            km, qm = both(k[p, rows, :]), both(q[p, rows, :])
            em = both(e_all[p, rows, :])
            pre = pre_all[u, p]
            sig = sigmoid(pre)
            act = pre * sig
            actb = act.astype(BF16)
            slope = sig + act * (1.0 - sig)
            sigk, prek, slopek = sig[PAIR:], pre[PAIR:], slope[PAIR:]
            dev = u_all[u, p]
            curve = sigk * (1.0 - sigk) * (2.0 + prek * (1.0 - 2.0 * sigk))
            wgt = (dev * slopek).astype(BF16)
            back = bmp[p, rows, :].astype(F32) * gate[p, rows, :]
            rm = both(back.astype(BF16))
            dpre_q = (nn(rm, cb) * slope[:PAIR]).astype(BF16)
            mq[p, rows, :] = joined(nt(dpre_q, ab))
            dw = nn(km, dga)
            du = (dw * slopek).astype(BF16)
            cc = jnp.concatenate([dgc, cb], axis=1)
            de = joined(nt(jnp.concatenate([actb[PAIR:], du], axis=1), cc))
            dvs[p, rows, :] = dvs[p, rows, :] - de
            dem = both(de.astype(BF16))
            dsk = nn(jnp.concatenate([em, dem], axis=1), jnp.concatenate([dgc, cb], axis=0))
            dpre = (dsk * slopek + dw * dev * curve).astype(BF16)
            dks[p, rows, :] = dks[p, rows, :] + joined(nt(jnp.concatenate([wgt, dpre], axis=1), jnp.concatenate([dga, ab], axis=1)))
            ga = tn(jnp.concatenate([km, qm], axis=0), jnp.concatenate([dpre, dpre_q], axis=0))
            gc = tn(jnp.concatenate([em, dem], axis=0), jnp.concatenate([du, actb[PAIR:]], axis=0))
            gc = gc + tn(rm, actb[:PAIR])
            da = scaled(da, al) + ga
            dc = scaled(dc, al) + gc
            dfirst[p] = dfirst[p] + jnp.where(fresh, da, 0.0)
            dsecond[p] = dsecond[p] + jnp.where(fresh, dc, 0.0)
            da_s[p] = jnp.where(fresh, 0.0, da)
            dc_s[p] = jnp.where(fresh, 0.0, dc)
            dsa_s[p] = jnp.where(fresh, 0.0, scaled(dsa, eta))
            dsc_s[p] = jnp.where(fresh, 0.0, scaled(dsc, eta))

    def attention_unit(qb, head):
        p, half = head // 2, head % 2
        rows = pl.ds(qb * ROWS, ROWS)
        qh = keep(q[p, rows, :], half) * jnp.asarray(HEAD_DIM ** -0.5, BF16)
        gh = keep(bmp[p, rows, :], half)
        lrow, drow = lse[head, :, rows], dd[head, :, rows]
        acc = jnp.zeros((HEAD_DIM, ROWS), F32)
        for kb in range(qb + 1):
            krows = slice(kb * ROWS, (kb + 1) * ROWS)
            s = nt(k[p, krows, :], qh) - lrow
            if kb == qb:
                s = s + diagonal[...]
            else:
                s = earlier(s, starts, kb, qb, per)
            prob = jnp.exp(s)
            ds = (prob * (nt(v[p, krows, :], gh) - drow)).astype(BF16)
            dvs[p, krows, :] = dvs[p, krows, :] + nn(prob.astype(BF16), gh)
            dks[p, krows, :] = dks[p, krows, :] + nn(ds, qh)
            acc = acc + nn(kt[head, :, krows], ds)
        prob = jnp.exp(nt(pk[p], qh) - lrow)
        ds = (prob * (nt(pv[p], gh) - drow)).astype(BF16)
        dpv[p] = dpv[p] + nn(prob.astype(BF16), gh)
        dpk[p] = dpk[p] + nn(ds, qh)
        acc = acc + nn(pkt[head], ds)
        dqt[head, :, rows] = acc * (HEAD_DIM ** -0.5)


    def fold(ref, begin, value):
        rows = value.shape[0] // 2
        ref[begin:begin + rows, :wide] = value[:rows].astype(BF16)
        ref[begin:begin + rows, wide:] = value[rows:].astype(BF16)

    rows_a = out_a.shape[0]
    rest = facc.shape[0] - rows_a
    src_b[:rest, :] = facc[rows_a:, :]
    fold(src_b, rest + wide, tn(h1[...], dg[...]))
    greet([(flipped(dp, m), t) for m in range(1, PEERS)] + [other])
    n = Sum.refs(LONG_ORDER)
    sum_a = Sum(dp, t, facc, 0, out_a, LONG_ORDER, sums[:n])
    sum_b = Sum(dp, t, src_b, 0, out_b, LONG_ORDER, sums[n:2 * n])
    sum_c = Sum(dp, t, src_c, 0, out_c, SHORT_ORDER, sums[2 * n:])
    seconds = [
        remote(src, dst, y_sems.at[0, i], y_sems.at[1, i], other) for i, (src, dst) in enumerate(((gother, gother_r), (second_s, second_r)))
    ]
    lo_copies = {}

    def background(point):
        if point == 0:
            for copy in seconds:
                copy.start()
        if point in (0, 1, 3, 4, 5, 6, 7):
            sum_a.step()
        if point == 3:
            seconds[0].wait()
            src_b[rest:rest + wide, :] = (gout[...] + gother_r[...].astype(F32)).astype(BF16)
        if point in (3, 4, 6, 7):
            sum_b.step()
        if point == 4:
            seconds[1].wait()
            lo[...] = (second_own[...] + second_r[...].astype(F32)).astype(BF16)
        if point == 5:
            lo_copies.update(spread(rec_l, dp, t, lo, l_sems, SAME_CORE + OTHER_CORE))

    for qb in reversed(range(nblocks)):
        fill_diagonal(diagonal, starts[qb * per])

        def run(i, _, qb=qb):
            memory_step(qb * per + per - 1 - i)
            attention_unit(qb, i)
            return 0
        for part in range(2):
            background((nblocks - 1 - qb) * 2 + part)
            lax.fori_loop(part * per // 2, (part + 1) * per // 2, run, 0)
    for b in range(nblocks):
        rows = pl.ds(b * ROWS, ROWS)
        for p in range(pairs):
            cols = slice(p * PAIR, (p + 1) * PAIR)
            got = jnp.concatenate([dqt[2 * p, :, rows], dqt[2 * p + 1, :, rows]], axis=0)
            dq[rows, cols] = (jnp.transpose(got) + mq[p, rows, :]).astype(BF16)
            dk[rows, cols] = dks[p, rows, :].astype(BF16)
            dv[rows, cols] = dvs[p, rows, :].astype(BF16)
    sum_b.step()

    def partial(rows):
        result = jnp.zeros((ROWS, width), F32)
        for b, w in ((dq, wq), (dk, wk), (dv, wv), (dg, wg)):
            result = result + nt(nn(gt[rows, :], b[...]).astype(BF16), w[...])
        return result

    chunks = [pl.ds(pl.multiple_of(c * ROWS, ROWS), ROWS) for c in (core, 1 - core)]
    copies = []
    for i, here in enumerate(chunks):
        c = core if i == 0 else 1 - core
        part_s[here, :] = partial(at_rows((1 - t) * half + c * ROWS, ROWS)).astype(BF16)
        copies.append(remote(part_s.at[here], part_r.at[here], y_sems.at[0, 2 + i], y_sems.at[1, 2 + i], other))
        copies[-1].start()
    for i, b in enumerate((dq, dk, dv)):
        fold(src_c, i * wide, tn(h1[...], b[...]))
    at = 3 * wide
    src_c[at + PAIR:, :] = jnp.zeros((src_c.shape[0] - at - PAIR, width), BF16)
    for i in range(4):
        lanes = slice(i * PAIR, (i + 1) * PAIR)
        src_c[at:at + PAIR, lanes] = (dfirst, dsecond)[i // 2][i % 2].astype(BF16)
        src_c[at + PAIR:at + PAIR + few, lanes] = (dpk, dpv)[i // 2][i % 2].astype(BF16)
    sum_c.step()
    sum_a.step()
    sum_b.step()
    owns = [partial(at_rows(t * half + c * ROWS, ROWS)) for c in (core, 1 - core)]
    sum_c.step()
    passed_l = pass_on(rec_l, dp, t, lo_copies, ly_sems)
    mgain = jnp.zeros((8, width), F32)
    back_x = {}
    for i, here in enumerate(chunks):
        c = core if i == 0 else 1 - core
        rows = at_rows(t * half + c * ROWS, ROWS)
        copies[i].wait()
        back = owns[i] + part_r[here, :].astype(F32)
        x = xs[rows, :].astype(F32)
        factor = lax.rsqrt(jnp.mean(x * x, axis=-1, keepdims=True) + EPSILON)
        norm = x * factor
        inner = back * gain[...]
        bx[here, :] = (br[here, :] + factor * (inner - norm * jnp.mean(inner * norm, axis=-1, keepdims=True))).astype(BF16)
        mgain = mgain + jnp.sum((back * norm).reshape(ROWS // 8, 8, width), axis=0)
        back_x.update(spread(rec_x, dp, t, bx, x_sems, OTHER_CORE if i else SAME_CORE))
    gains_s[0, 0] = mgain
    gains_s[0, 1] = dgain[...]
    c2 = lax.div(dp, 4)
    groups = [[other], [(flipped(dp, 1), t)], [(flipped(dp, 2), t)], [(dp + 4 * ((c2 + i) % 4 - c2), t) for i in (1, 2, 3)]]
    gain_copies = []

    def gain_step(i):
        if i:
            for copy in gain_copies:
                copy.wait()
            gain_copies.clear()
            value = gains_s[i - 1]
            for j in range(len(groups[i - 1])):
                value = value + gains_r[i - 1, j]
            gains_s[i] = value
        if i < 4:
            for j, peer in enumerate(groups[i]):
                copy = remote(gains_s.at[i], gains_r.at[i, j], g_sems.at[0, i, j], g_sems.at[1, i, j], peer)
                copy.start()
                gain_copies.append(copy)

    gain_step(0)
    sum_a.step()
    sum_b.step()
    sum_c.step()
    asks = asked[...]
    asks_high = jnp.floor(asks * (1.0 / 32.0))
    asks_low = asks - 32.0 * asks_high
    slot = iota(PAIR, count, 1)
    rank = lax.div(slot, half) * HALF_SHARE + slot % HALF_SHARE
    pick = jnp.where(iota(PAIR, count, 0) == rank, 1.0, 0.0).astype(BF16)
    slot = iota(PEERS, count, 1)
    mine = lot(iota(PEERS, count, 0)) == lax.div(slot % half, HALF_SHARE)
    spread_out = 32.0 * nn(asks_high.astype(BF16), pick) + nn(asks_low.astype(BF16), pick)
    row = jnp.sum(jnp.where(mine, spread_out, 0.0), axis=0, keepdims=True)
    for c in range(count // ROWS):
        ht[c * ROWS:(c + 1) * ROWS, :] = jnp.where((iota(ROWS, count, 0) + c * ROWS).astype(F32) == row, 1.0, 0.0).astype(BF16)
    gain_step(1)
    for copy in passed_l:
        copy.wait()
    final[0] = nn(ht[...], rec_l[...]).astype(BF16)
    passed_x = pass_on(rec_x, dp, t, back_x, xy_sems)
    gain_step(2)
    sum_b.step()
    sum_c.step()
    sum_b.step()
    writes = [pltpu.make_async_copy(src, dst, o_sems.at[i]) for i, (src, dst) in enumerate((
        (out_a, fa_out), (out_b, fb_out), (final.at[0], ret.at[0]), (final.at[1], ret.at[1]), (gains_s.at[4], gains_out), (out_c, qc_out),
    ))]
    for write in writes[:3]:
        write.start()
    gain_step(3)
    sum_c.step()
    for copy in passed_x:
        copy.wait()
    final[1] = nn(ht[...], rec_x[...]).astype(BF16)
    writes[3].start()
    gain_step(4)
    writes[4].start()
    sum_c.step()
    sum_c.step()
    writes[5].start()
    for write in writes:
        write.wait()


ANY = pl.BlockSpec(memory_space=pl.ANY)


def back(starts, rates, bm, q, k, v, gate, recall, kt, pk, pkt, pv, lse, a_all, c_all, pre_all, e_all, u_all, atth,
         facc, second_s, second_own, gout, gother, h1, gt, wq, wk, wv, wg, xs, br, gain, asked, dgain):
    count, wide = bm.shape
    width = h1.shape[1]
    half = count // 2
    pairs = q.shape[0]
    heads = 2 * pairs
    early = facc.shape[0] + 2 * wide
    rows_b = early // 512 * 256
    rows_a = early - rows_b
    rows_c = -(-(3 * wide + PAIR + pk.shape[1]) // 256) * 256
    state = pltpu.VMEM((pairs, PAIR, PAIR), F32)
    flat = pltpu.VMEM((pairs, count, PAIR), F32)
    low = lambda *dims: pltpu.VMEM(dims, BF16)
    sems = pltpu.SemaphoreType.DMA((2, PEERS))
    args = (
        starts, rates, bm, q, k, v, gate, recall, kt, pk, pkt, pv, lse, a_all, c_all, pre_all, e_all, u_all, atth,
        facc, second_s, second_own, gout, gother, h1, gt, wq, wk, wv, wg, xs, br, gain, asked, dgain,
    )
    return pl.pallas_call(
        back_kernel,
        out_shape=(
            shape(rows_a, width, dtype=BF16), shape(rows_b, width, dtype=BF16), shape(rows_c, width, dtype=BF16),
            shape(2, 8, width), shape(2, count, width, dtype=BF16),
        ),
        in_specs=[SMEM, SMEM] + [VMEM] * (len(args) - 2),
        out_specs=[ANY] * 5,
        scratch_shapes=[
            pltpu.VMEM((heads, HEAD_DIM, count), F32), pltpu.VMEM((heads, 1, count), F32), flat, flat, flat,
            low(pairs, count, PAIR), pltpu.VMEM((ROWS, ROWS), F32), state, state, state, state,
            pltpu.VMEM(pk.shape, F32), pltpu.VMEM(pv.shape, F32), state, state,
            low(count, wide), low(count, wide), low(count, wide), low(count, wide),
            low(rows_b, width), low(rows_c, width), low(rows_a, width), low(rows_b, width), low(rows_c, width),
            low(half, width), low(wide, width), low(half, width), low(count, width), low(half, width), low(half, width),
            low(half, width), low(count, width), pltpu.VMEM((5, 2, 8, width), F32), pltpu.VMEM((4, 3, 2, 8, width), F32),
            low(count, count), low(2, count, width),
            pltpu.SemaphoreType.DMA((2, 4)), sems, sems, sems, sems, pltpu.SemaphoreType.DMA((2, 4, 3)), pltpu.SemaphoreType.DMA((6,)),
            *Sum.scratch(rows_a, width, LONG_ORDER), *Sum.scratch(rows_b, width, LONG_ORDER), *Sum.scratch(rows_c, width, SHORT_ORDER),
        ],
        compiler_params=pltpu.CompilerParams(collective_id=2, has_side_effects=True, vmem_limit_bytes=60 * 1024 * 1024),
        name="back",
    )(*args)


def finish_kernel(
    fa, fb, qc, gains, ret, lo, bx, mgain, gq, gk, gv, gg, gout, gpk, gpv, first, second, dgain, ggate, glift, gdown,
):
    hidden, width = ggate.shape
    padded = -(-hidden // 256) * 256
    wide = gq.shape[1]
    few = gpk.shape[0]

    def fetch(pair, begin, rows, lanes=slice(None)):
        a, b = pair
        cut = a.shape[0]
        pieces = []
        if begin < cut:
            pieces.append(a[begin:min(begin + rows, cut), lanes])
        if begin + rows > cut:
            pieces.append(b[max(begin - cut, 0):begin + rows - cut, lanes])
        return jnp.concatenate(pieces, axis=0).astype(F32) if len(pieces) > 1 else pieces[0].astype(F32)

    lo[...] = ret[0]
    bx[...] = ret[1]
    mgain[...] = jnp.sum(gains[0], axis=0, keepdims=True)
    dgain[...] = jnp.sum(gains[1], axis=0, keepdims=True)
    for n, ref in enumerate((ggate, glift, gdown)):
        ref[...] = fetch((fa, fb), n * padded, hidden)
    def unfold(ref, pair, begin):
        rows = fetch(pair, begin, wide)
        ref[:wide, :] = rows[:, :wide]
        ref[wide:, :] = rows[:, wide:]

    for n, ref in enumerate((gq, gk, gv)):
        unfold(ref, (qc, qc), n * wide)
    gout[...] = fetch((fa, fb), 3 * padded, wide)
    unfold(gg, (fa, fb), 3 * padded + wide)
    at = 3 * wide
    for n in range(4):
        lanes = slice(n * PAIR, (n + 1) * PAIR)
        (first, second)[n // 2][n % 2] = fetch((qc, qc), at, PAIR, lanes)
        (gpk, gpv)[n // 2][:, (n % 2) * PAIR:(n % 2 + 1) * PAIR] = fetch((qc, qc), at + PAIR, few, lanes)


def finish(fa, fb, qc, gains, ret, hidden, wide, few):
    count, width = ret.shape[1:]
    pairs = wide // PAIR
    rows = shape(count, width, dtype=BF16)
    square = shape(width, wide)
    state = shape(pairs, PAIR, PAIR)
    outs = (
        rows, rows, shape(1, width), square, square, square, square, shape(wide, width), shape(few, wide), shape(few, wide),
        state, state, shape(1, width), shape(hidden, width), shape(hidden, width), shape(hidden, width),
    )
    return pl.pallas_call(
        finish_kernel,
        out_shape=outs,
        in_specs=[VMEM] * 5,
        out_specs=[VMEM] * len(outs),
        compiler_params=pltpu.CompilerParams(vmem_limit_bytes=LIMIT),
        name="finish",
    )(fa, fb, qc, gains, ret)


def forward_remote(
    starts, rates, tok, gain, wq, wk, wv, wg, pk, pvt, first, second, sent_c, op,
    h1, q, k, v, gate, recall, mixed, cs_out, ops_out, kt, lse, a_all, c_all, pre_all, e_all, u_all, atth,
    vt, att, diagonal, a_s, c_s, sa_s, sc_s, mx, cs, ops, c_sems, cy_sems, y_sems,
):
    dp, t = place()
    other = (dp, 1 - t)
    count = tok.shape[0]
    pairs = first.shape[0]
    per = ROWS // STRETCH

    def project(b, _):
        rows = pl.ds(pl.multiple_of(b * ROWS, ROWS), ROWS)
        x = tok[rows, :].astype(F32)
        factor = lax.rsqrt(jnp.mean(x * x, axis=-1, keepdims=True) + EPSILON)
        h = (x * factor * gain[...]).astype(BF16)
        h1[rows, :] = h
        for part, (ref, w) in enumerate(((q, wq), (k, wk), (v, wv))):
            made = nn(h, w[...])
            low = made.astype(BF16)
            for p in range(pairs):
                ref[p, rows, :] = low[:, p * PAIR:(p + 1) * PAIR]
            if part > 0:
                made_t = jnp.transpose(made).astype(BF16)
                target = kt if part == 1 else vt
                for h_i in range(2 * pairs):
                    target[h_i, :, rows] = made_t[h_i * HEAD_DIM:(h_i + 1) * HEAD_DIM]
        g = sigmoid(nn(h, wg[...]))
        for p in range(pairs):
            gate[p, rows, :] = g[:, p * PAIR:(p + 1) * PAIR]
        return 0

    lax.fori_loop(0, count // ROWS, project, 0)
    greet([(flipped(dp, m), t) for m in range(1, PEERS)] + [other])
    ops[t] = op[...]
    waits = [remote(ops.at[t], ops.at[t], y_sems.at[0, 0], y_sems.at[1, 0], other)]
    waits[0].start()
    cot_copies = spread(cs, dp, t, sent_c, c_sems, SAME_CORE + OTHER_CORE)
    a_s[...] = first[...]
    c_s[...] = second[...]
    sa_s[...] = jnp.zeros_like(sa_s)
    sc_s[...] = jnp.zeros_like(sc_s)

    def memory_step(u):
        rows = pl.ds(pl.multiple_of(u * STRETCH, STRETCH), STRETCH)
        fresh = starts[u] > 0
        for p in range(pairs):
            a = jnp.where(fresh, first[p], a_s[p])
            c = jnp.where(fresh, second[p], c_s[p])
            sa = jnp.where(fresh, 0.0, sa_s[p])
            sc = jnp.where(fresh, 0.0, sc_s[p])
            ab, cb = a.astype(BF16), c.astype(BF16)
            a_all[u, p] = ab
            c_all[u, p] = cb
            km = both(k[p, rows, :])
            lhs = jnp.concatenate([both(q[p, rows, :]), km], axis=0)
            pre = nn(lhs, ab)
            pre_all[u, p] = pre
            sig = sigmoid(pre)
            act = pre * sig
            actb = act.astype(BF16)
            out = nt(actb, cb)
            recall[p, rows, :] = joined(out[:PAIR])
            e = joined(out[PAIR:]) - v[p, rows, :].astype(F32)
            eb = e.astype(BF16)
            e_all[p, rows, :] = eb
            em = both(eb)
            dev = nn(em, cb)
            u_all[u, p] = dev
            sigk, actk = sig[PAIR:], act[PAIR:]
            wgt = (dev * (sigk + actk * (1.0 - sigk))).astype(BF16)
            ga = tn(km, wgt)
            gc = tn(em, actb[PAIR:])
            th = [rates[0, 2 * p + i, u] * (1.0 / STRETCH) for i in range(2)]
            eta = [rates[1, 2 * p + i, u] for i in range(2)]
            al = [1.0 - rates[2, 2 * p + i, u] for i in range(2)]
            sa = scaled(sa, eta) - scaled(ga, th)
            sc = scaled(sc, eta) - scaled(gc, th)
            sa_s[p] = sa
            sc_s[p] = sc
            a_s[p] = scaled(a, al) + sa
            c_s[p] = scaled(c, al) + sc

    def attention_unit(qb, head):
        p, half = head // 2, head % 2
        rows = pl.ds(qb * ROWS, ROWS)
        qh = keep(q[p, rows, :], half) * jnp.asarray(HEAD_DIM ** -0.5, BF16)
        scores = []
        for kb in range(qb + 1):
            s = nt(k[p, kb * ROWS:(kb + 1) * ROWS, :], qh)
            if kb == qb:
                s = s + diagonal[...]
            else:
                s = earlier(s, starts, kb, qb, per)
            scores.append(s)
        sp = nt(pk[p], qh)
        peak = jnp.max(sp, axis=0, keepdims=True)
        for s in scores:
            peak = jnp.maximum(peak, jnp.max(s, axis=0, keepdims=True))
        ep = jnp.exp(sp - peak)
        total = jnp.sum(ep, axis=0, keepdims=True)
        out = nn(pvt[head], ep.astype(BF16))
        for kb, s in enumerate(scores):
            e = jnp.exp(s - peak)
            total = total + jnp.sum(e, axis=0, keepdims=True)
            out = out + nn(vt[head, :, kb * ROWS:(kb + 1) * ROWS], e.astype(BF16))
        att[head, :, rows] = out * (1.0 / total)
        lse[head, :, rows] = peak + jnp.log(total)

    heads = 2 * pairs
    for qb in range(count // ROWS):
        fill_diagonal(diagonal, starts[qb * per])

        def run(i, _, qb=qb):
            memory_step(qb * per + i)
            attention_unit(qb, i)
            return 0
        lax.fori_loop(0, per, run, 0)
        rows = pl.ds(qb * ROWS, ROWS)
        for p in range(pairs):
            got = jnp.concatenate([att[2 * p, :, rows], att[2 * p + 1, :, rows]], axis=0)
            wide_att = jnp.transpose(got)
            atth[p, rows, :] = wide_att
            mx[t, rows, p * PAIR:(p + 1) * PAIR] = (wide_att + gate[p, rows, :] * recall[p, rows, :]).astype(BF16)
        copy = remote(mx.at[t, rows], mx.at[t, rows], y_sems.at[0, 1 + qb], y_sems.at[1, 1 + qb], other)
        copy.start()
        waits.append(copy)
        if qb == 1:
            waits.extend(pass_on(cs, dp, t, cot_copies, cy_sems))
    for copy in waits:
        copy.wait()
    mixed[...] = mx[...]
    cs_out[...] = cs[...]
    ops_out[...] = ops[...]


def remote_forward(starts, rates, tok, gain, wq, wk, wv, wg, pk, pvt, first, second, sent_c, op):
    count, width = tok.shape
    pairs = first.shape[0]
    heads, steps = 2 * pairs, starts.shape[0]
    flat = lambda dtype: shape(pairs, count, PAIR, dtype=dtype)
    outs = (
        shape(count, width, dtype=BF16), flat(BF16), flat(BF16), flat(BF16), flat(F32), flat(F32),
        shape(2, count, pairs * PAIR, dtype=BF16),
        shape(count, width, dtype=BF16), shape(2, *op.shape, dtype=BF16), shape(heads, HEAD_DIM, count, dtype=BF16), shape(heads, 1, count),
        shape(steps, pairs, PAIR, PAIR, dtype=BF16), shape(steps, pairs, PAIR, PAIR, dtype=BF16),
        shape(steps, pairs, 2 * PAIR, PAIR), flat(BF16), shape(steps, pairs, PAIR, PAIR), flat(F32),
    )
    sems = pltpu.SemaphoreType.DMA((2, PEERS))
    state = pltpu.VMEM((pairs, PAIR, PAIR), F32)
    return pl.pallas_call(
        forward_remote,
        out_shape=outs,
        in_specs=[SMEM, SMEM] + [VMEM] * 12,
        out_specs=[VMEM] * len(outs),
        scratch_shapes=[
            pltpu.VMEM((heads, HEAD_DIM, count), BF16), pltpu.VMEM((heads, HEAD_DIM, count), F32),
            pltpu.VMEM((ROWS, ROWS), F32), state, state, state, state,
            pltpu.VMEM((2, count, pairs * PAIR), BF16), pltpu.VMEM((count, width), BF16), pltpu.VMEM((2,) + op.shape, BF16),
            sems, sems, pltpu.SemaphoreType.DMA((2, 8)),
        ],
        compiler_params=pltpu.CompilerParams(collective_id=3, has_side_effects=True, vmem_limit_bytes=LIMIT),
        name="mixer_forward",
    )(starts, rates, tok, gain, wq, wk, wv, wg, pk, pvt, first, second, sent_c, op)


def block_body(
    tokens, cotangent, source_index, tract_starts, memory_rates, mixer_gain, query_proj, key_proj, value_proj, gate_proj,
    out_proj, persist_keys, persist_values, memory_first, memory_second, dense_gain, dense_gate, dense_lift, dense_down,
):
    pairs = query_proj.shape[1] // PAIR
    by_pair = lambda value: value.reshape(-1, pairs, PAIR).transpose(1, 0, 2)
    by_head = lambda value: value.T.reshape(2 * pairs, HEAD_DIM, -1)
    rates = memory_rates.transpose(0, 2, 1)
    pk, pv = by_pair(persist_keys), by_pair(persist_values)
    pkt, pvt = by_head(persist_keys), by_head(persist_values)
    first = memory_first.reshape(pairs, PAIR, PAIR)
    second = memory_second.transpose(0, 2, 1).reshape(pairs, PAIR, PAIR)
    xs, sent_c, seq, g, gt, asked = rows_in(source_index, tokens, cotangent)
    h1, query, keys, values, gate, recall, mixed, cs, ops, keys_t, lse, a_all, c_all, pre_all, e_all, u_all, attended = remote_forward(
        tract_starts, rates, seq, mixer_gain[None], query_proj, key_proj, value_proj, gate_proj, pk, pvt, first, second, sent_c, out_proj
    )
    back_mixed, second_s, second_own, back_resid, dense_grads, gout, gother, gain_two = dense(
        mixed, gt, g, xs, cs, ops, dense_gate.T, dense_lift.T, dense_down, dense_gain[None]
    )
    fa, fb, qc, gains, ret = back(
        tract_starts, rates, back_mixed, query, keys, values, gate, recall, keys_t, pk, pkt, pv,
        lse, a_all, c_all, pre_all, e_all, u_all, attended, dense_grads, second_s, second_own, gout, gother,
        h1, gt, query_proj, key_proj, value_proj, gate_proj, xs, back_resid, mixer_gain[None], asked, gain_two,
    )
    outs = list(finish(fa, fb, qc, gains, ret, dense_gate.shape[1], query_proj.shape[1], persist_keys.shape[0]))
    outs[2] = outs[2][0]
    outs[10] = outs[10].reshape(memory_first.shape)
    outs[11] = outs[11].reshape(memory_first.shape).transpose(0, 2, 1)
    outs[12] = outs[12][0]
    outs[13], outs[14] = outs[13].T, outs[14].T
    return tuple(outs)


def body(
    tokens,
    cotangent,
    source_index,
    tract_starts,
    memory_rates,
    mixer_gain,
    query_proj,
    key_proj,
    value_proj,
    gate_proj,
    out_proj,
    persist_keys,
    persist_values,
    memory_first,
    memory_second,
    dense_gain,
    dense_gate,
    dense_lift,
    dense_down,
):
    count = tokens.shape[0]
    width = tokens.shape[1]
    peers = lax.axis_size("dp")
    share = count // peers
    arrival = jnp.argsort(source_index)
    wanted = (source_index[arrival] % count).reshape(peers, share)
    asked = lax.all_to_all(wanted, "dp", split_axis=0, concat_axis=0, tiled=True).reshape(count)
    got_tokens, got_cot = (
        lax.all_to_all(
            tokens[asked].reshape(peers, share, width),
            "dp",
            split_axis=0,
            concat_axis=0,
            tiled=True,
        ),
        lax.all_to_all(
            cotangent[asked].reshape(peers, share, width),
            "dp",
            split_axis=0,
            concat_axis=0,
            tiled=True,
        ),
    )
    placing = jnp.argsort(arrival)
    seq_tokens = got_tokens.reshape(count, width)[placing]
    seq_cot = got_cot.reshape(count, width)[placing]
    seq_x = seq_tokens.astype(jnp.float32)
    first_norm, factor_one = norm_forward(seq_x)
    pairs = query_proj.shape[1] // PAIR
    by_pair = lambda value: value.reshape(-1, pairs, PAIR).transpose(1, 0, 2)
    by_head = lambda value: value.T.reshape(2 * pairs, HEAD_DIM, -1)
    weights = jnp.concatenate([query_proj, key_proj, value_proj, gate_proj], axis=1)
    pk, pv = by_pair(persist_keys), by_pair(persist_values)
    first = memory_first.reshape(pairs, PAIR, PAIR)
    second = memory_second.transpose(0, 2, 1).reshape(pairs, PAIR, PAIR)
    h_one, query, keys, values, gate, recall, mixed, keys_t, lse, a_all, c_all, pre_all, e_all, u_all, attended = mixer_forward(
        tract_starts, memory_rates, seq_tokens, mixer_gain[None], weights, pk, by_head(persist_values), first, second
    )
    first_out = lax.psum(product(mixed, out_proj), "tensor")
    resid = seq_x + first_out
    norm_two, factor_two = norm_forward(resid)
    h_two = (norm_two * dense_gain).astype(jnp.bfloat16)
    gated = product(h_two, dense_gate)
    lifted = product(h_two, dense_lift)
    sigma = jax.nn.sigmoid(gated)
    active = gated * sigma
    hidden = (active * lifted).astype(jnp.bfloat16)
    second_out = lax.psum(product(hidden, dense_down).astype(jnp.bfloat16), "tensor").astype(
        jnp.float32
    )
    seq_out = (resid + second_out).astype(jnp.bfloat16)
    grad_down = product(hidden.T, seq_cot)
    back_hidden = product(seq_cot, dense_down.T)
    back_gated = (back_hidden * lifted * (sigma + gated * sigma * (1.0 - sigma))).astype(
        jnp.bfloat16
    )
    back_lifted = (back_hidden * active).astype(jnp.bfloat16)
    grad_gate = product(h_two.T, back_gated)
    grad_lift = product(h_two.T, back_lifted)
    back_two = lax.psum(
        product(back_gated, dense_gate.T) + product(back_lifted, dense_lift.T), "tensor"
    )
    back_norm_two, grad_dgain = norm_backward(back_two, norm_two, factor_two, dense_gain)
    residual_gradient = seq_cot.astype(jnp.float32) + back_norm_two
    back_first = residual_gradient.astype(jnp.bfloat16)
    grad_out = product(mixed.T, back_first)
    back_mixed = product(back_first, out_proj.T).astype(jnp.bfloat16)
    back_query, back_keys, cotangent_payloads, back_gate, grad_pk, grad_pv, grad_first, grad_second = mixer_backward(
        tract_starts, memory_rates, back_mixed, query, keys, values, gate, recall, keys_t, pk, by_head(persist_keys), pv,
        lse, a_all, c_all, pre_all, e_all, u_all, attended,
    )
    grad_first = grad_first.reshape(memory_first.shape)
    grad_second = grad_second.reshape(memory_first.shape).transpose(0, 2, 1)
    grad_query = product(h_one.T, back_query)
    grad_key = product(h_one.T, back_keys)
    grad_value = product(h_one.T, cotangent_payloads)
    grad_gproj = product(h_one.T, back_gate)
    back_one = lax.psum(
        product(back_query, query_proj.T)
        + product(back_keys, key_proj.T)
        + product(cotangent_payloads, value_proj.T)
        + product(back_gate, gate_proj.T),
        "tensor",
    )
    back_norm_one, grad_mgain = norm_backward(back_one, first_norm, factor_one, mixer_gain)
    back_x = (residual_gradient + back_norm_one).astype(jnp.bfloat16)
    grad_pkeys = grad_pk.transpose(1, 0, 2).reshape(persist_keys.shape)
    grad_pvalues = grad_pv.transpose(1, 0, 2).reshape(persist_values.shape)
    (
        grad_mgain,
        grad_query,
        grad_key,
        grad_value,
        grad_gproj,
        grad_out,
        grad_pkeys,
        grad_pvalues,
        grad_first,
        grad_second,
        grad_dgain,
        grad_gate,
        grad_lift,
        grad_down,
    ) = lax.psum(
        (
            grad_mgain,
            grad_query,
            grad_key,
            grad_value,
            grad_gproj,
            grad_out,
            grad_pkeys,
            grad_pvalues,
            grad_first,
            grad_second,
            grad_dgain,
            grad_gate,
            grad_lift,
            grad_down,
        ),
        "dp",
    )
    ret_out, ret_grad = (
        lax.all_to_all(
            seq_out[arrival].reshape(peers, share, width),
            "dp",
            split_axis=0,
            concat_axis=0,
            tiled=True,
        ),
        lax.all_to_all(
            back_x[arrival].reshape(peers, share, width),
            "dp",
            split_axis=0,
            concat_axis=0,
            tiled=True,
        ),
    )
    undo = jnp.argsort(asked)
    layer_output = ret_out.reshape(count, width)[undo]
    input_grad = ret_grad.reshape(count, width)[undo]
    return (
        layer_output,
        input_grad,
        grad_mgain,
        grad_query,
        grad_key,
        grad_value,
        grad_gproj,
        grad_out,
        grad_pkeys,
        grad_pvalues,
        grad_first,
        grad_second,
        grad_dgain,
        grad_gate,
        grad_lift,
        grad_down,
    )


def solution(mesh):
    chosen = block_body if mesh.shape["dp"] == PEERS else body
    in_specs = (
        P("dp", None),
        P("dp", None),
        P("dp"),
        P("dp"),
        P(None, "dp", "tensor"),
        P(),
        P(None, "tensor"),
        P(None, "tensor"),
        P(None, "tensor"),
        P(None, "tensor"),
        P("tensor", None),
        P(None, "tensor"),
        P(None, "tensor"),
        P("tensor", None, None),
        P("tensor", None, None),
        P(),
        P(None, "tensor"),
        P(None, "tensor"),
        P("tensor", None),
    )
    out_specs = (
        P("dp", None),
        P("dp", None),
        P(),
        P(None, "tensor"),
        P(None, "tensor"),
        P(None, "tensor"),
        P(None, "tensor"),
        P("tensor", None),
        P(None, "tensor"),
        P(None, "tensor"),
        P("tensor", None, None),
        P("tensor", None, None),
        P(),
        P(None, "tensor"),
        P(None, "tensor"),
        P("tensor", None),
    )
    return jax.shard_map(chosen, mesh=mesh, in_specs=in_specs, out_specs=out_specs, check_vma=False)
```

```python
import jax
import jax.numpy as jnp
from jax import lax
from jax.experimental import pallas as pl
from jax.experimental.pallas import tpu as pltpu
from jax.sharding import PartitionSpec as P

HEAD_DIM = 64


EPSILON = 1e-06
MASKED = -1e30


def product(left, right):
    return jnp.dot(left, right, preferred_element_type=jnp.float32)


def norm_forward(value):
    factor = lax.rsqrt(jnp.mean(value * value, axis=-1, keepdims=True) + EPSILON)
    return (value * factor, factor)


def norm_backward(grad, normed, factor, gain):
    inner = grad * gain
    back = factor * (inner - normed * jnp.mean(inner * normed, axis=-1, keepdims=True))
    return (back, jnp.sum(grad * normed, axis=0))


F32, BF16 = jnp.float32, jnp.bfloat16
PAIR = 2 * HEAD_DIM
ROWS = 256
STRETCH = 64


def nn(a, b):
    return lax.dot_general(a, b, (((1,), (0,)), ((), ())), preferred_element_type=F32)


def nt(a, b):
    return lax.dot_general(a, b, (((1,), (1,)), ((), ())), preferred_element_type=F32)


def tn(a, b):
    return lax.dot_general(a, b, (((0,), (0,)), ((), ())), preferred_element_type=F32)


def sigmoid(v):
    return 1.0 / (1.0 + jnp.exp(-v))


def lanes_of(half, rows=1):
    return (lax.broadcasted_iota(jnp.int32, (rows, PAIR), 1) // HEAD_DIM) == half


def keep(value, half):
    return jnp.where(lanes_of(half), value, jnp.zeros_like(value))


def both(value):
    return jnp.concatenate([keep(value, 0), keep(value, 1)], axis=0)


def joined(stacked):
    rows = stacked.shape[0] // 2
    return jnp.where(lanes_of(0), stacked[:rows], stacked[rows:])


def scaled(pair, scalars):
    return jnp.concatenate([pair[:HEAD_DIM] * scalars[0], pair[HEAD_DIM:] * scalars[1]], axis=0)


def same_sequence(starts, early, late, per):
    count = jnp.int32(0)
    for c in range(early * per + 1, late * per + 1):
        count = count + starts[c]
    return count == 0


def earlier(s, starts, kb, qb, per):
    open_all = jnp.where(same_sequence(starts, kb, qb, per), 0.0, MASKED).astype(F32)
    open_head = jnp.where(starts[kb * per] > 0, MASKED, open_all).astype(F32)
    row = lax.broadcasted_iota(jnp.int32, (STRETCH, s.shape[1]), 0)
    top = s[:STRETCH] + jnp.where(row < STRETCH - 1, open_head, open_all)
    return jnp.concatenate([top, s[STRETCH:] + open_all], axis=0)


def fill_diagonal(ref, start):
    key = lax.broadcasted_iota(jnp.int32, ref.shape, 0)
    query = lax.broadcasted_iota(jnp.int32, ref.shape, 1)
    plain = jnp.where(key <= query, 0.0, MASKED)
    opening = jnp.where((key == query) | ((key < query) & (key >= STRETCH - 1)), 0.0, MASKED)
    ref[...] = jnp.where(start > 0, opening, plain).astype(F32)


def forward_kernel(
    starts, rates, tok, gain, w, pk, pvt, first, second,
    h1, q, k, v, gate, recall, mixed, kt, lse, a_all, c_all, pre_all, e_all, u_all, atth,
    vt, att, diagonal, a_s, c_s, sa_s, sc_s,
):
    count = tok.shape[0]
    pairs = first.shape[0]
    wide = pairs * PAIR
    per = ROWS // STRETCH

    def project(b, _):
        rows = pl.ds(pl.multiple_of(b * ROWS, ROWS), ROWS)
        x = tok[rows, :].astype(F32)
        factor = lax.rsqrt(jnp.mean(x * x, axis=-1, keepdims=True) + EPSILON)
        h = (x * factor * gain[...]).astype(BF16)
        h1[rows, :] = h
        for part, ref in ((0, q), (1, k), (2, v)):
            made = nn(h, w[:, part * wide:(part + 1) * wide])
            low = made.astype(BF16)
            for p in range(pairs):
                ref[p, rows, :] = low[:, p * PAIR:(p + 1) * PAIR]
            if part > 0:
                made_t = jnp.transpose(made).astype(BF16)
                target = kt if part == 1 else vt
                for h_i in range(2 * pairs):
                    target[h_i, :, rows] = made_t[h_i * HEAD_DIM:(h_i + 1) * HEAD_DIM]
        g = sigmoid(nn(h, w[:, 3 * wide:]))
        for p in range(pairs):
            gate[p, rows, :] = g[:, p * PAIR:(p + 1) * PAIR]
        return 0

    lax.fori_loop(0, count // ROWS, project, 0)
    a_s[...] = first[...]
    c_s[...] = second[...]
    sa_s[...] = jnp.zeros_like(sa_s)
    sc_s[...] = jnp.zeros_like(sc_s)

    def memory_step(t):
        rows = pl.ds(pl.multiple_of(t * STRETCH, STRETCH), STRETCH)
        fresh = starts[t] > 0
        for p in range(pairs):
            a = jnp.where(fresh, first[p], a_s[p])
            c = jnp.where(fresh, second[p], c_s[p])
            sa = jnp.where(fresh, 0.0, sa_s[p])
            sc = jnp.where(fresh, 0.0, sc_s[p])
            ab, cb = a.astype(BF16), c.astype(BF16)
            a_all[t, p] = ab
            c_all[t, p] = cb
            km = both(k[p, rows, :])
            lhs = jnp.concatenate([both(q[p, rows, :]), km], axis=0)
            pre = nn(lhs, ab)
            pre_all[t, p] = pre
            sig = sigmoid(pre)
            act = pre * sig
            actb = act.astype(BF16)
            out = nt(actb, cb)
            recall[p, rows, :] = joined(out[:PAIR])
            e = joined(out[PAIR:]) - v[p, rows, :].astype(F32)
            eb = e.astype(BF16)
            e_all[p, rows, :] = eb
            em = both(eb)
            u = nn(em, cb)
            u_all[t, p] = u
            sigk, actk = sig[PAIR:], act[PAIR:]
            wgt = (u * (sigk + actk * (1.0 - sigk))).astype(BF16)
            ga = tn(km, wgt)
            gc = tn(em, actb[PAIR:])
            th = [rates[0, t, 2 * p + i] * (1.0 / STRETCH) for i in range(2)]
            eta = [rates[1, t, 2 * p + i] for i in range(2)]
            al = [1.0 - rates[2, t, 2 * p + i] for i in range(2)]
            sa = scaled(sa, eta) - scaled(ga, th)
            sc = scaled(sc, eta) - scaled(gc, th)
            sa_s[p] = sa
            sc_s[p] = sc
            a_s[p] = scaled(a, al) + sa
            c_s[p] = scaled(c, al) + sc

    def attention_unit(qb, head):
        p, half = head // 2, head % 2
        rows = pl.ds(qb * ROWS, ROWS)
        qh = keep(q[p, rows, :], half) * jnp.asarray(HEAD_DIM ** -0.5, BF16)
        scores = []
        for kb in range(qb + 1):
            s = nt(k[p, kb * ROWS:(kb + 1) * ROWS, :], qh)
            if kb == qb:
                s = s + diagonal[...]
            else:
                s = earlier(s, starts, kb, qb, per)
            scores.append(s)
        sp = nt(pk[p], qh)
        peak = jnp.max(sp, axis=0, keepdims=True)
        for s in scores:
            peak = jnp.maximum(peak, jnp.max(s, axis=0, keepdims=True))
        ep = jnp.exp(sp - peak)
        total = jnp.sum(ep, axis=0, keepdims=True)
        out = nn(pvt[head], ep.astype(BF16))
        for kb, s in enumerate(scores):
            e = jnp.exp(s - peak)
            total = total + jnp.sum(e, axis=0, keepdims=True)
            out = out + nn(vt[head, :, kb * ROWS:(kb + 1) * ROWS], e.astype(BF16))
        att[head, :, rows] = out * (1.0 / total)
        lse[head, :, rows] = peak + jnp.log(total)

    heads = 2 * pairs
    for qb in range(count // ROWS):
        fill_diagonal(diagonal, starts[qb * per])

        def run(i, _, qb=qb):
            memory_step(qb * per + i)
            attention_unit(qb, i)
            return 0
        lax.fori_loop(0, per, run, 0)
    for b in range(count // ROWS):
        rows = pl.ds(b * ROWS, ROWS)
        for p in range(pairs):
            got = jnp.concatenate([att[2 * p, :, rows], att[2 * p + 1, :, rows]], axis=0)
            wide_att = jnp.transpose(got)
            atth[p, rows, :] = wide_att
            mixed[rows, p * PAIR:(p + 1) * PAIR] = (wide_att + gate[p, rows, :] * recall[p, rows, :]).astype(BF16)


def backward_kernel(
    starts, rates, bm, q, k, v, gate, recall, kt, pk, pkt, pv, lse, a_all, c_all, pre_all, e_all, u_all, atth,
    dq, dk, dv, dg, dpk, dpv, dfirst, dsecond,
    dqt, dd, dks, dvs, mq, bmp, diagonal, da_s, dc_s, dsa_s, dsc_s,
):
    count = bm.shape[0]
    pairs = q.shape[0]
    heads = 2 * pairs
    per = ROWS // STRETCH
    nblocks = count // ROWS
    ones = [jnp.where(lanes_of(i, 8), 1.0, 0.0).astype(F32) for i in range(2)]
    for b in range(nblocks):
        rows = pl.ds(b * ROWS, ROWS)
        for p in range(pairs):
            gb = bm[rows, p * PAIR:(p + 1) * PAIR]
            bmp[p, rows, :] = gb
            g = gb.astype(F32)
            inner = g * atth[p, rows, :]
            for i in range(2):
                row = lax.dot_general(ones[i], inner, (((1,), (1,)), ((), ())), precision=lax.Precision.HIGHEST, preferred_element_type=F32)
                dd[2 * p + i, :, rows] = row[:1]
            gt = gate[p, rows, :]
            dg[rows, p * PAIR:(p + 1) * PAIR] = (g * recall[p, rows, :] * gt * (1.0 - gt)).astype(BF16)
    for ref in (dpk, dpv, dfirst, dsecond, dks, dvs, da_s, dc_s, dsa_s, dsc_s):
        ref[...] = jnp.zeros_like(ref)

    def memory_step(t):
        rows = pl.ds(pl.multiple_of(t * STRETCH, STRETCH), STRETCH)
        fresh = starts[t] > 0
        for p in range(pairs):
            th = [rates[0, t, 2 * p + i] * (-1.0 / STRETCH) for i in range(2)]
            eta = [rates[1, t, 2 * p + i] for i in range(2)]
            al = [1.0 - rates[2, t, 2 * p + i] for i in range(2)]
            da, dc = da_s[p], dc_s[p]
            dsa = dsa_s[p] + da
            dsc = dsc_s[p] + dc
            dga = scaled(dsa, th).astype(BF16)
            dgc = scaled(dsc, th).astype(BF16)
            ab, cb = a_all[t, p], c_all[t, p]
            km, qm = both(k[p, rows, :]), both(q[p, rows, :])
            em = both(e_all[p, rows, :])
            pre = pre_all[t, p]
            sig = sigmoid(pre)
            act = pre * sig
            actb = act.astype(BF16)
            slope = sig + act * (1.0 - sig)
            sigk, prek, slopek = sig[PAIR:], pre[PAIR:], slope[PAIR:]
            u = u_all[t, p]
            curve = sigk * (1.0 - sigk) * (2.0 + prek * (1.0 - 2.0 * sigk))
            wgt = (u * slopek).astype(BF16)
            back = bmp[p, rows, :].astype(F32) * gate[p, rows, :]
            rm = both(back.astype(BF16))
            dpre_q = (nn(rm, cb) * slope[:PAIR]).astype(BF16)
            mq[0, p, rows, :] = joined(nt(dpre_q, ab))
            dw = nn(km, dga)
            du = (dw * slopek).astype(BF16)
            cc = jnp.concatenate([dgc, cb], axis=1)
            de = joined(nt(jnp.concatenate([actb[PAIR:], du], axis=1), cc))
            mq[2, p, rows, :] = -de
            dem = both(de.astype(BF16))
            dsk = nn(jnp.concatenate([em, dem], axis=1), jnp.concatenate([dgc, cb], axis=0))
            dpre = (dsk * slopek + dw * u * curve).astype(BF16)
            mq[1, p, rows, :] = joined(nt(jnp.concatenate([wgt, dpre], axis=1), jnp.concatenate([dga, ab], axis=1)))
            ga = tn(jnp.concatenate([km, qm], axis=0), jnp.concatenate([dpre, dpre_q], axis=0))
            gc = tn(jnp.concatenate([em, dem], axis=0), jnp.concatenate([du, actb[PAIR:]], axis=0))
            gc = gc + tn(rm, actb[:PAIR])
            da = scaled(da, al) + ga
            dc = scaled(dc, al) + gc
            dfirst[p] = dfirst[p] + jnp.where(fresh, da, 0.0)
            dsecond[p] = dsecond[p] + jnp.where(fresh, dc, 0.0)
            da_s[p] = jnp.where(fresh, 0.0, da)
            dc_s[p] = jnp.where(fresh, 0.0, dc)
            dsa_s[p] = jnp.where(fresh, 0.0, scaled(dsa, eta))
            dsc_s[p] = jnp.where(fresh, 0.0, scaled(dsc, eta))

    def attention_unit(qb, head):
        p, half = head // 2, head % 2
        rows = pl.ds(qb * ROWS, ROWS)
        qh = keep(q[p, rows, :], half) * jnp.asarray(HEAD_DIM ** -0.5, BF16)
        gh = keep(bmp[p, rows, :], half)
        lrow, drow = lse[head, :, rows], dd[head, :, rows]
        acc = jnp.zeros((HEAD_DIM, ROWS), F32)
        for kb in range(qb + 1):
            krows = slice(kb * ROWS, (kb + 1) * ROWS)
            s = nt(k[p, krows, :], qh) - lrow
            if kb == qb:
                s = s + diagonal[...]
            else:
                s = earlier(s, starts, kb, qb, per)
            prob = jnp.exp(s)
            ds = (prob * (nt(v[p, krows, :], gh) - drow)).astype(BF16)
            dvs[p, krows, :] = dvs[p, krows, :] + nn(prob.astype(BF16), gh)
            dks[p, krows, :] = dks[p, krows, :] + nn(ds, qh)
            acc = acc + nn(kt[head, :, krows], ds)
        prob = jnp.exp(nt(pk[p], qh) - lrow)
        ds = (prob * (nt(pv[p], gh) - drow)).astype(BF16)
        dpv[p] = dpv[p] + nn(prob.astype(BF16), gh)
        dpk[p] = dpk[p] + nn(ds, qh)
        acc = acc + nn(pkt[head], ds)
        dqt[head, :, rows] = acc * (HEAD_DIM ** -0.5)

    for qb in reversed(range(nblocks)):
        fill_diagonal(diagonal, starts[qb * per])

        def run(i, _, qb=qb):
            memory_step(qb * per + per - 1 - i)
            attention_unit(qb, i)
            return 0
        lax.fori_loop(0, per, run, 0)
    for b in range(nblocks):
        rows = pl.ds(b * ROWS, ROWS)
        for p in range(pairs):
            cols = slice(p * PAIR, (p + 1) * PAIR)
            got = jnp.concatenate([dqt[2 * p, :, rows], dqt[2 * p + 1, :, rows]], axis=0)
            dq[rows, cols] = (jnp.transpose(got) + mq[0, p, rows, :]).astype(BF16)
            dk[rows, cols] = (dks[p, rows, :] + mq[1, p, rows, :]).astype(BF16)
            dv[rows, cols] = (dvs[p, rows, :] + mq[2, p, rows, :]).astype(BF16)


def shape(*dims, dtype=F32):
    return jax.ShapeDtypeStruct(dims, dtype)


VMEM = pl.BlockSpec(memory_space=pltpu.VMEM)
SMEM = pl.BlockSpec(memory_space=pltpu.SMEM)
LIMIT = 56 * 1024 * 1024


def mixer_forward(starts, rates, tok, gain, w, pk, pvt, first, second):
    count, width = tok.shape
    pairs = first.shape[0]
    heads, steps = 2 * pairs, starts.shape[0]
    flat = lambda dtype: shape(pairs, count, PAIR, dtype=dtype)
    outs = (
        shape(count, width, dtype=BF16), flat(BF16), flat(BF16), flat(BF16), flat(F32), flat(F32),
        shape(count, pairs * PAIR, dtype=BF16), shape(heads, HEAD_DIM, count, dtype=BF16), shape(heads, 1, count),
        shape(steps, pairs, PAIR, PAIR, dtype=BF16), shape(steps, pairs, PAIR, PAIR, dtype=BF16),
        shape(steps, pairs, 2 * PAIR, PAIR), flat(BF16), shape(steps, pairs, PAIR, PAIR), flat(F32),
    )
    state = pltpu.VMEM((pairs, PAIR, PAIR), F32)
    return pl.pallas_call(
        forward_kernel,
        out_shape=outs,
        in_specs=[SMEM, SMEM] + [VMEM] * 7,
        out_specs=[VMEM] * len(outs),
        scratch_shapes=[
            pltpu.VMEM((heads, HEAD_DIM, count), BF16), pltpu.VMEM((heads, HEAD_DIM, count), F32),
            pltpu.VMEM((ROWS, ROWS), F32), state, state, state, state,
        ],
        compiler_params=pltpu.CompilerParams(vmem_limit_bytes=LIMIT),
        name="mixer_forward",
    )(starts, rates, tok, gain, w, pk, pvt, first, second)


def mixer_backward(starts, rates, bm, q, k, v, gate, recall, kt, pk, pkt, pv, lse, a_all, c_all, pre_all, e_all, u_all, atth):
    count, wide = bm.shape
    pairs = q.shape[0]
    heads = 2 * pairs
    outs = (
        shape(count, wide, dtype=BF16), shape(count, wide, dtype=BF16), shape(count, wide, dtype=BF16), shape(count, wide, dtype=BF16),
        shape(*pk.shape), shape(*pv.shape), shape(pairs, PAIR, PAIR), shape(pairs, PAIR, PAIR),
    )
    state = pltpu.VMEM((pairs, PAIR, PAIR), F32)
    flat = pltpu.VMEM((pairs, count, PAIR), F32)
    return pl.pallas_call(
        backward_kernel,
        out_shape=outs,
        in_specs=[SMEM, SMEM] + [VMEM] * 17,
        out_specs=[VMEM] * len(outs),
        scratch_shapes=[
            pltpu.VMEM((heads, HEAD_DIM, count), F32), pltpu.VMEM((heads, 1, count), F32), flat, flat,
            pltpu.VMEM((3, pairs, count, PAIR), F32), pltpu.VMEM((pairs, count, PAIR), BF16),
            pltpu.VMEM((ROWS, ROWS), F32), state, state, state, state,
        ],
        compiler_params=pltpu.CompilerParams(vmem_limit_bytes=LIMIT),
        name="mixer_backward",
    )(starts, rates, bm, q, k, v, gate, recall, kt, pk, pkt, pv, lse, a_all, c_all, pre_all, e_all, u_all, atth)


MESH = pl.DeviceIdType.MESH
HALF_SHARE = 32
PEERS = 16


def place():
    return lax.axis_index("dp"), lax.axis_index("tensor")


def flipped(index, mask):
    result = index
    bit = 1
    while bit <= mask:
        if mask & bit:
            result = result + bit * (1 - 2 * (lax.div(index, bit) % 2))
        bit *= 2
    return result


def greet(devices):
    barrier = pltpu.get_barrier_semaphore()
    for device in devices:
        pl.semaphore_signal(barrier, inc=1, device_id=device, device_id_type=MESH)
    pl.semaphore_wait(barrier, len(devices))


def remote(src, dst, send_sem, recv_sem, device):
    return pltpu.make_async_remote_copy(
        src_ref=src, dst_ref=dst, send_sem=send_sem, recv_sem=recv_sem, device_id=device, device_id_type=MESH
    )


def iota(rows, columns, dimension):
    return lax.broadcasted_iota(jnp.int32, (rows, columns), dimension)


def at_rows(start, size):
    return pl.ds(pl.multiple_of(start, size), size)


def lot(peer):
    return peer % 2 * (PEERS // 2) + lax.div(peer, 2)


SAME_CORE, OTHER_CORE = tuple(range(0, PEERS, 2)), tuple(range(1, PEERS, 2))


def spread(ref, dp, t, sent, sems, masks):
    base = t * (PEERS * HALF_SHARE) + lot(dp) * HALF_SHARE
    copies = {}
    for m in masks:
        if m == 0:
            ref[at_rows(base, HALF_SHARE), :] = sent[at_rows(lot(dp) * HALF_SHARE, HALF_SHARE), :]
            continue
        peer = flipped(dp, m)
        copies[m] = remote(
            sent.at[at_rows(lot(peer) * HALF_SHARE, HALF_SHARE)], ref.at[at_rows(base, HALF_SHARE)],
            sems.at[0, m], sems.at[1, m], (peer, t),
        )
        copies[m].start()
    return copies


def pass_on(ref, dp, t, copies, sems):
    for m in SAME_CORE + OTHER_CORE:
        if m:
            copies[m].wait_recv()
        passing(ref, dp, t, m, sems).start()
    for copy in copies.values():
        copy.wait_send()


def passing(ref, dp, t, m, sems):
    rows = at_rows(t * (PEERS * HALF_SHARE) + lot(flipped(dp, m)) * HALF_SHARE, HALF_SHARE)
    return remote(ref.at[rows], ref.at[rows], sems.at[0, m], sems.at[1, m], (dp, 1 - t))


def passed_on(ref, dp, t, sems):
    for m in range(PEERS):
        passing(ref, dp, t, m, sems).wait()


def sixteens(start, size):
    return pl.ds(pl.multiple_of(start, 16), size)


class Sum:
    def __init__(self, dp, t, src, base, out, order, scratch):
        self.dp, self.t, self.src, self.base, self.out, self.order = dp, t, src, base, out, order
        n = len(order)
        self.acc, self.sems = scratch[0], scratch[1]
        self.rcv = scratch[2:2 + n]
        self.snd = (None,) + tuple(scratch[2 + n:1 + 2 * n])
        self.at = [lax.div(dp, stride) % size for stride, size in order]
        self.rows = [out.shape[0]]
        self.start = [0]
        for (stride, size), c in zip(order, self.at):
            self.rows.append(self.rows[-1] // size)
            self.start.append(self.start[-1] + c * self.rows[-1])
        self.live = []
        self.next = 0

    @staticmethod
    def scratch(rows, lanes, order):
        counts, sizes = [], [rows]
        for stride, size in order:
            sizes.append(sizes[-1] // size)
            counts.append(size - 1)
        blocks = [pltpu.VMEM((count, size, lanes), BF16) for count, size in zip(counts, sizes[1:])]
        return [pltpu.VMEM((sizes[1], lanes), F32), pltpu.SemaphoreType.DMA((2, 2 * sum(counts)))] + blocks + blocks[1:]

    @staticmethod
    def refs(order):
        return 1 + 2 * len(order)

    def peer(self, s, k):
        stride, size = self.order[s]
        d = (self.at[s] + k) % size
        return d, self.dp + stride * (d - self.at[s])

    def go(self, back, s, k, src, dst, peer):
        n = sum(size - 1 for _, size in self.order[:s]) + k - 1
        if back:
            n += sum(size - 1 for _, size in self.order)
        copy = remote(src, dst, self.sems.at[0, n], self.sems.at[1, n], (peer, self.t))
        copy.start()
        self.live.append(copy)

    def step(self):
        n, stages = self.next, len(self.order)
        self.next += 1
        for copy in self.live:
            copy.wait()
        self.live = []
        if n == 0:
            for k in range(1, self.order[0][1]):
                d, peer = self.peer(0, k)
                self.go(False, 0, k, self.src.at[sixteens(self.base + d * self.rows[1], self.rows[1])], self.rcv[0].at[k - 1], peer)
        elif n < stages:
            size = self.rows[n + 1]
            inside = self.start[n] - self.start[1]
            for k in list(range(1, self.order[n][1])) + [0]:
                d, peer = self.peer(n, k)
                here = sixteens(inside + d * size, size)
                if n == 1:
                    total = self.src[sixteens(self.base + self.start[1] + d * size, size), :].astype(F32)
                else:
                    total = self.acc[here, :]
                for j in range(self.order[n - 1][1] - 1):
                    total = total + self.rcv[n - 1][j, sixteens(d * size, size), :].astype(F32)
                if k:
                    self.snd[n][k - 1] = total.astype(BF16)
                    self.go(False, n, k, self.snd[n].at[k - 1], self.rcv[n].at[k - 1], peer)
                else:
                    self.acc[here, :] = total
        elif n < 2 * stages:
            if n == stages:
                size = self.rows[stages]
                total = self.acc[sixteens(self.start[stages] - self.start[1], size), :]
                for j in range(self.order[-1][1] - 1):
                    total = total + self.rcv[stages - 1][j].astype(F32)
                self.out[sixteens(self.start[stages], size), :] = total.astype(BF16)
            s = 2 * stages - 1 - n
            rows = sixteens(self.start[s + 1], self.rows[s + 1])
            for k in range(1, self.order[s][1]):
                self.go(True, s, k, self.out.at[rows], self.out.at[rows], self.peer(s, k)[1])


ANY = pl.BlockSpec(memory_space=pl.ANY)
LONG_ORDER = ((1, 2), (2, 2), (4, 2), (8, 2))
XZ_ORDER = ((1, 2), (2, 2), (4, 4))
ZX_ORDER = ((1, 2), (4, 4), (2, 2))
SUM_ORDERS = (LONG_ORDER, LONG_ORDER, XZ_ORDER, ZX_ORDER)


def mega_kernel(
    starts, rates, idx, tok_in, cot_in, gain1, wq, wk, wv, wg, op, pk_in, pv_in, first, second, gain2, dgw, dlw, ddw,
    fa_out, fb_out, qa_out, qb_out, gains_out, ret,
    xs, cs, mx, ops, asked, want, sent_c, g, gt, h1, q, k, v, gate, recall, kt, lse, a_all, c_all, pre_all, e_all, u_all, atth,
    pk, pv, pkt, pvt, bmp, diagonal, br, own_s, ps_s, pb_r, bms, facc, gout, gother, dgain,
    second_r, gother_r, rec_l, rec_x, part_r, src_b, src_c, out_a, out_b, out_c1, out_c2, gains_s, gains_r,
    a_s, c_s, sa_s, sc_s,
    in_sems, ask_sems, t_sems, ty_sems, c_sems, cy_sems, m_sems, d_sems, y_sems, l_sems, ly_sems, x_sems, xy_sems, g_sems, o_sems,
    *sums,
):
    dp, t = place()
    other = (dp, 1 - t)
    core = dp % 2
    count, width = xs.shape
    half = count // 2
    pairs = first.shape[0]
    heads = 2 * pairs
    wide = pairs * PAIR
    few = pk_in.shape[0]
    per = ROWS // STRETCH
    nblocks = count // ROWS
    hidden = dgw.shape[0]
    padded = facc.shape[0] // 3
    scale = HEAD_DIM ** -0.5

    def enter(tok, cot, sent_t):
        reads = [pltpu.make_async_copy(src, dst, in_sems.at[i]) for i, (src, dst) in enumerate(((tok_in, tok), (cot_in, cot)))]
        for read in reads:
            read.start()
        index = idx[...]
        dev = lax.div(index, count)
        row = index - dev * count
        held = jnp.where(iota(PEERS, count, 0) == dev, 1.0, 0.0).astype(BF16)
        upper = jnp.where(iota(PAIR, PAIR, 0) < iota(PAIR, PAIR, 1), 1.0, 0.0).astype(BF16)
        run = jnp.zeros((PEERS, 1), F32)
        ranks = []
        for c in range(count // PAIR):
            part = held[:, c * PAIR:(c + 1) * PAIR]
            wide_part = part.astype(F32)
            ranks.append(jnp.sum(wide_part * (nn(part, upper) + run), axis=0, keepdims=True))
            run = run + jnp.sum(wide_part, axis=1, keepdims=True)
        rank = jnp.concatenate(ranks, axis=1)
        column = jnp.transpose(jnp.broadcast_to(rank, (PAIR, count)))
        pick = jnp.where(column == iota(count, PAIR, 1).astype(F32), 1.0, 0.0).astype(BF16)
        high = lax.div(row, 32)
        low = row - high * 32
        held_wide = held.astype(F32)
        wanted = 32.0 * nn((held_wide * high.astype(F32)).astype(BF16), pick) + nn((held_wide * low.astype(F32)).astype(BF16), pick)
        for j in range(PEERS):
            want[j] = jnp.broadcast_to(wanted[j:j + 1], (8, PAIR))
        greet([(flipped(dp, m), t) for m in range(1, PEERS)] + [other])
        asks = []
        for m in range(1, PEERS):
            peer = flipped(dp, m)
            copy = remote(want.at[peer], asked.at[dp], ask_sems.at[0, m], ask_sems.at[1, m], (peer, t))
            copy.start()
            asks.append(copy)
        asked[dp] = want[dp]
        rank_i = rank.astype(jnp.int32)
        half_of = lax.div(rank_i, HALF_SHARE)
        slot = half_of * (half - HALF_SHARE) + lot(dev) * HALF_SHARE + rank_i
        for c in range(count // ROWS):
            gt[c * ROWS:(c + 1) * ROWS, :] = jnp.where(iota(ROWS, count, 0) + c * ROWS == slot, 1.0, 0.0).astype(BF16)
        slots = jnp.transpose(jnp.broadcast_to(slot.astype(F32), (PAIR, count)))
        for copy in asks:
            copy.wait()
        asks_in = asked[:, 0, :]
        asks_high = jnp.floor(asks_in * (1.0 / 32.0))
        asks_low = asks_in - 32.0 * asks_high
        owner = jnp.where(lax.div(iota(half, PEERS, 0), HALF_SHARE) == lot(iota(half, PEERS, 1)), 1.0, 0.0).astype(BF16)
        lane = iota(half, PAIR, 1) == iota(half, PAIR, 0) % HALF_SHARE + t * HALF_SHARE
        ones = jnp.ones((PAIR, PAIR), BF16)
        value = jnp.zeros((half, PAIR), F32)
        for digit, weight in ((asks_high, 32.0), (asks_low, 1.0)):
            picked = jnp.where(lane, nn(owner, digit.astype(BF16)), 0.0).astype(BF16)
            value = value + weight * nn(picked, ones)
        chosen = jnp.concatenate(
            [jnp.where(value == (iota(half, PAIR, 1) + c * PAIR).astype(F32), 1.0, 0.0).astype(BF16) for c in range(count // PAIR)], axis=1
        )
        for read in reads:
            read.wait()
        sent_t[...] = nn(chosen, tok[...]).astype(BF16)
        copies = spread(xs, dp, t, sent_t, t_sems, SAME_CORE + OTHER_CORE)
        sent_c[...] = nn(chosen, cot[...]).astype(BF16)
        for c in range(count // PAIR):
            g[:, c * PAIR:(c + 1) * PAIR] = jnp.where(slots == (iota(count, PAIR, 1) + c * PAIR).astype(F32), 1.0, 0.0).astype(BF16)
        for half_i in range(2):
            for ref_in, by_pair, by_head in ((pk_in, pk, pkt), (pv_in, pv, pvt)):
                part = ref_in[:, half_i * PAIR:(half_i + 1) * PAIR]
                by_pair[half_i] = part
                flat = jnp.transpose(part.astype(F32)).astype(BF16)
                by_head[2 * half_i] = flat[:HEAD_DIM]
                by_head[2 * half_i + 1] = flat[HEAD_DIM:]
        pass_on(xs, dp, t, copies, ty_sems)
        passed_on(xs, dp, t, ty_sems)

    pl.run_scoped(enter, pltpu.VMEM((count, width), BF16), pltpu.VMEM((count, width), BF16), pltpu.VMEM((half, width), BF16))

    def ops_copy():
        return remote(ops.at[t], ops.at[t], m_sems.at[0, nblocks], m_sems.at[1, nblocks], other)

    def mixed_copy(qb):
        rows = pl.ds(qb * ROWS, ROWS)
        return remote(mx.at[t, rows], mx.at[t, rows], m_sems.at[0, qb], m_sems.at[1, qb], other)

    ops[t] = op[...]
    ops_copy().start()
    cot_copies = spread(cs, dp, t, sent_c, c_sems, SAME_CORE + OTHER_CORE)

    def forward(vt, att):
        def project(b, _):
            rows = pl.ds(pl.multiple_of(b * ROWS, ROWS), ROWS)
            x = nn(g[rows, :], xs[...])
            factor = lax.rsqrt(jnp.mean(x * x, axis=-1, keepdims=True) + EPSILON)
            h = (x * factor * gain1[...]).astype(BF16)
            h1[rows, :] = h
            for part, (ref, w) in enumerate(((q, wq), (k, wk), (v, wv))):
                made = nn(h, w[...])
                low = made.astype(BF16)
                for p in range(pairs):
                    ref[p, rows, :] = low[:, p * PAIR:(p + 1) * PAIR]
                if part > 0:
                    made_t = jnp.transpose(made).astype(BF16)
                    target = kt if part == 1 else vt
                    for i in range(heads):
                        target[i, :, rows] = made_t[i * HEAD_DIM:(i + 1) * HEAD_DIM]
            made = sigmoid(nn(h, wg[...]))
            for p in range(pairs):
                gate[p, rows, :] = made[:, p * PAIR:(p + 1) * PAIR]
            return 0

        lax.fori_loop(0, nblocks, project, 0)
        a_s[...] = first[...]
        c_s[...] = second[...]
        sa_s[...] = jnp.zeros_like(sa_s)
        sc_s[...] = jnp.zeros_like(sc_s)

        def memory_step(n):
            rows = pl.ds(pl.multiple_of(n * STRETCH, STRETCH), STRETCH)
            fresh = starts[n] > 0
            for p in range(pairs):
                a = jnp.where(fresh, first[p], a_s[p])
                c = jnp.where(fresh, second[p], c_s[p])
                sa = jnp.where(fresh, 0.0, sa_s[p])
                sc = jnp.where(fresh, 0.0, sc_s[p])
                ab, cb = a.astype(BF16), c.astype(BF16)
                a_all[n, p] = ab
                c_all[n, p] = cb
                km = both(k[p, rows, :])
                pre = nn(jnp.concatenate([both(q[p, rows, :]), km], axis=0), ab)
                pre_all[n, p] = pre
                sig = sigmoid(pre)
                act = pre * sig
                actb = act.astype(BF16)
                out = nt(actb, cb)
                recall[p, rows, :] = joined(out[:PAIR])
                eb = (joined(out[PAIR:]) - v[p, rows, :].astype(F32)).astype(BF16)
                e_all[p, rows, :] = eb
                em = both(eb)
                u = nn(em, cb)
                u_all[n, p] = u.astype(BF16)
                sigk, actk = sig[PAIR:], act[PAIR:]
                ga = tn(km, (u * (sigk + actk * (1.0 - sigk))).astype(BF16))
                gc = tn(em, actb[PAIR:])
                th = [rates[0, 2 * p + i, n] * (1.0 / STRETCH) for i in range(2)]
                eta = [rates[1, 2 * p + i, n] for i in range(2)]
                al = [1.0 - rates[2, 2 * p + i, n] for i in range(2)]
                sa = scaled(sa, eta) - scaled(ga, th)
                sc = scaled(sc, eta) - scaled(gc, th)
                sa_s[p] = sa
                sc_s[p] = sc
                a_s[p] = scaled(a, al) + sa
                c_s[p] = scaled(c, al) + sc

        def attention_unit(qb, head):
            p, side = head // 2, head % 2
            rows = pl.ds(qb * ROWS, ROWS)
            qh = keep(q[p, rows, :], side) * jnp.asarray(scale, BF16)
            scores = []
            for kb in range(qb + 1):
                s = nt(k[p, kb * ROWS:(kb + 1) * ROWS, :], qh)
                scores.append(s + diagonal[...] if kb == qb else earlier(s, starts, kb, qb, per))
            sp = nt(pk[p], qh)
            peak = jnp.max(sp, axis=0, keepdims=True)
            for s in scores:
                peak = jnp.maximum(peak, jnp.max(s, axis=0, keepdims=True))
            ep = jnp.exp(sp - peak)
            total = jnp.sum(ep, axis=0, keepdims=True)
            out = nn(pvt[head], ep.astype(BF16))
            for kb, s in enumerate(scores):
                e = jnp.exp(s - peak)
                total = total + jnp.sum(e, axis=0, keepdims=True)
                out = out + nn(vt[head, :, kb * ROWS:(kb + 1) * ROWS], e.astype(BF16))
            att[head, :, rows] = out * (1.0 / total)
            lse[head, :, rows] = peak + jnp.log(total)

        for qb in range(nblocks):
            fill_diagonal(diagonal, starts[qb * per])

            def run(i, _, qb=qb):
                memory_step(qb * per + i)
                attention_unit(qb, i)
                return 0

            lax.fori_loop(0, per, run, 0)
            rows = pl.ds(qb * ROWS, ROWS)
            for p in range(pairs):
                got = jnp.transpose(jnp.concatenate([att[2 * p, :, rows], att[2 * p + 1, :, rows]], axis=0))
                atth[p, rows, :] = got.astype(BF16)
                mx[t, rows, p * PAIR:(p + 1) * PAIR] = (got + gate[p, rows, :] * recall[p, rows, :]).astype(BF16)
            mixed_copy(qb).start()
            if qb == nblocks - 3:
                pass_on(cs, dp, t, cot_copies, cy_sems)

    pl.run_scoped(forward, pltpu.VMEM((heads, HEAD_DIM, count), BF16), pltpu.VMEM((heads, HEAD_DIM, count), F32))

    def dense_part(ms, hid, bgs, bls, bms_s):
        h2s, pb_s, bf = src_b.at[:count], src_c.at[:half], src_c.at[half:]
        resid, own_b = sums[0].at[:half], sums[Sum.refs(SUM_ORDERS[0])].at[:half]
        pad = jnp.zeros((count, PAIR), BF16)
        for ref in (hid, bgs, bls):
            ref[:, padded - PAIR:] = pad
        ms[t] = nn(gt[...], mx[t]).astype(BF16)
        ops_copy().wait()
        for qb in range(nblocks):
            mixed_copy(qb).wait()
        passed_on(cs, dp, t, cy_sems)
        ms[1 - t] = nn(gt[...], mx[1 - t]).astype(BF16)

        def chunk(rows, store):
            x = xs[rows, :].astype(F32) + nn(ms[0, rows, :], ops[0]) + nn(ms[1, rows, :], ops[1])
            factor = lax.rsqrt(jnp.mean(x * x, axis=-1, keepdims=True) + EPSILON)
            h2 = (x * factor * gain2[...]).astype(BF16)
            h2s[rows, :] = h2
            gated, lifted = nt(h2, dgw[...]), nt(h2, dlw[...])
            sig = sigmoid(gated)
            act = gated * sig
            low = (act * lifted).astype(BF16)
            hid[rows, :hidden] = low
            back = nt(cs[rows, :], ddw[...])
            back_g = (back * lifted * (sig + act * (1.0 - sig))).astype(BF16)
            back_l = (back * act).astype(BF16)
            bgs[rows, :hidden] = back_g
            bls[rows, :hidden] = back_l
            store(x, low, nn(back_g, dgw[...]) + nn(back_l, dlw[...]))

        copies = []
        for c in range(half // ROWS):
            here = pl.ds(c * ROWS, ROWS)

            def send(x, low, back, here=here):
                pb_s[here, :] = back.astype(BF16)
                ps_s[here, :] = nn(low, ddw[...]).astype(BF16)

            chunk(at_rows((1 - t) * half + c * ROWS, ROWS), send)
            copy = remote(pb_s.at[here], pb_r.at[here], d_sems.at[0, c], d_sems.at[1, c], other)
            copy.start()
            copies.append(copy)
        for c in range(half // ROWS):
            here = pl.ds(c * ROWS, ROWS)

            def hold(x, low, back, here=here):
                resid[here, :] = x
                own_s[here, :] = x + nn(low, ddw[...])
                own_b[here, :] = back

            chunk(at_rows(t * half + c * ROWS, ROWS), hold)
        total = jnp.zeros((8, width), F32)
        back_copies = []
        for c in range(half // ROWS):
            here = pl.ds(c * ROWS, ROWS)
            rows = at_rows(t * half + c * ROWS, ROWS)
            copies[c].wait()
            x = resid[here, :]
            factor = lax.rsqrt(jnp.mean(x * x, axis=-1, keepdims=True) + EPSILON)
            norm = x * factor
            back = own_b[here, :] + pb_r[here, :].astype(F32)
            inner = back * gain2[...]
            result = cs[rows, :].astype(F32) + factor * (inner - norm * jnp.mean(inner * norm, axis=-1, keepdims=True))
            br[here, :] = result
            low = result.astype(BF16)
            bf[here, :] = low
            bms_s[here, :] = nt(low, ops[1 - t]).astype(BF16)
            copy = remote(bms_s.at[here], bms.at[rows], d_sems.at[0, 2 + c], d_sems.at[1, 2 + c], other)
            copy.start()
            back_copies.append(copy)
            bms[rows, :] = nt(low, ops[t]).astype(BF16)
            total = total + jnp.sum((back * norm).reshape(ROWS // 8, 8, width), axis=0)
        dgain[...] = total
        facc[:padded, :] = tn(bgs[...], h2s[...]).astype(BF16)
        facc[padded:2 * padded, :] = tn(bls[...], h2s[...]).astype(BF16)
        facc[2 * padded:, :] = tn(hid[...], cs[...]).astype(BF16)
        mine = at_rows(t * half, half)
        gout[...] = tn(ms[t, mine, :], bf[...])
        gother[...] = tn(ms[1 - t, mine, :], bf[...]).astype(BF16)
        for copy in back_copies:
            copy.wait()
        for b in range(nblocks):
            rows = pl.ds(b * ROWS, ROWS)
            got = nn(g[rows, :], bms[...]).astype(BF16)
            for p in range(pairs):
                bmp[p, rows, :] = got[:, p * PAIR:(p + 1) * PAIR]

    half16 = pltpu.VMEM((half, width), BF16)
    hiddens = pltpu.VMEM((count, padded), BF16)
    pl.run_scoped(
        dense_part, pltpu.VMEM((2, count, wide), BF16), hiddens, hiddens, hiddens, pltpu.VMEM((half, wide), BF16),
    )

    def backward(dqt, dks, dvs, mq, dd, dpk, dpv, dfirst, dsecond, dv, dg, bx):
        lo, part_s, dq, dk = sent_c, ps_s, mx.at[0], mx.at[1]
        da_s, dc_s, dsa_s, dsc_s = a_s, c_s, sa_s, sc_s
        ones = [jnp.where(lanes_of(i, 8), 1.0, 0.0).astype(F32) for i in range(2)]
        for b in range(nblocks):
            rows = pl.ds(b * ROWS, ROWS)
            for p in range(pairs):
                gr = bmp[p, rows, :].astype(F32)
                inner = gr * atth[p, rows, :].astype(F32)
                for i in range(2):
                    line = lax.dot_general(ones[i], inner, (((1,), (1,)), ((), ())), precision=lax.Precision.HIGHEST, preferred_element_type=F32)
                    dd[2 * p + i, :, rows] = line[:1]
                gv = gate[p, rows, :]
                dg[rows, p * PAIR:(p + 1) * PAIR] = (gr * recall[p, rows, :] * gv * (1.0 - gv)).astype(BF16)
        for ref in (dpk, dpv, dfirst, dsecond, dks, dvs, da_s, dc_s, dsa_s, dsc_s):
            ref[...] = jnp.zeros_like(ref)

        def memory_step(n):
            rows = pl.ds(pl.multiple_of(n * STRETCH, STRETCH), STRETCH)
            fresh = starts[n] > 0
            for p in range(pairs):
                th = [rates[0, 2 * p + i, n] * (-1.0 / STRETCH) for i in range(2)]
                eta = [rates[1, 2 * p + i, n] for i in range(2)]
                al = [1.0 - rates[2, 2 * p + i, n] for i in range(2)]
                da, dc = da_s[p], dc_s[p]
                dsa = dsa_s[p] + da
                dsc = dsc_s[p] + dc
                dga = scaled(dsa, th).astype(BF16)
                dgc = scaled(dsc, th).astype(BF16)
                ab, cb = a_all[n, p], c_all[n, p]
                km, qm = both(k[p, rows, :]), both(q[p, rows, :])
                em = both(e_all[p, rows, :])
                pre = pre_all[n, p]
                sig = sigmoid(pre)
                act = pre * sig
                actb = act.astype(BF16)
                slope = sig + act * (1.0 - sig)
                sigk, prek, slopek = sig[PAIR:], pre[PAIR:], slope[PAIR:]
                u = u_all[n, p].astype(F32)
                curve = sigk * (1.0 - sigk) * (2.0 + prek * (1.0 - 2.0 * sigk))
                wgt = (u * slopek).astype(BF16)
                rm = both((bmp[p, rows, :].astype(F32) * gate[p, rows, :]).astype(BF16))
                dpre_q = (nn(rm, cb) * slope[:PAIR]).astype(BF16)
                mq[p, rows, :] = joined(nt(dpre_q, ab))
                dw = nn(km, dga)
                du = (dw * slopek).astype(BF16)
                de = joined(nt(jnp.concatenate([actb[PAIR:], du], axis=1), jnp.concatenate([dgc, cb], axis=1)))
                dvs[p, rows, :] = dvs[p, rows, :] - de
                dem = both(de.astype(BF16))
                dsk = nn(jnp.concatenate([em, dem], axis=1), jnp.concatenate([dgc, cb], axis=0))
                dpre = (dsk * slopek + dw * u * curve).astype(BF16)
                dks[p, rows, :] = dks[p, rows, :] + joined(nt(jnp.concatenate([wgt, dpre], axis=1), jnp.concatenate([dga, ab], axis=1)))
                ga = tn(jnp.concatenate([km, qm], axis=0), jnp.concatenate([dpre, dpre_q], axis=0))
                gc = tn(jnp.concatenate([em, dem], axis=0), jnp.concatenate([du, actb[PAIR:]], axis=0))
                gc = gc + tn(rm, actb[:PAIR])
                da = scaled(da, al) + ga
                dc = scaled(dc, al) + gc
                dfirst[p] = dfirst[p] + jnp.where(fresh, da, 0.0)
                dsecond[p] = dsecond[p] + jnp.where(fresh, dc, 0.0)
                da_s[p] = jnp.where(fresh, 0.0, da)
                dc_s[p] = jnp.where(fresh, 0.0, dc)
                dsa_s[p] = jnp.where(fresh, 0.0, scaled(dsa, eta))
                dsc_s[p] = jnp.where(fresh, 0.0, scaled(dsc, eta))

        def attention_unit(qb, head):
            p, side = head // 2, head % 2
            rows = pl.ds(qb * ROWS, ROWS)
            qh = keep(q[p, rows, :], side) * jnp.asarray(scale, BF16)
            gh = keep(bmp[p, rows, :], side)
            lrow, drow = lse[head, :, rows], dd[head, :, rows]
            acc = jnp.zeros((HEAD_DIM, ROWS), F32)
            for kb in range(qb + 1):
                krows = slice(kb * ROWS, (kb + 1) * ROWS)
                s = nt(k[p, krows, :], qh) - lrow
                s = s + diagonal[...] if kb == qb else earlier(s, starts, kb, qb, per)
                prob = jnp.exp(s)
                ds = (prob * (nt(v[p, krows, :], gh) - drow)).astype(BF16)
                dvs[p, krows, :] = dvs[p, krows, :] + nn(prob.astype(BF16), gh)
                dks[p, krows, :] = dks[p, krows, :] + nn(ds, qh)
                acc = acc + nn(kt[head, :, krows], ds)
            prob = jnp.exp(nt(pk[p], qh) - lrow)
            ds = (prob * (nt(pv[p], gh) - drow)).astype(BF16)
            dpv[p] = dpv[p] + nn(prob.astype(BF16), gh)
            dpk[p] = dpk[p] + nn(ds, qh)
            acc = acc + nn(pkt[head], ds)
            dqt[head, :, rows] = acc * scale

        def fold(ref, begin, value):
            rows = value.shape[0] // 2
            ref[begin:begin + rows, :wide] = value[:rows].astype(BF16)
            ref[begin:begin + rows, wide:] = value[rows:].astype(BF16)

        rows_a = out_a.shape[0]
        rest = facc.shape[0] - rows_a
        cuts = [0]
        for order in SUM_ORDERS:
            cuts.append(cuts[-1] + Sum.refs(order))
        sum_a, sum_b, sum_c1, sum_c2 = [
            Sum(dp, t, src, base, out, order, sums[cuts[i]:cuts[i + 1]])
            for i, (src, base, out, order) in enumerate((
                (facc, 0, out_a, SUM_ORDERS[0]), (src_b, 0, out_b, SUM_ORDERS[1]),
                (src_c, 0, out_c1, SUM_ORDERS[2]), (src_c, out_c1.shape[0], out_c2, SUM_ORDERS[3]),
            ))
        ]
        seconds = [
            remote(src, dst, y_sems.at[0, i], y_sems.at[1, i], other) for i, (src, dst) in enumerate(((gother, gother_r), (ps_s, second_r)))
        ]
        lo_copies = {}

        def background(point):
            if point == 0:
                for copy in seconds:
                    copy.start()
            if point in (0, 1, 3, 5, 7):
                sum_a.step()
            if point == 0:
                src_b[:rest, :] = facc[rows_a:, :]
                fold(src_b, rest + wide, tn(h1[...], dg[...]))
            if point == 2:
                seconds[0].wait()
                src_b[rest:rest + wide, :] = (gout[...] + gother_r[...].astype(F32)).astype(BF16)
            if point in (2, 3, 6):
                sum_b.step()
            if point == 4:
                seconds[1].wait()
                lo[...] = (own_s[...] + second_r[...].astype(F32)).astype(BF16)
                lo_copies.update(spread(rec_l, dp, t, lo, l_sems, SAME_CORE + OTHER_CORE))
            if point == 7:
                pass_on(rec_l, dp, t, lo_copies, ly_sems)

        for qb in reversed(range(nblocks)):
            fill_diagonal(diagonal, starts[qb * per])

            def run(i, _, qb=qb):
                memory_step(qb * per + per - 1 - i)
                attention_unit(qb, i)
                return 0

            for part in range(2):
                background((nblocks - 1 - qb) * 2 + part)
                lax.fori_loop(part * per // 2, (part + 1) * per // 2, run, 0)
        for b in range(nblocks):
            rows = pl.ds(b * ROWS, ROWS)
            for p in range(pairs):
                cols = slice(p * PAIR, (p + 1) * PAIR)
                got = jnp.concatenate([dqt[2 * p, :, rows], dqt[2 * p + 1, :, rows]], axis=0)
                dq[rows, cols] = (jnp.transpose(got) + mq[p, rows, :]).astype(BF16)
                dk[rows, cols] = dks[p, rows, :].astype(BF16)
                dv[rows, cols] = dvs[p, rows, :].astype(BF16)
        sum_b.step()
        for i, b in enumerate((dq, dk, dv)):
            fold(src_c, i * wide, tn(h1[...], b[...]))
        at = 3 * wide
        src_c[at + PAIR:, :] = jnp.zeros((src_c.shape[0] - at - PAIR, width), BF16)
        for i in range(4):
            lanes = slice(i * PAIR, (i + 1) * PAIR)
            src_c[at:at + PAIR, lanes] = (dfirst, dsecond)[i // 2][i % 2].astype(BF16)
            src_c[at + PAIR:at + PAIR + few, lanes] = (dpk, dpv)[i // 2][i % 2].astype(BF16)

        def step_c():
            sum_c1.step()
            sum_c2.step()

        step_c()

        def partial(rows):
            result = jnp.zeros((ROWS, width), F32)
            for b, w in ((dq, wq), (dk, wk), (dv, wv), (dg, wg)):
                result = result + nt(nn(gt[rows, :], b[...]).astype(BF16), w[...])
            return result

        chunks = [pl.ds(pl.multiple_of(c * ROWS, ROWS), ROWS) for c in (core, 1 - core)]
        copies = []
        for i, here in enumerate(chunks):
            c = core if i == 0 else 1 - core
            part_s[here, :] = partial(at_rows((1 - t) * half + c * ROWS, ROWS)).astype(BF16)
            copies.append(remote(part_s.at[here], part_r.at[here], y_sems.at[0, 2 + i], y_sems.at[1, 2 + i], other))
            copies[-1].start()
            if i == 0:
                sum_a.step()
        step_c()
        owns = [partial(at_rows(t * half + c * ROWS, ROWS)) for c in (core, 1 - core)]
        sum_b.step()
        asks = asked[:, 0, :]
        asks_high = jnp.floor(asks * (1.0 / 32.0))
        asks_low = asks - 32.0 * asks_high
        slot = iota(PAIR, count, 1)
        rank = lax.div(slot, half) * HALF_SHARE + slot % HALF_SHARE
        pick = jnp.where(iota(PAIR, count, 0) == rank, 1.0, 0.0).astype(BF16)
        slot = iota(PEERS, count, 1)
        mine = lot(iota(PEERS, count, 0)) == lax.div(slot % half, HALF_SHARE)
        spread_out = 32.0 * nn(asks_high.astype(BF16), pick) + nn(asks_low.astype(BF16), pick)
        row = jnp.sum(jnp.where(mine, spread_out, 0.0), axis=0, keepdims=True)
        for c in range(count // ROWS):
            g[c * ROWS:(c + 1) * ROWS, :] = jnp.where((iota(ROWS, count, 0) + c * ROWS).astype(F32) == row, 1.0, 0.0).astype(BF16)
        step_c()
        sum_a.step()
        mgain = jnp.zeros((8, width), F32)
        back_x = {}
        for i, here in enumerate(chunks):
            c = core if i == 0 else 1 - core
            rows = at_rows(t * half + c * ROWS, ROWS)
            copies[i].wait()
            back = owns[i] + part_r[here, :].astype(F32)
            x = xs[rows, :].astype(F32)
            factor = lax.rsqrt(jnp.mean(x * x, axis=-1, keepdims=True) + EPSILON)
            norm = x * factor
            inner = back * gain1[...]
            bx[here, :] = (br[here, :] + factor * (inner - norm * jnp.mean(inner * norm, axis=-1, keepdims=True))).astype(BF16)
            mgain = mgain + jnp.sum((back * norm).reshape(ROWS // 8, 8, width), axis=0)
            back_x.update(spread(rec_x, dp, t, bx, x_sems, OTHER_CORE if i else SAME_CORE))
        step_c()
        gains_s[0, 0] = mgain
        gains_s[0, 1] = dgain[...]
        c2 = lax.div(dp, 4)
        groups = [[other], [(flipped(dp, 1), t)], [(flipped(dp, 2), t)], [(dp + 4 * ((c2 + i) % 4 - c2), t) for i in (1, 2, 3)]]
        gain_copies = []

        def gain_step(i):
            if i:
                for copy in gain_copies:
                    copy.wait()
                gain_copies.clear()
                value = gains_s[i - 1]
                for j in range(len(groups[i - 1])):
                    value = value + gains_r[i - 1, j]
                gains_s[i] = value
            if i < 4:
                for j, peer in enumerate(groups[i]):
                    copy = remote(gains_s.at[i], gains_r.at[i, j], g_sems.at[0, i, j], g_sems.at[1, i, j], peer)
                    copy.start()
                    gain_copies.append(copy)

        gain_step(0)
        sum_b.step()
        passed_on(rec_l, dp, t, ly_sems)
        cs[...] = nn(g[...], rec_l[...]).astype(BF16)
        writes = [pltpu.make_async_copy(src, dst, o_sems.at[i]) for i, (src, dst) in enumerate((
            (cs, ret.at[0]), (xs, ret.at[1]), (gains_s.at[4], gains_out), (out_a, fa_out), (out_b, fb_out), (out_c1, qa_out), (out_c2, qb_out),
        ))]
        writes[0].start()
        gain_step(1)
        step_c()
        pass_on(rec_x, dp, t, back_x, xy_sems)
        gain_step(2)
        sum_a.step()
        sum_b.step()
        step_c()
        gain_step(3)
        passed_on(rec_x, dp, t, xy_sems)
        xs[...] = nn(g[...], rec_x[...]).astype(BF16)
        writes[1].start()
        gain_step(4)
        writes[2].start()
        sum_a.step()
        writes[3].start()
        sum_b.step()
        step_c()
        writes[5].start()
        writes[6].start()
        sum_b.step()
        writes[4].start()
        for write in writes:
            write.wait()

    flat = pltpu.VMEM((pairs, count, PAIR), F32)
    state = pltpu.VMEM((pairs, PAIR, PAIR), F32)
    tall = pltpu.VMEM((count, wide), BF16)
    pl.run_scoped(
        backward, pltpu.VMEM((heads, HEAD_DIM, count), F32), flat, flat, flat, pltpu.VMEM((heads, 1, count), F32),
        pltpu.VMEM((pairs, few, PAIR), F32), pltpu.VMEM((pairs, few, PAIR), F32), state, state,
        tall, tall, half16,
    )


def mega(starts, rates, idx, tokens, cotangent, gain1, wq, wk, wv, wg, op, pk, pv, first, second, gain2, dg, dl, dd):
    count, width = tokens.shape
    half = count // 2
    wide = wq.shape[1]
    pairs = wide // PAIR
    heads = 2 * pairs
    few = pk.shape[0]
    steps = starts.shape[0]
    padded = -(-dg.shape[0] // 256) * 256
    early = 3 * padded + 2 * wide
    rows_b = early // 512 * 256
    rows_a = early - rows_b
    rows_c = -(-(3 * wide + PAIR + few) // 512) * 256
    low = lambda *dims: pltpu.VMEM(dims, BF16)
    full = lambda *dims: pltpu.VMEM(dims, F32)
    sems = pltpu.SemaphoreType.DMA((2, PEERS))
    dma = pltpu.SemaphoreType.DMA
    square = low(count, count)
    state = full(pairs, PAIR, PAIR)
    args = (starts, rates, idx, tokens, cotangent, gain1, wq, wk, wv, wg, op, pk, pv, first, second, gain2, dg, dl, dd)
    return pl.pallas_call(
        mega_kernel,
        out_shape=(
            shape(rows_a, width, dtype=BF16), shape(rows_b, width, dtype=BF16), shape(rows_c, width, dtype=BF16), shape(rows_c, width, dtype=BF16),
            shape(2, 8, width), shape(2, count, width, dtype=BF16),
        ),
        in_specs=[SMEM, SMEM, VMEM, ANY, ANY] + [VMEM] * (len(args) - 5),
        out_specs=[ANY] * 6,
        scratch_shapes=[
            low(count, width), low(count, width), low(2, count, wide), low(2, *op.shape), full(PEERS, 8, PAIR), full(PEERS, 8, PAIR),
            low(half, width), square, square, low(count, width), low(pairs, count, PAIR), low(pairs, count, PAIR), low(pairs, count, PAIR),
            full(pairs, count, PAIR), full(pairs, count, PAIR), low(heads, HEAD_DIM, count), full(heads, 1, count),
            low(steps, pairs, PAIR, PAIR), low(steps, pairs, PAIR, PAIR), full(steps, pairs, 2 * PAIR, PAIR), low(pairs, count, PAIR),
            low(steps, pairs, PAIR, PAIR), low(pairs, count, PAIR),
            low(pairs, few, PAIR), low(pairs, few, PAIR), low(heads, HEAD_DIM, few), low(heads, HEAD_DIM, few), low(pairs, count, PAIR),
            full(ROWS, ROWS), full(half, width), full(half, width), low(half, width), low(half, width), low(count, wide),
            low(3 * padded, width), full(wide, width), low(wide, width), full(8, width),
            low(half, width), low(wide, width), low(count, width), low(count, width), low(half, width),
            low(rows_b, width), low(2 * rows_c, width), low(rows_a, width), low(rows_b, width), low(rows_c, width), low(rows_c, width),
            full(5, 2, 8, width), full(4, 3, 2, 8, width),
            state, state, state, state,
            dma((2,)), sems, sems, sems, sems, sems, dma((2, 8)), dma((2, 4)), dma((2, 4)), sems, sems, sems, sems, dma((2, 4, 3)), dma((7,)),
            *Sum.scratch(rows_a, width, SUM_ORDERS[0]), *Sum.scratch(rows_b, width, SUM_ORDERS[1]),
            *Sum.scratch(rows_c, width, SUM_ORDERS[2]), *Sum.scratch(rows_c, width, SUM_ORDERS[3]),
        ],
        compiler_params=pltpu.CompilerParams(collective_id=0, has_side_effects=True, vmem_limit_bytes=62 * 1024 * 1024),
        name="block",
    )(*args)


def finish_kernel(
    fa, fb, qa, qb, gains, ret, lo, bx, mgain, gq, gk, gv, gg, gout, gpk, gpv, first, second, dgain, ggate, glift, gdown,
):
    hidden, width = ggate.shape
    padded = -(-hidden // 256) * 256
    wide = gq.shape[1]
    few = gpk.shape[0]

    def fetch(pair, begin, rows, lanes=slice(None)):
        a, b = pair
        cut = a.shape[0]
        pieces = []
        if begin < cut:
            pieces.append(a[begin:min(begin + rows, cut), lanes])
        if begin + rows > cut:
            pieces.append(b[max(begin - cut, 0):begin + rows - cut, lanes])
        return jnp.concatenate(pieces, axis=0).astype(F32) if len(pieces) > 1 else pieces[0].astype(F32)

    lo[...] = ret[0]
    bx[...] = ret[1]
    mgain[...] = jnp.sum(gains[0], axis=0, keepdims=True)
    dgain[...] = jnp.sum(gains[1], axis=0, keepdims=True)
    for n, ref in enumerate((ggate, glift, gdown)):
        ref[...] = fetch((fa, fb), n * padded, hidden)
    def unfold(ref, pair, begin):
        rows = fetch(pair, begin, wide)
        ref[:wide, :] = rows[:, :wide]
        ref[wide:, :] = rows[:, wide:]

    for n, ref in enumerate((gq, gk, gv)):
        unfold(ref, (qa, qb), n * wide)
    gout[...] = fetch((fa, fb), 3 * padded, wide)
    unfold(gg, (fa, fb), 3 * padded + wide)
    at = 3 * wide
    for n in range(4):
        lanes = slice(n * PAIR, (n + 1) * PAIR)
        (first, second)[n // 2][n % 2] = fetch((qa, qb), at, PAIR, lanes)
        (gpk, gpv)[n // 2][:, (n % 2) * PAIR:(n % 2 + 1) * PAIR] = fetch((qa, qb), at + PAIR, few, lanes)


def finish(fa, fb, qa, qb, gains, ret, hidden, wide, few):
    count, width = ret.shape[1:]
    pairs = wide // PAIR
    rows = shape(count, width, dtype=BF16)
    square = shape(width, wide)
    state = shape(pairs, PAIR, PAIR)
    outs = (
        rows, rows, shape(1, width), square, square, square, square, shape(wide, width), shape(few, wide), shape(few, wide),
        state, state, shape(1, width), shape(hidden, width), shape(hidden, width), shape(hidden, width),
    )
    return pl.pallas_call(
        finish_kernel,
        out_shape=outs,
        in_specs=[VMEM] * 6,
        out_specs=[VMEM] * len(outs),
        compiler_params=pltpu.CompilerParams(vmem_limit_bytes=LIMIT),
        name="finish",
    )(fa, fb, qa, qb, gains, ret)


def block_body(
    tokens, cotangent, source_index, tract_starts, memory_rates, mixer_gain, query_proj, key_proj, value_proj, gate_proj,
    out_proj, persist_keys, persist_values, memory_first, memory_second, dense_gain, dense_gate, dense_lift, dense_down,
):
    pairs = query_proj.shape[1] // PAIR
    first = memory_first.reshape(pairs, PAIR, PAIR)
    second = memory_second.transpose(0, 2, 1).reshape(pairs, PAIR, PAIR)
    summed = mega(
        tract_starts, memory_rates.transpose(0, 2, 1), source_index.reshape(1, -1), tokens, cotangent, mixer_gain[None],
        query_proj, key_proj, value_proj, gate_proj, out_proj, persist_keys, persist_values, first, second,
        dense_gain[None], dense_gate.T, dense_lift.T, dense_down,
    )
    outs = list(finish(*summed, dense_gate.shape[1], query_proj.shape[1], persist_keys.shape[0]))
    outs[2] = outs[2][0]
    outs[10] = outs[10].reshape(memory_first.shape)
    outs[11] = outs[11].reshape(memory_first.shape).transpose(0, 2, 1)
    outs[12] = outs[12][0]
    outs[13], outs[14] = outs[13].T, outs[14].T
    return tuple(outs)


def body(
    tokens,
    cotangent,
    source_index,
    tract_starts,
    memory_rates,
    mixer_gain,
    query_proj,
    key_proj,
    value_proj,
    gate_proj,
    out_proj,
    persist_keys,
    persist_values,
    memory_first,
    memory_second,
    dense_gain,
    dense_gate,
    dense_lift,
    dense_down,
):
    count = tokens.shape[0]
    width = tokens.shape[1]
    peers = lax.axis_size("dp")
    share = count // peers
    arrival = jnp.argsort(source_index)
    wanted = (source_index[arrival] % count).reshape(peers, share)
    asked = lax.all_to_all(wanted, "dp", split_axis=0, concat_axis=0, tiled=True).reshape(count)
    got_tokens, got_cot = (
        lax.all_to_all(
            tokens[asked].reshape(peers, share, width),
            "dp",
            split_axis=0,
            concat_axis=0,
            tiled=True,
        ),
        lax.all_to_all(
            cotangent[asked].reshape(peers, share, width),
            "dp",
            split_axis=0,
            concat_axis=0,
            tiled=True,
        ),
    )
    placing = jnp.argsort(arrival)
    seq_tokens = got_tokens.reshape(count, width)[placing]
    seq_cot = got_cot.reshape(count, width)[placing]
    seq_x = seq_tokens.astype(jnp.float32)
    first_norm, factor_one = norm_forward(seq_x)
    pairs = query_proj.shape[1] // PAIR
    by_pair = lambda value: value.reshape(-1, pairs, PAIR).transpose(1, 0, 2)
    by_head = lambda value: value.T.reshape(2 * pairs, HEAD_DIM, -1)
    weights = jnp.concatenate([query_proj, key_proj, value_proj, gate_proj], axis=1)
    pk, pv = by_pair(persist_keys), by_pair(persist_values)
    first = memory_first.reshape(pairs, PAIR, PAIR)
    second = memory_second.transpose(0, 2, 1).reshape(pairs, PAIR, PAIR)
    h_one, query, keys, values, gate, recall, mixed, keys_t, lse, a_all, c_all, pre_all, e_all, u_all, attended = mixer_forward(
        tract_starts, memory_rates, seq_tokens, mixer_gain[None], weights, pk, by_head(persist_values), first, second
    )
    first_out = lax.psum(product(mixed, out_proj), "tensor")
    resid = seq_x + first_out
    norm_two, factor_two = norm_forward(resid)
    h_two = (norm_two * dense_gain).astype(jnp.bfloat16)
    gated = product(h_two, dense_gate)
    lifted = product(h_two, dense_lift)
    sigma = jax.nn.sigmoid(gated)
    active = gated * sigma
    hidden = (active * lifted).astype(jnp.bfloat16)
    second_out = lax.psum(product(hidden, dense_down).astype(jnp.bfloat16), "tensor").astype(
        jnp.float32
    )
    seq_out = (resid + second_out).astype(jnp.bfloat16)
    grad_down = product(hidden.T, seq_cot)
    back_hidden = product(seq_cot, dense_down.T)
    back_gated = (back_hidden * lifted * (sigma + gated * sigma * (1.0 - sigma))).astype(
        jnp.bfloat16
    )
    back_lifted = (back_hidden * active).astype(jnp.bfloat16)
    grad_gate = product(h_two.T, back_gated)
    grad_lift = product(h_two.T, back_lifted)
    back_two = lax.psum(
        product(back_gated, dense_gate.T) + product(back_lifted, dense_lift.T), "tensor"
    )
    back_norm_two, grad_dgain = norm_backward(back_two, norm_two, factor_two, dense_gain)
    residual_gradient = seq_cot.astype(jnp.float32) + back_norm_two
    back_first = residual_gradient.astype(jnp.bfloat16)
    grad_out = product(mixed.T, back_first)
    back_mixed = product(back_first, out_proj.T).astype(jnp.bfloat16)
    back_query, back_keys, cotangent_payloads, back_gate, grad_pk, grad_pv, grad_first, grad_second = mixer_backward(
        tract_starts, memory_rates, back_mixed, query, keys, values, gate, recall, keys_t, pk, by_head(persist_keys), pv,
        lse, a_all, c_all, pre_all, e_all, u_all, attended,
    )
    grad_first = grad_first.reshape(memory_first.shape)
    grad_second = grad_second.reshape(memory_first.shape).transpose(0, 2, 1)
    grad_query = product(h_one.T, back_query)
    grad_key = product(h_one.T, back_keys)
    grad_value = product(h_one.T, cotangent_payloads)
    grad_gproj = product(h_one.T, back_gate)
    back_one = lax.psum(
        product(back_query, query_proj.T)
        + product(back_keys, key_proj.T)
        + product(cotangent_payloads, value_proj.T)
        + product(back_gate, gate_proj.T),
        "tensor",
    )
    back_norm_one, grad_mgain = norm_backward(back_one, first_norm, factor_one, mixer_gain)
    back_x = (residual_gradient + back_norm_one).astype(jnp.bfloat16)
    grad_pkeys = grad_pk.transpose(1, 0, 2).reshape(persist_keys.shape)
    grad_pvalues = grad_pv.transpose(1, 0, 2).reshape(persist_values.shape)
    (
        grad_mgain,
        grad_query,
        grad_key,
        grad_value,
        grad_gproj,
        grad_out,
        grad_pkeys,
        grad_pvalues,
        grad_first,
        grad_second,
        grad_dgain,
        grad_gate,
        grad_lift,
        grad_down,
    ) = lax.psum(
        (
            grad_mgain,
            grad_query,
            grad_key,
            grad_value,
            grad_gproj,
            grad_out,
            grad_pkeys,
            grad_pvalues,
            grad_first,
            grad_second,
            grad_dgain,
            grad_gate,
            grad_lift,
            grad_down,
        ),
        "dp",
    )
    ret_out, ret_grad = (
        lax.all_to_all(
            seq_out[arrival].reshape(peers, share, width),
            "dp",
            split_axis=0,
            concat_axis=0,
            tiled=True,
        ),
        lax.all_to_all(
            back_x[arrival].reshape(peers, share, width),
            "dp",
            split_axis=0,
            concat_axis=0,
            tiled=True,
        ),
    )
    undo = jnp.argsort(asked)
    layer_output = ret_out.reshape(count, width)[undo]
    input_grad = ret_grad.reshape(count, width)[undo]
    return (
        layer_output,
        input_grad,
        grad_mgain,
        grad_query,
        grad_key,
        grad_value,
        grad_gproj,
        grad_out,
        grad_pkeys,
        grad_pvalues,
        grad_first,
        grad_second,
        grad_dgain,
        grad_gate,
        grad_lift,
        grad_down,
    )


def solution(mesh):
    chosen = block_body if mesh.shape["dp"] == PEERS else body
    in_specs = (
        P("dp", None),
        P("dp", None),
        P("dp"),
        P("dp"),
        P(None, "dp", "tensor"),
        P(),
        P(None, "tensor"),
        P(None, "tensor"),
        P(None, "tensor"),
        P(None, "tensor"),
        P("tensor", None),
        P(None, "tensor"),
        P(None, "tensor"),
        P("tensor", None, None),
        P("tensor", None, None),
        P(),
        P(None, "tensor"),
        P(None, "tensor"),
        P("tensor", None),
    )
    out_specs = (
        P("dp", None),
        P("dp", None),
        P(),
        P(None, "tensor"),
        P(None, "tensor"),
        P(None, "tensor"),
        P(None, "tensor"),
        P("tensor", None),
        P(None, "tensor"),
        P(None, "tensor"),
        P("tensor", None, None),
        P("tensor", None, None),
        P(),
        P(None, "tensor"),
        P(None, "tensor"),
        P("tensor", None),
    )
    return jax.shard_map(chosen, mesh=mesh, in_specs=in_specs, out_specs=out_specs, check_vma=False)
```

```python
import jax
import jax.numpy as jnp
from jax import lax
from jax.experimental import pallas as pl
from jax.experimental.pallas import tpu as pltpu
from jax.sharding import PartitionSpec as P

HEAD_DIM = 64


EPSILON = 1e-06
MASKED = -1e30


def product(left, right):
    return jnp.dot(left, right, preferred_element_type=jnp.float32)


def norm_forward(value):
    factor = lax.rsqrt(jnp.mean(value * value, axis=-1, keepdims=True) + EPSILON)
    return (value * factor, factor)


def norm_backward(grad, normed, factor, gain):
    inner = grad * gain
    back = factor * (inner - normed * jnp.mean(inner * normed, axis=-1, keepdims=True))
    return (back, jnp.sum(grad * normed, axis=0))


F32, BF16 = jnp.float32, jnp.bfloat16
PAIR = 2 * HEAD_DIM
ROWS = 256
STRETCH = 64


def nn(a, b):
    return lax.dot_general(a, b, (((1,), (0,)), ((), ())), preferred_element_type=F32)


def nt(a, b):
    return lax.dot_general(a, b, (((1,), (1,)), ((), ())), preferred_element_type=F32)


def tn(a, b):
    return lax.dot_general(a, b, (((0,), (0,)), ((), ())), preferred_element_type=F32)


def sigmoid(v):
    return 1.0 / (1.0 + jnp.exp(-v))


def lanes_of(half, rows=1):
    return (lax.broadcasted_iota(jnp.int32, (rows, PAIR), 1) // HEAD_DIM) == half


def keep(value, half):
    return jnp.where(lanes_of(half), value, jnp.zeros_like(value))


def both(value):
    return jnp.concatenate([keep(value, 0), keep(value, 1)], axis=0)


def joined(stacked):
    rows = stacked.shape[0] // 2
    return jnp.where(lanes_of(0), stacked[:rows], stacked[rows:])


def scaled(pair, scalars):
    return jnp.concatenate([pair[:HEAD_DIM] * scalars[0], pair[HEAD_DIM:] * scalars[1]], axis=0)


def same_sequence(starts, early, late, per):
    count = jnp.int32(0)
    for c in range(early * per + 1, late * per + 1):
        count = count + starts[c]
    return count == 0


def earlier(s, starts, kb, qb, per):
    open_all = jnp.where(same_sequence(starts, kb, qb, per), 0.0, MASKED).astype(F32)
    open_head = jnp.where(starts[kb * per] > 0, MASKED, open_all).astype(F32)
    row = lax.broadcasted_iota(jnp.int32, (STRETCH, s.shape[1]), 0)
    top = s[:STRETCH] + jnp.where(row < STRETCH - 1, open_head, open_all)
    return jnp.concatenate([top, s[STRETCH:] + open_all], axis=0)


def fill_diagonal(ref, start):
    key = lax.broadcasted_iota(jnp.int32, ref.shape, 0)
    query = lax.broadcasted_iota(jnp.int32, ref.shape, 1)
    plain = jnp.where(key <= query, 0.0, MASKED)
    opening = jnp.where((key == query) | ((key < query) & (key >= STRETCH - 1)), 0.0, MASKED)
    ref[...] = jnp.where(start > 0, opening, plain).astype(F32)


def forward_kernel(
    starts, rates, tok, gain, w, pk, pvt, first, second,
    h1, q, k, v, gate, recall, mixed, kt, lse, a_all, c_all, pre_all, e_all, u_all, atth,
    vt, att, diagonal, a_s, c_s, sa_s, sc_s,
):
    count = tok.shape[0]
    pairs = first.shape[0]
    wide = pairs * PAIR
    per = ROWS // STRETCH

    def project(b, _):
        rows = pl.ds(pl.multiple_of(b * ROWS, ROWS), ROWS)
        x = tok[rows, :].astype(F32)
        factor = lax.rsqrt(jnp.mean(x * x, axis=-1, keepdims=True) + EPSILON)
        h = (x * factor * gain[...]).astype(BF16)
        h1[rows, :] = h
        for part, ref in ((0, q), (1, k), (2, v)):
            made = nn(h, w[:, part * wide:(part + 1) * wide])
            low = made.astype(BF16)
            for p in range(pairs):
                ref[p, rows, :] = low[:, p * PAIR:(p + 1) * PAIR]
            if part > 0:
                made_t = jnp.transpose(made).astype(BF16)
                target = kt if part == 1 else vt
                for h_i in range(2 * pairs):
                    target[h_i, :, rows] = made_t[h_i * HEAD_DIM:(h_i + 1) * HEAD_DIM]
        g = sigmoid(nn(h, w[:, 3 * wide:]))
        for p in range(pairs):
            gate[p, rows, :] = g[:, p * PAIR:(p + 1) * PAIR]
        return 0

    lax.fori_loop(0, count // ROWS, project, 0)
    a_s[...] = first[...]
    c_s[...] = second[...]
    sa_s[...] = jnp.zeros_like(sa_s)
    sc_s[...] = jnp.zeros_like(sc_s)

    def memory_step(t):
        rows = pl.ds(pl.multiple_of(t * STRETCH, STRETCH), STRETCH)
        fresh = starts[t] > 0
        for p in range(pairs):
            a = jnp.where(fresh, first[p], a_s[p])
            c = jnp.where(fresh, second[p], c_s[p])
            sa = jnp.where(fresh, 0.0, sa_s[p])
            sc = jnp.where(fresh, 0.0, sc_s[p])
            ab, cb = a.astype(BF16), c.astype(BF16)
            a_all[t, p] = ab
            c_all[t, p] = cb
            km = both(k[p, rows, :])
            lhs = jnp.concatenate([both(q[p, rows, :]), km], axis=0)
            pre = nn(lhs, ab)
            pre_all[t, p] = pre
            sig = sigmoid(pre)
            act = pre * sig
            actb = act.astype(BF16)
            out = nt(actb, cb)
            recall[p, rows, :] = joined(out[:PAIR])
            e = joined(out[PAIR:]) - v[p, rows, :].astype(F32)
            eb = e.astype(BF16)
            e_all[p, rows, :] = eb
            em = both(eb)
            u = nn(em, cb)
            u_all[t, p] = u
            sigk, actk = sig[PAIR:], act[PAIR:]
            wgt = (u * (sigk + actk * (1.0 - sigk))).astype(BF16)
            ga = tn(km, wgt)
            gc = tn(em, actb[PAIR:])
            th = [rates[0, t, 2 * p + i] * (1.0 / STRETCH) for i in range(2)]
            eta = [rates[1, t, 2 * p + i] for i in range(2)]
            al = [1.0 - rates[2, t, 2 * p + i] for i in range(2)]
            sa = scaled(sa, eta) - scaled(ga, th)
            sc = scaled(sc, eta) - scaled(gc, th)
            sa_s[p] = sa
            sc_s[p] = sc
            a_s[p] = scaled(a, al) + sa
            c_s[p] = scaled(c, al) + sc

    def attention_unit(qb, head):
        p, half = head // 2, head % 2
        rows = pl.ds(qb * ROWS, ROWS)
        qh = keep(q[p, rows, :], half) * jnp.asarray(HEAD_DIM ** -0.5, BF16)
        scores = []
        for kb in range(qb + 1):
            s = nt(k[p, kb * ROWS:(kb + 1) * ROWS, :], qh)
            if kb == qb:
                s = s + diagonal[...]
            else:
                s = earlier(s, starts, kb, qb, per)
            scores.append(s)
        sp = nt(pk[p], qh)
        peak = jnp.max(sp, axis=0, keepdims=True)
        for s in scores:
            peak = jnp.maximum(peak, jnp.max(s, axis=0, keepdims=True))
        ep = jnp.exp(sp - peak)
        total = jnp.sum(ep, axis=0, keepdims=True)
        out = nn(pvt[head], ep.astype(BF16))
        for kb, s in enumerate(scores):
            e = jnp.exp(s - peak)
            total = total + jnp.sum(e, axis=0, keepdims=True)
            out = out + nn(vt[head, :, kb * ROWS:(kb + 1) * ROWS], e.astype(BF16))
        att[head, :, rows] = out * (1.0 / total)
        lse[head, :, rows] = peak + jnp.log(total)

    heads = 2 * pairs
    for qb in range(count // ROWS):
        fill_diagonal(diagonal, starts[qb * per])

        def run(i, _, qb=qb):
            memory_step(qb * per + i)
            attention_unit(qb, i)
            return 0
        lax.fori_loop(0, per, run, 0)
    for b in range(count // ROWS):
        rows = pl.ds(b * ROWS, ROWS)
        for p in range(pairs):
            got = jnp.concatenate([att[2 * p, :, rows], att[2 * p + 1, :, rows]], axis=0)
            wide_att = jnp.transpose(got)
            atth[p, rows, :] = wide_att
            mixed[rows, p * PAIR:(p + 1) * PAIR] = (wide_att + gate[p, rows, :] * recall[p, rows, :]).astype(BF16)


def backward_kernel(
    starts, rates, bm, q, k, v, gate, recall, kt, pk, pkt, pv, lse, a_all, c_all, pre_all, e_all, u_all, atth,
    dq, dk, dv, dg, dpk, dpv, dfirst, dsecond,
    dqt, dd, dks, dvs, mq, bmp, diagonal, da_s, dc_s, dsa_s, dsc_s,
):
    count = bm.shape[0]
    pairs = q.shape[0]
    heads = 2 * pairs
    per = ROWS // STRETCH
    nblocks = count // ROWS
    ones = [jnp.where(lanes_of(i, 8), 1.0, 0.0).astype(F32) for i in range(2)]
    for b in range(nblocks):
        rows = pl.ds(b * ROWS, ROWS)
        for p in range(pairs):
            gb = bm[rows, p * PAIR:(p + 1) * PAIR]
            bmp[p, rows, :] = gb
            g = gb.astype(F32)
            inner = g * atth[p, rows, :]
            for i in range(2):
                row = lax.dot_general(ones[i], inner, (((1,), (1,)), ((), ())), precision=lax.Precision.HIGHEST, preferred_element_type=F32)
                dd[2 * p + i, :, rows] = row[:1]
            gt = gate[p, rows, :]
            dg[rows, p * PAIR:(p + 1) * PAIR] = (g * recall[p, rows, :] * gt * (1.0 - gt)).astype(BF16)
    for ref in (dpk, dpv, dfirst, dsecond, dks, dvs, da_s, dc_s, dsa_s, dsc_s):
        ref[...] = jnp.zeros_like(ref)

    def memory_step(t):
        rows = pl.ds(pl.multiple_of(t * STRETCH, STRETCH), STRETCH)
        fresh = starts[t] > 0
        for p in range(pairs):
            th = [rates[0, t, 2 * p + i] * (-1.0 / STRETCH) for i in range(2)]
            eta = [rates[1, t, 2 * p + i] for i in range(2)]
            al = [1.0 - rates[2, t, 2 * p + i] for i in range(2)]
            da, dc = da_s[p], dc_s[p]
            dsa = dsa_s[p] + da
            dsc = dsc_s[p] + dc
            dga = scaled(dsa, th).astype(BF16)
            dgc = scaled(dsc, th).astype(BF16)
            ab, cb = a_all[t, p], c_all[t, p]
            km, qm = both(k[p, rows, :]), both(q[p, rows, :])
            em = both(e_all[p, rows, :])
            pre = pre_all[t, p]
            sig = sigmoid(pre)
            act = pre * sig
            actb = act.astype(BF16)
            slope = sig + act * (1.0 - sig)
            sigk, prek, slopek = sig[PAIR:], pre[PAIR:], slope[PAIR:]
            u = u_all[t, p]
            curve = sigk * (1.0 - sigk) * (2.0 + prek * (1.0 - 2.0 * sigk))
            wgt = (u * slopek).astype(BF16)
            back = bmp[p, rows, :].astype(F32) * gate[p, rows, :]
            rm = both(back.astype(BF16))
            dpre_q = (nn(rm, cb) * slope[:PAIR]).astype(BF16)
            mq[0, p, rows, :] = joined(nt(dpre_q, ab))
            dw = nn(km, dga)
            du = (dw * slopek).astype(BF16)
            cc = jnp.concatenate([dgc, cb], axis=1)
            de = joined(nt(jnp.concatenate([actb[PAIR:], du], axis=1), cc))
            mq[2, p, rows, :] = -de
            dem = both(de.astype(BF16))
            dsk = nn(jnp.concatenate([em, dem], axis=1), jnp.concatenate([dgc, cb], axis=0))
            dpre = (dsk * slopek + dw * u * curve).astype(BF16)
            mq[1, p, rows, :] = joined(nt(jnp.concatenate([wgt, dpre], axis=1), jnp.concatenate([dga, ab], axis=1)))
            ga = tn(jnp.concatenate([km, qm], axis=0), jnp.concatenate([dpre, dpre_q], axis=0))
            gc = tn(jnp.concatenate([em, dem], axis=0), jnp.concatenate([du, actb[PAIR:]], axis=0))
            gc = gc + tn(rm, actb[:PAIR])
            da = scaled(da, al) + ga
            dc = scaled(dc, al) + gc
            dfirst[p] = dfirst[p] + jnp.where(fresh, da, 0.0)
            dsecond[p] = dsecond[p] + jnp.where(fresh, dc, 0.0)
            da_s[p] = jnp.where(fresh, 0.0, da)
            dc_s[p] = jnp.where(fresh, 0.0, dc)
            dsa_s[p] = jnp.where(fresh, 0.0, scaled(dsa, eta))
            dsc_s[p] = jnp.where(fresh, 0.0, scaled(dsc, eta))

    def attention_unit(qb, head):
        p, half = head // 2, head % 2
        rows = pl.ds(qb * ROWS, ROWS)
        qh = keep(q[p, rows, :], half) * jnp.asarray(HEAD_DIM ** -0.5, BF16)
        gh = keep(bmp[p, rows, :], half)
        lrow, drow = lse[head, :, rows], dd[head, :, rows]
        acc = jnp.zeros((HEAD_DIM, ROWS), F32)
        for kb in range(qb + 1):
            krows = slice(kb * ROWS, (kb + 1) * ROWS)
            s = nt(k[p, krows, :], qh) - lrow
            if kb == qb:
                s = s + diagonal[...]
            else:
                s = earlier(s, starts, kb, qb, per)
            prob = jnp.exp(s)
            ds = (prob * (nt(v[p, krows, :], gh) - drow)).astype(BF16)
            dvs[p, krows, :] = dvs[p, krows, :] + nn(prob.astype(BF16), gh)
            dks[p, krows, :] = dks[p, krows, :] + nn(ds, qh)
            acc = acc + nn(kt[head, :, krows], ds)
        prob = jnp.exp(nt(pk[p], qh) - lrow)
        ds = (prob * (nt(pv[p], gh) - drow)).astype(BF16)
        dpv[p] = dpv[p] + nn(prob.astype(BF16), gh)
        dpk[p] = dpk[p] + nn(ds, qh)
        acc = acc + nn(pkt[head], ds)
        dqt[head, :, rows] = acc * (HEAD_DIM ** -0.5)

    for qb in reversed(range(nblocks)):
        fill_diagonal(diagonal, starts[qb * per])

        def run(i, _, qb=qb):
            memory_step(qb * per + per - 1 - i)
            attention_unit(qb, i)
            return 0
        lax.fori_loop(0, per, run, 0)
    for b in range(nblocks):
        rows = pl.ds(b * ROWS, ROWS)
        for p in range(pairs):
            cols = slice(p * PAIR, (p + 1) * PAIR)
            got = jnp.concatenate([dqt[2 * p, :, rows], dqt[2 * p + 1, :, rows]], axis=0)
            dq[rows, cols] = (jnp.transpose(got) + mq[0, p, rows, :]).astype(BF16)
            dk[rows, cols] = (dks[p, rows, :] + mq[1, p, rows, :]).astype(BF16)
            dv[rows, cols] = (dvs[p, rows, :] + mq[2, p, rows, :]).astype(BF16)


def shape(*dims, dtype=F32):
    return jax.ShapeDtypeStruct(dims, dtype)


VMEM = pl.BlockSpec(memory_space=pltpu.VMEM)
SMEM = pl.BlockSpec(memory_space=pltpu.SMEM)
LIMIT = 56 * 1024 * 1024


def mixer_forward(starts, rates, tok, gain, w, pk, pvt, first, second):
    count, width = tok.shape
    pairs = first.shape[0]
    heads, steps = 2 * pairs, starts.shape[0]
    flat = lambda dtype: shape(pairs, count, PAIR, dtype=dtype)
    outs = (
        shape(count, width, dtype=BF16), flat(BF16), flat(BF16), flat(BF16), flat(F32), flat(F32),
        shape(count, pairs * PAIR, dtype=BF16), shape(heads, HEAD_DIM, count, dtype=BF16), shape(heads, 1, count),
        shape(steps, pairs, PAIR, PAIR, dtype=BF16), shape(steps, pairs, PAIR, PAIR, dtype=BF16),
        shape(steps, pairs, 2 * PAIR, PAIR), flat(BF16), shape(steps, pairs, PAIR, PAIR), flat(F32),
    )
    state = pltpu.VMEM((pairs, PAIR, PAIR), F32)
    return pl.pallas_call(
        forward_kernel,
        out_shape=outs,
        in_specs=[SMEM, SMEM] + [VMEM] * 7,
        out_specs=[VMEM] * len(outs),
        scratch_shapes=[
            pltpu.VMEM((heads, HEAD_DIM, count), BF16), pltpu.VMEM((heads, HEAD_DIM, count), F32),
            pltpu.VMEM((ROWS, ROWS), F32), state, state, state, state,
        ],
        compiler_params=pltpu.CompilerParams(vmem_limit_bytes=LIMIT),
        name="mixer_forward",
    )(starts, rates, tok, gain, w, pk, pvt, first, second)


def mixer_backward(starts, rates, bm, q, k, v, gate, recall, kt, pk, pkt, pv, lse, a_all, c_all, pre_all, e_all, u_all, atth):
    count, wide = bm.shape
    pairs = q.shape[0]
    heads = 2 * pairs
    outs = (
        shape(count, wide, dtype=BF16), shape(count, wide, dtype=BF16), shape(count, wide, dtype=BF16), shape(count, wide, dtype=BF16),
        shape(*pk.shape), shape(*pv.shape), shape(pairs, PAIR, PAIR), shape(pairs, PAIR, PAIR),
    )
    state = pltpu.VMEM((pairs, PAIR, PAIR), F32)
    flat = pltpu.VMEM((pairs, count, PAIR), F32)
    return pl.pallas_call(
        backward_kernel,
        out_shape=outs,
        in_specs=[SMEM, SMEM] + [VMEM] * 17,
        out_specs=[VMEM] * len(outs),
        scratch_shapes=[
            pltpu.VMEM((heads, HEAD_DIM, count), F32), pltpu.VMEM((heads, 1, count), F32), flat, flat,
            pltpu.VMEM((3, pairs, count, PAIR), F32), pltpu.VMEM((pairs, count, PAIR), BF16),
            pltpu.VMEM((ROWS, ROWS), F32), state, state, state, state,
        ],
        compiler_params=pltpu.CompilerParams(vmem_limit_bytes=LIMIT),
        name="mixer_backward",
    )(starts, rates, bm, q, k, v, gate, recall, kt, pk, pkt, pv, lse, a_all, c_all, pre_all, e_all, u_all, atth)


MESH = pl.DeviceIdType.MESH
HALF_SHARE = 32
PEERS = 16


def place():
    return lax.axis_index("dp"), lax.axis_index("tensor")


def flipped(index, mask):
    result = index
    bit = 1
    while bit <= mask:
        if mask & bit:
            result = result + bit * (1 - 2 * (lax.div(index, bit) % 2))
        bit *= 2
    return result


def greet(devices):
    for device in devices:
        pl.semaphore_signal(pltpu.get_barrier_semaphore(), inc=1, device_id=device, device_id_type=MESH)


def greeted(devices):
    pl.semaphore_wait(pltpu.get_barrier_semaphore(), len(devices))


def remote(src, dst, send_sem, recv_sem, device):
    return pltpu.make_async_remote_copy(
        src_ref=src, dst_ref=dst, send_sem=send_sem, recv_sem=recv_sem, device_id=device, device_id_type=MESH
    )


def iota(rows, columns, dimension):
    return lax.broadcasted_iota(jnp.int32, (rows, columns), dimension)


def at_rows(start, size):
    return pl.ds(pl.multiple_of(start, size), size)


def lot(peer):
    return peer % 2 * (PEERS // 2) + lax.div(peer, 2) % 2 * (PEERS // 4) + lax.div(peer, 4)


QUARTERS = tuple(tuple(range(first, PEERS, 4)) for first in (0, 2, 1, 3))
ALL_PEERS = sum(QUARTERS, ())


def spreading(ref, dp, t, side, sent, sems, m):
    peer = flipped(dp, m)
    return remote(
        sent.at[at_rows(lot(peer) * HALF_SHARE, HALF_SHARE)], ref.at[at_rows(side * (PEERS * HALF_SHARE) + lot(dp) * HALF_SHARE, HALF_SHARE)],
        sems.at[0, m], sems.at[1, m], (peer, t),
    )


def spread(ref, dp, t, side, sent, sems, masks):
    for m in masks:
        if m:
            spreading(ref, dp, t, side, sent, sems, m).start()
        else:
            here = lot(dp) * HALF_SHARE
            ref[at_rows(side * (PEERS * HALF_SHARE) + here, HALF_SHARE), :] = sent[at_rows(here, HALF_SHARE), :]


def pass_on(ref, dp, t, sent, sems, y_sems):
    for m in ALL_PEERS:
        if m:
            spreading(ref, dp, t, t, sent, sems, m).wait()
        passing(ref, dp, t, m, y_sems).start()


def passing(ref, dp, t, m, sems):
    rows = at_rows(t * (PEERS * HALF_SHARE) + lot(flipped(dp, m)) * HALF_SHARE, HALF_SHARE)
    return remote(ref.at[rows], ref.at[rows], sems.at[0, m], sems.at[1, m], (dp, 1 - t))


def passed_on(ref, dp, t, sems):
    for m in range(PEERS):
        passing(ref, dp, t, m, sems).wait()


def sixteens(start, size):
    return pl.ds(pl.multiple_of(start, 16), size)


class Sum:
    def __init__(self, dp, t, src, base, out, order, scratch):
        self.dp, self.t, self.src, self.base, self.out, self.order = dp, t, src, base, out, order
        n = len(order)
        self.acc, self.sems = scratch[0], scratch[1]
        self.rcv = scratch[2:2 + n]
        self.snd = (None,) + tuple(scratch[2 + n:1 + 2 * n])
        self.at = [lax.div(dp, stride) % size for stride, size in order]
        self.rows = [out.shape[0]]
        self.start = [0]
        for (stride, size), c in zip(order, self.at):
            self.rows.append(self.rows[-1] // size)
            self.start.append(self.start[-1] + c * self.rows[-1])
        self.next = 0

    @staticmethod
    def scratch(rows, lanes, order):
        counts, sizes = [], [rows]
        for stride, size in order:
            sizes.append(sizes[-1] // size)
            counts.append(size - 1)
        blocks = [pltpu.VMEM((count, size, lanes), BF16) for count, size in zip(counts, sizes[1:])]
        return [pltpu.VMEM((sizes[1], lanes), BF16), pltpu.SemaphoreType.DMA((2, 2 * sum(counts)))] + blocks + blocks[1:]

    @staticmethod
    def refs(order):
        return 1 + 2 * len(order)

    def peer(self, s, k):
        stride, size = self.order[s]
        d = (self.at[s] + k) % size
        return d, self.dp + stride * (d - self.at[s])

    def copies(self, n):
        made = []
        stages = len(self.order)
        counts = [size - 1 for _, size in self.order]
        s = n if n < stages else 2 * stages - 1 - n
        for k in range(1, self.order[s][1]):
            d, peer = self.peer(s, k)
            if n >= stages:
                src = dst = self.out.at[sixteens(self.start[s + 1], self.rows[s + 1])]
            else:
                src = self.snd[s].at[k - 1] if s else self.src.at[sixteens(self.base + d * self.rows[1], self.rows[1])]
                dst = self.rcv[s].at[k - 1]
            i = sum(counts[:s]) + k - 1 + (sum(counts) if n >= stages else 0)
            made.append(remote(src, dst, self.sems.at[0, i], self.sems.at[1, i], (peer, self.t)))
        return made

    def added(self, own, s, rows):
        count = self.order[s][1] - 1
        if count == 1:
            return own + self.rcv[s][0, rows, :]
        total = own.astype(F32)
        for j in range(count):
            total = total + self.rcv[s][j, rows, :].astype(F32)
        return total.astype(BF16)

    def step(self):
        n, stages = self.next, len(self.order)
        self.next += 1
        if n:
            for copy in self.copies(n - 1):
                copy.wait()
        if 0 < n < stages:
            size = self.rows[n + 1]
            inside = self.start[n] - self.start[1]
            for k in list(range(1, self.order[n][1])) + [0]:
                d, _ = self.peer(n, k)
                here = sixteens(inside + d * size, size)
                own = self.src[sixteens(self.base + self.start[1] + d * size, size), :] if n == 1 else self.acc[here, :]
                total = self.added(own, n - 1, sixteens(d * size, size))
                if k:
                    self.snd[n][k - 1] = total
                else:
                    self.acc[here, :] = total
        if n == stages:
            size = self.rows[stages]
            own = self.acc[sixteens(self.start[stages] - self.start[1], size), :]
            self.out[sixteens(self.start[stages], size), :] = self.added(own, stages - 1, pl.ds(0, size))
        if n < 2 * stages:
            for copy in self.copies(n):
                copy.start()


ANY = pl.BlockSpec(memory_space=pl.ANY)
LONG_ORDER = ((1, 2), (2, 2), (4, 2), (8, 2))
XZ_ORDER = ((1, 2), (2, 2), (4, 4))
ZX_ORDER = ((1, 2), (4, 4), (2, 2))
SUM_ORDERS = (LONG_ORDER, XZ_ORDER, XZ_ORDER, ZX_ORDER)


def mega_kernel(
    starts, rates, idx, tok_in, cot_in, gain1, wq_in, wk_in, wv_in, wg_in, op_in, pk_in, pv_in, first, second, gain2, dgw_in, dlw_in, ddw_in,
    fa_out, fb_out, qa_out, qb_out, gains_out, ret,
    xs, cs, mx, ops, asked, want, sent_c, g, gt, h1, q, k, v, gate, recall, kt, lse, a_all, c_all, pre_all, e_all, u_all, atth,
    pk, pv, pkt, pvt, bmp, diagonal, br, own_s, ps_s, pb_r, bms, facc, gout, gother, dgain,
    second_r, gother_r, rec_l, rec_x, part_r, src_b, src_c, out_a, out_b, out_c1, out_c2, gains_s, gains_r,
    a_s, c_s, sa_s, sc_s, wq, wk, wv, wg, op, dgw, dlw, ddw,
    in_sems, ask_sems, t_sems, ty_sems, c_sems, m_sems, d_sems, y_sems, l_sems, ly_sems, x_sems, xy_sems, g_sems, o_sems,
    *sums,
):
    dp, t = place()
    other = (dp, 1 - t)
    core = dp % 2
    count, width = xs.shape
    half = count // 2
    pairs = first.shape[0]
    heads = 2 * pairs
    wide = pairs * PAIR
    few = pk_in.shape[0]
    per = ROWS // STRETCH
    nblocks = count // ROWS
    hidden = dgw.shape[0]
    padded = facc.shape[0] // 3
    scale = HEAD_DIM ** -0.5

    rows_a = out_a.shape[0]
    rest = facc.shape[0] - rows_a
    cuts = [0]
    for order in SUM_ORDERS:
        cuts.append(cuts[-1] + Sum.refs(order))
    sum_a, sum_b, sum_c1, sum_c2 = [
        Sum(dp, t, src, base, out, order, sums[cuts[i]:cuts[i + 1]])
        for i, (src, base, out, order) in enumerate((
            (facc, 0, out_a, SUM_ORDERS[0]), (src_b, 0, out_b, SUM_ORDERS[1]),
            (src_c, 0, out_c1, SUM_ORDERS[2]), (src_c, out_c1.shape[0], out_c2, SUM_ORDERS[3]),
        ))
    ]

    def second_copy(i):
        src, dst = ((ps_s, second_r), (gother, gother_r))[i]
        return remote(src, dst, y_sems.at[0, i], y_sems.at[1, i], other)

    weights = [
        pltpu.make_async_copy(src, dst, in_sems.at[2 + i])
        for i, (src, dst) in enumerate((
            (wq_in, wq), (wk_in, wk), (wv_in, wv), (wg_in, wg), (op_in, op), (dgw_in, dgw), (dlw_in, dlw), (ddw_in, ddw),
        ))
    ]
    friends = [(flipped(dp, m), t) for m in range(1, PEERS)] + [other]
    greet(friends)
    def enter(tok, cot, sent_t):
        reads = [pltpu.make_async_copy(src, dst, in_sems.at[i]) for i, (src, dst) in enumerate(((tok_in, tok), (cot_in, cot)))]
        for read in reads + weights:
            read.start()
        index = idx[...]
        dev = lax.div(index, count)
        row = index - dev * count
        held = jnp.where(iota(PEERS, count, 0) == dev, 1.0, 0.0).astype(BF16)
        upper = jnp.where(iota(PAIR, PAIR, 0) < iota(PAIR, PAIR, 1), 1.0, 0.0).astype(BF16)
        run = jnp.zeros((PEERS, 1), F32)
        ranks = []
        for c in range(count // PAIR):
            part = held[:, c * PAIR:(c + 1) * PAIR]
            wide_part = part.astype(F32)
            ranks.append(jnp.sum(wide_part * (nn(part, upper) + run), axis=0, keepdims=True))
            run = run + jnp.sum(wide_part, axis=1, keepdims=True)
        rank = jnp.concatenate(ranks, axis=1)
        column = jnp.transpose(jnp.broadcast_to(rank, (PAIR, count)))
        pick = jnp.where(column == iota(count, PAIR, 1).astype(F32), 1.0, 0.0).astype(BF16)
        high = lax.div(row, 32)
        low = row - high * 32
        held_wide = held.astype(F32)
        wanted = 32.0 * nn((held_wide * high.astype(F32)).astype(BF16), pick) + nn((held_wide * low.astype(F32)).astype(BF16), pick)
        for j in range(PEERS):
            want[j] = jnp.broadcast_to(wanted[j:j + 1], (8, PAIR))
        greeted(friends)
        asks = []
        for m in range(1, PEERS):
            peer = flipped(dp, m)
            copy = remote(want.at[peer], asked.at[dp], ask_sems.at[0, m], ask_sems.at[1, m], (peer, t))
            copy.start()
            asks.append(copy)
        asked[dp] = want[dp]
        rank_i = rank.astype(jnp.int32)
        half_of = lax.div(rank_i, HALF_SHARE)
        slot = half_of * (half - HALF_SHARE) + lot(dev) * HALF_SHARE + rank_i
        for c in range(count // ROWS):
            gt[c * ROWS:(c + 1) * ROWS, :] = jnp.where(iota(ROWS, count, 0) + c * ROWS == slot, 1.0, 0.0).astype(BF16)
        slots = jnp.transpose(jnp.broadcast_to(slot.astype(F32), (PAIR, count)))
        for copy in asks:
            copy.wait()
        asks_in = asked[:, 0, :]
        asks_high = jnp.floor(asks_in * (1.0 / 32.0))
        asks_low = asks_in - 32.0 * asks_high
        owner = jnp.where(lax.div(iota(half, PEERS, 0), HALF_SHARE) == lot(iota(half, PEERS, 1)), 1.0, 0.0).astype(BF16)
        ones = jnp.ones((PAIR, PAIR), BF16)

        def choose(side):
            lane = iota(half, PAIR, 1) == iota(half, PAIR, 0) % HALF_SHARE + side * HALF_SHARE
            value = jnp.zeros((half, PAIR), F32)
            for digit, weight in ((asks_high, 32.0), (asks_low, 1.0)):
                picked = jnp.where(lane, nn(owner, digit.astype(BF16)), 0.0).astype(BF16)
                value = value + weight * nn(picked, ones)
            return jnp.concatenate(
                [jnp.where(value == (iota(half, PAIR, 1) + c * PAIR).astype(F32), 1.0, 0.0).astype(BF16) for c in range(count // PAIR)], axis=1
            )

        chosen = choose(t)
        for read in reads + weights:
            read.wait()
        sent_t[...] = nn(chosen, tok[...]).astype(BF16)
        spread(xs, dp, t, t, sent_t, t_sems, ALL_PEERS)
        sent_c[0] = nn(chosen, cot[...]).astype(BF16)
        sent_c[1] = nn(choose(1 - t), cot[...]).astype(BF16)
        for c in range(count // PAIR):
            g[:, c * PAIR:(c + 1) * PAIR] = jnp.where(slots == (iota(count, PAIR, 1) + c * PAIR).astype(F32), 1.0, 0.0).astype(BF16)
        for half_i in range(2):
            for ref_in, by_pair, by_head in ((pk_in, pk, pkt), (pv_in, pv, pvt)):
                part = ref_in[:, half_i * PAIR:(half_i + 1) * PAIR]
                by_pair[half_i] = part
                flat = jnp.transpose(part.astype(F32)).astype(BF16)
                by_head[2 * half_i] = flat[:HEAD_DIM]
                by_head[2 * half_i + 1] = flat[HEAD_DIM:]
        pass_on(xs, dp, t, sent_t, t_sems, ty_sems)
        passed_on(xs, dp, t, ty_sems)

    pl.run_scoped(enter, pltpu.VMEM((count, width), BF16), pltpu.VMEM((count, width), BF16), pltpu.VMEM((half, width), BF16))

    def ops_copy():
        return remote(ops.at[t], ops.at[t], m_sems.at[0, nblocks], m_sems.at[1, nblocks], other)

    def mixed_copy(qb):
        rows = pl.ds(qb * ROWS, ROWS)
        return remote(mx.at[t, rows], mx.at[t, rows], m_sems.at[0, qb], m_sems.at[1, qb], other)

    ops[t] = op[...]
    ops_copy().start()
    for i, side in enumerate((t, 1 - t)):
        spread(cs, dp, t, side, sent_c.at[i], c_sems.at[i], ALL_PEERS)

    def forward(vt, att):
        def project(b, _):
            rows = pl.ds(pl.multiple_of(b * ROWS, ROWS), ROWS)
            x = nn(g[rows, :], xs[...])
            factor = lax.rsqrt(jnp.mean(x * x, axis=-1, keepdims=True) + EPSILON)
            h = (x * factor * gain1[...]).astype(BF16)
            h1[rows, :] = h
            for part, (ref, w) in enumerate(((q, wq), (k, wk), (v, wv))):
                made = nn(h, w[...])
                low = made.astype(BF16)
                for p in range(pairs):
                    ref[p, rows, :] = low[:, p * PAIR:(p + 1) * PAIR]
                if part > 0:
                    made_t = jnp.transpose(made).astype(BF16)
                    target = kt if part == 1 else vt
                    for i in range(heads):
                        target[i, :, rows] = made_t[i * HEAD_DIM:(i + 1) * HEAD_DIM]
            made = sigmoid(nn(h, wg[...]))
            for p in range(pairs):
                gate[p, rows, :] = made[:, p * PAIR:(p + 1) * PAIR]
            return 0

        lax.fori_loop(0, nblocks, project, 0)
        a_s[...] = first[...]
        c_s[...] = second[...]
        sa_s[...] = jnp.zeros_like(sa_s)
        sc_s[...] = jnp.zeros_like(sc_s)

        def memory_step(n):
            rows = pl.ds(pl.multiple_of(n * STRETCH, STRETCH), STRETCH)
            fresh = starts[n] > 0
            for p in range(pairs):
                a = jnp.where(fresh, first[p], a_s[p])
                c = jnp.where(fresh, second[p], c_s[p])
                sa = jnp.where(fresh, 0.0, sa_s[p])
                sc = jnp.where(fresh, 0.0, sc_s[p])
                ab, cb = a.astype(BF16), c.astype(BF16)
                a_all[n, p] = ab
                c_all[n, p] = cb
                km = both(k[p, rows, :])
                pre = nn(jnp.concatenate([both(q[p, rows, :]), km], axis=0), ab)
                pre_all[n, p] = pre
                sig = sigmoid(pre)
                act = pre * sig
                actb = act.astype(BF16)
                out = nt(actb, cb)
                recall[p, rows, :] = joined(out[:PAIR])
                eb = (joined(out[PAIR:]) - v[p, rows, :].astype(F32)).astype(BF16)
                e_all[p, rows, :] = eb
                em = both(eb)
                u = nn(em, cb)
                u_all[n, p] = u.astype(BF16)
                sigk, actk = sig[PAIR:], act[PAIR:]
                ga = tn(km, (u * (sigk + actk * (1.0 - sigk))).astype(BF16))
                gc = tn(em, actb[PAIR:])
                th = [rates[0, 2 * p + i, n] * (1.0 / STRETCH) for i in range(2)]
                eta = [rates[1, 2 * p + i, n] for i in range(2)]
                al = [1.0 - rates[2, 2 * p + i, n] for i in range(2)]
                sa = scaled(sa, eta) - scaled(ga, th)
                sc = scaled(sc, eta) - scaled(gc, th)
                sa_s[p] = sa
                sc_s[p] = sc
                a_s[p] = scaled(a, al) + sa
                c_s[p] = scaled(c, al) + sc

        def attention_unit(qb, head):
            p, side = head // 2, head % 2
            rows = pl.ds(qb * ROWS, ROWS)
            qh = keep(q[p, rows, :], side) * jnp.asarray(scale, BF16)
            scores = []
            for kb in range(qb + 1):
                s = nt(k[p, kb * ROWS:(kb + 1) * ROWS, :], qh)
                scores.append(s + diagonal[...] if kb == qb else earlier(s, starts, kb, qb, per))
            sp = nt(pk[p], qh)
            peak = jnp.max(sp, axis=0, keepdims=True)
            for s in scores:
                peak = jnp.maximum(peak, jnp.max(s, axis=0, keepdims=True))
            ep = jnp.exp(sp - peak)
            total = jnp.sum(ep, axis=0, keepdims=True)
            out = nn(pvt[head], ep.astype(BF16))
            for kb, s in enumerate(scores):
                e = jnp.exp(s - peak)
                total = total + jnp.sum(e, axis=0, keepdims=True)
                out = out + nn(vt[head, :, kb * ROWS:(kb + 1) * ROWS], e.astype(BF16))
            att[head, :, rows] = out * (1.0 / total)
            lse[head, :, rows] = peak + jnp.log(total)

        for qb in range(nblocks):
            fill_diagonal(diagonal, starts[qb * per])

            def run(i, _, qb=qb):
                memory_step(qb * per + i)
                attention_unit(qb, i)
                return 0

            lax.fori_loop(0, per, run, 0)
            rows = pl.ds(qb * ROWS, ROWS)
            for p in range(pairs):
                got = jnp.transpose(jnp.concatenate([att[2 * p, :, rows], att[2 * p + 1, :, rows]], axis=0))
                atth[p, rows, :] = got.astype(BF16)
                mx[t, rows, p * PAIR:(p + 1) * PAIR] = (got + gate[p, rows, :] * recall[p, rows, :]).astype(BF16)
            mixed_copy(qb).start()

    pl.run_scoped(forward, pltpu.VMEM((heads, HEAD_DIM, count), BF16), pltpu.VMEM((heads, HEAD_DIM, count), F32))

    def dense_part(ms, hid, bgs, bls, bms_s, resid, own_b):
        h2s, pb_s, bf = src_b.at[:count], src_c.at[:half], src_c.at[half:]
        pad = jnp.zeros((count, PAIR), BF16)
        for ref in (hid, bgs, bls):
            ref[:, padded - PAIR:] = pad
        ms[t] = nn(gt[...], mx[t]).astype(BF16)
        ops_copy().wait()
        for qb in range(nblocks):
            mixed_copy(qb).wait()
        for i, side in enumerate((t, 1 - t)):
            for m in ALL_PEERS[1:]:
                spreading(cs, dp, t, side, sent_c.at[i], c_sems.at[i], m).wait()
        ms[1 - t] = nn(gt[...], mx[1 - t]).astype(BF16)

        def chunk(rows, store):
            x = xs[rows, :].astype(F32) + nn(ms[0, rows, :], ops[0]) + nn(ms[1, rows, :], ops[1])
            factor = lax.rsqrt(jnp.mean(x * x, axis=-1, keepdims=True) + EPSILON)
            h2 = (x * factor * gain2[...]).astype(BF16)
            h2s[rows, :] = h2
            for begin in range(0, hidden, ROWS):
                cols = slice(begin, min(begin + ROWS, hidden))
                gated, lifted = nt(h2, dgw[cols, :]), nt(h2, dlw[cols, :])
                sig = sigmoid(gated)
                act = gated * sig
                hid[rows, cols] = (act * lifted).astype(BF16)
                back = nt(cs[rows, :], ddw[cols, :])
                bgs[rows, cols] = (back * lifted * (sig + act * (1.0 - sig))).astype(BF16)
                bls[rows, cols] = (back * act).astype(BF16)
            store(x, nn(bgs[rows, :hidden], dgw[...]) + nn(bls[rows, :hidden], dlw[...]), rows)

        copies = []
        for c in range(half // ROWS):
            here = pl.ds(c * ROWS, ROWS)

            def send(x, back, rows, here=here):
                pb_s[here, :] = back.astype(BF16)

            chunk(at_rows((1 - t) * half + c * ROWS, ROWS), send)
            copy = remote(pb_s.at[here], pb_r.at[here], d_sems.at[0, c], d_sems.at[1, c], other)
            copy.start()
            copies.append(copy)
            ps_s[here, :] = nn(hid[at_rows((1 - t) * half + c * ROWS, ROWS), :hidden], ddw[...]).astype(BF16)
        for c in range(half // ROWS):
            here = pl.ds(c * ROWS, ROWS)

            def hold(x, back, rows, here=here):
                resid[here, :] = x
                own_s[here, :] = x + nn(hid[rows, :hidden], ddw[...])
                own_b[here, :] = back

            chunk(at_rows(t * half + c * ROWS, ROWS), hold)
        facc[:padded, :] = tn(bgs[...], h2s[...]).astype(BF16)
        facc[padded:2 * padded, :] = tn(bls[...], h2s[...]).astype(BF16)
        sum_a.step()
        total = jnp.zeros((8, width), F32)
        back_copies = []
        for c in range(half // ROWS):
            here = pl.ds(c * ROWS, ROWS)
            rows = at_rows(t * half + c * ROWS, ROWS)
            copies[c].wait()
            x = resid[here, :]
            factor = lax.rsqrt(jnp.mean(x * x, axis=-1, keepdims=True) + EPSILON)
            norm = x * factor
            back = own_b[here, :] + pb_r[here, :].astype(F32)
            inner = back * gain2[...]
            result = cs[rows, :].astype(F32) + factor * (inner - norm * jnp.mean(inner * norm, axis=-1, keepdims=True))
            br[here, :] = result
            low = result.astype(BF16)
            bf[here, :] = low
            bms_s[here, :] = nt(low, ops[1 - t]).astype(BF16)
            copy = remote(bms_s.at[here], bms.at[rows], d_sems.at[0, 2 + c], d_sems.at[1, 2 + c], other)
            copy.start()
            back_copies.append(copy)
            bms[rows, :] = nt(low, ops[t]).astype(BF16)
            total = total + jnp.sum((back * norm).reshape(ROWS // 8, 8, width), axis=0)
            if c == 0:
                sum_a.step()
        dgain[...] = total
        second_copy(0).start()
        facc[2 * padded:, :] = tn(hid[...], cs[...]).astype(BF16)
        mine = at_rows(t * half, half)
        gout[...] = tn(ms[t, mine, :], bf[...])
        gother[...] = tn(ms[1 - t, mine, :], bf[...]).astype(BF16)
        second_copy(1).start()
        for copy in back_copies:
            copy.wait()
        for b in range(nblocks):
            rows = pl.ds(b * ROWS, ROWS)
            got = nn(g[rows, :], bms[...]).astype(BF16)
            for p in range(pairs):
                bmp[p, rows, :] = got[:, p * PAIR:(p + 1) * PAIR]

    half16 = pltpu.VMEM((half, width), BF16)
    hiddens = pltpu.VMEM((count, padded), BF16)
    pl.run_scoped(
        dense_part, pltpu.VMEM((2, count, wide), BF16), hiddens, hiddens, hiddens, pltpu.VMEM((half, wide), BF16),
        pltpu.VMEM((half, width), F32), pltpu.VMEM((half, width), F32),
    )

    def backward(dqt, dks, dvs, mq, dd, dpk, dpv, dfirst, dsecond, dv, dg, bx):
        lo, part_s, dq, dk = sent_c.at[0], ps_s, mx.at[0], mx.at[1]
        da_s, dc_s, dsa_s, dsc_s = a_s, c_s, sa_s, sc_s
        ones = [jnp.where(lanes_of(i, 8), 1.0, 0.0).astype(BF16) for i in range(2)]
        for b in range(nblocks):
            rows = pl.ds(b * ROWS, ROWS)
            for p in range(pairs):
                gr = bmp[p, rows, :].astype(F32)
                inner = (gr * atth[p, rows, :].astype(F32)).astype(BF16)
                for i in range(2):
                    dd[2 * p + i, :, rows] = nt(ones[i], inner)[:1]
                gv = gate[p, rows, :]
                dg[rows, p * PAIR:(p + 1) * PAIR] = (gr * recall[p, rows, :] * gv * (1.0 - gv)).astype(BF16)
        for ref in (dpk, dpv, dfirst, dsecond, dks, dvs, da_s, dc_s, dsa_s, dsc_s):
            ref[...] = jnp.zeros_like(ref)

        def memory_step(n):
            rows = pl.ds(pl.multiple_of(n * STRETCH, STRETCH), STRETCH)
            fresh = starts[n] > 0
            for p in range(pairs):
                th = [rates[0, 2 * p + i, n] * (-1.0 / STRETCH) for i in range(2)]
                eta = [rates[1, 2 * p + i, n] for i in range(2)]
                al = [1.0 - rates[2, 2 * p + i, n] for i in range(2)]
                da, dc = da_s[p], dc_s[p]
                dsa = dsa_s[p] + da
                dsc = dsc_s[p] + dc
                dga = scaled(dsa, th).astype(BF16)
                dgc = scaled(dsc, th).astype(BF16)
                ab, cb = a_all[n, p], c_all[n, p]
                km, qm = both(k[p, rows, :]), both(q[p, rows, :])
                em = both(e_all[p, rows, :])
                pre = pre_all[n, p]
                sig = sigmoid(pre)
                act = pre * sig
                actb = act.astype(BF16)
                slope = sig + act * (1.0 - sig)
                sigk, prek, slopek = sig[PAIR:], pre[PAIR:], slope[PAIR:]
                u = u_all[n, p].astype(F32)
                curve = sigk * (1.0 - sigk) * (2.0 + prek * (1.0 - 2.0 * sigk))
                wgt = (u * slopek).astype(BF16)
                rm = both((bmp[p, rows, :].astype(F32) * gate[p, rows, :]).astype(BF16))
                dpre_q = (nn(rm, cb) * slope[:PAIR]).astype(BF16)
                mq[p, rows, :] = joined(nt(dpre_q, ab))
                dw = nn(km, dga)
                du = (dw * slopek).astype(BF16)
                de = joined(nt(jnp.concatenate([actb[PAIR:], du], axis=1), jnp.concatenate([dgc, cb], axis=1)))
                dvs[p, rows, :] = dvs[p, rows, :] - de
                dem = both(de.astype(BF16))
                dsk = nn(jnp.concatenate([em, dem], axis=1), jnp.concatenate([dgc, cb], axis=0))
                dpre = (dsk * slopek + dw * u * curve).astype(BF16)
                dks[p, rows, :] = dks[p, rows, :] + joined(nt(jnp.concatenate([wgt, dpre], axis=1), jnp.concatenate([dga, ab], axis=1)))
                ga = tn(jnp.concatenate([km, qm], axis=0), jnp.concatenate([dpre, dpre_q], axis=0))
                gc = tn(jnp.concatenate([em, dem], axis=0), jnp.concatenate([du, actb[PAIR:]], axis=0))
                gc = gc + tn(rm, actb[:PAIR])
                da = scaled(da, al) + ga
                dc = scaled(dc, al) + gc
                dfirst[p] = dfirst[p] + jnp.where(fresh, da, 0.0)
                dsecond[p] = dsecond[p] + jnp.where(fresh, dc, 0.0)
                da_s[p] = jnp.where(fresh, 0.0, da)
                dc_s[p] = jnp.where(fresh, 0.0, dc)
                dsa_s[p] = jnp.where(fresh, 0.0, scaled(dsa, eta))
                dsc_s[p] = jnp.where(fresh, 0.0, scaled(dsc, eta))

        def attention_unit(qb, head):
            p, side = head // 2, head % 2
            rows = pl.ds(qb * ROWS, ROWS)
            qh = keep(q[p, rows, :], side) * jnp.asarray(scale, BF16)
            gh = keep(bmp[p, rows, :], side)
            lrow, drow = lse[head, :, rows], dd[head, :, rows]
            acc = jnp.zeros((HEAD_DIM, ROWS), F32)
            for kb in range(qb + 1):
                krows = slice(kb * ROWS, (kb + 1) * ROWS)
                s = nt(k[p, krows, :], qh) - lrow
                s = s + diagonal[...] if kb == qb else earlier(s, starts, kb, qb, per)
                prob = jnp.exp(s)
                ds = (prob * (nt(v[p, krows, :], gh) - drow)).astype(BF16)
                dvs[p, krows, :] = dvs[p, krows, :] + nn(prob.astype(BF16), gh)
                dks[p, krows, :] = dks[p, krows, :] + nn(ds, qh)
                acc = acc + nn(kt[head, :, krows], ds)
            prob = jnp.exp(nt(pk[p], qh) - lrow)
            ds = (prob * (nt(pv[p], gh) - drow)).astype(BF16)
            dpv[p] = dpv[p] + nn(prob.astype(BF16), gh)
            dpk[p] = dpk[p] + nn(ds, qh)
            acc = acc + nn(pkt[head], ds)
            dqt[head, :, rows] = acc * scale

        def fold(ref, begin, value):
            rows = value.shape[0] // 2
            ref[begin:begin + rows, :wide] = value[:rows].astype(BF16)
            ref[begin:begin + rows, wide:] = value[rows:].astype(BF16)

        src_b[:rest, :] = facc[rows_a:, :]
        fold(src_b, rest, tn(h1[...], dg[...]))

        def background(point):
            if point in (1, 3, 5, 7):
                sum_a.step()
            if point == 2:
                second_copy(0).wait()
                lo[...] = (own_s[...] + second_r[...].astype(F32)).astype(BF16)
                spread(rec_l, dp, t, t, lo, l_sems, ALL_PEERS)
            if point == 3:
                second_copy(1).wait()
                src_b[rest + wide:, :] = (gout[...] + gother_r[...].astype(F32)).astype(BF16)
            if point in (3, 4, 7):
                sum_b.step()
            if point == 6:
                pass_on(rec_l, dp, t, lo, l_sems, ly_sems)

        for qb in reversed(range(nblocks)):
            fill_diagonal(diagonal, starts[qb * per])

            def run(i, _, qb=qb):
                memory_step(qb * per + per - 1 - i)
                attention_unit(qb, i)
                return 0

            for part in range(2):
                background((nblocks - 1 - qb) * 2 + part)
                lax.fori_loop(part * per // 2, (part + 1) * per // 2, run, 0)
        for b in range(nblocks):
            rows = pl.ds(b * ROWS, ROWS)
            for p in range(pairs):
                cols = slice(p * PAIR, (p + 1) * PAIR)
                got = jnp.concatenate([dqt[2 * p, :, rows], dqt[2 * p + 1, :, rows]], axis=0)
                dq[rows, cols] = (jnp.transpose(got) + mq[p, rows, :]).astype(BF16)
                dk[rows, cols] = dks[p, rows, :].astype(BF16)
                dv[rows, cols] = dvs[p, rows, :].astype(BF16)
        made = tn(h1[...], jnp.concatenate([dq[...], dk[...], dv[...]], axis=1))
        for i in range(3):
            fold(src_c, i * wide, made[:, i * wide:(i + 1) * wide])
        at = 3 * wide
        src_c[at + PAIR:, :] = jnp.zeros((src_c.shape[0] - at - PAIR, width), BF16)
        for i in range(4):
            lanes = slice(i * PAIR, (i + 1) * PAIR)
            src_c[at:at + PAIR, lanes] = (dfirst, dsecond)[i // 2][i % 2].astype(BF16)
            src_c[at + PAIR:at + PAIR + few, lanes] = (dpk, dpv)[i // 2][i % 2].astype(BF16)

        def step_c():
            sum_c1.step()
            sum_c2.step()

        step_c()

        for b in range(nblocks):
            rows = pl.ds(b * ROWS, ROWS)
            result = nt(dq[rows, :], wq[...])
            for back, w in ((dk, wk), (dv, wv), (dg, wg)):
                result = result + nt(back[rows, :], w[...])
            facc[rows, :] = result.astype(BF16)

        def partial(rows):
            return nn(gt[rows, :], facc[:count, :])

        column = lax.div(dp, 2) % 2
        quarter = half // 4
        places = []
        for b0, b1 in ((0, 0), (0, 1), (1, 0), (1, 1)):
            c, x = core + b0 * (1 - 2 * core), column + b1 * (1 - 2 * column)
            places.append(c * (2 * quarter) + x * quarter)

        def part_copy(i):
            here = at_rows(places[i], quarter)
            return remote(part_s.at[here], part_r.at[here], y_sems.at[0, 2 + i], y_sems.at[1, 2 + i], other)

        for i, begin in enumerate(places):
            part_s[at_rows(begin, quarter), :] = partial(at_rows((1 - t) * half + begin, quarter)).astype(BF16)
            part_copy(i).start()
            if i == 1:
                sum_a.step()
        step_c()
        owns = [partial(at_rows(t * half + begin, quarter)) for begin in places]
        sum_b.step()
        asks = asked[:, 0, :]
        asks_high = jnp.floor(asks * (1.0 / 32.0))
        asks_low = asks - 32.0 * asks_high
        slot = iota(PAIR, count, 1)
        rank = lax.div(slot, half) * HALF_SHARE + slot % HALF_SHARE
        pick = jnp.where(iota(PAIR, count, 0) == rank, 1.0, 0.0).astype(BF16)
        slot = iota(PEERS, count, 1)
        mine = lot(iota(PEERS, count, 0)) == lax.div(slot % half, HALF_SHARE)
        spread_out = 32.0 * nn(asks_high.astype(BF16), pick) + nn(asks_low.astype(BF16), pick)
        row = jnp.sum(jnp.where(mine, spread_out, 0.0), axis=0, keepdims=True)
        for c in range(count // ROWS):
            g[c * ROWS:(c + 1) * ROWS, :] = jnp.where((iota(ROWS, count, 0) + c * ROWS).astype(F32) == row, 1.0, 0.0).astype(BF16)
        passed_on(rec_l, dp, t, ly_sems)
        cs[...] = nn(g[...], rec_l[...]).astype(BF16)
        mgain = jnp.zeros((8, width), F32)
        for i, begin in enumerate(places):
            here, rows = at_rows(begin, quarter), at_rows(t * half + begin, quarter)
            part_copy(i).wait()
            back = owns[i] + part_r[here, :].astype(F32)
            x = xs[rows, :].astype(F32)
            factor = lax.rsqrt(jnp.mean(x * x, axis=-1, keepdims=True) + EPSILON)
            norm = x * factor
            inner = back * gain1[...]
            bx[here, :] = (br[here, :] + factor * (inner - norm * jnp.mean(inner * norm, axis=-1, keepdims=True))).astype(BF16)
            mgain = mgain + jnp.sum((back * norm).reshape(quarter // 8, 8, width), axis=0)
            spread(rec_x, dp, t, t, bx, x_sems, QUARTERS[i])
            if i == 1:
                step_c()
        gains_s[0, 0] = mgain
        gains_s[0, 1] = dgain[...]
        c2 = lax.div(dp, 4)
        groups = [[other], [(flipped(dp, 1), t)], [(flipped(dp, 2), t)], [(dp + 4 * ((c2 + i) % 4 - c2), t) for i in (1, 2, 3)]]
        gain_copies = []

        def gain_step(i):
            if i:
                for copy in gain_copies:
                    copy.wait()
                gain_copies.clear()
                value = gains_s[i - 1]
                for j in range(len(groups[i - 1])):
                    value = value + gains_r[i - 1 + j]
                gains_s[i] = value
            if i < 4:
                for j, peer in enumerate(groups[i]):
                    copy = remote(gains_s.at[i], gains_r.at[i + j], g_sems.at[0, i, j], g_sems.at[1, i, j], peer)
                    copy.start()
                    gain_copies.append(copy)

        writes = [pltpu.make_async_copy(src, dst, o_sems.at[i]) for i, (src, dst) in enumerate((
            (cs, ret.at[0]), (xs, ret.at[1]), (gains_s.at[4], gains_out), (out_a, fa_out), (out_b, fb_out), (out_c1, qa_out), (out_c2, qb_out),
        ))]
        writes[0].start()
        gain_step(0)
        sum_b.step()
        sum_a.step()
        step_c()
        gain_step(1)
        pass_on(rec_x, dp, t, bx, x_sems, xy_sems)
        gain_step(2)
        mine_rows, other_rows = at_rows(t * half, half), at_rows((1 - t) * half, half)
        mine_part = nn(g[:, mine_rows], rec_x[mine_rows, :])
        step_c()
        sum_b.step()
        sum_a.step()
        writes[3].start()
        gain_step(3)
        passed_on(rec_x, dp, t, xy_sems)
        xs[...] = (mine_part + nn(g[:, other_rows], rec_x[other_rows, :])).astype(BF16)
        writes[1].start()
        gain_step(4)
        writes[2].start()
        step_c()
        sum_b.step()
        writes[4].start()
        step_c()
        writes[5].start()
        writes[6].start()
        for write in writes:
            write.wait()

    flat = pltpu.VMEM((pairs, count, PAIR), F32)
    state = pltpu.VMEM((pairs, PAIR, PAIR), F32)
    tall = pltpu.VMEM((count, wide), BF16)
    pl.run_scoped(
        backward, pltpu.VMEM((heads, HEAD_DIM, count), F32), flat, flat, flat, pltpu.VMEM((heads, 1, count), F32),
        pltpu.VMEM((pairs, few, PAIR), F32), pltpu.VMEM((pairs, few, PAIR), F32), state, state,
        tall, tall, half16,
    )


def mega(starts, rates, idx, tokens, cotangent, gain1, wq, wk, wv, wg, op, pk, pv, first, second, gain2, dg, dl, dd):
    count, width = tokens.shape
    half = count // 2
    wide = wq.shape[1]
    pairs = wide // PAIR
    heads = 2 * pairs
    few = pk.shape[0]
    steps = starts.shape[0]
    padded = -(-dg.shape[0] // 256) * 256
    rows_a = 2 * padded
    rows_b = padded + 2 * wide
    rows_c = 3 * wide
    rows_d = -(-(PAIR + few) // 256) * 256
    low = lambda *dims: pltpu.VMEM(dims, BF16)
    full = lambda *dims: pltpu.VMEM(dims, F32)
    sems = pltpu.SemaphoreType.DMA((2, PEERS))
    dma = pltpu.SemaphoreType.DMA
    square = low(count, count)
    state = full(pairs, PAIR, PAIR)
    args = (starts, rates, idx, tokens, cotangent, gain1, wq, wk, wv, wg, op, pk, pv, first, second, gain2, dg, dl, dd)
    return pl.pallas_call(
        mega_kernel,
        out_shape=(
            shape(rows_a, width, dtype=BF16), shape(rows_b, width, dtype=BF16), shape(rows_c, width, dtype=BF16), shape(rows_d, width, dtype=BF16),
            shape(2, 8, width), shape(2, count, width, dtype=BF16),
        ),
        in_specs=[ANY if n in (3, 4, 6, 7, 8, 9, 10, 16, 17, 18) else SMEM if n < 2 else VMEM for n in range(len(args))],
        out_specs=[ANY] * 6,
        scratch_shapes=[
            low(count, width), low(count, width), low(2, count, wide), low(2, *op.shape), full(PEERS, 8, PAIR), full(PEERS, 8, PAIR),
            low(2, half, width), square, square, low(count, width), low(pairs, count, PAIR), low(pairs, count, PAIR), low(pairs, count, PAIR),
            full(pairs, count, PAIR), full(pairs, count, PAIR), low(heads, HEAD_DIM, count), full(heads, 1, count),
            low(steps, pairs, PAIR, PAIR), low(steps, pairs, PAIR, PAIR), full(steps, pairs, 2 * PAIR, PAIR), low(pairs, count, PAIR),
            low(steps, pairs, PAIR, PAIR), low(pairs, count, PAIR),
            low(pairs, few, PAIR), low(pairs, few, PAIR), low(heads, HEAD_DIM, few), low(heads, HEAD_DIM, few), low(pairs, count, PAIR),
            full(ROWS, ROWS), full(half, width), full(half, width), low(half, width), low(half, width), low(count, wide),
            low(3 * padded, width), full(wide, width), low(wide, width), full(8, width),
            low(half, width), low(wide, width), low(count, width), low(count, width), low(half, width),
            low(rows_b, width), low(rows_c + rows_d, width), low(rows_a, width), low(rows_b, width), low(rows_c, width), low(rows_d, width),
            full(5, 2, 8, width), full(6, 2, 8, width),
            state, state, state, state, *[low(*weight.shape) for weight in (wq, wk, wv, wg, op, dg, dl, dd)],
            dma((10,)), sems, sems, sems, dma((2, 2, PEERS)), dma((2, 8)), dma((2, 4)), dma((2, 6)), sems, sems, sems, sems, dma((2, 4, 3)), dma((7,)),
            *Sum.scratch(rows_a, width, SUM_ORDERS[0]), *Sum.scratch(rows_b, width, SUM_ORDERS[1]),
            *Sum.scratch(rows_c, width, SUM_ORDERS[2]), *Sum.scratch(rows_d, width, SUM_ORDERS[3]),
        ],
        compiler_params=pltpu.CompilerParams(collective_id=0, has_side_effects=True, vmem_limit_bytes=62 * 1024 * 1024),
        name="block",
    )(*args)


def finish_kernel(
    fa, fb, qa, qb, gains, ret, lo, bx, mgain, gq, gk, gv, gg, gout, gpk, gpv, first, second, dgain, ggate, glift, gdown,
    fa_s, fb_s, qa_s, qb_s, ret_s, wide_s, tall_s, out_s, state_s, in_sems, out_sems,
):
    hidden, width = ggate.shape
    wide = gq.shape[1]
    few = gpk.shape[0]
    padded = -(-hidden // 256) * 256
    moves = []
    reads = [
        pltpu.make_async_copy(src, dst, in_sems.at[i])
        for i, (src, dst) in enumerate(((fa, fa_s), (fb, fb_s), (ret, ret_s), (qa, qa_s), (qb, qb_s)))
    ]
    for copy in reads:
        copy.start()

    def send(src, dst):
        moves.append(pltpu.make_async_copy(src, dst, out_sems.at[len(moves)]))
        moves[-1].start()

    def square(n, src, begin, ref):
        rows = src[begin:begin + wide, :].astype(F32)
        tall_s[n, :wide, :] = rows[:, :wide]
        tall_s[n, wide:, :] = rows[:, wide:]
        send(tall_s.at[n], ref)

    mgain[...] = jnp.sum(gains[0], axis=0, keepdims=True)
    dgain[...] = jnp.sum(gains[1], axis=0, keepdims=True)
    reads[0].wait()
    for n, ref in enumerate((ggate, glift)):
        wide_s[n] = fa_s[n * padded:n * padded + hidden, :].astype(F32)
        send(wide_s.at[n], ref)
    reads[1].wait()
    wide_s[2] = fb_s[:hidden, :].astype(F32)
    send(wide_s.at[2], gdown)
    square(3, fb_s, padded, gg)
    out_s[...] = fb_s[padded + wide:, :].astype(F32)
    send(out_s, gout)
    reads[2].wait()
    send(ret_s.at[0], lo)
    send(ret_s.at[1], bx)
    reads[3].wait()
    for n, ref in enumerate((gq, gk, gv)):
        square(n, qa_s, n * wide, ref)
    reads[4].wait()
    for n in range(4):
        lanes = slice(n * PAIR, (n + 1) * PAIR)
        state_s[n] = qb_s[:PAIR, lanes].astype(F32)
        (gpk, gpv)[n // 2][:, (n % 2) * PAIR:(n % 2 + 1) * PAIR] = qb_s[PAIR:PAIR + few, lanes].astype(F32)
    send(state_s.at[:2], first)
    send(state_s.at[2:], second)
    for copy in moves:
        copy.wait()


def finish(fa, fb, qa, qb, gains, ret, hidden, wide, few):
    count, width = ret.shape[1:]
    pairs = wide // PAIR
    rows = shape(count, width, dtype=BF16)
    square = shape(width, wide)
    state = shape(pairs, PAIR, PAIR)
    outs = (
        rows, rows, shape(1, width), square, square, square, square, shape(wide, width), shape(few, wide), shape(few, wide),
        state, state, shape(1, width), shape(hidden, width), shape(hidden, width), shape(hidden, width),
    )
    small = (2, 8, 9, 12)
    return pl.pallas_call(
        finish_kernel,
        out_shape=outs,
        in_specs=[ANY] * 4 + [VMEM, ANY],
        out_specs=[VMEM if n in small else ANY for n in range(len(outs))],
        scratch_shapes=[
            pltpu.VMEM(fa.shape, BF16), pltpu.VMEM(fb.shape, BF16), pltpu.VMEM(qa.shape, BF16), pltpu.VMEM(qb.shape, BF16), pltpu.VMEM(ret.shape, BF16),
            pltpu.VMEM((3, hidden, width), F32), pltpu.VMEM((4, width, wide), F32), pltpu.VMEM((wide, width), F32),
            pltpu.VMEM((4, PAIR, PAIR), F32), pltpu.SemaphoreType.DMA((5,)), pltpu.SemaphoreType.DMA((12,)),
        ],
        compiler_params=pltpu.CompilerParams(vmem_limit_bytes=LIMIT),
        name="finish",
    )(fa, fb, qa, qb, gains, ret)


def block_body(
    tokens, cotangent, source_index, tract_starts, memory_rates, mixer_gain, query_proj, key_proj, value_proj, gate_proj,
    out_proj, persist_keys, persist_values, memory_first, memory_second, dense_gain, dense_gate, dense_lift, dense_down,
):
    pairs = query_proj.shape[1] // PAIR
    first = memory_first.reshape(pairs, PAIR, PAIR)
    second = memory_second.transpose(0, 2, 1).reshape(pairs, PAIR, PAIR)
    summed = mega(
        tract_starts, memory_rates.transpose(0, 2, 1), source_index.reshape(1, -1), tokens, cotangent, mixer_gain[None],
        query_proj, key_proj, value_proj, gate_proj, out_proj, persist_keys, persist_values, first, second,
        dense_gain[None], dense_gate.T, dense_lift.T, dense_down,
    )
    outs = list(finish(*summed, dense_gate.shape[1], query_proj.shape[1], persist_keys.shape[0]))
    outs[2] = outs[2][0]
    outs[10] = outs[10].reshape(memory_first.shape)
    outs[11] = outs[11].reshape(memory_first.shape).transpose(0, 2, 1)
    outs[12] = outs[12][0]
    outs[13], outs[14] = outs[13].T, outs[14].T
    return tuple(outs)


def body(
    tokens,
    cotangent,
    source_index,
    tract_starts,
    memory_rates,
    mixer_gain,
    query_proj,
    key_proj,
    value_proj,
    gate_proj,
    out_proj,
    persist_keys,
    persist_values,
    memory_first,
    memory_second,
    dense_gain,
    dense_gate,
    dense_lift,
    dense_down,
):
    count = tokens.shape[0]
    width = tokens.shape[1]
    peers = lax.axis_size("dp")
    share = count // peers
    arrival = jnp.argsort(source_index)
    wanted = (source_index[arrival] % count).reshape(peers, share)
    asked = lax.all_to_all(wanted, "dp", split_axis=0, concat_axis=0, tiled=True).reshape(count)
    got_tokens, got_cot = (
        lax.all_to_all(
            tokens[asked].reshape(peers, share, width),
            "dp",
            split_axis=0,
            concat_axis=0,
            tiled=True,
        ),
        lax.all_to_all(
            cotangent[asked].reshape(peers, share, width),
            "dp",
            split_axis=0,
            concat_axis=0,
            tiled=True,
        ),
    )
    placing = jnp.argsort(arrival)
    seq_tokens = got_tokens.reshape(count, width)[placing]
    seq_cot = got_cot.reshape(count, width)[placing]
    seq_x = seq_tokens.astype(jnp.float32)
    first_norm, factor_one = norm_forward(seq_x)
    pairs = query_proj.shape[1] // PAIR
    by_pair = lambda value: value.reshape(-1, pairs, PAIR).transpose(1, 0, 2)
    by_head = lambda value: value.T.reshape(2 * pairs, HEAD_DIM, -1)
    weights = jnp.concatenate([query_proj, key_proj, value_proj, gate_proj], axis=1)
    pk, pv = by_pair(persist_keys), by_pair(persist_values)
    first = memory_first.reshape(pairs, PAIR, PAIR)
    second = memory_second.transpose(0, 2, 1).reshape(pairs, PAIR, PAIR)
    h_one, query, keys, values, gate, recall, mixed, keys_t, lse, a_all, c_all, pre_all, e_all, u_all, attended = mixer_forward(
        tract_starts, memory_rates, seq_tokens, mixer_gain[None], weights, pk, by_head(persist_values), first, second
    )
    first_out = lax.psum(product(mixed, out_proj), "tensor")
    resid = seq_x + first_out
    norm_two, factor_two = norm_forward(resid)
    h_two = (norm_two * dense_gain).astype(jnp.bfloat16)
    gated = product(h_two, dense_gate)
    lifted = product(h_two, dense_lift)
    sigma = jax.nn.sigmoid(gated)
    active = gated * sigma
    hidden = (active * lifted).astype(jnp.bfloat16)
    second_out = lax.psum(product(hidden, dense_down).astype(jnp.bfloat16), "tensor").astype(
        jnp.float32
    )
    seq_out = (resid + second_out).astype(jnp.bfloat16)
    grad_down = product(hidden.T, seq_cot)
    back_hidden = product(seq_cot, dense_down.T)
    back_gated = (back_hidden * lifted * (sigma + gated * sigma * (1.0 - sigma))).astype(
        jnp.bfloat16
    )
    back_lifted = (back_hidden * active).astype(jnp.bfloat16)
    grad_gate = product(h_two.T, back_gated)
    grad_lift = product(h_two.T, back_lifted)
    back_two = lax.psum(
        product(back_gated, dense_gate.T) + product(back_lifted, dense_lift.T), "tensor"
    )
    back_norm_two, grad_dgain = norm_backward(back_two, norm_two, factor_two, dense_gain)
    residual_gradient = seq_cot.astype(jnp.float32) + back_norm_two
    back_first = residual_gradient.astype(jnp.bfloat16)
    grad_out = product(mixed.T, back_first)
    back_mixed = product(back_first, out_proj.T).astype(jnp.bfloat16)
    back_query, back_keys, cotangent_payloads, back_gate, grad_pk, grad_pv, grad_first, grad_second = mixer_backward(
        tract_starts, memory_rates, back_mixed, query, keys, values, gate, recall, keys_t, pk, by_head(persist_keys), pv,
        lse, a_all, c_all, pre_all, e_all, u_all, attended,
    )
    grad_first = grad_first.reshape(memory_first.shape)
    grad_second = grad_second.reshape(memory_first.shape).transpose(0, 2, 1)
    grad_query = product(h_one.T, back_query)
    grad_key = product(h_one.T, back_keys)
    grad_value = product(h_one.T, cotangent_payloads)
    grad_gproj = product(h_one.T, back_gate)
    back_one = lax.psum(
        product(back_query, query_proj.T)
        + product(back_keys, key_proj.T)
        + product(cotangent_payloads, value_proj.T)
        + product(back_gate, gate_proj.T),
        "tensor",
    )
    back_norm_one, grad_mgain = norm_backward(back_one, first_norm, factor_one, mixer_gain)
    back_x = (residual_gradient + back_norm_one).astype(jnp.bfloat16)
    grad_pkeys = grad_pk.transpose(1, 0, 2).reshape(persist_keys.shape)
    grad_pvalues = grad_pv.transpose(1, 0, 2).reshape(persist_values.shape)
    (
        grad_mgain,
        grad_query,
        grad_key,
        grad_value,
        grad_gproj,
        grad_out,
        grad_pkeys,
        grad_pvalues,
        grad_first,
        grad_second,
        grad_dgain,
        grad_gate,
        grad_lift,
        grad_down,
    ) = lax.psum(
        (
            grad_mgain,
            grad_query,
            grad_key,
            grad_value,
            grad_gproj,
            grad_out,
            grad_pkeys,
            grad_pvalues,
            grad_first,
            grad_second,
            grad_dgain,
            grad_gate,
            grad_lift,
            grad_down,
        ),
        "dp",
    )
    ret_out, ret_grad = (
        lax.all_to_all(
            seq_out[arrival].reshape(peers, share, width),
            "dp",
            split_axis=0,
            concat_axis=0,
            tiled=True,
        ),
        lax.all_to_all(
            back_x[arrival].reshape(peers, share, width),
            "dp",
            split_axis=0,
            concat_axis=0,
            tiled=True,
        ),
    )
    undo = jnp.argsort(asked)
    layer_output = ret_out.reshape(count, width)[undo]
    input_grad = ret_grad.reshape(count, width)[undo]
    return (
        layer_output,
        input_grad,
        grad_mgain,
        grad_query,
        grad_key,
        grad_value,
        grad_gproj,
        grad_out,
        grad_pkeys,
        grad_pvalues,
        grad_first,
        grad_second,
        grad_dgain,
        grad_gate,
        grad_lift,
        grad_down,
    )


def solution(mesh):
    chosen = block_body if mesh.shape["dp"] == PEERS else body
    in_specs = (
        P("dp", None),
        P("dp", None),
        P("dp"),
        P("dp"),
        P(None, "dp", "tensor"),
        P(),
        P(None, "tensor"),
        P(None, "tensor"),
        P(None, "tensor"),
        P(None, "tensor"),
        P("tensor", None),
        P(None, "tensor"),
        P(None, "tensor"),
        P("tensor", None, None),
        P("tensor", None, None),
        P(),
        P(None, "tensor"),
        P(None, "tensor"),
        P("tensor", None),
    )
    out_specs = (
        P("dp", None),
        P("dp", None),
        P(),
        P(None, "tensor"),
        P(None, "tensor"),
        P(None, "tensor"),
        P(None, "tensor"),
        P("tensor", None),
        P(None, "tensor"),
        P(None, "tensor"),
        P("tensor", None, None),
        P("tensor", None, None),
        P(),
        P(None, "tensor"),
        P(None, "tensor"),
        P("tensor", None),
    )
    return jax.shard_map(chosen, mesh=mesh, in_specs=in_specs, out_specs=out_specs, check_vma=False)
```

```python
import jax
import jax.numpy as jnp
from jax import lax
from jax.experimental import pallas as pl
from jax.experimental.pallas import tpu as pltpu
from jax.sharding import PartitionSpec as P

HEAD_DIM = 64


EPSILON = 1e-06
MASKED = -1e30


def product(left, right):
    return jnp.dot(left, right, preferred_element_type=jnp.float32)


def norm_forward(value):
    factor = lax.rsqrt(jnp.mean(value * value, axis=-1, keepdims=True) + EPSILON)
    return (value * factor, factor)


def norm_backward(grad, normed, factor, gain):
    inner = grad * gain
    back = factor * (inner - normed * jnp.mean(inner * normed, axis=-1, keepdims=True))
    return (back, jnp.sum(grad * normed, axis=0))


F32, BF16 = jnp.float32, jnp.bfloat16
PAIR = 2 * HEAD_DIM
ROWS = 256
STRETCH = 64


def nn(a, b):
    return lax.dot_general(a, b, (((1,), (0,)), ((), ())), preferred_element_type=F32)


def nt(a, b):
    return lax.dot_general(a, b, (((1,), (1,)), ((), ())), preferred_element_type=F32)


def tn(a, b):
    return lax.dot_general(a, b, (((0,), (0,)), ((), ())), preferred_element_type=F32)


def sigmoid(v):
    return 1.0 / (1.0 + jnp.exp(-v))


def lanes_of(half, rows=1):
    return (lax.broadcasted_iota(jnp.int32, (rows, PAIR), 1) // HEAD_DIM) == half


def keep(value, half):
    return jnp.where(lanes_of(half), value, jnp.zeros_like(value))


def both(value):
    return jnp.concatenate([keep(value, 0), keep(value, 1)], axis=0)


def joined(stacked):
    rows = stacked.shape[0] // 2
    return jnp.where(lanes_of(0), stacked[:rows], stacked[rows:])


def scaled(pair, scalars):
    return jnp.concatenate([pair[:HEAD_DIM] * scalars[0], pair[HEAD_DIM:] * scalars[1]], axis=0)


def same_sequence(starts, early, late, per):
    count = jnp.int32(0)
    for c in range(early * per + 1, late * per + 1):
        count = count + starts[c]
    return count == 0


def earlier(s, starts, kb, qb, per):
    open_all = jnp.where(same_sequence(starts, kb, qb, per), 0.0, MASKED).astype(F32)
    open_head = jnp.where(starts[kb * per] > 0, MASKED, open_all).astype(F32)
    row = lax.broadcasted_iota(jnp.int32, (STRETCH, s.shape[1]), 0)
    top = s[:STRETCH] + jnp.where(row < STRETCH - 1, open_head, open_all)
    return jnp.concatenate([top, s[STRETCH:] + open_all], axis=0)


def fill_diagonal(ref, start):
    key = lax.broadcasted_iota(jnp.int32, ref.shape, 0)
    query = lax.broadcasted_iota(jnp.int32, ref.shape, 1)
    plain = jnp.where(key <= query, 0.0, MASKED)
    opening = jnp.where((key == query) | ((key < query) & (key >= STRETCH - 1)), 0.0, MASKED)
    ref[...] = jnp.where(start > 0, opening, plain).astype(F32)


def forward_kernel(
    starts, rates, tok, gain, w, pk, pvt, first, second,
    h1, q, k, v, gate, recall, mixed, kt, lse, a_all, c_all, pre_all, e_all, u_all, atth,
    vt, att, diagonal, a_s, c_s, sa_s, sc_s,
):
    count = tok.shape[0]
    pairs = first.shape[0]
    wide = pairs * PAIR
    per = ROWS // STRETCH

    def project(b, _):
        rows = pl.ds(pl.multiple_of(b * ROWS, ROWS), ROWS)
        x = tok[rows, :].astype(F32)
        factor = lax.rsqrt(jnp.mean(x * x, axis=-1, keepdims=True) + EPSILON)
        h = (x * factor * gain[...]).astype(BF16)
        h1[rows, :] = h
        for part, ref in ((0, q), (1, k), (2, v)):
            made = nn(h, w[:, part * wide:(part + 1) * wide])
            low = made.astype(BF16)
            for p in range(pairs):
                ref[p, rows, :] = low[:, p * PAIR:(p + 1) * PAIR]
            if part > 0:
                made_t = jnp.transpose(made).astype(BF16)
                target = kt if part == 1 else vt
                for h_i in range(2 * pairs):
                    target[h_i, :, rows] = made_t[h_i * HEAD_DIM:(h_i + 1) * HEAD_DIM]
        g = sigmoid(nn(h, w[:, 3 * wide:]))
        for p in range(pairs):
            gate[p, rows, :] = g[:, p * PAIR:(p + 1) * PAIR]
        return 0

    lax.fori_loop(0, count // ROWS, project, 0)
    a_s[...] = first[...]
    c_s[...] = second[...]
    sa_s[...] = jnp.zeros_like(sa_s)
    sc_s[...] = jnp.zeros_like(sc_s)

    def memory_step(t):
        rows = pl.ds(pl.multiple_of(t * STRETCH, STRETCH), STRETCH)
        fresh = starts[t] > 0
        for p in range(pairs):
            a = jnp.where(fresh, first[p], a_s[p])
            c = jnp.where(fresh, second[p], c_s[p])
            sa = jnp.where(fresh, 0.0, sa_s[p])
            sc = jnp.where(fresh, 0.0, sc_s[p])
            ab, cb = a.astype(BF16), c.astype(BF16)
            a_all[t, p] = ab
            c_all[t, p] = cb
            km = both(k[p, rows, :])
            lhs = jnp.concatenate([both(q[p, rows, :]), km], axis=0)
            pre = nn(lhs, ab)
            pre_all[t, p] = pre
            sig = sigmoid(pre)
            act = pre * sig
            actb = act.astype(BF16)
            out = nt(actb, cb)
            recall[p, rows, :] = joined(out[:PAIR])
            e = joined(out[PAIR:]) - v[p, rows, :].astype(F32)
            eb = e.astype(BF16)
            e_all[p, rows, :] = eb
            em = both(eb)
            u = nn(em, cb)
            u_all[t, p] = u
            sigk, actk = sig[PAIR:], act[PAIR:]
            wgt = (u * (sigk + actk * (1.0 - sigk))).astype(BF16)
            ga = tn(km, wgt)
            gc = tn(em, actb[PAIR:])
            th = [rates[0, t, 2 * p + i] * (1.0 / STRETCH) for i in range(2)]
            eta = [rates[1, t, 2 * p + i] for i in range(2)]
            al = [1.0 - rates[2, t, 2 * p + i] for i in range(2)]
            sa = scaled(sa, eta) - scaled(ga, th)
            sc = scaled(sc, eta) - scaled(gc, th)
            sa_s[p] = sa
            sc_s[p] = sc
            a_s[p] = scaled(a, al) + sa
            c_s[p] = scaled(c, al) + sc

    def attention_unit(qb, head):
        p, half = head // 2, head % 2
        rows = pl.ds(qb * ROWS, ROWS)
        qh = keep(q[p, rows, :], half) * jnp.asarray(HEAD_DIM ** -0.5, BF16)
        scores = []
        for kb in range(qb + 1):
            s = nt(k[p, kb * ROWS:(kb + 1) * ROWS, :], qh)
            if kb == qb:
                s = s + diagonal[...]
            else:
                s = earlier(s, starts, kb, qb, per)
            scores.append(s)
        sp = nt(pk[p], qh)
        peak = jnp.max(sp, axis=0, keepdims=True)
        for s in scores:
            peak = jnp.maximum(peak, jnp.max(s, axis=0, keepdims=True))
        ep = jnp.exp(sp - peak)
        total = jnp.sum(ep, axis=0, keepdims=True)
        out = nn(pvt[head], ep.astype(BF16))
        for kb, s in enumerate(scores):
            e = jnp.exp(s - peak)
            total = total + jnp.sum(e, axis=0, keepdims=True)
            out = out + nn(vt[head, :, kb * ROWS:(kb + 1) * ROWS], e.astype(BF16))
        att[head, :, rows] = out * (1.0 / total)
        lse[head, :, rows] = peak + jnp.log(total)

    heads = 2 * pairs
    for qb in range(count // ROWS):
        fill_diagonal(diagonal, starts[qb * per])

        def run(i, _, qb=qb):
            memory_step(qb * per + i)
            attention_unit(qb, i)
            return 0
        lax.fori_loop(0, per, run, 0)
    for b in range(count // ROWS):
        rows = pl.ds(b * ROWS, ROWS)
        for p in range(pairs):
            got = jnp.concatenate([att[2 * p, :, rows], att[2 * p + 1, :, rows]], axis=0)
            wide_att = jnp.transpose(got)
            atth[p, rows, :] = wide_att
            mixed[rows, p * PAIR:(p + 1) * PAIR] = (wide_att + gate[p, rows, :] * recall[p, rows, :]).astype(BF16)


def backward_kernel(
    starts, rates, bm, q, k, v, gate, recall, kt, pk, pkt, pv, lse, a_all, c_all, pre_all, e_all, u_all, atth,
    dq, dk, dv, dg, dpk, dpv, dfirst, dsecond,
    dqt, dd, dks, dvs, mq, bmp, diagonal, da_s, dc_s, dsa_s, dsc_s,
):
    count = bm.shape[0]
    pairs = q.shape[0]
    heads = 2 * pairs
    per = ROWS // STRETCH
    nblocks = count // ROWS
    ones = [jnp.where(lanes_of(i, 8), 1.0, 0.0).astype(F32) for i in range(2)]
    for b in range(nblocks):
        rows = pl.ds(b * ROWS, ROWS)
        for p in range(pairs):
            gb = bm[rows, p * PAIR:(p + 1) * PAIR]
            bmp[p, rows, :] = gb
            g = gb.astype(F32)
            inner = g * atth[p, rows, :]
            for i in range(2):
                row = lax.dot_general(ones[i], inner, (((1,), (1,)), ((), ())), precision=lax.Precision.HIGHEST, preferred_element_type=F32)
                dd[2 * p + i, :, rows] = row[:1]
            gt = gate[p, rows, :]
            dg[rows, p * PAIR:(p + 1) * PAIR] = (g * recall[p, rows, :] * gt * (1.0 - gt)).astype(BF16)
    for ref in (dpk, dpv, dfirst, dsecond, dks, dvs, da_s, dc_s, dsa_s, dsc_s):
        ref[...] = jnp.zeros_like(ref)

    def memory_step(t):
        rows = pl.ds(pl.multiple_of(t * STRETCH, STRETCH), STRETCH)
        fresh = starts[t] > 0
        for p in range(pairs):
            th = [rates[0, t, 2 * p + i] * (-1.0 / STRETCH) for i in range(2)]
            eta = [rates[1, t, 2 * p + i] for i in range(2)]
            al = [1.0 - rates[2, t, 2 * p + i] for i in range(2)]
            da, dc = da_s[p], dc_s[p]
            dsa = dsa_s[p] + da
            dsc = dsc_s[p] + dc
            dga = scaled(dsa, th).astype(BF16)
            dgc = scaled(dsc, th).astype(BF16)
            ab, cb = a_all[t, p], c_all[t, p]
            km, qm = both(k[p, rows, :]), both(q[p, rows, :])
            em = both(e_all[p, rows, :])
            pre = pre_all[t, p]
            sig = sigmoid(pre)
            act = pre * sig
            actb = act.astype(BF16)
            slope = sig + act * (1.0 - sig)
            sigk, prek, slopek = sig[PAIR:], pre[PAIR:], slope[PAIR:]
            u = u_all[t, p]
            curve = sigk * (1.0 - sigk) * (2.0 + prek * (1.0 - 2.0 * sigk))
            wgt = (u * slopek).astype(BF16)
            back = bmp[p, rows, :].astype(F32) * gate[p, rows, :]
            rm = both(back.astype(BF16))
            dpre_q = (nn(rm, cb) * slope[:PAIR]).astype(BF16)
            mq[0, p, rows, :] = joined(nt(dpre_q, ab))
            dw = nn(km, dga)
            du = (dw * slopek).astype(BF16)
            cc = jnp.concatenate([dgc, cb], axis=1)
            de = joined(nt(jnp.concatenate([actb[PAIR:], du], axis=1), cc))
            mq[2, p, rows, :] = -de
            dem = both(de.astype(BF16))
            dsk = nn(jnp.concatenate([em, dem], axis=1), jnp.concatenate([dgc, cb], axis=0))
            dpre = (dsk * slopek + dw * u * curve).astype(BF16)
            mq[1, p, rows, :] = joined(nt(jnp.concatenate([wgt, dpre], axis=1), jnp.concatenate([dga, ab], axis=1)))
            ga = tn(jnp.concatenate([km, qm], axis=0), jnp.concatenate([dpre, dpre_q], axis=0))
            gc = tn(jnp.concatenate([em, dem], axis=0), jnp.concatenate([du, actb[PAIR:]], axis=0))
            gc = gc + tn(rm, actb[:PAIR])
            da = scaled(da, al) + ga
            dc = scaled(dc, al) + gc
            dfirst[p] = dfirst[p] + jnp.where(fresh, da, 0.0)
            dsecond[p] = dsecond[p] + jnp.where(fresh, dc, 0.0)
            da_s[p] = jnp.where(fresh, 0.0, da)
            dc_s[p] = jnp.where(fresh, 0.0, dc)
            dsa_s[p] = jnp.where(fresh, 0.0, scaled(dsa, eta))
            dsc_s[p] = jnp.where(fresh, 0.0, scaled(dsc, eta))

    def attention_unit(qb, head):
        p, half = head // 2, head % 2
        rows = pl.ds(qb * ROWS, ROWS)
        qh = keep(q[p, rows, :], half) * jnp.asarray(HEAD_DIM ** -0.5, BF16)
        gh = keep(bmp[p, rows, :], half)
        lrow, drow = lse[head, :, rows], dd[head, :, rows]
        acc = jnp.zeros((HEAD_DIM, ROWS), F32)
        for kb in range(qb + 1):
            krows = slice(kb * ROWS, (kb + 1) * ROWS)
            s = nt(k[p, krows, :], qh) - lrow
            if kb == qb:
                s = s + diagonal[...]
            else:
                s = earlier(s, starts, kb, qb, per)
            prob = jnp.exp(s)
            ds = (prob * (nt(v[p, krows, :], gh) - drow)).astype(BF16)
            dvs[p, krows, :] = dvs[p, krows, :] + nn(prob.astype(BF16), gh)
            dks[p, krows, :] = dks[p, krows, :] + nn(ds, qh)
            acc = acc + nn(kt[head, :, krows], ds)
        prob = jnp.exp(nt(pk[p], qh) - lrow)
        ds = (prob * (nt(pv[p], gh) - drow)).astype(BF16)
        dpv[p] = dpv[p] + nn(prob.astype(BF16), gh)
        dpk[p] = dpk[p] + nn(ds, qh)
        acc = acc + nn(pkt[head], ds)
        dqt[head, :, rows] = acc * (HEAD_DIM ** -0.5)

    for qb in reversed(range(nblocks)):
        fill_diagonal(diagonal, starts[qb * per])

        def run(i, _, qb=qb):
            memory_step(qb * per + per - 1 - i)
            attention_unit(qb, i)
            return 0
        lax.fori_loop(0, per, run, 0)
    for b in range(nblocks):
        rows = pl.ds(b * ROWS, ROWS)
        for p in range(pairs):
            cols = slice(p * PAIR, (p + 1) * PAIR)
            got = jnp.concatenate([dqt[2 * p, :, rows], dqt[2 * p + 1, :, rows]], axis=0)
            dq[rows, cols] = (jnp.transpose(got) + mq[0, p, rows, :]).astype(BF16)
            dk[rows, cols] = (dks[p, rows, :] + mq[1, p, rows, :]).astype(BF16)
            dv[rows, cols] = (dvs[p, rows, :] + mq[2, p, rows, :]).astype(BF16)


def shape(*dims, dtype=F32):
    return jax.ShapeDtypeStruct(dims, dtype)


VMEM = pl.BlockSpec(memory_space=pltpu.VMEM)
SMEM = pl.BlockSpec(memory_space=pltpu.SMEM)
LIMIT = 56 * 1024 * 1024


def mixer_forward(starts, rates, tok, gain, w, pk, pvt, first, second):
    count, width = tok.shape
    pairs = first.shape[0]
    heads, steps = 2 * pairs, starts.shape[0]
    flat = lambda dtype: shape(pairs, count, PAIR, dtype=dtype)
    outs = (
        shape(count, width, dtype=BF16), flat(BF16), flat(BF16), flat(BF16), flat(F32), flat(F32),
        shape(count, pairs * PAIR, dtype=BF16), shape(heads, HEAD_DIM, count, dtype=BF16), shape(heads, 1, count),
        shape(steps, pairs, PAIR, PAIR, dtype=BF16), shape(steps, pairs, PAIR, PAIR, dtype=BF16),
        shape(steps, pairs, 2 * PAIR, PAIR), flat(BF16), shape(steps, pairs, PAIR, PAIR), flat(F32),
    )
    state = pltpu.VMEM((pairs, PAIR, PAIR), F32)
    return pl.pallas_call(
        forward_kernel,
        out_shape=outs,
        in_specs=[SMEM, SMEM] + [VMEM] * 7,
        out_specs=[VMEM] * len(outs),
        scratch_shapes=[
            pltpu.VMEM((heads, HEAD_DIM, count), BF16), pltpu.VMEM((heads, HEAD_DIM, count), F32),
            pltpu.VMEM((ROWS, ROWS), F32), state, state, state, state,
        ],
        compiler_params=pltpu.CompilerParams(vmem_limit_bytes=LIMIT),
        name="mixer_forward",
    )(starts, rates, tok, gain, w, pk, pvt, first, second)


def mixer_backward(starts, rates, bm, q, k, v, gate, recall, kt, pk, pkt, pv, lse, a_all, c_all, pre_all, e_all, u_all, atth):
    count, wide = bm.shape
    pairs = q.shape[0]
    heads = 2 * pairs
    outs = (
        shape(count, wide, dtype=BF16), shape(count, wide, dtype=BF16), shape(count, wide, dtype=BF16), shape(count, wide, dtype=BF16),
        shape(*pk.shape), shape(*pv.shape), shape(pairs, PAIR, PAIR), shape(pairs, PAIR, PAIR),
    )
    state = pltpu.VMEM((pairs, PAIR, PAIR), F32)
    flat = pltpu.VMEM((pairs, count, PAIR), F32)
    return pl.pallas_call(
        backward_kernel,
        out_shape=outs,
        in_specs=[SMEM, SMEM] + [VMEM] * 17,
        out_specs=[VMEM] * len(outs),
        scratch_shapes=[
            pltpu.VMEM((heads, HEAD_DIM, count), F32), pltpu.VMEM((heads, 1, count), F32), flat, flat,
            pltpu.VMEM((3, pairs, count, PAIR), F32), pltpu.VMEM((pairs, count, PAIR), BF16),
            pltpu.VMEM((ROWS, ROWS), F32), state, state, state, state,
        ],
        compiler_params=pltpu.CompilerParams(vmem_limit_bytes=LIMIT),
        name="mixer_backward",
    )(starts, rates, bm, q, k, v, gate, recall, kt, pk, pkt, pv, lse, a_all, c_all, pre_all, e_all, u_all, atth)


MESH = pl.DeviceIdType.MESH
HALF_SHARE = 32
PEERS = 16


def place():
    return lax.axis_index("dp"), lax.axis_index("tensor")


def flipped(index, mask):
    result = index
    bit = 1
    while bit <= mask:
        if mask & bit:
            result = result + bit * (1 - 2 * (lax.div(index, bit) % 2))
        bit *= 2
    return result


def greet(devices):
    for device in devices:
        pl.semaphore_signal(pltpu.get_barrier_semaphore(), inc=1, device_id=device, device_id_type=MESH)


def greeted(devices):
    pl.semaphore_wait(pltpu.get_barrier_semaphore(), len(devices))


def remote(src, dst, send_sem, recv_sem, device):
    return pltpu.make_async_remote_copy(
        src_ref=src, dst_ref=dst, send_sem=send_sem, recv_sem=recv_sem, device_id=device, device_id_type=MESH
    )


def iota(rows, columns, dimension):
    return lax.broadcasted_iota(jnp.int32, (rows, columns), dimension)


def at_rows(start, size):
    return pl.ds(pl.multiple_of(start, size), size)


def lot(peer):
    return peer % 2 * (PEERS // 2) + lax.div(peer, 2) % 2 * (PEERS // 4) + lax.div(peer, 4)


QUARTERS = tuple(tuple(range(first, PEERS, 4)) for first in (0, 2, 1, 3))
ALL_PEERS = sum(QUARTERS, ())


def spreading(ref, dp, t, side, sent, sems, m):
    peer = flipped(dp, m)
    return remote(
        sent.at[at_rows(lot(peer) * HALF_SHARE, HALF_SHARE)], ref.at[at_rows(side * (PEERS * HALF_SHARE) + lot(dp) * HALF_SHARE, HALF_SHARE)],
        sems.at[0, m], sems.at[1, m], (peer, t),
    )


def spread(ref, dp, t, side, sent, sems, masks):
    for m in masks:
        if m:
            spreading(ref, dp, t, side, sent, sems, m).start()
        else:
            here = lot(dp) * HALF_SHARE
            ref[at_rows(side * (PEERS * HALF_SHARE) + here, HALF_SHARE), :] = sent[at_rows(here, HALF_SHARE), :]


def pass_on(ref, dp, t, sent, sems, y_sems):
    for m in ALL_PEERS:
        if m:
            spreading(ref, dp, t, t, sent, sems, m).wait()
        passing(ref, dp, t, m, y_sems).start()


def passing(ref, dp, t, m, sems):
    rows = at_rows(t * (PEERS * HALF_SHARE) + lot(flipped(dp, m)) * HALF_SHARE, HALF_SHARE)
    return remote(ref.at[rows], ref.at[rows], sems.at[0, m], sems.at[1, m], (dp, 1 - t))


def passed_on(ref, dp, t, sems):
    for m in range(PEERS):
        passing(ref, dp, t, m, sems).wait()


def weave(chains, filler, per_stage, between):
    chains = list(chains)
    end = object()
    while chains:
        live = []
        for i, chain in enumerate(chains):
            if next(chain, end) is not end:
                live.append(chain)
            if between:
                for _ in range((per_stage + i) // len(chains)):
                    next(filler, end)
        chains = live
        if not between:
            for _ in range(per_stage):
                next(filler, end)
    for _ in filler:
        pass


def sixteens(start, size):
    return pl.ds(pl.multiple_of(start, 16), size)


class Sum:
    def __init__(self, dp, t, src, base, out, order, scratch):
        self.dp, self.t, self.src, self.base, self.out, self.order = dp, t, src, base, out, order
        n = len(order)
        self.acc, self.sems = scratch[0], scratch[1]
        self.rcv = scratch[2:2 + n]
        self.snd = (None,) + tuple(scratch[2 + n:1 + 2 * n])
        self.at = [lax.div(dp, stride) % size for stride, size in order]
        self.rows = [out.shape[0]]
        self.start = [0]
        for (stride, size), c in zip(order, self.at):
            self.rows.append(self.rows[-1] // size)
            self.start.append(self.start[-1] + c * self.rows[-1])
        self.next = 0

    @staticmethod
    def scratch(rows, lanes, order):
        counts, sizes = [], [rows]
        for stride, size in order:
            sizes.append(sizes[-1] // size)
            counts.append(size - 1)
        blocks = [pltpu.VMEM((count, size, lanes), BF16) for count, size in zip(counts, sizes[1:])]
        return [pltpu.VMEM((sizes[1], lanes), BF16), pltpu.SemaphoreType.DMA((2, 2 * sum(counts)))] + blocks + blocks[1:]

    @staticmethod
    def refs(order):
        return 1 + 2 * len(order)

    def peer(self, s, k):
        stride, size = self.order[s]
        d = (self.at[s] + k) % size
        return d, self.dp + stride * (d - self.at[s])

    def copies(self, n):
        made = []
        stages = len(self.order)
        counts = [size - 1 for _, size in self.order]
        s = n if n < stages else 2 * stages - 1 - n
        for k in range(1, self.order[s][1]):
            d, peer = self.peer(s, k)
            if n >= stages:
                src = dst = self.out.at[sixteens(self.start[s + 1], self.rows[s + 1])]
            else:
                src = self.snd[s].at[k - 1] if s else self.src.at[sixteens(self.base + d * self.rows[1], self.rows[1])]
                dst = self.rcv[s].at[k - 1]
            i = sum(counts[:s]) + k - 1 + (sum(counts) if n >= stages else 0)
            made.append(remote(src, dst, self.sems.at[0, i], self.sems.at[1, i], (peer, self.t)))
        return made

    def added(self, own, s, rows):
        count = self.order[s][1] - 1
        if count == 1:
            return own + self.rcv[s][0, rows, :]
        total = own.astype(F32)
        for j in range(count):
            total = total + self.rcv[s][j, rows, :].astype(F32)
        return total.astype(BF16)

    def step(self):
        n, stages = self.next, len(self.order)
        self.next += 1
        if n:
            for copy in self.copies(n - 1):
                copy.wait()
        if 0 < n < stages:
            size = self.rows[n + 1]
            inside = self.start[n] - self.start[1]
            for k in list(range(1, self.order[n][1])) + [0]:
                d, _ = self.peer(n, k)
                here = sixteens(inside + d * size, size)
                own = self.src[sixteens(self.base + self.start[1] + d * size, size), :] if n == 1 else self.acc[here, :]
                total = self.added(own, n - 1, sixteens(d * size, size))
                if k:
                    self.snd[n][k - 1] = total
                else:
                    self.acc[here, :] = total
        if n == stages:
            size = self.rows[stages]
            own = self.acc[sixteens(self.start[stages] - self.start[1], size), :]
            self.out[sixteens(self.start[stages], size), :] = self.added(own, stages - 1, pl.ds(0, size))
        if n < 2 * stages:
            for copy in self.copies(n):
                copy.start()


ANY = pl.BlockSpec(memory_space=pl.ANY)
LONG_ORDER = ((1, 2), (2, 2), (4, 2), (8, 2))
XZ_ORDER = ((1, 2), (2, 2), (4, 4))
ZX_ORDER = ((1, 2), (4, 4), (2, 2))
SUM_ORDERS = (LONG_ORDER, LONG_ORDER, XZ_ORDER, ZX_ORDER)


def mega_kernel(
    starts, rates, idx, tok_in, cot_in, gain1, wq_in, wk_in, wv_in, wg_in, op_in, pk_in, pv_in, first, second, gain2, dgw_in, dlw_in, ddw_in,
    fa_out, fb_out, qa_out, qb_out, gains_out, ret,
    xs, cs, mx, ops, asked, want, sent_c, g, gt, h1, q, k, v, gate, recall, kt, lse, a_all, c_all, pre_all, e_all, u_all, atth,
    pk, pv, pkt, pvt, bmp, diagonal, br, own_s, ps_s, pb_r, bms, facc, gout, gother, dgain,
    second_r, gother_r, rec_l, rec_x, part_r, src_b, src_c, out_a, out_b, out_c1, out_c2, gains_s, gains_r,
    a_s, c_s, sa_s, sc_s, wq, wk, wv, wg, op, dgw, dlw, ddw,
    in_sems, ask_sems, t_sems, ty_sems, c_sems, m_sems, d_sems, y_sems, l_sems, ly_sems, x_sems, xy_sems, g_sems, o_sems,
    *sums,
):
    dp, t = place()
    other = (dp, 1 - t)
    core = dp % 2
    count, width = xs.shape
    half = count // 2
    pairs = first.shape[0]
    heads = 2 * pairs
    wide = pairs * PAIR
    few = pk_in.shape[0]
    per = ROWS // STRETCH
    nblocks = count // ROWS
    hidden = dgw.shape[0]
    padded = facc.shape[0] // 3
    scale = HEAD_DIM ** -0.5

    rows_a = out_a.shape[0]
    rest = facc.shape[0] - rows_a
    cuts = [0]
    for order in SUM_ORDERS:
        cuts.append(cuts[-1] + Sum.refs(order))
    sum_a, sum_b, sum_c1, sum_c2 = [
        Sum(dp, t, src, base, out, order, sums[cuts[i]:cuts[i + 1]])
        for i, (src, base, out, order) in enumerate((
            (facc, 0, out_a, SUM_ORDERS[0]), (src_b, 0, out_b, SUM_ORDERS[1]),
            (src_c, 0, out_c1, SUM_ORDERS[2]), (src_c, out_c1.shape[0], out_c2, SUM_ORDERS[3]),
        ))
    ]

    def second_copy(i):
        src, dst = ((ps_s, second_r), (gother, gother_r))[i]
        return remote(src, dst, y_sems.at[0, i], y_sems.at[1, i], other)

    weights = [
        pltpu.make_async_copy(src, dst, in_sems.at[2 + i])
        for i, (src, dst) in enumerate((
            (wq_in, wq), (wk_in, wk), (wv_in, wv), (wg_in, wg), (op_in, op), (dgw_in, dgw), (dlw_in, dlw), (ddw_in, ddw),
        ))
    ]
    friends = [(flipped(dp, m), t) for m in range(1, PEERS)] + [other]
    greet(friends)
    def enter(tok, cot, sent_t):
        reads = [pltpu.make_async_copy(src, dst, in_sems.at[i]) for i, (src, dst) in enumerate(((tok_in, tok), (cot_in, cot)))]
        for read in reads + weights:
            read.start()
        index = idx[...]
        dev = lax.div(index, count)
        row = index - dev * count
        held = jnp.where(iota(PEERS, count, 0) == dev, 1.0, 0.0).astype(BF16)
        upper = jnp.where(iota(PAIR, PAIR, 0) < iota(PAIR, PAIR, 1), 1.0, 0.0).astype(BF16)
        run = jnp.zeros((PEERS, 1), F32)
        ranks = []
        for c in range(count // PAIR):
            part = held[:, c * PAIR:(c + 1) * PAIR]
            wide_part = part.astype(F32)
            ranks.append(jnp.sum(wide_part * (nn(part, upper) + run), axis=0, keepdims=True))
            run = run + jnp.sum(wide_part, axis=1, keepdims=True)
        rank = jnp.concatenate(ranks, axis=1)
        column = jnp.transpose(jnp.broadcast_to(rank, (PAIR, count)))
        pick = jnp.where(column == iota(count, PAIR, 1).astype(F32), 1.0, 0.0).astype(BF16)
        high = lax.div(row, 32)
        low = row - high * 32
        held_wide = held.astype(F32)
        wanted = 32.0 * nn((held_wide * high.astype(F32)).astype(BF16), pick) + nn((held_wide * low.astype(F32)).astype(BF16), pick)
        for j in range(PEERS):
            want[j] = jnp.broadcast_to(wanted[j:j + 1], (8, PAIR))
        greeted(friends)
        asks = []
        for m in range(1, PEERS):
            peer = flipped(dp, m)
            copy = remote(want.at[peer], asked.at[dp], ask_sems.at[0, m], ask_sems.at[1, m], (peer, t))
            copy.start()
            asks.append(copy)
        asked[dp] = want[dp]
        rank_i = rank.astype(jnp.int32)
        half_of = lax.div(rank_i, HALF_SHARE)
        slot = half_of * (half - HALF_SHARE) + lot(dev) * HALF_SHARE + rank_i
        for c in range(count // ROWS):
            gt[c * ROWS:(c + 1) * ROWS, :] = jnp.where(iota(ROWS, count, 0) + c * ROWS == slot, 1.0, 0.0).astype(BF16)
        slots = jnp.transpose(jnp.broadcast_to(slot.astype(F32), (PAIR, count)))
        for copy in asks:
            copy.wait()
        asks_in = asked[:, 0, :]
        asks_high = jnp.floor(asks_in * (1.0 / 32.0))
        asks_low = asks_in - 32.0 * asks_high
        owner = jnp.where(lax.div(iota(half, PEERS, 0), HALF_SHARE) == lot(iota(half, PEERS, 1)), 1.0, 0.0).astype(BF16)
        ones = jnp.ones((PAIR, PAIR), BF16)

        def choose(side):
            lane = iota(half, PAIR, 1) == iota(half, PAIR, 0) % HALF_SHARE + side * HALF_SHARE
            value = jnp.zeros((half, PAIR), F32)
            for digit, weight in ((asks_high, 32.0), (asks_low, 1.0)):
                picked = jnp.where(lane, nn(owner, digit.astype(BF16)), 0.0).astype(BF16)
                value = value + weight * nn(picked, ones)
            return jnp.concatenate(
                [jnp.where(value == (iota(half, PAIR, 1) + c * PAIR).astype(F32), 1.0, 0.0).astype(BF16) for c in range(count // PAIR)], axis=1
            )

        chosen = choose(t)
        for read in reads + weights:
            read.wait()
        sent_t[...] = nn(chosen, tok[...]).astype(BF16)
        spread(xs, dp, t, t, sent_t, t_sems, ALL_PEERS)
        sent_c[0] = nn(chosen, cot[...]).astype(BF16)
        sent_c[1] = nn(choose(1 - t), cot[...]).astype(BF16)
        for c in range(count // PAIR):
            g[:, c * PAIR:(c + 1) * PAIR] = jnp.where(slots == (iota(count, PAIR, 1) + c * PAIR).astype(F32), 1.0, 0.0).astype(BF16)
        for half_i in range(2):
            for ref_in, by_pair, by_head in ((pk_in, pk, pkt), (pv_in, pv, pvt)):
                part = ref_in[:, half_i * PAIR:(half_i + 1) * PAIR]
                by_pair[half_i] = part
                flat = jnp.transpose(part.astype(F32)).astype(BF16)
                by_head[2 * half_i] = flat[:HEAD_DIM]
                by_head[2 * half_i + 1] = flat[HEAD_DIM:]
        pass_on(xs, dp, t, sent_t, t_sems, ty_sems)
        passed_on(xs, dp, t, ty_sems)

    pl.run_scoped(enter, pltpu.VMEM((count, width), BF16), pltpu.VMEM((count, width), BF16), pltpu.VMEM((half, width), BF16))

    def ops_copy():
        return remote(ops.at[t], ops.at[t], m_sems.at[0, nblocks], m_sems.at[1, nblocks], other)

    def mixed_copy(qb):
        rows = pl.ds(qb * ROWS, ROWS)
        return remote(mx.at[t, rows], mx.at[t, rows], m_sems.at[0, qb], m_sems.at[1, qb], other)

    ops[t] = op[...]
    ops_copy().start()
    for i, side in enumerate((t, 1 - t)):
        spread(cs, dp, t, side, sent_c.at[i], c_sems.at[i], ALL_PEERS)

    def forward(vt, att):
        def project(b, _):
            rows = pl.ds(pl.multiple_of(b * ROWS, ROWS), ROWS)
            x = nn(g[rows, :], xs[...])
            factor = lax.rsqrt(jnp.mean(x * x, axis=-1, keepdims=True) + EPSILON)
            h = (x * factor * gain1[...]).astype(BF16)
            h1[rows, :] = h
            for part, (ref, w) in enumerate(((q, wq), (k, wk), (v, wv))):
                made = nn(h, w[...])
                low = made.astype(BF16)
                for p in range(pairs):
                    ref[p, rows, :] = low[:, p * PAIR:(p + 1) * PAIR]
                if part > 0:
                    made_t = jnp.transpose(made).astype(BF16)
                    target = kt if part == 1 else vt
                    for i in range(heads):
                        target[i, :, rows] = made_t[i * HEAD_DIM:(i + 1) * HEAD_DIM]
            made = sigmoid(nn(h, wg[...]))
            for p in range(pairs):
                gate[p, rows, :] = made[:, p * PAIR:(p + 1) * PAIR]
            return 0

        lax.fori_loop(0, nblocks, project, 0)
        a_s[...] = first[...]
        c_s[...] = second[...]
        sa_s[...] = jnp.zeros_like(sa_s)
        sc_s[...] = jnp.zeros_like(sc_s)

        def memory_step(n, p):
            rows = pl.ds(pl.multiple_of(n * STRETCH, STRETCH), STRETCH)
            fresh = starts[n] > 0
            a = jnp.where(fresh, first[p], a_s[p])
            ab = a.astype(BF16)
            km = both(k[p, rows, :])
            pre = nn(jnp.concatenate([both(q[p, rows, :]), km], axis=0), ab)
            yield
            c = jnp.where(fresh, second[p], c_s[p])
            cb = c.astype(BF16)
            a_all[n, p] = ab
            c_all[n, p] = cb
            pre_all[n, p] = pre
            sig = sigmoid(pre)
            act = pre * sig
            actb = act.astype(BF16)
            out = nt(actb, cb)
            yield
            eb = (joined(out[PAIR:]) - v[p, rows, :].astype(F32)).astype(BF16)
            em = both(eb)
            u = nn(em, cb)
            gc = tn(em, actb[PAIR:])
            yield
            recall[p, rows, :] = joined(out[:PAIR])
            e_all[p, rows, :] = eb
            sigk, actk = sig[PAIR:], act[PAIR:]
            ga = tn(km, (u * (sigk + actk * (1.0 - sigk))).astype(BF16))
            yield
            u_all[n, p] = u.astype(BF16)
            th = [rates[0, 2 * p + i, n] * (1.0 / STRETCH) for i in range(2)]
            eta = [rates[1, 2 * p + i, n] for i in range(2)]
            al = [1.0 - rates[2, 2 * p + i, n] for i in range(2)]
            sc = scaled(jnp.where(fresh, 0.0, sc_s[p]), eta) - scaled(gc, th)
            sc_s[p] = sc
            c_s[p] = scaled(c, al) + sc
            sa = scaled(jnp.where(fresh, 0.0, sa_s[p]), eta) - scaled(ga, th)
            sa_s[p] = sa
            a_s[p] = scaled(a, al) + sa

        def attention_unit(qb, head):
            p, side = head // 2, head % 2
            rows = pl.ds(qb * ROWS, ROWS)
            qh = keep(q[p, rows, :], side) * jnp.asarray(scale, BF16)
            scores = []
            for kb in range(qb + 1):
                s = nt(k[p, kb * ROWS:(kb + 1) * ROWS, :], qh)
                scores.append(s + diagonal[...] if kb == qb else earlier(s, starts, kb, qb, per))
                yield
            sp = nt(pk[p], qh)
            peak = jnp.max(sp, axis=0, keepdims=True)
            for s in scores:
                peak = jnp.maximum(peak, jnp.max(s, axis=0, keepdims=True))
            ep = jnp.exp(sp - peak)
            total = jnp.sum(ep, axis=0, keepdims=True)
            out = nn(pvt[head], ep.astype(BF16))
            yield
            for kb, s in enumerate(scores):
                e = jnp.exp(s - peak)
                total = total + jnp.sum(e, axis=0, keepdims=True)
                out = out + nn(vt[head, :, kb * ROWS:(kb + 1) * ROWS], e.astype(BF16))
                yield
            att[head, :, rows] = out * (1.0 / total)
            lse[head, :, rows] = peak + jnp.log(total)

        for qb in range(nblocks):
            fill_diagonal(diagonal, starts[qb * per])

            def run(i, _, qb=qb):
                weave([memory_step(qb * per + i, p) for p in range(pairs)], attention_unit(qb, i), (qb + 3) // 2, qb > 1)
                return 0

            lax.fori_loop(0, per, run, 0)
            rows = pl.ds(qb * ROWS, ROWS)
            for p in range(pairs):
                got = jnp.transpose(jnp.concatenate([att[2 * p, :, rows], att[2 * p + 1, :, rows]], axis=0))
                atth[p, rows, :] = got.astype(BF16)
                mx[t, rows, p * PAIR:(p + 1) * PAIR] = (got + gate[p, rows, :] * recall[p, rows, :]).astype(BF16)
            mixed_copy(qb).start()

    pl.run_scoped(forward, pltpu.VMEM((heads, HEAD_DIM, count), BF16), pltpu.VMEM((heads, HEAD_DIM, count), F32))

    def dense_part(ms, hid, bgs, bls, bms_s, resid, own_b):
        h2s, pb_s, bf = src_b.at[:count], src_c.at[:half], src_c.at[half:]
        pad = jnp.zeros((count, PAIR), BF16)
        for ref in (hid, bgs, bls):
            ref[:, padded - PAIR:] = pad
        ms[t] = nn(gt[...], mx[t]).astype(BF16)
        ops_copy().wait()
        for qb in range(nblocks):
            mixed_copy(qb).wait()
        for i, side in enumerate((t, 1 - t)):
            for m in ALL_PEERS[1:]:
                spreading(cs, dp, t, side, sent_c.at[i], c_sems.at[i], m).wait()
        ms[1 - t] = nn(gt[...], mx[1 - t]).astype(BF16)

        def chunk(rows, store):
            x = xs[rows, :].astype(F32) + nn(ms[0, rows, :], ops[0]) + nn(ms[1, rows, :], ops[1])
            factor = lax.rsqrt(jnp.mean(x * x, axis=-1, keepdims=True) + EPSILON)
            h2 = (x * factor * gain2[...]).astype(BF16)
            h2s[rows, :] = h2
            for begin in range(0, hidden, ROWS):
                cols = slice(begin, min(begin + ROWS, hidden))
                gated, lifted = nt(h2, dgw[cols, :]), nt(h2, dlw[cols, :])
                sig = sigmoid(gated)
                act = gated * sig
                hid[rows, cols] = (act * lifted).astype(BF16)
                back = nt(cs[rows, :], ddw[cols, :])
                bgs[rows, cols] = (back * lifted * (sig + act * (1.0 - sig))).astype(BF16)
                bls[rows, cols] = (back * act).astype(BF16)
            store(x, nn(bgs[rows, :hidden], dgw[...]) + nn(bls[rows, :hidden], dlw[...]), rows)

        copies = []
        for c in range(half // ROWS):
            here = pl.ds(c * ROWS, ROWS)

            def send(x, back, rows, here=here):
                pb_s[here, :] = back.astype(BF16)

            chunk(at_rows((1 - t) * half + c * ROWS, ROWS), send)
            copy = remote(pb_s.at[here], pb_r.at[here], d_sems.at[0, c], d_sems.at[1, c], other)
            copy.start()
            copies.append(copy)
            ps_s[here, :] = nn(hid[at_rows((1 - t) * half + c * ROWS, ROWS), :hidden], ddw[...]).astype(BF16)
        for c in range(half // ROWS):
            here = pl.ds(c * ROWS, ROWS)

            def hold(x, back, rows, here=here):
                resid[here, :] = x
                own_s[here, :] = x + nn(hid[rows, :hidden], ddw[...])
                own_b[here, :] = back

            chunk(at_rows(t * half + c * ROWS, ROWS), hold)
        facc[:padded, :] = tn(bgs[...], h2s[...]).astype(BF16)
        facc[padded:2 * padded, :] = tn(bls[...], h2s[...]).astype(BF16)
        sum_a.step()
        total = jnp.zeros((8, width), F32)
        back_copies = []
        for c in range(half // ROWS):
            here = pl.ds(c * ROWS, ROWS)
            rows = at_rows(t * half + c * ROWS, ROWS)
            copies[c].wait()
            for b in range(ROWS // STRETCH):
                few_rows = pl.ds(c * ROWS + b * STRETCH, STRETCH)
                x = resid[few_rows, :]
                factor = lax.rsqrt(jnp.mean(x * x, axis=-1, keepdims=True) + EPSILON)
                norm = x * factor
                back = own_b[few_rows, :] + pb_r[few_rows, :].astype(F32)
                inner = back * gain2[...]
                result = cs[at_rows(t * half + c * ROWS + b * STRETCH, STRETCH), :].astype(F32) + factor * (
                    inner - norm * jnp.mean(inner * norm, axis=-1, keepdims=True)
                )
                br[few_rows, :] = result
                bf[few_rows, :] = result.astype(BF16)
                total = total + jnp.sum((back * norm).reshape(STRETCH // 8, 8, width), axis=0)
            low = bf[here, :]
            bms_s[here, :] = nt(low, ops[1 - t]).astype(BF16)
            copy = remote(bms_s.at[here], bms.at[rows], d_sems.at[0, 2 + c], d_sems.at[1, 2 + c], other)
            copy.start()
            back_copies.append(copy)
            bms[rows, :] = nt(low, ops[t]).astype(BF16)
            if c == 0:
                sum_a.step()
        dgain[...] = total
        second_copy(0).start()
        facc[2 * padded:, :] = tn(hid[...], cs[...]).astype(BF16)
        mine = at_rows(t * half, half)
        gout[...] = tn(ms[t, mine, :], bf[...])
        gother[...] = tn(ms[1 - t, mine, :], bf[...]).astype(BF16)
        second_copy(1).start()
        for copy in back_copies:
            copy.wait()
        for b in range(nblocks):
            rows = pl.ds(b * ROWS, ROWS)
            got = nn(g[rows, :], bms[...]).astype(BF16)
            for p in range(pairs):
                bmp[p, rows, :] = got[:, p * PAIR:(p + 1) * PAIR]

    hiddens = pltpu.VMEM((count, padded), BF16)
    pl.run_scoped(
        dense_part, pltpu.VMEM((2, count, wide), BF16), hiddens, hiddens, hiddens, pltpu.VMEM((half, wide), BF16),
        pltpu.VMEM((half, width), F32), pltpu.VMEM((half, width), F32),
    )

    def backward(dqt, dks, dvs, mq, mk, mv, dd, dpk, dpv, dfirst, dsecond, dv, dg):
        lo, part_s, dq, dk, bx = sent_c.at[0], ps_s, mx.at[0], mx.at[1], second_r
        da_s, dc_s, dsa_s, dsc_s = a_s, c_s, sa_s, sc_s
        ones = [jnp.where(lanes_of(i, 8), 1.0, 0.0).astype(BF16) for i in range(2)]
        for b in range(nblocks):
            rows = pl.ds(b * ROWS, ROWS)
            for p in range(pairs):
                gr = bmp[p, rows, :].astype(F32)
                inner = (gr * atth[p, rows, :].astype(F32)).astype(BF16)
                for i in range(2):
                    dd[2 * p + i, :, rows] = nt(ones[i], inner)[:1]
                gv = gate[p, rows, :]
                dg[rows, p * PAIR:(p + 1) * PAIR] = (gr * recall[p, rows, :] * gv * (1.0 - gv)).astype(BF16)
        for ref in (dpk, dpv, dfirst, dsecond, dks, dvs, da_s, dc_s, dsa_s, dsc_s):
            ref[...] = jnp.zeros_like(ref)

        def memory_step(n, p):
            rows = pl.ds(pl.multiple_of(n * STRETCH, STRETCH), STRETCH)
            fresh = starts[n] > 0
            th = [rates[0, 2 * p + i, n] * (-1.0 / STRETCH) for i in range(2)]
            eta = [rates[1, 2 * p + i, n] for i in range(2)]
            al = [1.0 - rates[2, 2 * p + i, n] for i in range(2)]
            da, dc = da_s[p], dc_s[p]
            dsa = dsa_s[p] + da
            dga = scaled(dsa, th).astype(BF16)
            km = both(k[p, rows, :])
            dw = nn(km, dga)
            dsc = dsc_s[p] + dc
            dgc = scaled(dsc, th).astype(BF16)
            ab, cb = a_all[n, p], c_all[n, p]
            pre = pre_all[n, p]
            sig = sigmoid(pre)
            act = pre * sig
            actb = act.astype(BF16)
            slope = sig + act * (1.0 - sig)
            sigk, prek, slopek = sig[PAIR:], pre[PAIR:], slope[PAIR:]
            yield
            du = (dw * slopek).astype(BF16)
            de = joined(nt(jnp.concatenate([actb[PAIR:], du], axis=1), jnp.concatenate([dgc, cb], axis=1)))
            rm = both((bmp[p, rows, :].astype(F32) * gate[p, rows, :]).astype(BF16))
            dpre_q = (nn(rm, cb) * slope[:PAIR]).astype(BF16)
            u = u_all[n, p].astype(F32)
            curve = sigk * (1.0 - sigk) * (2.0 + prek * (1.0 - 2.0 * sigk))
            yield
            em = both(e_all[p, rows, :])
            dem = both(de.astype(BF16))
            dsk = nn(jnp.concatenate([em, dem], axis=1), jnp.concatenate([dgc, cb], axis=0))
            mv[p, rows, :] = de
            mq[p, rows, :] = joined(nt(dpre_q, ab))
            gc = tn(jnp.concatenate([em, dem], axis=0), jnp.concatenate([du, actb[PAIR:]], axis=0)) + tn(rm, actb[:PAIR])
            yield
            wgt = (u * slopek).astype(BF16)
            dpre = (dsk * slopek + dw * u * curve).astype(BF16)
            ga = tn(jnp.concatenate([km, both(q[p, rows, :])], axis=0), jnp.concatenate([dpre, dpre_q], axis=0))
            mk[p, rows, :] = joined(nt(jnp.concatenate([wgt, dpre], axis=1), jnp.concatenate([dga, ab], axis=1)))
            yield
            dc = scaled(dc, al) + gc
            dsecond[p] = dsecond[p] + jnp.where(fresh, dc, 0.0)
            dc_s[p] = jnp.where(fresh, 0.0, dc)
            dsc_s[p] = jnp.where(fresh, 0.0, scaled(dsc, eta))
            da = scaled(da, al) + ga
            dfirst[p] = dfirst[p] + jnp.where(fresh, da, 0.0)
            da_s[p] = jnp.where(fresh, 0.0, da)
            dsa_s[p] = jnp.where(fresh, 0.0, scaled(dsa, eta))

        def attention_unit(qb, head):
            p, side = head // 2, head % 2
            rows = pl.ds(qb * ROWS, ROWS)
            qh = keep(q[p, rows, :], side) * jnp.asarray(scale, BF16)
            gh = keep(bmp[p, rows, :], side)
            lrow, drow = lse[head, :, rows], dd[head, :, rows]
            acc = jnp.zeros((HEAD_DIM, ROWS), F32)
            for kb in range(qb + 1):
                krows = slice(kb * ROWS, (kb + 1) * ROWS)
                s = nt(k[p, krows, :], qh)
                dprob = nt(v[p, krows, :], gh)
                yield
                s = s - lrow
                s = s + diagonal[...] if kb == qb else earlier(s, starts, kb, qb, per)
                prob = jnp.exp(s)
                ds = (prob * (dprob - drow)).astype(BF16)
                yield
                dvs[p, krows, :] = dvs[p, krows, :] + nn(prob.astype(BF16), gh)
                dks[p, krows, :] = dks[p, krows, :] + nn(ds, qh)
                acc = acc + nn(kt[head, :, krows], ds)
                yield
            prob = jnp.exp(nt(pk[p], qh) - lrow)
            ds = (prob * (nt(pv[p], gh) - drow)).astype(BF16)
            dpv[p] = dpv[p] + nn(prob.astype(BF16), gh)
            dpk[p] = dpk[p] + nn(ds, qh)
            acc = acc + nn(pkt[head], ds)
            dqt[head, :, rows] = acc * scale

        def fold(ref, begin, value):
            rows = value.shape[0] // 2
            ref[begin:begin + rows, :wide] = value[:rows].astype(BF16)
            ref[begin:begin + rows, wide:] = value[rows:].astype(BF16)

        src_b[:rest, :] = facc[rows_a:, :]
        fold(src_b, rest, tn(h1[...], dg[...]))

        def background(point):
            if point in (1, 3, 6):
                sum_a.step()
            if point == 3:
                second_copy(0).wait()
                lo[...] = (own_s[...] + second_r[...].astype(F32)).astype(BF16)
                spread(rec_l, dp, t, t, lo, l_sems, ALL_PEERS)
            if point == 4:
                second_copy(1).wait()
                src_b[rest + wide:, :] = (gout[...] + gother_r[...].astype(F32)).astype(BF16)
            if point in (4, 5, 7):
                sum_b.step()
            if point == 7:
                pass_on(rec_l, dp, t, lo, l_sems, ly_sems)

        for qb in reversed(range(nblocks)):
            fill_diagonal(diagonal, starts[qb * per])

            def run(i, _, qb=qb):
                weave([memory_step(qb * per + per - 1 - i, p) for p in range(pairs)], attention_unit(qb, i), (3 * qb + 6) // 4, qb > 1)
                return 0

            for part in range(2):
                background((nblocks - 1 - qb) * 2 + part)
                lax.fori_loop(part * per // 2, (part + 1) * per // 2, run, 0)
        for b in range(nblocks):
            rows = pl.ds(b * ROWS, ROWS)
            for p in range(pairs):
                cols = slice(p * PAIR, (p + 1) * PAIR)
                got = jnp.concatenate([dqt[2 * p, :, rows], dqt[2 * p + 1, :, rows]], axis=0)
                dq[rows, cols] = (jnp.transpose(got) + mq[p, rows, :]).astype(BF16)
                dk[rows, cols] = (dks[p, rows, :] + mk[p, rows, :]).astype(BF16)
                dv[rows, cols] = (dvs[p, rows, :] - mv[p, rows, :]).astype(BF16)
        made = tn(h1[...], jnp.concatenate([dq[...], dk[...], dv[...]], axis=1))
        for i in range(3):
            fold(src_c, i * wide, made[:, i * wide:(i + 1) * wide])
        at = 3 * wide
        src_c[at + PAIR:, :] = jnp.zeros((src_c.shape[0] - at - PAIR, width), BF16)
        for i in range(4):
            lanes = slice(i * PAIR, (i + 1) * PAIR)
            src_c[at:at + PAIR, lanes] = (dfirst, dsecond)[i // 2][i % 2].astype(BF16)
            src_c[at + PAIR:at + PAIR + few, lanes] = (dpk, dpv)[i // 2][i % 2].astype(BF16)

        def step_c():
            sum_c1.step()
            sum_c2.step()

        step_c()

        for b in range(nblocks):
            rows = pl.ds(b * ROWS, ROWS)
            result = nt(dq[rows, :], wq[...])
            for back, w in ((dk, wk), (dv, wv), (dg, wg)):
                result = result + nt(back[rows, :], w[...])
            facc[rows, :] = result.astype(BF16)

        def partial(rows):
            return nn(gt[rows, :], facc[:count, :])

        column = lax.div(dp, 2) % 2
        quarter = half // 4
        places = []
        for b0, b1 in ((0, 0), (0, 1), (1, 0), (1, 1)):
            c, x = core + b0 * (1 - 2 * core), column + b1 * (1 - 2 * column)
            places.append(c * (2 * quarter) + x * quarter)

        def part_copy(i):
            here = at_rows(places[i], quarter)
            return remote(part_s.at[here], part_r.at[here], y_sems.at[0, 2 + i], y_sems.at[1, 2 + i], other)

        for i, begin in enumerate(places):
            part_s[at_rows(begin, quarter), :] = partial(at_rows((1 - t) * half + begin, quarter)).astype(BF16)
            part_copy(i).start()
            if i == 0:
                sum_a.step()
            if i == 2:
                sum_b.step()
        step_c()
        owns = [partial(at_rows(t * half + begin, quarter)) for begin in places]
        sum_a.step()
        sum_b.step()
        asks = asked[:, 0, :]
        asks_high = jnp.floor(asks * (1.0 / 32.0))
        asks_low = asks - 32.0 * asks_high
        slot = iota(PAIR, count, 1)
        rank = lax.div(slot, half) * HALF_SHARE + slot % HALF_SHARE
        pick = jnp.where(iota(PAIR, count, 0) == rank, 1.0, 0.0).astype(BF16)
        slot = iota(PEERS, count, 1)
        mine = lot(iota(PEERS, count, 0)) == lax.div(slot % half, HALF_SHARE)
        spread_out = 32.0 * nn(asks_high.astype(BF16), pick) + nn(asks_low.astype(BF16), pick)
        row = jnp.sum(jnp.where(mine, spread_out, 0.0), axis=0, keepdims=True)
        for c in range(count // ROWS):
            g[c * ROWS:(c + 1) * ROWS, :] = jnp.where((iota(ROWS, count, 0) + c * ROWS).astype(F32) == row, 1.0, 0.0).astype(BF16)
        passed_on(rec_l, dp, t, ly_sems)
        cs[...] = nn(g[...], rec_l[...]).astype(BF16)
        mgain = jnp.zeros((8, width), F32)
        for i, begin in enumerate(places):
            part_copy(i).wait()
            for b in range(quarter // STRETCH):
                few_rows = at_rows(begin + b * STRETCH, STRETCH)
                back = owns[i][b * STRETCH:(b + 1) * STRETCH] + part_r[few_rows, :].astype(F32)
                x = xs[at_rows(t * half + begin + b * STRETCH, STRETCH), :].astype(F32)
                factor = lax.rsqrt(jnp.mean(x * x, axis=-1, keepdims=True) + EPSILON)
                norm = x * factor
                inner = back * gain1[...]
                bx[few_rows, :] = (
                    br[few_rows, :] + factor * (inner - norm * jnp.mean(inner * norm, axis=-1, keepdims=True))
                ).astype(BF16)
                mgain = mgain + jnp.sum((back * norm).reshape(STRETCH // 8, 8, width), axis=0)
            spread(rec_x, dp, t, t, bx, x_sems, QUARTERS[i])
            if i == 1:
                step_c()
                sum_b.step()
        gains_s[0, 0] = mgain
        gains_s[0, 1] = dgain[...]
        c2 = lax.div(dp, 4)
        groups = [[other], [(flipped(dp, 1), t)], [(flipped(dp, 2), t)], [(dp + 4 * ((c2 + i) % 4 - c2), t) for i in (1, 2, 3)]]
        gain_copies = []

        def gain_step(i):
            if i:
                for copy in gain_copies:
                    copy.wait()
                gain_copies.clear()
                value = gains_s[i - 1]
                for j in range(len(groups[i - 1])):
                    value = value + gains_r[i - 1 + j]
                gains_s[i] = value
            if i < 4:
                for j, peer in enumerate(groups[i]):
                    copy = remote(gains_s.at[i], gains_r.at[i + j], g_sems.at[0, i, j], g_sems.at[1, i, j], peer)
                    copy.start()
                    gain_copies.append(copy)

        writes = [pltpu.make_async_copy(src, dst, o_sems.at[i]) for i, (src, dst) in enumerate((
            (cs, ret.at[0]), (xs, ret.at[1]), (gains_s.at[4], gains_out), (out_a, fa_out), (out_b, fb_out), (out_c1, qa_out), (out_c2, qb_out),
        ))]
        writes[0].start()
        gain_step(0)
        sum_b.step()
        sum_a.step()
        step_c()
        gain_step(1)
        pass_on(rec_x, dp, t, bx, x_sems, xy_sems)
        gain_step(2)
        mine_rows, other_rows = at_rows(t * half, half), at_rows((1 - t) * half, half)
        mine_part = nn(g[:, mine_rows], rec_x[mine_rows, :])
        step_c()
        sum_b.step()
        sum_a.step()
        writes[3].start()
        gain_step(3)
        passed_on(rec_x, dp, t, xy_sems)
        xs[...] = (mine_part + nn(g[:, other_rows], rec_x[other_rows, :])).astype(BF16)
        writes[1].start()
        gain_step(4)
        writes[2].start()
        step_c()
        sum_b.step()
        writes[4].start()
        step_c()
        writes[5].start()
        writes[6].start()
        for write in writes:
            write.wait()

    flat = pltpu.VMEM((pairs, count, PAIR), F32)
    state = pltpu.VMEM((pairs, PAIR, PAIR), F32)
    tall = pltpu.VMEM((count, wide), BF16)
    pl.run_scoped(
        backward, pltpu.VMEM((heads, HEAD_DIM, count), F32), flat, flat, flat, flat, flat, pltpu.VMEM((heads, 1, count), F32),
        pltpu.VMEM((pairs, few, PAIR), F32), pltpu.VMEM((pairs, few, PAIR), F32), state, state,
        tall, tall,
    )


def mega(starts, rates, idx, tokens, cotangent, gain1, wq, wk, wv, wg, op, pk, pv, first, second, gain2, dg, dl, dd):
    count, width = tokens.shape
    half = count // 2
    wide = wq.shape[1]
    pairs = wide // PAIR
    heads = 2 * pairs
    few = pk.shape[0]
    steps = starts.shape[0]
    padded = -(-dg.shape[0] // 256) * 256
    rows_a = 2 * padded
    rows_b = padded + 2 * wide
    rows_c = 3 * wide
    rows_d = -(-(PAIR + few) // 256) * 256
    low = lambda *dims: pltpu.VMEM(dims, BF16)
    full = lambda *dims: pltpu.VMEM(dims, F32)
    sems = pltpu.SemaphoreType.DMA((2, PEERS))
    dma = pltpu.SemaphoreType.DMA
    square = low(count, count)
    state = full(pairs, PAIR, PAIR)
    args = (starts, rates, idx, tokens, cotangent, gain1, wq, wk, wv, wg, op, pk, pv, first, second, gain2, dg, dl, dd)
    return pl.pallas_call(
        mega_kernel,
        out_shape=(
            shape(rows_a, width, dtype=BF16), shape(rows_b, width, dtype=BF16), shape(rows_c, width, dtype=BF16), shape(rows_d, width, dtype=BF16),
            shape(2, 8, width), shape(2, count, width, dtype=BF16),
        ),
        in_specs=[ANY if n in (3, 4, 6, 7, 8, 9, 10, 16, 17, 18) else SMEM if n < 2 else VMEM for n in range(len(args))],
        out_specs=[ANY] * 6,
        scratch_shapes=[
            low(count, width), low(count, width), low(2, count, wide), low(2, *op.shape), full(PEERS, 8, PAIR), full(PEERS, 8, PAIR),
            low(2, half, width), square, square, low(count, width), low(pairs, count, PAIR), low(pairs, count, PAIR), low(pairs, count, PAIR),
            full(pairs, count, PAIR), full(pairs, count, PAIR), low(heads, HEAD_DIM, count), full(heads, 1, count),
            low(steps, pairs, PAIR, PAIR), low(steps, pairs, PAIR, PAIR), full(steps, pairs, 2 * PAIR, PAIR), low(pairs, count, PAIR),
            low(steps, pairs, PAIR, PAIR), low(pairs, count, PAIR),
            low(pairs, few, PAIR), low(pairs, few, PAIR), low(heads, HEAD_DIM, few), low(heads, HEAD_DIM, few), low(pairs, count, PAIR),
            full(ROWS, ROWS), full(half, width), full(half, width), low(half, width), low(half, width), low(count, wide),
            low(3 * padded, width), full(wide, width), low(wide, width), full(8, width),
            low(half, width), low(wide, width), low(count, width), low(count, width), low(half, width),
            low(rows_b, width), low(rows_c + rows_d, width), low(rows_a, width), low(rows_b, width), low(rows_c, width), low(rows_d, width),
            full(5, 2, 8, width), full(6, 2, 8, width),
            state, state, state, state, *[low(*weight.shape) for weight in (wq, wk, wv, wg, op, dg, dl, dd)],
            dma((10,)), sems, sems, sems, dma((2, 2, PEERS)), dma((2, 8)), dma((2, 4)), dma((2, 6)), sems, sems, sems, sems, dma((2, 4, 3)), dma((7,)),
            *Sum.scratch(rows_a, width, SUM_ORDERS[0]), *Sum.scratch(rows_b, width, SUM_ORDERS[1]),
            *Sum.scratch(rows_c, width, SUM_ORDERS[2]), *Sum.scratch(rows_d, width, SUM_ORDERS[3]),
        ],
        compiler_params=pltpu.CompilerParams(collective_id=0, has_side_effects=True, vmem_limit_bytes=62 * 1024 * 1024),
        name="block",
    )(*args)


def finish_kernel(
    fa, fb, qa, qb, gains, ret, lo, bx, mgain, gq, gk, gv, gg, gout, gpk, gpv, first, second, dgain, ggate, glift, gdown,
    fa_s, fb_s, qa_s, qb_s, ret_s, wide_s, tall_s, out_s, state_s, in_sems, out_sems,
):
    hidden, width = ggate.shape
    wide = gq.shape[1]
    few = gpk.shape[0]
    padded = -(-hidden // 256) * 256
    moves = []
    reads = [
        pltpu.make_async_copy(src, dst, in_sems.at[i])
        for i, (src, dst) in enumerate(((fa, fa_s), (fb, fb_s), (ret, ret_s), (qa, qa_s), (qb, qb_s)))
    ]
    for copy in reads:
        copy.start()

    def send(src, dst):
        moves.append(pltpu.make_async_copy(src, dst, out_sems.at[len(moves)]))
        moves[-1].start()

    def square(n, src, begin, ref):
        rows = src[begin:begin + wide, :].astype(F32)
        tall_s[n, :wide, :] = rows[:, :wide]
        tall_s[n, wide:, :] = rows[:, wide:]
        send(tall_s.at[n], ref)

    mgain[...] = jnp.sum(gains[0], axis=0, keepdims=True)
    dgain[...] = jnp.sum(gains[1], axis=0, keepdims=True)
    reads[0].wait()
    for n, ref in enumerate((ggate, glift)):
        wide_s[n] = fa_s[n * padded:n * padded + hidden, :].astype(F32)
        send(wide_s.at[n], ref)
    reads[1].wait()
    wide_s[2] = fb_s[:hidden, :].astype(F32)
    send(wide_s.at[2], gdown)
    square(3, fb_s, padded, gg)
    out_s[...] = fb_s[padded + wide:, :].astype(F32)
    send(out_s, gout)
    reads[2].wait()
    send(ret_s.at[0], lo)
    send(ret_s.at[1], bx)
    reads[3].wait()
    for n, ref in enumerate((gq, gk, gv)):
        square(n, qa_s, n * wide, ref)
    reads[4].wait()
    for n in range(4):
        lanes = slice(n * PAIR, (n + 1) * PAIR)
        state_s[n] = qb_s[:PAIR, lanes].astype(F32)
        (gpk, gpv)[n // 2][:, (n % 2) * PAIR:(n % 2 + 1) * PAIR] = qb_s[PAIR:PAIR + few, lanes].astype(F32)
    send(state_s.at[:2], first)
    send(state_s.at[2:], second)
    for copy in moves:
        copy.wait()


def finish(fa, fb, qa, qb, gains, ret, hidden, wide, few):
    count, width = ret.shape[1:]
    pairs = wide // PAIR
    rows = shape(count, width, dtype=BF16)
    square = shape(width, wide)
    state = shape(pairs, PAIR, PAIR)
    outs = (
        rows, rows, shape(1, width), square, square, square, square, shape(wide, width), shape(few, wide), shape(few, wide),
        state, state, shape(1, width), shape(hidden, width), shape(hidden, width), shape(hidden, width),
    )
    small = (2, 8, 9, 12)
    return pl.pallas_call(
        finish_kernel,
        out_shape=outs,
        in_specs=[ANY] * 4 + [VMEM, ANY],
        out_specs=[VMEM if n in small else ANY for n in range(len(outs))],
        scratch_shapes=[
            pltpu.VMEM(fa.shape, BF16), pltpu.VMEM(fb.shape, BF16), pltpu.VMEM(qa.shape, BF16), pltpu.VMEM(qb.shape, BF16), pltpu.VMEM(ret.shape, BF16),
            pltpu.VMEM((3, hidden, width), F32), pltpu.VMEM((4, width, wide), F32), pltpu.VMEM((wide, width), F32),
            pltpu.VMEM((4, PAIR, PAIR), F32), pltpu.SemaphoreType.DMA((5,)), pltpu.SemaphoreType.DMA((12,)),
        ],
        compiler_params=pltpu.CompilerParams(vmem_limit_bytes=LIMIT),
        name="finish",
    )(fa, fb, qa, qb, gains, ret)


def block_body(
    tokens, cotangent, source_index, tract_starts, memory_rates, mixer_gain, query_proj, key_proj, value_proj, gate_proj,
    out_proj, persist_keys, persist_values, memory_first, memory_second, dense_gain, dense_gate, dense_lift, dense_down,
):
    pairs = query_proj.shape[1] // PAIR
    first = memory_first.reshape(pairs, PAIR, PAIR)
    second = memory_second.transpose(0, 2, 1).reshape(pairs, PAIR, PAIR)
    summed = mega(
        tract_starts, memory_rates.transpose(0, 2, 1), source_index.reshape(1, -1), tokens, cotangent, mixer_gain[None],
        query_proj, key_proj, value_proj, gate_proj, out_proj, persist_keys, persist_values, first, second,
        dense_gain[None], dense_gate.T, dense_lift.T, dense_down,
    )
    outs = list(finish(*summed, dense_gate.shape[1], query_proj.shape[1], persist_keys.shape[0]))
    outs[2] = outs[2][0]
    outs[10] = outs[10].reshape(memory_first.shape)
    outs[11] = outs[11].reshape(memory_first.shape).transpose(0, 2, 1)
    outs[12] = outs[12][0]
    outs[13], outs[14] = outs[13].T, outs[14].T
    return tuple(outs)


def body(
    tokens,
    cotangent,
    source_index,
    tract_starts,
    memory_rates,
    mixer_gain,
    query_proj,
    key_proj,
    value_proj,
    gate_proj,
    out_proj,
    persist_keys,
    persist_values,
    memory_first,
    memory_second,
    dense_gain,
    dense_gate,
    dense_lift,
    dense_down,
):
    count = tokens.shape[0]
    width = tokens.shape[1]
    peers = lax.axis_size("dp")
    share = count // peers
    arrival = jnp.argsort(source_index)
    wanted = (source_index[arrival] % count).reshape(peers, share)
    asked = lax.all_to_all(wanted, "dp", split_axis=0, concat_axis=0, tiled=True).reshape(count)
    got_tokens, got_cot = (
        lax.all_to_all(
            tokens[asked].reshape(peers, share, width),
            "dp",
            split_axis=0,
            concat_axis=0,
            tiled=True,
        ),
        lax.all_to_all(
            cotangent[asked].reshape(peers, share, width),
            "dp",
            split_axis=0,
            concat_axis=0,
            tiled=True,
        ),
    )
    placing = jnp.argsort(arrival)
    seq_tokens = got_tokens.reshape(count, width)[placing]
    seq_cot = got_cot.reshape(count, width)[placing]
    seq_x = seq_tokens.astype(jnp.float32)
    first_norm, factor_one = norm_forward(seq_x)
    pairs = query_proj.shape[1] // PAIR
    by_pair = lambda value: value.reshape(-1, pairs, PAIR).transpose(1, 0, 2)
    by_head = lambda value: value.T.reshape(2 * pairs, HEAD_DIM, -1)
    weights = jnp.concatenate([query_proj, key_proj, value_proj, gate_proj], axis=1)
    pk, pv = by_pair(persist_keys), by_pair(persist_values)
    first = memory_first.reshape(pairs, PAIR, PAIR)
    second = memory_second.transpose(0, 2, 1).reshape(pairs, PAIR, PAIR)
    h_one, query, keys, values, gate, recall, mixed, keys_t, lse, a_all, c_all, pre_all, e_all, u_all, attended = mixer_forward(
        tract_starts, memory_rates, seq_tokens, mixer_gain[None], weights, pk, by_head(persist_values), first, second
    )
    first_out = lax.psum(product(mixed, out_proj), "tensor")
    resid = seq_x + first_out
    norm_two, factor_two = norm_forward(resid)
    h_two = (norm_two * dense_gain).astype(jnp.bfloat16)
    gated = product(h_two, dense_gate)
    lifted = product(h_two, dense_lift)
    sigma = jax.nn.sigmoid(gated)
    active = gated * sigma
    hidden = (active * lifted).astype(jnp.bfloat16)
    second_out = lax.psum(product(hidden, dense_down).astype(jnp.bfloat16), "tensor").astype(
        jnp.float32
    )
    seq_out = (resid + second_out).astype(jnp.bfloat16)
    grad_down = product(hidden.T, seq_cot)
    back_hidden = product(seq_cot, dense_down.T)
    back_gated = (back_hidden * lifted * (sigma + gated * sigma * (1.0 - sigma))).astype(
        jnp.bfloat16
    )
    back_lifted = (back_hidden * active).astype(jnp.bfloat16)
    grad_gate = product(h_two.T, back_gated)
    grad_lift = product(h_two.T, back_lifted)
    back_two = lax.psum(
        product(back_gated, dense_gate.T) + product(back_lifted, dense_lift.T), "tensor"
    )
    back_norm_two, grad_dgain = norm_backward(back_two, norm_two, factor_two, dense_gain)
    residual_gradient = seq_cot.astype(jnp.float32) + back_norm_two
    back_first = residual_gradient.astype(jnp.bfloat16)
    grad_out = product(mixed.T, back_first)
    back_mixed = product(back_first, out_proj.T).astype(jnp.bfloat16)
    back_query, back_keys, cotangent_payloads, back_gate, grad_pk, grad_pv, grad_first, grad_second = mixer_backward(
        tract_starts, memory_rates, back_mixed, query, keys, values, gate, recall, keys_t, pk, by_head(persist_keys), pv,
        lse, a_all, c_all, pre_all, e_all, u_all, attended,
    )
    grad_first = grad_first.reshape(memory_first.shape)
    grad_second = grad_second.reshape(memory_first.shape).transpose(0, 2, 1)
    grad_query = product(h_one.T, back_query)
    grad_key = product(h_one.T, back_keys)
    grad_value = product(h_one.T, cotangent_payloads)
    grad_gproj = product(h_one.T, back_gate)
    back_one = lax.psum(
        product(back_query, query_proj.T)
        + product(back_keys, key_proj.T)
        + product(cotangent_payloads, value_proj.T)
        + product(back_gate, gate_proj.T),
        "tensor",
    )
    back_norm_one, grad_mgain = norm_backward(back_one, first_norm, factor_one, mixer_gain)
    back_x = (residual_gradient + back_norm_one).astype(jnp.bfloat16)
    grad_pkeys = grad_pk.transpose(1, 0, 2).reshape(persist_keys.shape)
    grad_pvalues = grad_pv.transpose(1, 0, 2).reshape(persist_values.shape)
    (
        grad_mgain,
        grad_query,
        grad_key,
        grad_value,
        grad_gproj,
        grad_out,
        grad_pkeys,
        grad_pvalues,
        grad_first,
        grad_second,
        grad_dgain,
        grad_gate,
        grad_lift,
        grad_down,
    ) = lax.psum(
        (
            grad_mgain,
            grad_query,
            grad_key,
            grad_value,
            grad_gproj,
            grad_out,
            grad_pkeys,
            grad_pvalues,
            grad_first,
            grad_second,
            grad_dgain,
            grad_gate,
            grad_lift,
            grad_down,
        ),
        "dp",
    )
    ret_out, ret_grad = (
        lax.all_to_all(
            seq_out[arrival].reshape(peers, share, width),
            "dp",
            split_axis=0,
            concat_axis=0,
            tiled=True,
        ),
        lax.all_to_all(
            back_x[arrival].reshape(peers, share, width),
            "dp",
            split_axis=0,
            concat_axis=0,
            tiled=True,
        ),
    )
    undo = jnp.argsort(asked)
    layer_output = ret_out.reshape(count, width)[undo]
    input_grad = ret_grad.reshape(count, width)[undo]
    return (
        layer_output,
        input_grad,
        grad_mgain,
        grad_query,
        grad_key,
        grad_value,
        grad_gproj,
        grad_out,
        grad_pkeys,
        grad_pvalues,
        grad_first,
        grad_second,
        grad_dgain,
        grad_gate,
        grad_lift,
        grad_down,
    )


def solution(mesh):
    chosen = block_body if mesh.shape["dp"] == PEERS else body
    in_specs = (
        P("dp", None),
        P("dp", None),
        P("dp"),
        P("dp"),
        P(None, "dp", "tensor"),
        P(),
        P(None, "tensor"),
        P(None, "tensor"),
        P(None, "tensor"),
        P(None, "tensor"),
        P("tensor", None),
        P(None, "tensor"),
        P(None, "tensor"),
        P("tensor", None, None),
        P("tensor", None, None),
        P(),
        P(None, "tensor"),
        P(None, "tensor"),
        P("tensor", None),
    )
    out_specs = (
        P("dp", None),
        P("dp", None),
        P(),
        P(None, "tensor"),
        P(None, "tensor"),
        P(None, "tensor"),
        P(None, "tensor"),
        P("tensor", None),
        P(None, "tensor"),
        P(None, "tensor"),
        P("tensor", None, None),
        P("tensor", None, None),
        P(),
        P(None, "tensor"),
        P(None, "tensor"),
        P("tensor", None),
    )
    return jax.shard_map(chosen, mesh=mesh, in_specs=in_specs, out_specs=out_specs, check_vma=False)
```

```python
import jax
import jax.numpy as jnp
from jax import lax
from jax.experimental import pallas as pl
from jax.experimental.pallas import tpu as pltpu
from jax.sharding import PartitionSpec as P

HEAD_DIM = 64


EPSILON = 1e-06
MASKED = -1e30


def product(left, right):
    return jnp.dot(left, right, preferred_element_type=jnp.float32)


def norm_forward(value):
    factor = lax.rsqrt(jnp.mean(value * value, axis=-1, keepdims=True) + EPSILON)
    return (value * factor, factor)


def norm_backward(grad, normed, factor, gain):
    inner = grad * gain
    back = factor * (inner - normed * jnp.mean(inner * normed, axis=-1, keepdims=True))
    return (back, jnp.sum(grad * normed, axis=0))


F32, BF16 = jnp.float32, jnp.bfloat16
PAIR = 2 * HEAD_DIM
ROWS = 256
STRETCH = 64


def nn(a, b):
    return lax.dot_general(a, b, (((1,), (0,)), ((), ())), preferred_element_type=F32)


def nt(a, b):
    return lax.dot_general(a, b, (((1,), (1,)), ((), ())), preferred_element_type=F32)


def tn(a, b):
    return lax.dot_general(a, b, (((0,), (0,)), ((), ())), preferred_element_type=F32)


def sigmoid(v):
    return 1.0 / (1.0 + jnp.exp(-v))


def lanes_of(half, rows=1):
    return (lax.broadcasted_iota(jnp.int32, (rows, PAIR), 1) // HEAD_DIM) == half


def keep(value, half):
    return jnp.where(lanes_of(half), value, jnp.zeros_like(value))


def both(value):
    return jnp.concatenate([keep(value, 0), keep(value, 1)], axis=0)


def joined(stacked):
    rows = stacked.shape[0] // 2
    return jnp.where(lanes_of(0), stacked[:rows], stacked[rows:])


def scaled(pair, scalars):
    return jnp.concatenate([pair[:HEAD_DIM] * scalars[0], pair[HEAD_DIM:] * scalars[1]], axis=0)


def same_sequence(starts, early, late, per):
    count = jnp.int32(0)
    for c in range(early * per + 1, late * per + 1):
        count = count + starts[c]
    return count == 0


def earlier(s, starts, kb, qb, per):
    open_all = jnp.where(same_sequence(starts, kb, qb, per), 0.0, MASKED).astype(F32)
    open_head = jnp.where(starts[kb * per] > 0, MASKED, open_all).astype(F32)
    row = lax.broadcasted_iota(jnp.int32, (STRETCH, s.shape[1]), 0)
    top = s[:STRETCH] + jnp.where(row < STRETCH - 1, open_head, open_all)
    return jnp.concatenate([top, s[STRETCH:] + open_all], axis=0)


def fill_diagonal(ref, start):
    key = lax.broadcasted_iota(jnp.int32, ref.shape, 0)
    query = lax.broadcasted_iota(jnp.int32, ref.shape, 1)
    plain = jnp.where(key <= query, 0.0, MASKED)
    opening = jnp.where((key == query) | ((key < query) & (key >= STRETCH - 1)), 0.0, MASKED)
    ref[...] = jnp.where(start > 0, opening, plain).astype(F32)


def forward_kernel(
    starts, rates, tok, gain, w, pk, pvt, first, second,
    h1, q, k, v, gate, recall, mixed, kt, lse, a_all, c_all, pre_all, e_all, u_all, atth,
    vt, att, diagonal, a_s, c_s, sa_s, sc_s,
):
    count = tok.shape[0]
    pairs = first.shape[0]
    wide = pairs * PAIR
    per = ROWS // STRETCH

    def project(b, _):
        rows = pl.ds(pl.multiple_of(b * ROWS, ROWS), ROWS)
        x = tok[rows, :].astype(F32)
        factor = lax.rsqrt(jnp.mean(x * x, axis=-1, keepdims=True) + EPSILON)
        h = (x * factor * gain[...]).astype(BF16)
        h1[rows, :] = h
        for part, ref in ((0, q), (1, k), (2, v)):
            made = nn(h, w[:, part * wide:(part + 1) * wide])
            low = made.astype(BF16)
            for p in range(pairs):
                ref[p, rows, :] = low[:, p * PAIR:(p + 1) * PAIR]
            if part > 0:
                made_t = jnp.transpose(made).astype(BF16)
                target = kt if part == 1 else vt
                for h_i in range(2 * pairs):
                    target[h_i, :, rows] = made_t[h_i * HEAD_DIM:(h_i + 1) * HEAD_DIM]
        g = sigmoid(nn(h, w[:, 3 * wide:]))
        for p in range(pairs):
            gate[p, rows, :] = g[:, p * PAIR:(p + 1) * PAIR]
        return 0

    lax.fori_loop(0, count // ROWS, project, 0)
    a_s[...] = first[...]
    c_s[...] = second[...]
    sa_s[...] = jnp.zeros_like(sa_s)
    sc_s[...] = jnp.zeros_like(sc_s)

    def memory_step(t):
        rows = pl.ds(pl.multiple_of(t * STRETCH, STRETCH), STRETCH)
        fresh = starts[t] > 0
        for p in range(pairs):
            a = jnp.where(fresh, first[p], a_s[p])
            c = jnp.where(fresh, second[p], c_s[p])
            sa = jnp.where(fresh, 0.0, sa_s[p])
            sc = jnp.where(fresh, 0.0, sc_s[p])
            ab, cb = a.astype(BF16), c.astype(BF16)
            a_all[t, p] = ab
            c_all[t, p] = cb
            km = both(k[p, rows, :])
            lhs = jnp.concatenate([both(q[p, rows, :]), km], axis=0)
            pre = nn(lhs, ab)
            pre_all[t, p] = pre
            sig = sigmoid(pre)
            act = pre * sig
            actb = act.astype(BF16)
            out = nt(actb, cb)
            recall[p, rows, :] = joined(out[:PAIR])
            e = joined(out[PAIR:]) - v[p, rows, :].astype(F32)
            eb = e.astype(BF16)
            e_all[p, rows, :] = eb
            em = both(eb)
            u = nn(em, cb)
            u_all[t, p] = u
            sigk, actk = sig[PAIR:], act[PAIR:]
            wgt = (u * (sigk + actk * (1.0 - sigk))).astype(BF16)
            ga = tn(km, wgt)
            gc = tn(em, actb[PAIR:])
            th = [rates[0, t, 2 * p + i] * (1.0 / STRETCH) for i in range(2)]
            eta = [rates[1, t, 2 * p + i] for i in range(2)]
            al = [1.0 - rates[2, t, 2 * p + i] for i in range(2)]
            sa = scaled(sa, eta) - scaled(ga, th)
            sc = scaled(sc, eta) - scaled(gc, th)
            sa_s[p] = sa
            sc_s[p] = sc
            a_s[p] = scaled(a, al) + sa
            c_s[p] = scaled(c, al) + sc

    def attention_unit(qb, head):
        p, half = head // 2, head % 2
        rows = pl.ds(qb * ROWS, ROWS)
        qh = keep(q[p, rows, :], half) * jnp.asarray(HEAD_DIM ** -0.5, BF16)
        scores = []
        for kb in range(qb + 1):
            s = nt(k[p, kb * ROWS:(kb + 1) * ROWS, :], qh)
            if kb == qb:
                s = s + diagonal[...]
            else:
                s = earlier(s, starts, kb, qb, per)
            scores.append(s)
        sp = nt(pk[p], qh)
        peak = jnp.max(sp, axis=0, keepdims=True)
        for s in scores:
            peak = jnp.maximum(peak, jnp.max(s, axis=0, keepdims=True))
        ep = jnp.exp(sp - peak)
        total = jnp.sum(ep, axis=0, keepdims=True)
        out = nn(pvt[head], ep.astype(BF16))
        for kb, s in enumerate(scores):
            e = jnp.exp(s - peak)
            total = total + jnp.sum(e, axis=0, keepdims=True)
            out = out + nn(vt[head, :, kb * ROWS:(kb + 1) * ROWS], e.astype(BF16))
        att[head, :, rows] = out * (1.0 / total)
        lse[head, :, rows] = peak + jnp.log(total)

    heads = 2 * pairs
    for qb in range(count // ROWS):
        fill_diagonal(diagonal, starts[qb * per])

        def run(i, _, qb=qb):
            memory_step(qb * per + i)
            attention_unit(qb, i)
            return 0
        lax.fori_loop(0, per, run, 0)
    for b in range(count // ROWS):
        rows = pl.ds(b * ROWS, ROWS)
        for p in range(pairs):
            got = jnp.concatenate([att[2 * p, :, rows], att[2 * p + 1, :, rows]], axis=0)
            wide_att = jnp.transpose(got)
            atth[p, rows, :] = wide_att
            mixed[rows, p * PAIR:(p + 1) * PAIR] = (wide_att + gate[p, rows, :] * recall[p, rows, :]).astype(BF16)


def backward_kernel(
    starts, rates, bm, q, k, v, gate, recall, kt, pk, pkt, pv, lse, a_all, c_all, pre_all, e_all, u_all, atth,
    dq, dk, dv, dg, dpk, dpv, dfirst, dsecond,
    dqt, dd, dks, dvs, mq, bmp, diagonal, da_s, dc_s, dsa_s, dsc_s,
):
    count = bm.shape[0]
    pairs = q.shape[0]
    heads = 2 * pairs
    per = ROWS // STRETCH
    nblocks = count // ROWS
    ones = [jnp.where(lanes_of(i, 8), 1.0, 0.0).astype(F32) for i in range(2)]
    for b in range(nblocks):
        rows = pl.ds(b * ROWS, ROWS)
        for p in range(pairs):
            gb = bm[rows, p * PAIR:(p + 1) * PAIR]
            bmp[p, rows, :] = gb
            g = gb.astype(F32)
            inner = g * atth[p, rows, :]
            for i in range(2):
                row = lax.dot_general(ones[i], inner, (((1,), (1,)), ((), ())), precision=lax.Precision.HIGHEST, preferred_element_type=F32)
                dd[2 * p + i, :, rows] = row[:1]
            gt = gate[p, rows, :]
            dg[rows, p * PAIR:(p + 1) * PAIR] = (g * recall[p, rows, :] * gt * (1.0 - gt)).astype(BF16)
    for ref in (dpk, dpv, dfirst, dsecond, dks, dvs, da_s, dc_s, dsa_s, dsc_s):
        ref[...] = jnp.zeros_like(ref)

    def memory_step(t):
        rows = pl.ds(pl.multiple_of(t * STRETCH, STRETCH), STRETCH)
        fresh = starts[t] > 0
        for p in range(pairs):
            th = [rates[0, t, 2 * p + i] * (-1.0 / STRETCH) for i in range(2)]
            eta = [rates[1, t, 2 * p + i] for i in range(2)]
            al = [1.0 - rates[2, t, 2 * p + i] for i in range(2)]
            da, dc = da_s[p], dc_s[p]
            dsa = dsa_s[p] + da
            dsc = dsc_s[p] + dc
            dga = scaled(dsa, th).astype(BF16)
            dgc = scaled(dsc, th).astype(BF16)
            ab, cb = a_all[t, p], c_all[t, p]
            km, qm = both(k[p, rows, :]), both(q[p, rows, :])
            em = both(e_all[p, rows, :])
            pre = pre_all[t, p]
            sig = sigmoid(pre)
            act = pre * sig
            actb = act.astype(BF16)
            slope = sig + act * (1.0 - sig)
            sigk, prek, slopek = sig[PAIR:], pre[PAIR:], slope[PAIR:]
            u = u_all[t, p]
            curve = sigk * (1.0 - sigk) * (2.0 + prek * (1.0 - 2.0 * sigk))
            wgt = (u * slopek).astype(BF16)
            back = bmp[p, rows, :].astype(F32) * gate[p, rows, :]
            rm = both(back.astype(BF16))
            dpre_q = (nn(rm, cb) * slope[:PAIR]).astype(BF16)
            mq[0, p, rows, :] = joined(nt(dpre_q, ab))
            dw = nn(km, dga)
            du = (dw * slopek).astype(BF16)
            cc = jnp.concatenate([dgc, cb], axis=1)
            de = joined(nt(jnp.concatenate([actb[PAIR:], du], axis=1), cc))
            mq[2, p, rows, :] = -de
            dem = both(de.astype(BF16))
            dsk = nn(jnp.concatenate([em, dem], axis=1), jnp.concatenate([dgc, cb], axis=0))
            dpre = (dsk * slopek + dw * u * curve).astype(BF16)
            mq[1, p, rows, :] = joined(nt(jnp.concatenate([wgt, dpre], axis=1), jnp.concatenate([dga, ab], axis=1)))
            ga = tn(jnp.concatenate([km, qm], axis=0), jnp.concatenate([dpre, dpre_q], axis=0))
            gc = tn(jnp.concatenate([em, dem], axis=0), jnp.concatenate([du, actb[PAIR:]], axis=0))
            gc = gc + tn(rm, actb[:PAIR])
            da = scaled(da, al) + ga
            dc = scaled(dc, al) + gc
            dfirst[p] = dfirst[p] + jnp.where(fresh, da, 0.0)
            dsecond[p] = dsecond[p] + jnp.where(fresh, dc, 0.0)
            da_s[p] = jnp.where(fresh, 0.0, da)
            dc_s[p] = jnp.where(fresh, 0.0, dc)
            dsa_s[p] = jnp.where(fresh, 0.0, scaled(dsa, eta))
            dsc_s[p] = jnp.where(fresh, 0.0, scaled(dsc, eta))

    def attention_unit(qb, head):
        p, half = head // 2, head % 2
        rows = pl.ds(qb * ROWS, ROWS)
        qh = keep(q[p, rows, :], half) * jnp.asarray(HEAD_DIM ** -0.5, BF16)
        gh = keep(bmp[p, rows, :], half)
        lrow, drow = lse[head, :, rows], dd[head, :, rows]
        acc = jnp.zeros((HEAD_DIM, ROWS), F32)
        for kb in range(qb + 1):
            krows = slice(kb * ROWS, (kb + 1) * ROWS)
            s = nt(k[p, krows, :], qh) - lrow
            if kb == qb:
                s = s + diagonal[...]
            else:
                s = earlier(s, starts, kb, qb, per)
            prob = jnp.exp(s)
            ds = (prob * (nt(v[p, krows, :], gh) - drow)).astype(BF16)
            dvs[p, krows, :] = dvs[p, krows, :] + nn(prob.astype(BF16), gh)
            dks[p, krows, :] = dks[p, krows, :] + nn(ds, qh)
            acc = acc + nn(kt[head, :, krows], ds)
        prob = jnp.exp(nt(pk[p], qh) - lrow)
        ds = (prob * (nt(pv[p], gh) - drow)).astype(BF16)
        dpv[p] = dpv[p] + nn(prob.astype(BF16), gh)
        dpk[p] = dpk[p] + nn(ds, qh)
        acc = acc + nn(pkt[head], ds)
        dqt[head, :, rows] = acc * (HEAD_DIM ** -0.5)

    for qb in reversed(range(nblocks)):
        fill_diagonal(diagonal, starts[qb * per])

        def run(i, _, qb=qb):
            memory_step(qb * per + per - 1 - i)
            attention_unit(qb, i)
            return 0
        lax.fori_loop(0, per, run, 0)
    for b in range(nblocks):
        rows = pl.ds(b * ROWS, ROWS)
        for p in range(pairs):
            cols = slice(p * PAIR, (p + 1) * PAIR)
            got = jnp.concatenate([dqt[2 * p, :, rows], dqt[2 * p + 1, :, rows]], axis=0)
            dq[rows, cols] = (jnp.transpose(got) + mq[0, p, rows, :]).astype(BF16)
            dk[rows, cols] = (dks[p, rows, :] + mq[1, p, rows, :]).astype(BF16)
            dv[rows, cols] = (dvs[p, rows, :] + mq[2, p, rows, :]).astype(BF16)


def shape(*dims, dtype=F32):
    return jax.ShapeDtypeStruct(dims, dtype)


VMEM = pl.BlockSpec(memory_space=pltpu.VMEM)
SMEM = pl.BlockSpec(memory_space=pltpu.SMEM)
LIMIT = 56 * 1024 * 1024


def mixer_forward(starts, rates, tok, gain, w, pk, pvt, first, second):
    count, width = tok.shape
    pairs = first.shape[0]
    heads, steps = 2 * pairs, starts.shape[0]
    flat = lambda dtype: shape(pairs, count, PAIR, dtype=dtype)
    outs = (
        shape(count, width, dtype=BF16), flat(BF16), flat(BF16), flat(BF16), flat(F32), flat(F32),
        shape(count, pairs * PAIR, dtype=BF16), shape(heads, HEAD_DIM, count, dtype=BF16), shape(heads, 1, count),
        shape(steps, pairs, PAIR, PAIR, dtype=BF16), shape(steps, pairs, PAIR, PAIR, dtype=BF16),
        shape(steps, pairs, 2 * PAIR, PAIR), flat(BF16), shape(steps, pairs, PAIR, PAIR), flat(F32),
    )
    state = pltpu.VMEM((pairs, PAIR, PAIR), F32)
    return pl.pallas_call(
        forward_kernel,
        out_shape=outs,
        in_specs=[SMEM, SMEM] + [VMEM] * 7,
        out_specs=[VMEM] * len(outs),
        scratch_shapes=[
            pltpu.VMEM((heads, HEAD_DIM, count), BF16), pltpu.VMEM((heads, HEAD_DIM, count), F32),
            pltpu.VMEM((ROWS, ROWS), F32), state, state, state, state,
        ],
        compiler_params=pltpu.CompilerParams(vmem_limit_bytes=LIMIT),
        name="mixer_forward",
    )(starts, rates, tok, gain, w, pk, pvt, first, second)


def mixer_backward(starts, rates, bm, q, k, v, gate, recall, kt, pk, pkt, pv, lse, a_all, c_all, pre_all, e_all, u_all, atth):
    count, wide = bm.shape
    pairs = q.shape[0]
    heads = 2 * pairs
    outs = (
        shape(count, wide, dtype=BF16), shape(count, wide, dtype=BF16), shape(count, wide, dtype=BF16), shape(count, wide, dtype=BF16),
        shape(*pk.shape), shape(*pv.shape), shape(pairs, PAIR, PAIR), shape(pairs, PAIR, PAIR),
    )
    state = pltpu.VMEM((pairs, PAIR, PAIR), F32)
    flat = pltpu.VMEM((pairs, count, PAIR), F32)
    return pl.pallas_call(
        backward_kernel,
        out_shape=outs,
        in_specs=[SMEM, SMEM] + [VMEM] * 17,
        out_specs=[VMEM] * len(outs),
        scratch_shapes=[
            pltpu.VMEM((heads, HEAD_DIM, count), F32), pltpu.VMEM((heads, 1, count), F32), flat, flat,
            pltpu.VMEM((3, pairs, count, PAIR), F32), pltpu.VMEM((pairs, count, PAIR), BF16),
            pltpu.VMEM((ROWS, ROWS), F32), state, state, state, state,
        ],
        compiler_params=pltpu.CompilerParams(vmem_limit_bytes=LIMIT),
        name="mixer_backward",
    )(starts, rates, bm, q, k, v, gate, recall, kt, pk, pkt, pv, lse, a_all, c_all, pre_all, e_all, u_all, atth)


MESH = pl.DeviceIdType.MESH
HALF_SHARE = 32
PEERS = 16


def place():
    return lax.axis_index("dp"), lax.axis_index("tensor")


def flipped(index, mask):
    result = index
    bit = 1
    while bit <= mask:
        if mask & bit:
            result = result + bit * (1 - 2 * (lax.div(index, bit) % 2))
        bit *= 2
    return result


def greet(devices):
    for device in devices:
        pl.semaphore_signal(pltpu.get_barrier_semaphore(), inc=1, device_id=device, device_id_type=MESH)


def greeted(devices):
    pl.semaphore_wait(pltpu.get_barrier_semaphore(), len(devices))


def remote(src, dst, send_sem, recv_sem, device):
    return pltpu.make_async_remote_copy(
        src_ref=src, dst_ref=dst, send_sem=send_sem, recv_sem=recv_sem, device_id=device, device_id_type=MESH
    )


def iota(rows, columns, dimension):
    return lax.broadcasted_iota(jnp.int32, (rows, columns), dimension)


def at_rows(start, size):
    return pl.ds(pl.multiple_of(start, size), size)


def lot(peer):
    return peer % 2 * (PEERS // 2) + lax.div(peer, 2) % 2 * (PEERS // 4) + lax.div(peer, 4)


QUARTERS = tuple(tuple(range(first, PEERS, 4)) for first in (0, 2, 1, 3))
ALL_PEERS = sum(QUARTERS, ())


def spreading(ref, dp, t, side, sent, sems, m):
    peer = flipped(dp, m)
    return remote(
        sent.at[at_rows(lot(peer) * HALF_SHARE, HALF_SHARE)], ref.at[at_rows(side * (PEERS * HALF_SHARE) + lot(dp) * HALF_SHARE, HALF_SHARE)],
        sems.at[0, m], sems.at[1, m], (peer, t),
    )


def spread(ref, dp, t, side, sent, sems, masks):
    for m in masks:
        if m:
            spreading(ref, dp, t, side, sent, sems, m).start()
        else:
            here = lot(dp) * HALF_SHARE
            ref[at_rows(side * (PEERS * HALF_SHARE) + here, HALF_SHARE), :] = sent[at_rows(here, HALF_SHARE), :]


def pass_on(ref, dp, t, sent, sems, y_sems, masks):
    for m in masks:
        if m:
            spreading(ref, dp, t, t, sent, sems, m).wait()
        passing(ref, dp, t, m, y_sems).start()


def passing(ref, dp, t, m, sems):
    rows = at_rows(t * (PEERS * HALF_SHARE) + lot(flipped(dp, m)) * HALF_SHARE, HALF_SHARE)
    return remote(ref.at[rows], ref.at[rows], sems.at[0, m], sems.at[1, m], (dp, 1 - t))


def passed_on(ref, dp, t, sems):
    for m in range(PEERS):
        passing(ref, dp, t, m, sems).wait()


def weave(chains, filler, per_stage, between):
    chains = list(chains)
    end = object()
    while chains:
        live = []
        for i, chain in enumerate(chains):
            if next(chain, end) is not end:
                live.append(chain)
            if between:
                for _ in range((per_stage + i) // len(chains)):
                    next(filler, end)
        chains = live
        if not between:
            for _ in range(per_stage):
                next(filler, end)
    for _ in filler:
        pass


def sixteens(start, size):
    return pl.ds(pl.multiple_of(start, 16), size)


class Sum:
    def __init__(self, dp, t, src, base, out, order, scratch):
        self.dp, self.t, self.src, self.base, self.out, self.order = dp, t, src, base, out, order
        n = len(order)
        self.acc, self.sems = scratch[0], scratch[1]
        self.rcv = scratch[2:2 + n]
        self.snd = (None,) + tuple(scratch[2 + n:1 + 2 * n])
        self.at = [lax.div(dp, stride) % size for stride, size in order]
        self.rows = [out.shape[0]]
        self.start = [0]
        for (stride, size), c in zip(order, self.at):
            self.rows.append(self.rows[-1] // size)
            self.start.append(self.start[-1] + c * self.rows[-1])
        self.next = 0

    @staticmethod
    def scratch(rows, lanes, order):
        counts, sizes = [], [rows]
        for stride, size in order:
            sizes.append(sizes[-1] // size)
            counts.append(size - 1)
        blocks = [pltpu.VMEM((count, size, lanes), BF16) for count, size in zip(counts, sizes[1:])]
        return [pltpu.VMEM((sizes[1], lanes), BF16), pltpu.SemaphoreType.DMA((2, 2 * sum(counts)))] + blocks + blocks[1:]

    @staticmethod
    def refs(order):
        return 1 + 2 * len(order)

    def peer(self, s, k):
        stride, size = self.order[s]
        d = (self.at[s] + k) % size
        return d, self.dp + stride * (d - self.at[s])

    def copies(self, n):
        made = []
        stages = len(self.order)
        counts = [size - 1 for _, size in self.order]
        s = n if n < stages else 2 * stages - 1 - n
        for k in range(1, self.order[s][1]):
            d, peer = self.peer(s, k)
            if n >= stages:
                src = dst = self.out.at[sixteens(self.start[s + 1], self.rows[s + 1])]
            else:
                src = self.snd[s].at[k - 1] if s else self.src.at[sixteens(self.base + d * self.rows[1], self.rows[1])]
                dst = self.rcv[s].at[k - 1]
            i = sum(counts[:s]) + k - 1 + (sum(counts) if n >= stages else 0)
            made.append(remote(src, dst, self.sems.at[0, i], self.sems.at[1, i], (peer, self.t)))
        return made

    def added(self, own, s, rows):
        count = self.order[s][1] - 1
        if count == 1:
            return own + self.rcv[s][0, rows, :]
        total = own.astype(F32)
        for j in range(count):
            total = total + self.rcv[s][j, rows, :].astype(F32)
        return total.astype(BF16)

    def step(self):
        n, stages = self.next, len(self.order)
        self.next += 1
        if n:
            for copy in self.copies(n - 1):
                copy.wait()
        if 0 < n < stages:
            size = self.rows[n + 1]
            inside = self.start[n] - self.start[1]
            for k in list(range(1, self.order[n][1])) + [0]:
                d, _ = self.peer(n, k)
                here = sixteens(inside + d * size, size)
                own = self.src[sixteens(self.base + self.start[1] + d * size, size), :] if n == 1 else self.acc[here, :]
                total = self.added(own, n - 1, sixteens(d * size, size))
                if k:
                    self.snd[n][k - 1] = total
                else:
                    self.acc[here, :] = total
        if n == stages:
            size = self.rows[stages]
            own = self.acc[sixteens(self.start[stages] - self.start[1], size), :]
            self.out[sixteens(self.start[stages], size), :] = self.added(own, stages - 1, pl.ds(0, size))
        if n < 2 * stages:
            for copy in self.copies(n):
                copy.start()


ANY = pl.BlockSpec(memory_space=pl.ANY)
LONG_ORDER = ((1, 2), (2, 2), (4, 2), (8, 2))
XZ_ORDER = ((1, 2), (2, 2), (4, 4))
ZX_ORDER = ((1, 2), (4, 4), (2, 2))
SUM_ORDERS = (LONG_ORDER, LONG_ORDER, XZ_ORDER, ZX_ORDER)


def mega_kernel(
    starts, rates, idx, tok_in, cot_in, gain1, wq_in, wk_in, wv_in, wg_in, op_in, pk_in, pv_in, first, second, gain2, dgw_in, dlw_in, ddw_in,
    fa_out, fb_out, qa_out, qb_out, gains_out, ret,
    xs, cs, mx, ops, asked, want, sent_c, g, gt, h1, q, k, v, gate, recall, kt, lse, a_all, c_all, pre_all, e_all, u_all, atth,
    pk, pv, pkt, pvt, bmp, diagonal, br, own_s, ps_s, pb_r, bms, facc, gout, gother, dgain,
    second_r, gother_r, rec_l, rec_x, part_r, src_b, src_c, out_a, out_b, out_c1, out_c2, gains_s, gains_r,
    a_s, c_s, sa_s, sc_s, wq, wk, wv, wg, op, dgw, dlw, ddw,
    in_sems, ask_sems, t_sems, ty_sems, c_sems, m_sems, d_sems, y_sems, l_sems, ly_sems, x_sems, xy_sems, g_sems, o_sems,
    *sums,
):
    dp, t = place()
    other = (dp, 1 - t)
    core = dp % 2
    count, width = xs.shape
    half = count // 2
    pairs = first.shape[0]
    heads = 2 * pairs
    wide = pairs * PAIR
    few = pk_in.shape[0]
    per = ROWS // STRETCH
    nblocks = count // ROWS
    hidden = dgw.shape[0]
    padded = facc.shape[0] // 3
    scale = HEAD_DIM ** -0.5

    rows_a = out_a.shape[0]
    rest = facc.shape[0] - rows_a
    cuts = [0]
    for order in SUM_ORDERS:
        cuts.append(cuts[-1] + Sum.refs(order))
    sum_a, sum_b, sum_c1, sum_c2 = [
        Sum(dp, t, src, base, out, order, sums[cuts[i]:cuts[i + 1]])
        for i, (src, base, out, order) in enumerate((
            (facc, 0, out_a, SUM_ORDERS[0]), (src_b, 0, out_b, SUM_ORDERS[1]),
            (src_c, 0, out_c1, SUM_ORDERS[2]), (src_c, out_c1.shape[0], out_c2, SUM_ORDERS[3]),
        ))
    ]

    def second_copy(i):
        src, dst = ((ps_s, second_r), (gother, gother_r))[i]
        return remote(src, dst, y_sems.at[0, i], y_sems.at[1, i], other)

    weights = [
        pltpu.make_async_copy(src, dst, in_sems.at[2 + i])
        for i, (src, dst) in enumerate((
            (wq_in, wq), (wk_in, wk), (wv_in, wv), (wg_in, wg), (op_in, op), (dgw_in, dgw), (dlw_in, dlw), (ddw_in, ddw),
        ))
    ]
    friends = [(flipped(dp, m), t) for m in range(1, PEERS)] + [other]
    greet(friends)
    def enter(tok, cot, sent_t):
        reads = [pltpu.make_async_copy(src, dst, in_sems.at[i]) for i, (src, dst) in enumerate(((tok_in, tok), (cot_in, cot)))]
        for read in reads + weights:
            read.start()
        index = idx[...]
        dev = lax.div(index, count)
        row = index - dev * count
        held = jnp.where(iota(PEERS, count, 0) == dev, 1.0, 0.0).astype(BF16)
        upper = jnp.where(iota(PAIR, PAIR, 0) < iota(PAIR, PAIR, 1), 1.0, 0.0).astype(BF16)
        run = jnp.zeros((PEERS, 1), F32)
        ranks = []
        for c in range(count // PAIR):
            part = held[:, c * PAIR:(c + 1) * PAIR]
            wide_part = part.astype(F32)
            ranks.append(jnp.sum(wide_part * (nn(part, upper) + run), axis=0, keepdims=True))
            run = run + jnp.sum(wide_part, axis=1, keepdims=True)
        rank = jnp.concatenate(ranks, axis=1)
        column = jnp.transpose(jnp.broadcast_to(rank, (PAIR, count)))
        pick = jnp.where(column == iota(count, PAIR, 1).astype(F32), 1.0, 0.0).astype(BF16)
        high = lax.div(row, 32)
        low = row - high * 32
        held_wide = held.astype(F32)
        wanted = 32.0 * nn((held_wide * high.astype(F32)).astype(BF16), pick) + nn((held_wide * low.astype(F32)).astype(BF16), pick)
        for j in range(PEERS):
            want[j] = jnp.broadcast_to(wanted[j:j + 1], (8, PAIR))
        greeted(friends)
        asks = []
        for m in range(1, PEERS):
            peer = flipped(dp, m)
            copy = remote(want.at[peer], asked.at[dp], ask_sems.at[0, m], ask_sems.at[1, m], (peer, t))
            copy.start()
            asks.append(copy)
        asked[dp] = want[dp]
        rank_i = rank.astype(jnp.int32)
        half_of = lax.div(rank_i, HALF_SHARE)
        slot = half_of * (half - HALF_SHARE) + lot(dev) * HALF_SHARE + rank_i
        for c in range(count // ROWS):
            gt[c * ROWS:(c + 1) * ROWS, :] = jnp.where(iota(ROWS, count, 0) + c * ROWS == slot, 1.0, 0.0).astype(BF16)
        slots = jnp.transpose(jnp.broadcast_to(slot.astype(F32), (PAIR, count)))
        for copy in asks:
            copy.wait()
        asks_in = asked[:, 0, :]
        asks_high = jnp.floor(asks_in * (1.0 / 32.0))
        asks_low = asks_in - 32.0 * asks_high
        owner = jnp.where(lax.div(iota(half, PEERS, 0), HALF_SHARE) == lot(iota(half, PEERS, 1)), 1.0, 0.0).astype(BF16)
        ones = jnp.ones((PAIR, PAIR), BF16)

        def choose(side):
            lane = iota(half, PAIR, 1) == iota(half, PAIR, 0) % HALF_SHARE + side * HALF_SHARE
            value = jnp.zeros((half, PAIR), F32)
            for digit, weight in ((asks_high, 32.0), (asks_low, 1.0)):
                picked = jnp.where(lane, nn(owner, digit.astype(BF16)), 0.0).astype(BF16)
                value = value + weight * nn(picked, ones)
            return jnp.concatenate(
                [jnp.where(value == (iota(half, PAIR, 1) + c * PAIR).astype(F32), 1.0, 0.0).astype(BF16) for c in range(count // PAIR)], axis=1
            )

        chosen = choose(t)
        for read in reads + weights:
            read.wait()
        sent_t[...] = nn(chosen, tok[...]).astype(BF16)
        spread(xs, dp, t, t, sent_t, t_sems, ALL_PEERS)
        sent_c[0] = nn(chosen, cot[...]).astype(BF16)
        sent_c[1] = nn(choose(1 - t), cot[...]).astype(BF16)
        for c in range(count // PAIR):
            g[:, c * PAIR:(c + 1) * PAIR] = jnp.where(slots == (iota(count, PAIR, 1) + c * PAIR).astype(F32), 1.0, 0.0).astype(BF16)
        for half_i in range(2):
            for ref_in, by_pair, by_head in ((pk_in, pk, pkt), (pv_in, pv, pvt)):
                part = ref_in[:, half_i * PAIR:(half_i + 1) * PAIR]
                by_pair[half_i] = part
                flat = jnp.transpose(part.astype(F32)).astype(BF16)
                by_head[2 * half_i] = flat[:HEAD_DIM]
                by_head[2 * half_i + 1] = flat[HEAD_DIM:]
        pass_on(xs, dp, t, sent_t, t_sems, ty_sems, ALL_PEERS)
        passed_on(xs, dp, t, ty_sems)

    pl.run_scoped(enter, pltpu.VMEM((count, width), BF16), pltpu.VMEM((count, width), BF16), pltpu.VMEM((half, width), BF16))

    def ops_copy():
        return remote(ops.at[t], ops.at[t], m_sems.at[0, nblocks], m_sems.at[1, nblocks], other)

    def mixed_copy(qb):
        rows = pl.ds(qb * ROWS, ROWS)
        return remote(mx.at[t, rows], mx.at[t, rows], m_sems.at[0, qb], m_sems.at[1, qb], other)

    ops[t] = op[...]
    ops_copy().start()
    for i, side in enumerate((t, 1 - t)):
        spread(cs, dp, t, side, sent_c.at[i], c_sems.at[i], ALL_PEERS)

    def forward(vt, att):
        def project(b, _):
            rows = pl.ds(pl.multiple_of(b * ROWS, ROWS), ROWS)
            x = nn(g[rows, :], xs[...])
            factor = lax.rsqrt(jnp.mean(x * x, axis=-1, keepdims=True) + EPSILON)
            h = (x * factor * gain1[...]).astype(BF16)
            h1[rows, :] = h
            for part, (ref, w) in enumerate(((q, wq), (k, wk), (v, wv))):
                made = nn(h, w[...])
                low = made.astype(BF16)
                for p in range(pairs):
                    ref[p, rows, :] = low[:, p * PAIR:(p + 1) * PAIR]
                if part > 0:
                    made_t = jnp.transpose(made).astype(BF16)
                    target = kt if part == 1 else vt
                    for i in range(heads):
                        target[i, :, rows] = made_t[i * HEAD_DIM:(i + 1) * HEAD_DIM]
            made = sigmoid(nn(h, wg[...]))
            for p in range(pairs):
                gate[p, rows, :] = made[:, p * PAIR:(p + 1) * PAIR]
            return 0

        lax.fori_loop(0, nblocks, project, 0)
        a_s[...] = first[...]
        c_s[...] = second[...]
        sa_s[...] = jnp.zeros_like(sa_s)
        sc_s[...] = jnp.zeros_like(sc_s)

        def memory_step(n, p):
            rows = pl.ds(pl.multiple_of(n * STRETCH, STRETCH), STRETCH)
            fresh = starts[n] > 0
            a = jnp.where(fresh, first[p], a_s[p])
            ab = a.astype(BF16)
            km = both(k[p, rows, :])
            pre = nn(jnp.concatenate([both(q[p, rows, :]), km], axis=0), ab)
            yield
            c = jnp.where(fresh, second[p], c_s[p])
            cb = c.astype(BF16)
            a_all[n, p] = ab
            c_all[n, p] = cb
            pre_all[n, p] = pre
            sig = sigmoid(pre)
            act = pre * sig
            actb = act.astype(BF16)
            out = nt(actb, cb)
            yield
            eb = (joined(out[PAIR:]) - v[p, rows, :].astype(F32)).astype(BF16)
            em = both(eb)
            u = nn(em, cb)
            gc = tn(em, actb[PAIR:])
            yield
            recall[p, rows, :] = joined(out[:PAIR])
            e_all[p, rows, :] = eb
            sigk, actk = sig[PAIR:], act[PAIR:]
            ga = tn(km, (u * (sigk + actk * (1.0 - sigk))).astype(BF16))
            yield
            u_all[n, p] = u.astype(BF16)
            th = [rates[0, 2 * p + i, n] * (1.0 / STRETCH) for i in range(2)]
            eta = [rates[1, 2 * p + i, n] for i in range(2)]
            al = [1.0 - rates[2, 2 * p + i, n] for i in range(2)]
            sc = scaled(jnp.where(fresh, 0.0, sc_s[p]), eta) - scaled(gc, th)
            sc_s[p] = sc
            c_s[p] = scaled(c, al) + sc
            sa = scaled(jnp.where(fresh, 0.0, sa_s[p]), eta) - scaled(ga, th)
            sa_s[p] = sa
            a_s[p] = scaled(a, al) + sa

        def attention_unit(qb, head):
            p, side = head // 2, head % 2
            rows = pl.ds(qb * ROWS, ROWS)
            qh = keep(q[p, rows, :], side) * jnp.asarray(scale, BF16)
            scores = []
            for kb in range(qb + 1):
                s = nt(k[p, kb * ROWS:(kb + 1) * ROWS, :], qh)
                scores.append(s + diagonal[...] if kb == qb else earlier(s, starts, kb, qb, per))
                yield
            sp = nt(pk[p], qh)
            peak = jnp.max(sp, axis=0, keepdims=True)
            for s in scores:
                peak = jnp.maximum(peak, jnp.max(s, axis=0, keepdims=True))
            ep = jnp.exp(sp - peak)
            total = jnp.sum(ep, axis=0, keepdims=True)
            out = nn(pvt[head], ep.astype(BF16))
            yield
            for kb, s in enumerate(scores):
                e = jnp.exp(s - peak)
                total = total + jnp.sum(e, axis=0, keepdims=True)
                out = out + nn(vt[head, :, kb * ROWS:(kb + 1) * ROWS], e.astype(BF16))
                yield
            att[head, :, rows] = out * (1.0 / total)
            lse[head, :, rows] = peak + jnp.log(total)

        for qb in range(nblocks):
            fill_diagonal(diagonal, starts[qb * per])

            def run(i, _, qb=qb):
                weave([memory_step(qb * per + i, p) for p in range(pairs)], attention_unit(qb, i), (qb + 3) // 2, qb > 1)
                return 0

            lax.fori_loop(0, per, run, 0)
            rows = pl.ds(qb * ROWS, ROWS)
            for p in range(pairs):
                got = jnp.transpose(jnp.concatenate([att[2 * p, :, rows], att[2 * p + 1, :, rows]], axis=0))
                atth[p, rows, :] = got.astype(BF16)
                mx[t, rows, p * PAIR:(p + 1) * PAIR] = (got + gate[p, rows, :] * recall[p, rows, :]).astype(BF16)
            mixed_copy(qb).start()

    pl.run_scoped(forward, pltpu.VMEM((heads, HEAD_DIM, count), BF16), pltpu.VMEM((heads, HEAD_DIM, count), F32))

    def dense_part(ms, hid, bgs, bls, bms_s, resid, own_b):
        h2s, pb_s, bf = src_b.at[:count], src_c.at[:half], src_c.at[half:]
        pad = jnp.zeros((count, PAIR), BF16)
        for ref in (hid, bgs, bls):
            ref[:, padded - PAIR:] = pad
        ms[t] = nn(gt[...], mx[t]).astype(BF16)
        ops_copy().wait()
        for qb in range(nblocks):
            mixed_copy(qb).wait()
        for i, side in enumerate((t, 1 - t)):
            for m in ALL_PEERS[1:]:
                spreading(cs, dp, t, side, sent_c.at[i], c_sems.at[i], m).wait()
        ms[1 - t] = nn(gt[...], mx[1 - t]).astype(BF16)

        def chunk(rows, store):
            x = xs[rows, :].astype(F32) + nn(ms[0, rows, :], ops[0]) + nn(ms[1, rows, :], ops[1])
            factor = lax.rsqrt(jnp.mean(x * x, axis=-1, keepdims=True) + EPSILON)
            h2 = (x * factor * gain2[...]).astype(BF16)
            h2s[rows, :] = h2
            for begin in range(0, hidden, ROWS):
                cols = slice(begin, min(begin + ROWS, hidden))
                gated, lifted = nt(h2, dgw[cols, :]), nt(h2, dlw[cols, :])
                sig = sigmoid(gated)
                act = gated * sig
                hid[rows, cols] = (act * lifted).astype(BF16)
                back = nt(cs[rows, :], ddw[cols, :])
                bgs[rows, cols] = (back * lifted * (sig + act * (1.0 - sig))).astype(BF16)
                bls[rows, cols] = (back * act).astype(BF16)
            store(x, nn(bgs[rows, :hidden], dgw[...]) + nn(bls[rows, :hidden], dlw[...]), rows)

        copies = []
        for c in range(half // ROWS):
            here = pl.ds(c * ROWS, ROWS)

            def send(x, back, rows, here=here):
                pb_s[here, :] = back.astype(BF16)

            chunk(at_rows((1 - t) * half + c * ROWS, ROWS), send)
            copy = remote(pb_s.at[here], pb_r.at[here], d_sems.at[0, c], d_sems.at[1, c], other)
            copy.start()
            copies.append(copy)
            ps_s[here, :] = nn(hid[at_rows((1 - t) * half + c * ROWS, ROWS), :hidden], ddw[...]).astype(BF16)
        for c in range(half // ROWS):
            here = pl.ds(c * ROWS, ROWS)

            def hold(x, back, rows, here=here):
                resid[here, :] = x
                own_s[here, :] = x + nn(hid[rows, :hidden], ddw[...])
                own_b[here, :] = back

            chunk(at_rows(t * half + c * ROWS, ROWS), hold)
        facc[:padded, :] = tn(bgs[...], h2s[...]).astype(BF16)
        facc[padded:2 * padded, :] = tn(bls[...], h2s[...]).astype(BF16)
        sum_a.step()
        total = jnp.zeros((8, width), F32)
        back_copies = []
        for c in range(half // ROWS):
            here = pl.ds(c * ROWS, ROWS)
            rows = at_rows(t * half + c * ROWS, ROWS)
            copies[c].wait()
            for b in range(ROWS // STRETCH):
                few_rows = pl.ds(c * ROWS + b * STRETCH, STRETCH)
                x = resid[few_rows, :]
                factor = lax.rsqrt(jnp.mean(x * x, axis=-1, keepdims=True) + EPSILON)
                norm = x * factor
                back = own_b[few_rows, :] + pb_r[few_rows, :].astype(F32)
                inner = back * gain2[...]
                result = cs[at_rows(t * half + c * ROWS + b * STRETCH, STRETCH), :].astype(F32) + factor * (
                    inner - norm * jnp.mean(inner * norm, axis=-1, keepdims=True)
                )
                br[few_rows, :] = result
                bf[few_rows, :] = result.astype(BF16)
                total = total + jnp.sum((back * norm).reshape(STRETCH // 8, 8, width), axis=0)
            low = bf[here, :]
            bms_s[here, :] = nt(low, ops[1 - t]).astype(BF16)
            copy = remote(bms_s.at[here], bms.at[rows], d_sems.at[0, 2 + c], d_sems.at[1, 2 + c], other)
            copy.start()
            back_copies.append(copy)
            bms[rows, :] = nt(low, ops[t]).astype(BF16)
            if c == 0:
                sum_a.step()
        dgain[...] = total
        second_copy(0).start()
        facc[2 * padded:, :] = tn(hid[...], cs[...]).astype(BF16)
        mine = at_rows(t * half, half)
        gout[...] = tn(ms[t, mine, :], bf[...])
        gother[...] = tn(ms[1 - t, mine, :], bf[...]).astype(BF16)
        second_copy(1).start()
        for copy in back_copies:
            copy.wait()
        for b in range(nblocks):
            rows = pl.ds(b * ROWS, ROWS)
            got = nn(g[rows, :], bms[...]).astype(BF16)
            for p in range(pairs):
                bmp[p, rows, :] = got[:, p * PAIR:(p + 1) * PAIR]

    hiddens = pltpu.VMEM((count, padded), BF16)
    pl.run_scoped(
        dense_part, pltpu.VMEM((2, count, wide), BF16), hiddens, hiddens, hiddens, pltpu.VMEM((half, wide), BF16),
        pltpu.VMEM((half, width), F32), pltpu.VMEM((half, width), F32),
    )

    def backward(dqt, dks, dvs, mq, mk, mv, dd, dpk, dpv, dfirst, dsecond, dv, dg):
        lo, part_s, dq, dk, bx = sent_c.at[0], ps_s, mx.at[0], mx.at[1], second_r
        da_s, dc_s, dsa_s, dsc_s = a_s, c_s, sa_s, sc_s
        ones = [jnp.where(lanes_of(i, 8), 1.0, 0.0).astype(BF16) for i in range(2)]
        for b in range(nblocks):
            rows = pl.ds(b * ROWS, ROWS)
            for p in range(pairs):
                gr = bmp[p, rows, :].astype(F32)
                inner = (gr * atth[p, rows, :].astype(F32)).astype(BF16)
                for i in range(2):
                    dd[2 * p + i, :, rows] = nt(ones[i], inner)[:1]
                gv = gate[p, rows, :]
                dg[rows, p * PAIR:(p + 1) * PAIR] = (gr * recall[p, rows, :] * gv * (1.0 - gv)).astype(BF16)
        for ref in (dpk, dpv, dfirst, dsecond, dks, dvs, da_s, dc_s, dsa_s, dsc_s):
            ref[...] = jnp.zeros_like(ref)

        def memory_step(n, p):
            rows = pl.ds(pl.multiple_of(n * STRETCH, STRETCH), STRETCH)
            fresh = starts[n] > 0
            th = [rates[0, 2 * p + i, n] * (-1.0 / STRETCH) for i in range(2)]
            eta = [rates[1, 2 * p + i, n] for i in range(2)]
            al = [1.0 - rates[2, 2 * p + i, n] for i in range(2)]
            da, dc = da_s[p], dc_s[p]
            dsa = dsa_s[p] + da
            dga = scaled(dsa, th).astype(BF16)
            km = both(k[p, rows, :])
            dw = nn(km, dga)
            dsc = dsc_s[p] + dc
            dgc = scaled(dsc, th).astype(BF16)
            ab, cb = a_all[n, p], c_all[n, p]
            pre = pre_all[n, p]
            sig = sigmoid(pre)
            act = pre * sig
            actb = act.astype(BF16)
            slope = sig + act * (1.0 - sig)
            sigk, prek, slopek = sig[PAIR:], pre[PAIR:], slope[PAIR:]
            yield
            du = (dw * slopek).astype(BF16)
            de = joined(nt(jnp.concatenate([actb[PAIR:], du], axis=1), jnp.concatenate([dgc, cb], axis=1)))
            rm = both((bmp[p, rows, :].astype(F32) * gate[p, rows, :]).astype(BF16))
            dpre_q = (nn(rm, cb) * slope[:PAIR]).astype(BF16)
            u = u_all[n, p].astype(F32)
            curve = sigk * (1.0 - sigk) * (2.0 + prek * (1.0 - 2.0 * sigk))
            yield
            em = both(e_all[p, rows, :])
            dem = both(de.astype(BF16))
            dsk = nn(jnp.concatenate([em, dem], axis=1), jnp.concatenate([dgc, cb], axis=0))
            mv[p, rows, :] = de
            mq[p, rows, :] = joined(nt(dpre_q, ab))
            gc = tn(jnp.concatenate([em, dem], axis=0), jnp.concatenate([du, actb[PAIR:]], axis=0)) + tn(rm, actb[:PAIR])
            yield
            wgt = (u * slopek).astype(BF16)
            dpre = (dsk * slopek + dw * u * curve).astype(BF16)
            ga = tn(jnp.concatenate([km, both(q[p, rows, :])], axis=0), jnp.concatenate([dpre, dpre_q], axis=0))
            mk[p, rows, :] = joined(nt(jnp.concatenate([wgt, dpre], axis=1), jnp.concatenate([dga, ab], axis=1)))
            yield
            dc = scaled(dc, al) + gc
            dsecond[p] = dsecond[p] + jnp.where(fresh, dc, 0.0)
            dc_s[p] = jnp.where(fresh, 0.0, dc)
            dsc_s[p] = jnp.where(fresh, 0.0, scaled(dsc, eta))
            da = scaled(da, al) + ga
            dfirst[p] = dfirst[p] + jnp.where(fresh, da, 0.0)
            da_s[p] = jnp.where(fresh, 0.0, da)
            dsa_s[p] = jnp.where(fresh, 0.0, scaled(dsa, eta))

        def attention_unit(qb, head):
            p, side = head // 2, head % 2
            rows = pl.ds(qb * ROWS, ROWS)
            qh = keep(q[p, rows, :], side) * jnp.asarray(scale, BF16)
            gh = keep(bmp[p, rows, :], side)
            lrow, drow = lse[head, :, rows], dd[head, :, rows]
            acc = jnp.zeros((HEAD_DIM, ROWS), F32)
            for kb in range(qb + 1):
                krows = slice(kb * ROWS, (kb + 1) * ROWS)
                s = nt(k[p, krows, :], qh)
                dprob = nt(v[p, krows, :], gh)
                yield
                s = s - lrow
                s = s + diagonal[...] if kb == qb else earlier(s, starts, kb, qb, per)
                prob = jnp.exp(s)
                ds = (prob * (dprob - drow)).astype(BF16)
                yield
                dvs[p, krows, :] = dvs[p, krows, :] + nn(prob.astype(BF16), gh)
                dks[p, krows, :] = dks[p, krows, :] + nn(ds, qh)
                acc = acc + nn(kt[head, :, krows], ds)
                yield
            prob = jnp.exp(nt(pk[p], qh) - lrow)
            ds = (prob * (nt(pv[p], gh) - drow)).astype(BF16)
            dpv[p] = dpv[p] + nn(prob.astype(BF16), gh)
            dpk[p] = dpk[p] + nn(ds, qh)
            acc = acc + nn(pkt[head], ds)
            dqt[head, :, rows] = acc * scale

        def fold(ref, begin, value):
            rows = value.shape[0] // 2
            ref[begin:begin + rows, :wide] = value[:rows].astype(BF16)
            ref[begin:begin + rows, wide:] = value[rows:].astype(BF16)

        src_b[:rest, :] = facc[rows_a:, :]
        fold(src_b, rest, tn(h1[...], dg[...]))

        def background(point):
            if point in (1, 4, 7):
                sum_a.step()
            if point == 3:
                second_copy(0).wait()
                lo[...] = (own_s[...] + second_r[...].astype(F32)).astype(BF16)
                spread(rec_l, dp, t, t, lo, l_sems, ALL_PEERS)
            if point == 4:
                second_copy(1).wait()
                src_b[rest + wide:, :] = (gout[...] + gother_r[...].astype(F32)).astype(BF16)
            if point in (4, 5, 7):
                sum_b.step()
            if point == 7:
                pass_on(rec_l, dp, t, lo, l_sems, ly_sems, ALL_PEERS)

        for qb in reversed(range(nblocks)):
            fill_diagonal(diagonal, starts[qb * per])

            def run(i, _, qb=qb):
                weave([memory_step(qb * per + per - 1 - i, p) for p in range(pairs)], attention_unit(qb, i), (3 * qb + 6) // 4, qb > 1)
                return 0

            for part in range(2):
                background((nblocks - 1 - qb) * 2 + part)
                lax.fori_loop(part * per // 2, (part + 1) * per // 2, run, 0)
        for b in range(nblocks):
            rows = pl.ds(b * ROWS, ROWS)
            for p in range(pairs):
                cols = slice(p * PAIR, (p + 1) * PAIR)
                got = jnp.concatenate([dqt[2 * p, :, rows], dqt[2 * p + 1, :, rows]], axis=0)
                dq[rows, cols] = (jnp.transpose(got) + mq[p, rows, :]).astype(BF16)
                dk[rows, cols] = (dks[p, rows, :] + mk[p, rows, :]).astype(BF16)
                dv[rows, cols] = (dvs[p, rows, :] - mv[p, rows, :]).astype(BF16)
        made = tn(h1[...], jnp.concatenate([dq[...], dk[...], dv[...]], axis=1))
        for i in range(3):
            fold(src_c, i * wide, made[:, i * wide:(i + 1) * wide])
        at = 3 * wide
        src_c[at + PAIR:, :] = jnp.zeros((src_c.shape[0] - at - PAIR, width), BF16)
        for i in range(4):
            lanes = slice(i * PAIR, (i + 1) * PAIR)
            src_c[at:at + PAIR, lanes] = (dfirst, dsecond)[i // 2][i % 2].astype(BF16)
            src_c[at + PAIR:at + PAIR + few, lanes] = (dpk, dpv)[i // 2][i % 2].astype(BF16)

        def step_c():
            sum_c1.step()
            sum_c2.step()

        step_c()

        for b in range(nblocks):
            rows = pl.ds(b * ROWS, ROWS)
            result = nt(dq[rows, :], wq[...])
            for back, w in ((dk, wk), (dv, wv), (dg, wg)):
                result = result + nt(back[rows, :], w[...])
            facc[rows, :] = result.astype(BF16)

        def partial(rows):
            return nn(gt[rows, :], facc[:count, :])

        column = lax.div(dp, 2) % 2
        quarter = half // 4
        places = []
        for b0, b1 in ((0, 0), (0, 1), (1, 0), (1, 1)):
            c, x = core + b0 * (1 - 2 * core), column + b1 * (1 - 2 * column)
            places.append(c * (2 * quarter) + x * quarter)

        def part_copy(i):
            here = at_rows(places[i], quarter)
            return remote(part_s.at[here], part_r.at[here], y_sems.at[0, 2 + i], y_sems.at[1, 2 + i], other)

        for i, begin in enumerate(places):
            part_s[at_rows(begin, quarter), :] = partial(at_rows((1 - t) * half + begin, quarter)).astype(BF16)
            part_copy(i).start()
            if i == 0:
                sum_a.step()
            if i == 2:
                sum_b.step()
        step_c()
        owns = [partial(at_rows(t * half + begin, quarter)) for begin in places]
        sum_a.step()
        sum_b.step()
        asks = asked[:, 0, :]
        asks_high = jnp.floor(asks * (1.0 / 32.0))
        asks_low = asks - 32.0 * asks_high
        slot = iota(PAIR, count, 1)
        rank = lax.div(slot, half) * HALF_SHARE + slot % HALF_SHARE
        pick = jnp.where(iota(PAIR, count, 0) == rank, 1.0, 0.0).astype(BF16)
        slot = iota(PEERS, count, 1)
        mine = lot(iota(PEERS, count, 0)) == lax.div(slot % half, HALF_SHARE)
        spread_out = 32.0 * nn(asks_high.astype(BF16), pick) + nn(asks_low.astype(BF16), pick)
        row = jnp.sum(jnp.where(mine, spread_out, 0.0), axis=0, keepdims=True)
        for c in range(count // ROWS):
            g[c * ROWS:(c + 1) * ROWS, :] = jnp.where((iota(ROWS, count, 0) + c * ROWS).astype(F32) == row, 1.0, 0.0).astype(BF16)
        mgain = jnp.zeros((8, width), F32)
        for i, begin in enumerate(places):
            part_copy(i).wait()
            for b in range(quarter // STRETCH):
                few_rows = at_rows(begin + b * STRETCH, STRETCH)
                back = owns[i][b * STRETCH:(b + 1) * STRETCH] + part_r[few_rows, :].astype(F32)
                x = xs[at_rows(t * half + begin + b * STRETCH, STRETCH), :].astype(F32)
                factor = lax.rsqrt(jnp.mean(x * x, axis=-1, keepdims=True) + EPSILON)
                norm = x * factor
                inner = back * gain1[...]
                bx[few_rows, :] = (
                    br[few_rows, :] + factor * (inner - norm * jnp.mean(inner * norm, axis=-1, keepdims=True))
                ).astype(BF16)
                mgain = mgain + jnp.sum((back * norm).reshape(STRETCH // 8, 8, width), axis=0)
            spread(rec_x, dp, t, t, bx, x_sems, QUARTERS[i])
            if i > 1:
                pass_on(rec_x, dp, t, bx, x_sems, xy_sems, QUARTERS[i - 2])
            if i == 1:
                step_c()
                sum_b.step()
        gains_s[0, 0] = mgain
        gains_s[0, 1] = dgain[...]
        c2 = lax.div(dp, 4)
        groups = [[other], [(flipped(dp, 1), t)], [(flipped(dp, 2), t)], [(dp + 4 * ((c2 + i) % 4 - c2), t) for i in (1, 2, 3)]]
        gain_copies = []

        def gain_step(i):
            if i:
                for copy in gain_copies:
                    copy.wait()
                gain_copies.clear()
                value = gains_s[i - 1]
                for j in range(len(groups[i - 1])):
                    value = value + gains_r[i - 1 + j]
                gains_s[i] = value
            if i < 4:
                for j, peer in enumerate(groups[i]):
                    copy = remote(gains_s.at[i], gains_r.at[i + j], g_sems.at[0, i, j], g_sems.at[1, i, j], peer)
                    copy.start()
                    gain_copies.append(copy)

        writes = [pltpu.make_async_copy(src, dst, o_sems.at[i]) for i, (src, dst) in enumerate((
            (cs, ret.at[0]), (xs, ret.at[1]), (gains_s.at[4], gains_out), (out_a, fa_out), (out_b, fb_out), (out_c1, qa_out), (out_c2, qb_out),
        ))]
        gain_step(0)
        sum_b.step()
        sum_a.step()
        step_c()
        pass_on(rec_x, dp, t, bx, x_sems, xy_sems, QUARTERS[2])
        gain_step(1)
        passed_on(rec_l, dp, t, ly_sems)
        cs[...] = nn(g[...], rec_l[...]).astype(BF16)
        writes[0].start()
        pass_on(rec_x, dp, t, bx, x_sems, xy_sems, QUARTERS[3])
        gain_step(2)
        mine_rows, other_rows = at_rows(t * half, half), at_rows((1 - t) * half, half)
        mine_part = nn(g[:, mine_rows], rec_x[mine_rows, :])
        step_c()
        sum_b.step()
        sum_a.step()
        writes[3].start()
        gain_step(3)
        passed_on(rec_x, dp, t, xy_sems)
        xs[...] = (mine_part + nn(g[:, other_rows], rec_x[other_rows, :])).astype(BF16)
        writes[1].start()
        gain_step(4)
        writes[2].start()
        step_c()
        sum_b.step()
        writes[4].start()
        step_c()
        writes[5].start()
        writes[6].start()
        for write in writes:
            write.wait()

    flat = pltpu.VMEM((pairs, count, PAIR), F32)
    state = pltpu.VMEM((pairs, PAIR, PAIR), F32)
    tall = pltpu.VMEM((count, wide), BF16)
    pl.run_scoped(
        backward, pltpu.VMEM((heads, HEAD_DIM, count), F32), flat, flat, flat, flat, flat, pltpu.VMEM((heads, 1, count), F32),
        pltpu.VMEM((pairs, few, PAIR), F32), pltpu.VMEM((pairs, few, PAIR), F32), state, state,
        tall, tall,
    )


def mega(starts, rates, idx, tokens, cotangent, gain1, wq, wk, wv, wg, op, pk, pv, first, second, gain2, dg, dl, dd):
    count, width = tokens.shape
    half = count // 2
    wide = wq.shape[1]
    pairs = wide // PAIR
    heads = 2 * pairs
    few = pk.shape[0]
    steps = starts.shape[0]
    padded = -(-dg.shape[0] // 256) * 256
    rows_a = 2 * padded
    rows_b = padded + 2 * wide
    rows_c = 3 * wide
    rows_d = -(-(PAIR + few) // 256) * 256
    low = lambda *dims: pltpu.VMEM(dims, BF16)
    full = lambda *dims: pltpu.VMEM(dims, F32)
    sems = pltpu.SemaphoreType.DMA((2, PEERS))
    dma = pltpu.SemaphoreType.DMA
    square = low(count, count)
    state = full(pairs, PAIR, PAIR)
    args = (starts, rates, idx, tokens, cotangent, gain1, wq, wk, wv, wg, op, pk, pv, first, second, gain2, dg, dl, dd)
    return pl.pallas_call(
        mega_kernel,
        out_shape=(
            shape(rows_a, width, dtype=BF16), shape(rows_b, width, dtype=BF16), shape(rows_c, width, dtype=BF16), shape(rows_d, width, dtype=BF16),
            shape(2, 8, width), shape(2, count, width, dtype=BF16),
        ),
        in_specs=[ANY if n in (3, 4, 6, 7, 8, 9, 10, 16, 17, 18) else SMEM if n < 2 else VMEM for n in range(len(args))],
        out_specs=[ANY] * 6,
        scratch_shapes=[
            low(count, width), low(count, width), low(2, count, wide), low(2, *op.shape), full(PEERS, 8, PAIR), full(PEERS, 8, PAIR),
            low(2, half, width), square, square, low(count, width), low(pairs, count, PAIR), low(pairs, count, PAIR), low(pairs, count, PAIR),
            full(pairs, count, PAIR), full(pairs, count, PAIR), low(heads, HEAD_DIM, count), full(heads, 1, count),
            low(steps, pairs, PAIR, PAIR), low(steps, pairs, PAIR, PAIR), full(steps, pairs, 2 * PAIR, PAIR), low(pairs, count, PAIR),
            low(steps, pairs, PAIR, PAIR), low(pairs, count, PAIR),
            low(pairs, few, PAIR), low(pairs, few, PAIR), low(heads, HEAD_DIM, few), low(heads, HEAD_DIM, few), low(pairs, count, PAIR),
            full(ROWS, ROWS), full(half, width), full(half, width), low(half, width), low(half, width), low(count, wide),
            low(3 * padded, width), full(wide, width), low(wide, width), full(8, width),
            low(half, width), low(wide, width), low(count, width), low(count, width), low(half, width),
            low(rows_b, width), low(rows_c + rows_d, width), low(rows_a, width), low(rows_b, width), low(rows_c, width), low(rows_d, width),
            full(5, 2, 8, width), full(6, 2, 8, width),
            state, state, state, state, *[low(*weight.shape) for weight in (wq, wk, wv, wg, op, dg, dl, dd)],
            dma((10,)), sems, sems, sems, dma((2, 2, PEERS)), dma((2, 8)), dma((2, 4)), dma((2, 6)), sems, sems, sems, sems, dma((2, 4, 3)), dma((7,)),
            *Sum.scratch(rows_a, width, SUM_ORDERS[0]), *Sum.scratch(rows_b, width, SUM_ORDERS[1]),
            *Sum.scratch(rows_c, width, SUM_ORDERS[2]), *Sum.scratch(rows_d, width, SUM_ORDERS[3]),
        ],
        compiler_params=pltpu.CompilerParams(collective_id=0, has_side_effects=True, vmem_limit_bytes=62 * 1024 * 1024),
        name="block",
    )(*args)


def finish_kernel(
    fa, fb, qa, qb, gains, ret, lo, bx, mgain, gq, gk, gv, gg, gout, gpk, gpv, first, second, dgain, ggate, glift, gdown,
    fa_s, fb_s, qa_s, qb_s, ret_s, wide_s, tall_s, out_s, state_s, in_sems, out_sems,
):
    hidden, width = ggate.shape
    wide = gq.shape[1]
    few = gpk.shape[0]
    padded = -(-hidden // 256) * 256
    moves = []
    reads = [
        pltpu.make_async_copy(src, dst, in_sems.at[i])
        for i, (src, dst) in enumerate(((fa, fa_s), (fb, fb_s), (ret, ret_s), (qa, qa_s), (qb, qb_s)))
    ]
    for copy in reads:
        copy.start()

    def send(src, dst):
        moves.append(pltpu.make_async_copy(src, dst, out_sems.at[len(moves)]))
        moves[-1].start()

    def square(n, src, begin, ref):
        rows = src[begin:begin + wide, :].astype(F32)
        tall_s[n, :wide, :] = rows[:, :wide]
        tall_s[n, wide:, :] = rows[:, wide:]
        send(tall_s.at[n], ref)

    mgain[...] = jnp.sum(gains[0], axis=0, keepdims=True)
    dgain[...] = jnp.sum(gains[1], axis=0, keepdims=True)
    reads[0].wait()
    for n, ref in enumerate((ggate, glift)):
        wide_s[n] = fa_s[n * padded:n * padded + hidden, :].astype(F32)
        send(wide_s.at[n], ref)
    reads[1].wait()
    wide_s[2] = fb_s[:hidden, :].astype(F32)
    send(wide_s.at[2], gdown)
    square(3, fb_s, padded, gg)
    out_s[...] = fb_s[padded + wide:, :].astype(F32)
    send(out_s, gout)
    reads[2].wait()
    send(ret_s.at[0], lo)
    send(ret_s.at[1], bx)
    reads[3].wait()
    for n, ref in enumerate((gq, gk, gv)):
        square(n, qa_s, n * wide, ref)
    reads[4].wait()
    for n in range(4):
        lanes = slice(n * PAIR, (n + 1) * PAIR)
        state_s[n] = qb_s[:PAIR, lanes].astype(F32)
        (gpk, gpv)[n // 2][:, (n % 2) * PAIR:(n % 2 + 1) * PAIR] = qb_s[PAIR:PAIR + few, lanes].astype(F32)
    send(state_s.at[:2], first)
    send(state_s.at[2:], second)
    for copy in moves:
        copy.wait()


def finish(fa, fb, qa, qb, gains, ret, hidden, wide, few):
    count, width = ret.shape[1:]
    pairs = wide // PAIR
    rows = shape(count, width, dtype=BF16)
    square = shape(width, wide)
    state = shape(pairs, PAIR, PAIR)
    outs = (
        rows, rows, shape(1, width), square, square, square, square, shape(wide, width), shape(few, wide), shape(few, wide),
        state, state, shape(1, width), shape(hidden, width), shape(hidden, width), shape(hidden, width),
    )
    small = (2, 8, 9, 12)
    return pl.pallas_call(
        finish_kernel,
        out_shape=outs,
        in_specs=[ANY] * 4 + [VMEM, ANY],
        out_specs=[VMEM if n in small else ANY for n in range(len(outs))],
        scratch_shapes=[
            pltpu.VMEM(fa.shape, BF16), pltpu.VMEM(fb.shape, BF16), pltpu.VMEM(qa.shape, BF16), pltpu.VMEM(qb.shape, BF16), pltpu.VMEM(ret.shape, BF16),
            pltpu.VMEM((3, hidden, width), F32), pltpu.VMEM((4, width, wide), F32), pltpu.VMEM((wide, width), F32),
            pltpu.VMEM((4, PAIR, PAIR), F32), pltpu.SemaphoreType.DMA((5,)), pltpu.SemaphoreType.DMA((12,)),
        ],
        compiler_params=pltpu.CompilerParams(vmem_limit_bytes=LIMIT),
        name="finish",
    )(fa, fb, qa, qb, gains, ret)


def block_body(
    tokens, cotangent, source_index, tract_starts, memory_rates, mixer_gain, query_proj, key_proj, value_proj, gate_proj,
    out_proj, persist_keys, persist_values, memory_first, memory_second, dense_gain, dense_gate, dense_lift, dense_down,
):
    pairs = query_proj.shape[1] // PAIR
    first = memory_first.reshape(pairs, PAIR, PAIR)
    second = memory_second.transpose(0, 2, 1).reshape(pairs, PAIR, PAIR)
    summed = mega(
        tract_starts, memory_rates.transpose(0, 2, 1), source_index.reshape(1, -1), tokens, cotangent, mixer_gain[None],
        query_proj, key_proj, value_proj, gate_proj, out_proj, persist_keys, persist_values, first, second,
        dense_gain[None], dense_gate.T, dense_lift.T, dense_down,
    )
    outs = list(finish(*summed, dense_gate.shape[1], query_proj.shape[1], persist_keys.shape[0]))
    outs[2] = outs[2][0]
    outs[10] = outs[10].reshape(memory_first.shape)
    outs[11] = outs[11].reshape(memory_first.shape).transpose(0, 2, 1)
    outs[12] = outs[12][0]
    outs[13], outs[14] = outs[13].T, outs[14].T
    return tuple(outs)


def body(
    tokens,
    cotangent,
    source_index,
    tract_starts,
    memory_rates,
    mixer_gain,
    query_proj,
    key_proj,
    value_proj,
    gate_proj,
    out_proj,
    persist_keys,
    persist_values,
    memory_first,
    memory_second,
    dense_gain,
    dense_gate,
    dense_lift,
    dense_down,
):
    count = tokens.shape[0]
    width = tokens.shape[1]
    peers = lax.axis_size("dp")
    share = count // peers
    arrival = jnp.argsort(source_index)
    wanted = (source_index[arrival] % count).reshape(peers, share)
    asked = lax.all_to_all(wanted, "dp", split_axis=0, concat_axis=0, tiled=True).reshape(count)
    got_tokens, got_cot = (
        lax.all_to_all(
            tokens[asked].reshape(peers, share, width),
            "dp",
            split_axis=0,
            concat_axis=0,
            tiled=True,
        ),
        lax.all_to_all(
            cotangent[asked].reshape(peers, share, width),
            "dp",
            split_axis=0,
            concat_axis=0,
            tiled=True,
        ),
    )
    placing = jnp.argsort(arrival)
    seq_tokens = got_tokens.reshape(count, width)[placing]
    seq_cot = got_cot.reshape(count, width)[placing]
    seq_x = seq_tokens.astype(jnp.float32)
    first_norm, factor_one = norm_forward(seq_x)
    pairs = query_proj.shape[1] // PAIR
    by_pair = lambda value: value.reshape(-1, pairs, PAIR).transpose(1, 0, 2)
    by_head = lambda value: value.T.reshape(2 * pairs, HEAD_DIM, -1)
    weights = jnp.concatenate([query_proj, key_proj, value_proj, gate_proj], axis=1)
    pk, pv = by_pair(persist_keys), by_pair(persist_values)
    first = memory_first.reshape(pairs, PAIR, PAIR)
    second = memory_second.transpose(0, 2, 1).reshape(pairs, PAIR, PAIR)
    h_one, query, keys, values, gate, recall, mixed, keys_t, lse, a_all, c_all, pre_all, e_all, u_all, attended = mixer_forward(
        tract_starts, memory_rates, seq_tokens, mixer_gain[None], weights, pk, by_head(persist_values), first, second
    )
    first_out = lax.psum(product(mixed, out_proj), "tensor")
    resid = seq_x + first_out
    norm_two, factor_two = norm_forward(resid)
    h_two = (norm_two * dense_gain).astype(jnp.bfloat16)
    gated = product(h_two, dense_gate)
    lifted = product(h_two, dense_lift)
    sigma = jax.nn.sigmoid(gated)
    active = gated * sigma
    hidden = (active * lifted).astype(jnp.bfloat16)
    second_out = lax.psum(product(hidden, dense_down).astype(jnp.bfloat16), "tensor").astype(
        jnp.float32
    )
    seq_out = (resid + second_out).astype(jnp.bfloat16)
    grad_down = product(hidden.T, seq_cot)
    back_hidden = product(seq_cot, dense_down.T)
    back_gated = (back_hidden * lifted * (sigma + gated * sigma * (1.0 - sigma))).astype(
        jnp.bfloat16
    )
    back_lifted = (back_hidden * active).astype(jnp.bfloat16)
    grad_gate = product(h_two.T, back_gated)
    grad_lift = product(h_two.T, back_lifted)
    back_two = lax.psum(
        product(back_gated, dense_gate.T) + product(back_lifted, dense_lift.T), "tensor"
    )
    back_norm_two, grad_dgain = norm_backward(back_two, norm_two, factor_two, dense_gain)
    residual_gradient = seq_cot.astype(jnp.float32) + back_norm_two
    back_first = residual_gradient.astype(jnp.bfloat16)
    grad_out = product(mixed.T, back_first)
    back_mixed = product(back_first, out_proj.T).astype(jnp.bfloat16)
    back_query, back_keys, cotangent_payloads, back_gate, grad_pk, grad_pv, grad_first, grad_second = mixer_backward(
        tract_starts, memory_rates, back_mixed, query, keys, values, gate, recall, keys_t, pk, by_head(persist_keys), pv,
        lse, a_all, c_all, pre_all, e_all, u_all, attended,
    )
    grad_first = grad_first.reshape(memory_first.shape)
    grad_second = grad_second.reshape(memory_first.shape).transpose(0, 2, 1)
    grad_query = product(h_one.T, back_query)
    grad_key = product(h_one.T, back_keys)
    grad_value = product(h_one.T, cotangent_payloads)
    grad_gproj = product(h_one.T, back_gate)
    back_one = lax.psum(
        product(back_query, query_proj.T)
        + product(back_keys, key_proj.T)
        + product(cotangent_payloads, value_proj.T)
        + product(back_gate, gate_proj.T),
        "tensor",
    )
    back_norm_one, grad_mgain = norm_backward(back_one, first_norm, factor_one, mixer_gain)
    back_x = (residual_gradient + back_norm_one).astype(jnp.bfloat16)
    grad_pkeys = grad_pk.transpose(1, 0, 2).reshape(persist_keys.shape)
    grad_pvalues = grad_pv.transpose(1, 0, 2).reshape(persist_values.shape)
    (
        grad_mgain,
        grad_query,
        grad_key,
        grad_value,
        grad_gproj,
        grad_out,
        grad_pkeys,
        grad_pvalues,
        grad_first,
        grad_second,
        grad_dgain,
        grad_gate,
        grad_lift,
        grad_down,
    ) = lax.psum(
        (
            grad_mgain,
            grad_query,
            grad_key,
            grad_value,
            grad_gproj,
            grad_out,
            grad_pkeys,
            grad_pvalues,
            grad_first,
            grad_second,
            grad_dgain,
            grad_gate,
            grad_lift,
            grad_down,
        ),
        "dp",
    )
    ret_out, ret_grad = (
        lax.all_to_all(
            seq_out[arrival].reshape(peers, share, width),
            "dp",
            split_axis=0,
            concat_axis=0,
            tiled=True,
        ),
        lax.all_to_all(
            back_x[arrival].reshape(peers, share, width),
            "dp",
            split_axis=0,
            concat_axis=0,
            tiled=True,
        ),
    )
    undo = jnp.argsort(asked)
    layer_output = ret_out.reshape(count, width)[undo]
    input_grad = ret_grad.reshape(count, width)[undo]
    return (
        layer_output,
        input_grad,
        grad_mgain,
        grad_query,
        grad_key,
        grad_value,
        grad_gproj,
        grad_out,
        grad_pkeys,
        grad_pvalues,
        grad_first,
        grad_second,
        grad_dgain,
        grad_gate,
        grad_lift,
        grad_down,
    )


def solution(mesh):
    chosen = block_body if mesh.shape["dp"] == PEERS else body
    in_specs = (
        P("dp", None),
        P("dp", None),
        P("dp"),
        P("dp"),
        P(None, "dp", "tensor"),
        P(),
        P(None, "tensor"),
        P(None, "tensor"),
        P(None, "tensor"),
        P(None, "tensor"),
        P("tensor", None),
        P(None, "tensor"),
        P(None, "tensor"),
        P("tensor", None, None),
        P("tensor", None, None),
        P(),
        P(None, "tensor"),
        P(None, "tensor"),
        P("tensor", None),
    )
    out_specs = (
        P("dp", None),
        P("dp", None),
        P(),
        P(None, "tensor"),
        P(None, "tensor"),
        P(None, "tensor"),
        P(None, "tensor"),
        P("tensor", None),
        P(None, "tensor"),
        P(None, "tensor"),
        P("tensor", None, None),
        P("tensor", None, None),
        P(),
        P(None, "tensor"),
        P(None, "tensor"),
        P("tensor", None),
    )
    return jax.shard_map(chosen, mesh=mesh, in_specs=in_specs, out_specs=out_specs, check_vma=False)
```
